32 devices in a mesh: batch: 8 (over z, x), head: 4 (over y, core).
Axes of the slice: x: 2, y: 2, z: 4, core: 2. Of those that a mesh axis runs over, the one named last changes fastest.
Arguments:
- hidden_in: bfloat16 [8, 2048, 1024], P('batch', None, 'head'), may hold values from -6 to 6
- cotangent: bfloat16 [8, 2048, 1024], P('batch', None, 'head'), may hold values from -6 to 6
- doc_ids: int32 [8, 2048], P('batch'), may hold values from 0 to 5, never falling along the last dimension, each value on 1 to 1024 neighbouring positions
- lengths: int32 [8], P('batch'), may hold values from 1536 to 2048
- w_query: bfloat16 [1024, 1024], P(None, 'head'), may hold values from -0.1875 to 0.1875
- w_key: bfloat16 [1024, 1024], P(None, 'head'), may hold values from -0.1875 to 0.1875
- w_value: bfloat16 [1024, 1024], P(None, 'head'), may hold values from -0.1875 to 0.1875
- w_out: bfloat16 [1024, 1024], P('head'), may hold values from -0.1875 to 0.1875
- w_up: bfloat16 [1024, 4096], P(None, 'head'), may hold values from -0.1875 to 0.1875
- w_gate: bfloat16 [1024, 4096], P(None, 'head'), may hold values from -0.1875 to 0.1875
- w_down: bfloat16 [4096, 1024], P('head'), may hold values from -0.09375 to 0.09375
- scale_qk: float32 [1024], P('head'), may hold values from 0.7 to 1.5
- scale_up: float32 [4096], P('head'), may hold values from 0.25 to 1.75
- scale_gate: float32 [4096], P('head'), may hold values from 0.5 to 2
- alpha_attn: float32 [1024], replicated, may hold values from 0.05 to 0.6
- alpha_ffn: float32 [1024], replicated, may hold values from 0.15 to 0.6
Outputs:
- hidden_out: bfloat16 [8, 2048, 1024], P('batch', None, 'head')
- grad_hidden: float32 [8, 2048, 1024], P('batch', None, 'head')
- grad_query: float32 [1024, 1024], P(None, 'head')
- grad_key: float32 [1024, 1024], P(None, 'head')
- grad_value: float32 [1024, 1024], P(None, 'head')
- grad_out: float32 [1024, 1024], P('head')
- grad_up: float32 [1024, 4096], P(None, 'head')
- grad_gate: float32 [1024, 4096], P(None, 'head')
- grad_down: float32 [4096, 1024], P('head')
- grad_scale_qk: float32 [1024], P('head')
- grad_scale_up: float32 [4096], P('head')
- grad_scale_gate: float32 [4096], P('head')
- grad_alpha_attn: float32 [1024], P('head')
- grad_alpha_ffn: float32 [1024], P('head')
The draws below stay inside these ranges and needn't reach their ends.
Inputs may be any that keep to these rules, and one draw needn't show every extreme that they name: `doc_ids`: document number of each slot: never falls along a row, each document holds 1 to 1024 slots, one exactly 1024, all 6 present. `lengths`: slots at or past the length are padding.
All inputs are finite; a program needn't handle non-finite values.
Results may differ from the reference program's by a relative error of at most 0.025.
Values may be sent and summed in bfloat16 or wider, within the bound.
No kernel may reach another device: no remote copies, remote signals or barrier semaphores. Data moves between devices by JAX's collectives and lax.ppermute only.
A program may use at most 256 MiB of HBM per device.

```python
import math
import jax
import jax.numpy as jnp
import numpy as np
from jax import lax

D = 1024
HEADS = 16
HD = 64
FF = 4096
ROW = 2048
DOCS = 6
ROWS = 8
N_HEAD = 4


def with_ends(array, own_key, least, largest):
    dims = array.shape
    spot = [jax.random.randint(jax.random.fold_in(own_key, axis), (), 0, dims[axis]) for axis in range(len(dims))]
    array = array.at[tuple(spot)].set(least)
    longest = dims.index(max(dims))
    spot[longest] = (spot[longest] + 1) % dims[longest]
    return array.at[tuple(spot)].set(largest)


def level_of(key, extent, split, low, high):
    def one(dim, shards_of):
        heights = jax.random.uniform(jax.random.fold_in(jax.random.fold_in(key, 6), dim), (shards_of,), jnp.float32, low / len(split), high / len(split))
        return jnp.repeat(jnp.exp(heights), extent[dim] // shards_of).reshape((-1,) + (1,) * (len(extent) - dim - 1))

    level = one(*split[0])
    for cut in split[1:]:
        level = level * one(*cut)
    return level


def split_up(number_of, total, bound, skew):
    portions = [(1 << 20) // math.isqrt(rank ** skew) + 1 for rank in range(2, number_of + 1)]
    spare, counts = total - bound - (number_of - 1), [1] * (number_of - 1)
    while spare > 0:
        candidates = [i for i in range(number_of - 1) if counts[i] < bound]
        whole, left = sum([portions[i] for i in candidates]), spare
        for i in candidates:
            more = min(bound - counts[i], max(1, left * portions[i] // whole), spare)
            counts[i] = counts[i] + more
            spare = spare - more
    return np.array([bound] + counts)


def uneven(stream_key, amount, total, bound, slope):
    if amount == 2:
        one = jax.random.randint(stream_key, (), max(1, total - bound), min(bound, total - 1) + 1)
        return jnp.stack([one, total - one])
    tallies = jnp.asarray(split_up(amount, total, bound, slope), jnp.int32)
    twos = (amount - 1) // 2
    source_of, taker = tallies[1:1 + 2 * twos:2], tallies[2:2 + 2 * twos:2]
    margin = jnp.minimum(source_of - 1, bound - taker)
    passed = jax.random.randint(jax.random.fold_in(stream_key, 1), (twos,), 0, 1 << 20) % (margin + 1)
    tallies = tallies.at[1:1 + 2 * twos:2].set(source_of - passed).at[2:2 + 2 * twos:2].set(taker + passed)
    return tallies[jax.random.permutation(jax.random.fold_in(stream_key, 2), amount)]


def centred(key, dims, width, most, cuts=(), held_as=jnp.bfloat16):
    drawn = width * jax.random.normal(key, dims, jnp.float32)
    if cuts:
        drawn = drawn * level_of(key, dims, cuts, -0.22, 0.18)
    return jnp.clip(drawn, -most, most).astype(held_as)


def setup_inputs(seed: int = 0) -> dict:
    streams_of = jax.random.split(jax.random.key(seed), 17)
    return {
        "hidden_in": centred(streams_of[0], (ROWS, ROW, D), 1.0, 6.0, ((0, 8), (2, 4))),
        "cotangent": centred(streams_of[1], (ROWS, ROW, D), 1.0, 6.0, ((0, 8), (2, 4))),
        "doc_ids": jax.vmap(lambda own: jnp.searchsorted(jnp.cumsum(uneven(own, DOCS, ROW, ROW // 2, 1)), jnp.arange(ROW), side="right"))(jax.random.split(streams_of[2], ROWS)).reshape((ROWS, ROW)).astype(jnp.int32),
        "lengths": with_ends(jax.random.randint(streams_of[3], (ROWS,), ROW - ROW // 4, ROW + 1), jax.random.fold_in(streams_of[3], 1), ROW - ROW // 4, ROW).astype(jnp.int32),
        "w_query": centred(streams_of[4], (D, D), D ** -0.5, 0.1875, ((1, 4),)),
        "w_key": centred(streams_of[5], (D, D), D ** -0.5, 0.1875, ((1, 4),)),
        "w_value": centred(streams_of[6], (D, D), D ** -0.5, 0.1875, ((1, 4),)),
        "w_out": centred(streams_of[7], (D, D), D ** -0.5, 0.1875, ((0, 4),)),
        "w_up": centred(streams_of[8], (D, FF), D ** -0.5, 0.1875, ((1, 4),)),
        "w_gate": centred(streams_of[9], (D, FF), D ** -0.5, 0.1875, ((1, 4),)),
        "w_down": centred(streams_of[10], (FF, D), FF ** -0.5, 0.09375, ((0, 4),)),
        "scale_qk": jnp.clip(jnp.exp(math.log(1.5) - 0.7621401 * jax.random.uniform(streams_of[11], (D,), jnp.float32) ** level_of(streams_of[11], (D,), ((0, 4),), -0.2, 0.2)), 0.7, 1.5),
        "scale_up": jnp.clip(1.0 + 0.15 * jax.random.normal(streams_of[12], (FF,), jnp.float32), 0.25, 1.75),
        "scale_gate": jnp.clip(jnp.exp(math.log(2.0) - 1.3862944 * jax.random.uniform(streams_of[13], (FF,), jnp.float32) ** level_of(streams_of[13], (FF,), ((0, 4),), -0.2, 0.2)), 0.5, 2.0),
        "alpha_attn": jnp.clip(jnp.exp(jax.random.uniform(streams_of[14], (D,), jnp.float32, math.log(0.05), math.log(0.6))), 0.05, 0.6),
        "alpha_ffn": jnp.clip(jnp.exp(jax.random.uniform(streams_of[15], (D,), jnp.float32, math.log(0.15), math.log(0.6))), 0.15, 0.6),
    }


@jax.custom_vjp
def low(v):
    return lax.optimization_barrier(v.astype(jnp.bfloat16)).astype(jnp.float32)

@jax.custom_vjp
def low_back(v):
    return v

def low_keep(v):
    return (low(v), None)

def low_pass(kept, grad):
    return (grad,)

def back_keep(v):
    return (v, None)

def back_low(kept, grad):
    return (low(grad),)
low.defvjp(low_keep, low_pass)
low_back.defvjp(back_keep, back_low)
EPSILON = 1e-06
PRECISE = lax.Precision.HIGHEST

def matmul(left_side, right_side):
    return jnp.dot(left_side, right_side, precision=PRECISE, preferred_element_type=jnp.float32)

def rms_norm(values):
    return values * lax.rsqrt(lax.optimization_barrier(jnp.mean(values * values, axis=-1, keepdims=True)) + EPSILON)

def rotate(tensor, cosine_table, sine_table):
    half_dim = tensor.shape[-1] // 2
    front_half = tensor[..., :half_dim]
    back_half = tensor[..., half_dim:]
    return jnp.concatenate([front_half * cosine_table - back_half * sine_table, back_half * cosine_table + front_half * sine_table], axis=-1)

def row_tables(doc_row, length):
    column = jnp.arange(ROW, dtype=jnp.int32)
    changed = jnp.concatenate([jnp.ones((1,), dtype=bool), doc_row[1:] != doc_row[:-1]])
    starts = lax.cummax(jnp.where(changed, column, 0), axis=0)
    positions = (column - starts).astype(jnp.float32)
    frequency = 10000.0 ** (-(jnp.arange(HD // 2, dtype=jnp.float32) * 2.0 / HD))
    angles = positions[:, None] * frequency[None, :]
    same_doc = doc_row[:, None] == doc_row[None, :]
    causal = column[None, :] <= column[:, None]
    usable = (column[None, :] < length) | (column[None, :] == column[:, None])
    visible = same_doc & causal & usable
    return (visible, jnp.cos(angles)[:, None, :], jnp.sin(angles)[:, None, :])

def layer(params, x_row, visible, cosine_table, sine_table):
    wq, wk, wv, wo, wu, wg, wd, sqk, su, sv, alpha_a, alpha_m = params
    cols = D // N_HEAD
    units = FF // N_HEAD
    heads_here = HEADS // N_HEAD
    factor = 1.0 / math.sqrt(HD)

    def one_head(operands):
        q_head, k_head, v_head = operands
        scores = low_back(matmul(q_head, k_head.T))
        scores = jnp.where(visible, scores * factor, -1e+30)
        return matmul(low(jax.nn.softmax(scores, axis=-1)), v_head)
    pieces = []
    for group in range(N_HEAD):
        col_range = slice(group * cols, (group + 1) * cols)
        h_group = low_back(x_row)
        q_raw = low_back(matmul(h_group, wq[:, col_range])).reshape(ROW, heads_here, HD)
        k_raw = low_back(matmul(h_group, wk[:, col_range])).reshape(ROW, heads_here, HD)
        v_low = low(low_back(matmul(h_group, wv[:, col_range]))).reshape(ROW, heads_here, HD)
        gain = sqk[col_range].reshape(heads_here, HD)
        q_tilde = low(rms_norm(rotate(q_raw, cosine_table, sine_table)) * gain)
        k_tilde = low(rms_norm(rotate(k_raw, cosine_table, sine_table)) * gain)
        attended = lax.map(jax.checkpoint(one_head), (q_tilde.transpose(1, 0, 2), k_tilde.transpose(1, 0, 2), v_low.transpose(1, 0, 2)))
        attended = low(low_back(attended.transpose(1, 0, 2).reshape(ROW, cols)))
        pieces.append(low(matmul(attended, wo[col_range, :])))
    y_sum = low_back(sum(pieces))
    h_attn = rms_norm(y_sum)
    h_one = rms_norm(x_row + alpha_a * (h_attn - x_row))
    h_one_low = low(h_one)
    pieces = []
    for group in range(N_HEAD):
        unit_range = slice(group * units, (group + 1) * units)
        h_group = low_back(h_one_low)
        up_act = low_back(matmul(h_group, wu[:, unit_range])) * su[unit_range]
        gate_act = low_back(matmul(h_group, wg[:, unit_range])) * sv[unit_range]
        mixed = low(up_act * jax.nn.silu(gate_act))
        pieces.append(low(matmul(mixed, wd[unit_range, :])))
    z_sum = low_back(sum(pieces))
    h_ffn = rms_norm(z_sum)
    return rms_norm(h_one + alpha_m * (h_ffn - h_one))

def reference(hidden_in, cotangent, doc_ids, lengths, w_query, w_key, w_value, w_out, w_up, w_gate, w_down, scale_qk, scale_up, scale_gate, alpha_attn, alpha_ffn):
    params = tuple((weight.astype(jnp.float32) for weight in (w_query, w_key, w_value, w_out, w_up, w_gate, w_down, scale_qk, scale_up, scale_gate, alpha_attn, alpha_ffn)))

    def row_step(carried, operands):
        x_row, cot_row, doc_row, length = operands
        visible, cosine_table, sine_table = row_tables(doc_row, length)
        out_row, pull = jax.vjp(lambda weights, inputs: layer(weights, inputs, visible, cosine_table, sine_table), params, x_row.astype(jnp.float32))
        grad_params, grad_row = pull(cot_row.astype(jnp.float32))
        carried = jax.tree.map(jnp.add, carried, grad_params)
        return (carried, (out_row.astype(jnp.bfloat16), grad_row))
    zeros = jax.tree.map(jnp.zeros_like, params)
    summed, outputs = lax.scan(row_step, zeros, (hidden_in, cotangent, doc_ids, lengths))
    hidden_out, grad_hidden = outputs
    return (hidden_out, grad_hidden, summed[0], summed[1], summed[2], summed[3], summed[4], summed[5], summed[6], summed[7], summed[8], summed[9], summed[10], summed[11])
```

```python
import functools
import math

import jax
import jax.numpy as jnp
from jax import lax
from jax.experimental import pallas as pl
from jax.experimental.pallas import tpu as pltpu
from jax.sharding import PartitionSpec as P

HD = 64
HALF = HD // 2
VALUE_ROWS = 80
EPSILON = 1e-06
BLOCK = 256
CHUNKS = 2
F32 = jnp.float32
BF16 = jnp.bfloat16
MIB = 1024 * 1024


def dot(left, right, left_dim=1, right_dim=0):
    return lax.dot_general(
        left, right, (((left_dim,), (right_dim,)), ((), ())), preferred_element_type=F32
    )


def shape(dims, dtype):
    return jax.ShapeDtypeStruct(dims, dtype)


def whole(dims):
    return pl.BlockSpec(dims, lambda *_: (0,) * len(dims))


def params(mib):
    return pltpu.CompilerParams(vmem_limit_bytes=mib * MIB)


def cost(flops, moved):
    return pl.CostEstimate(flops=int(flops), bytes_accessed=int(moved), transcendentals=0)


def swap(value, axis, mask, size):
    return lax.ppermute(value, axis, [(i, i ^ mask) for i in range(size)])


def gather_pieces(own, size):
    pieces = {0: own}
    bit = size // 2
    while bit:
        pieces.update({e | bit: swap(p, "head", bit, size) for e, p in pieces.items()})
        bit //= 2
    return [pieces[e] for e in range(size)]


def exchange_pieces(pieces, size):
    return [pieces[0]] + [swap(pieces[e], "head", e, size) for e in range(1, size)]


def total(terms):
    if len(terms) == 1:
        return terms[0]
    return sum(t.astype(F32) for t in terms).astype(BF16)


def reduce_pieces(pieces, size):
    held = {e: [p] for e, p in enumerate(pieces)}
    bit = 1
    while bit < size:
        for e in [e for e in held if e & bit]:
            held[e ^ bit].append(swap(total(held.pop(e)), "head", bit, size))
        bit *= 2
    return held[0]


def sum_small(value, axis, size):
    bit = 1
    while bit < size:
        value = value + swap(value, axis, bit, size)
        bit *= 2
    return value


def ring_place(index, size):
    return jnp.where(index % 2 == 0, index // 2, size - 1 - index // 2)


def ring_sum(values, sign, size):
    order = list(range(0, size, 2)) + list(range(size - 1, 0, -2))
    pairs = [(order[i], order[(i + sign) % size]) for i in range(size)]
    rows = values.shape[0] // size
    place = ring_place(lax.axis_index("batch"), size)

    def take(k):
        return lax.dynamic_slice_in_dim(values, (k + 2 * size) % size * rows, rows, 0)

    held = take(place)
    for t in range(1, size):
        held = total([lax.ppermute(held, "batch", pairs), take(place - sign * t)])
    parts = [held]
    for t in range(1, size):
        parts.append(lax.ppermute(parts[-1], "batch", pairs))
    return parts


def rings(values, size, signs=(1, -1)):
    rows = values.shape[0] // len(signs)
    if size > 8 or size % 2 or rows % (16 * size):
        return lax.psum(values, "batch")
    return [
        (i * rows, sign, ring_sum(values[i * rows : (i + 1) * rows], sign, size))
        for i, sign in enumerate(signs)
    ]


def store_parts(place, plan, refs, out):
    refs = list(refs)
    for first, sign, size, rows in plan:
        for t in range(size):
            at = (place + sign * (1 - t) + 2 * size) % size
            out[pl.ds(pl.multiple_of(first + at * rows, rows), rows), :] = refs.pop(0)[...].astype(
                out.dtype
            )


def unpack(summed):
    plan = [(first, sign, len(parts), parts[0].shape[0]) for first, sign, parts in summed]
    return plan, [p for _, _, parts in summed for p in parts]


def assemble(summed, place):
    if not isinstance(summed, list):
        return summed.astype(F32)
    plan, parts = unpack(summed)
    rows, width = sum(p.shape[0] for p in parts), parts[0].shape[1]

    def body(place, *refs):
        store_parts(place[0], plan, refs[:-1], refs[-1])

    return pl.pallas_call(
        body,
        grid_spec=pltpu.PrefetchScalarGridSpec(
            num_scalar_prefetch=1,
            grid=(1,),
            in_specs=[whole(p.shape) for p in parts],
            out_specs=whole((rows, width)),
        ),
        out_shape=shape((rows, width), F32),
        compiler_params=params(32),
        cost_estimate=cost(0, rows * width * 6),
        name="assemble",
    )(place, *parts)


def assemble_turned(summed, place, info, cols, n_head):
    if isinstance(summed, list):
        plan, parts = unpack(summed)
        held = [pltpu.VMEM((4 * cols, parts[0].shape[1]), F32)]
        model = parts[0].shape[1]
    else:
        plan, parts, held = None, [summed], []
        model = summed.shape[1]
    share = model // n_head

    def body(place, info, *refs):
        refs, outs = refs[: len(parts)], refs[len(parts) :]
        if plan is None:
            source = refs[0]
        else:
            source = outs[4]
            store_parts(place[0], plan, refs, source)
        for i in range(3):
            for e in range(n_head):
                at = pl.ds(pl.multiple_of((info[0] ^ e) * share, share), share)
                block = source[i * cols : (i + 1) * cols, e * share : (e + 1) * share]
                outs[i][at, :] = block.astype(F32).T
        outs[3][...] = source[3 * cols :, :].astype(F32)

    return pl.pallas_call(
        body,
        grid_spec=pltpu.PrefetchScalarGridSpec(
            num_scalar_prefetch=2,
            grid=(1,),
            in_specs=[whole(p.shape) for p in parts],
            out_specs=[whole((model, cols))] * 3 + [whole((cols, model))],
            scratch_shapes=held,
        ),
        out_shape=[shape((model, cols), F32)] * 3 + [shape((cols, model), F32)],
        compiler_params=params(32),
        cost_estimate=cost(0, cols * model * 24),
        name="assemble_turned",
    )(place, info, *parts)


def visible(first_key, first_query, starts, length, rows, cols):
    key = first_key + lax.broadcasted_iota(jnp.int32, (rows, cols), 0)
    query = first_query + lax.broadcasted_iota(jnp.int32, (rows, cols), 1)
    last = jnp.minimum(query, length - 1)
    return (key >= starts) & ((key <= last) | (key == query))


def attend_kernel(
    chunk, n_head, heads, chunk_len, share, info, *refs
):
    refs = list(refs)
    x_refs = [refs.pop(0) for _ in range(n_head)]
    w_ref, cos_ref, sin_ref, gain_ref, start_ref = [refs.pop(0) for _ in range(5)]
    old_k, old_v = None, None
    if chunk:
        old_k, old_v = refs.pop(0), refs.pop(0)
        refs = refs[7:]
    k_ref, ve_ref, v_ref, kt_ref, qt_ref, ot_ref, inv_ref, qf_ref, kf_ref, o_ref = refs[:10]
    raw, acc = refs[10:]
    me, length = info[0], info[1]
    cols = heads * HD
    for e in range(n_head):
        first = pl.multiple_of((me ^ e) * share, share)
        for part in range(3):
            rows = slice(part * cols, (part + 1) * cols)
            term = dot(w_ref[rows, pl.ds(first, share)], x_refs[e][...], 1, 1)
            if e == 0:
                raw[rows, :] = term
            else:
                raw[rows, :] += term
    cosine, sine = cos_ref[...], sin_ref[...]
    for h in range(heads):
        own = slice(h * HD, (h + 1) * HD)
        for part, factor_ref in ((0, qf_ref), (1, kf_ref)):
            base = part * cols + h * HD
            a, b = raw[base : base + HALF, :], raw[base + HALF : base + HD, :]
            front, back = a * cosine - b * sine, b * cosine + a * sine
            mean = jnp.sum(front * front + back * back, axis=0, keepdims=True) / HD
            factor = lax.rsqrt(mean + EPSILON)
            factor_ref[h] = factor
            unit = jnp.concatenate([front, back], axis=0) * factor
            low = (unit * gain_ref[own, :]).astype(BF16)
            if part == 0:
                qt_ref[own, :] = low * BF16(1.0 / math.sqrt(HD))
            else:
                kt_ref[own, :] = low
                k_ref[h] = low.T
        value = raw[2 * cols + h * HD : 2 * cols + (h + 1) * HD, :].astype(BF16)
        v_ref[h] = value.T
        ve_ref[h, :HD, :] = value
        ve_ref[h, HD:, :] = jnp.ones((VALUE_ROWS - HD, chunk_len), BF16)

    blocks = chunk_len // BLOCK
    before = chunk * blocks

    def step(local, key_first, k_of, v_of, starts):
        query = slice(local * BLOCK, (local + 1) * BLOCK)
        mask = visible(key_first, (before + local) * BLOCK, starts, length, BLOCK, BLOCK)
        for h in range(heads):
            scores = dot(k_of(h), qt_ref[h * HD : (h + 1) * HD, query])
            probs = jnp.where(mask, jnp.exp(scores), 0.0).astype(BF16)
            acc[h] += dot(v_of(h), probs)

    for local in range(blocks):
        query = slice(local * BLOCK, (local + 1) * BLOCK)
        starts = start_ref[:, query]
        lowest = info[2 + before + local]
        acc[...] = jnp.zeros_like(acc)
        if chunk:

            @pl.loop(lowest, before)
            def _(kb):
                at = pl.ds(pl.multiple_of(kb * BLOCK, BLOCK), BLOCK)
                step(
                    local, kb * BLOCK, lambda h: old_k[h, at, :], lambda h: old_v[h, :, at], starts
                )

        @pl.loop(jnp.maximum(lowest - before, 0), local + 1)
        def _(kb):
            at = pl.ds(pl.multiple_of(kb * BLOCK, BLOCK), BLOCK)
            step(
                local,
                (before + kb) * BLOCK,
                lambda h: k_ref[h, at, :],
                lambda h: ve_ref[h, :, at],
                starts,
            )

        for h in range(heads):
            inverse = 1.0 / acc[h, HD : HD + 1, :]
            inv_ref[h, :, query] = inverse
            out = acc[h, :HD, :] * inverse
            ot_ref[h * HD : (h + 1) * HD, query] = out.astype(BF16)
            o_ref[query, h * HD : (h + 1) * HD] = out.T.astype(BF16)


def attend_chunk(chunk, x_pieces, w_t, cosine, sine, gain, starts, info, buffers, row_len):
    n_head = len(x_pieces)
    chunk_len, share = x_pieces[0].shape
    cols = w_t.shape[0] // 3
    heads = cols // HD
    model = w_t.shape[1]
    body = functools.partial(attend_kernel, chunk, n_head, heads, chunk_len, share)
    by_lane = lambda rows: pl.BlockSpec((rows, chunk_len), lambda i, info: (0, chunk))
    specs = [whole((chunk_len, share))] * n_head + [
        whole((3 * cols, model)),
        by_lane(HALF),
        by_lane(HALF),
        whole((cols, 1)),
        by_lane(1),
    ]
    operands = [*x_pieces, w_t, cosine, sine, gain, starts]
    aliases = {}
    if chunk:
        aliases = {1 + len(operands) + i: i for i in range(9)}
        specs += [whole((heads, row_len, HD)), whole((heads, VALUE_ROWS, row_len))]
        specs += [pl.BlockSpec(memory_space=pl.ANY)] * 7
        operands += buffers
    lane3 = lambda rows: pl.BlockSpec((heads, rows, chunk_len), lambda i, info: (0, 0, chunk))
    row3 = pl.BlockSpec((heads, chunk_len, HD), lambda i, info: (0, chunk, 0))
    outs = pl.pallas_call(
        body,
        grid_spec=pltpu.PrefetchScalarGridSpec(
            num_scalar_prefetch=1,
            grid=(1,),
            in_specs=specs,
            out_specs=[
                row3,
                lane3(VALUE_ROWS),
                row3,
                by_lane(cols),
                by_lane(cols),
                by_lane(cols),
                lane3(1),
                lane3(1),
                lane3(1),
                whole((chunk_len, cols)),
            ],
            scratch_shapes=[
                pltpu.VMEM((3 * cols, chunk_len), F32),
                pltpu.VMEM((heads, VALUE_ROWS, BLOCK), F32),
            ],
        ),
        out_shape=[
            shape((heads, row_len, HD), BF16),
            shape((heads, VALUE_ROWS, row_len), BF16),
            shape((heads, row_len, HD), BF16),
            shape((cols, row_len), BF16),
            shape((cols, row_len), BF16),
            shape((cols, row_len), BF16),
            shape((heads, 1, row_len), F32),
            shape((heads, 1, row_len), F32),
            shape((heads, 1, row_len), F32),
            shape((chunk_len, cols), BF16),
        ],
        input_output_aliases=aliases,
        compiler_params=params(40),
        cost_estimate=cost(16e9 / CHUNKS, 8e6),
        name="attend",
    )(info, *operands)
    return outs[:9], outs[9]


def unattend_kernel(n_head, chunks, row_len, piece, pair, info, *refs):
    refs = list(refs)
    d_refs = [refs.pop(0) for _ in range(chunks * n_head)]
    k_ref, v_ref, kt_ref, qt_ref, ot_ref, inv_ref, qf_ref, kf_ref = [refs.pop(0) for _ in range(8)]
    start_ref, cos_ref, sin_ref, gain_ref = [refs.pop(0) for _ in range(4)]
    out_ref, gain_out, do_s, inner_s, dq_s, dk_s, dv_s = refs
    me, length = info[0], info[1]
    for c in range(chunks):
        for e in range(n_head):
            first = c * n_head * piece + (me ^ e) * piece
            do_s[:, pl.ds(pl.multiple_of(first, piece), piece)] = d_refs[c * n_head + e][...]
    for h in range(pair):
        own = slice(h * HD, (h + 1) * HD)
        product = do_s[own, :].astype(F32) * ot_ref[own, :].astype(F32)
        inner_s[h] = jnp.sum(product, axis=0, keepdims=True)
    dq_s[...] = jnp.zeros_like(dq_s)
    dk_s[...] = jnp.zeros_like(dk_s)
    dv_s[...] = jnp.zeros_like(dv_s)

    @pl.loop(0, row_len // BLOCK)
    def _(qb):
        query = pl.ds(pl.multiple_of(qb * BLOCK, BLOCK), BLOCK)
        starts = start_ref[:, query]

        @pl.loop(info[2 + qb], qb + 1)
        def _(kb):
            key = pl.ds(pl.multiple_of(kb * BLOCK, BLOCK), BLOCK)
            mask = visible(kb * BLOCK, qb * BLOCK, starts, length, BLOCK, BLOCK)
            for h in range(pair):
                own = slice(h * HD, (h + 1) * HD)
                q_block, do_block = qt_ref[own, query], do_s[own, query]
                scores = dot(k_ref[h, key, :], q_block)
                probs = jnp.where(mask, jnp.exp(scores), 0.0) * inv_ref[h, :, query]
                d_probs = dot(v_ref[h, key, :], do_block)
                d_scores = (probs * (d_probs - inner_s[h, :, query])).astype(BF16)
                dv_s[own, key] += dot(do_block, probs.astype(BF16), 1, 1)
                dk_s[own, key] += dot(q_block, d_scores, 1, 1)
                dq_s[own, query] += dot(kt_ref[own, key], d_scores)

    for h in range(pair):
        own = slice(h * HD, (h + 1) * HD)
        gain = gain_ref[own, :]
        summed = jnp.zeros((HD, 1), F32)
        for part, low_ref, grad_ref, factor_ref in (
            (0, qt_ref, dq_s, qf_ref),
            (1, kt_ref, dk_s, kf_ref),
        ):
            scale = math.sqrt(HD) if part == 0 else 1.0
            unit = low_ref[own, :].astype(F32) * (scale / gain)
            grad = grad_ref[own, :]
            if part == 0:
                grad = grad * (1.0 / math.sqrt(HD))
            summed += jnp.sum(grad * unit, axis=1, keepdims=True)
            grad = grad * gain
            mean = jnp.sum(grad * unit, axis=0, keepdims=True) / HD
            grad = (grad - unit * mean) * factor_ref[h]
            front, back = grad[:HALF], grad[HALF:]
            cosine, sine = cos_ref[...], sin_ref[...]
            out_ref[part, h * HD : h * HD + HALF, :] = (front * cosine + back * sine).astype(BF16)
            out_ref[part, h * HD + HALF : (h + 1) * HD, :] = (
                back * cosine - front * sine
            ).astype(BF16)
        out_ref[2, own, :] = dv_s[own, :].astype(BF16)
        gain_out[own, :] = summed


def unattend(do_pieces, buffers, starts, cosine, sine, gain, info, n_head):
    k, _, v, kt, qt, ot, inv, qf, kf = buffers
    chunks = len(do_pieces) // n_head
    cols, piece = do_pieces[0].shape
    heads, row_len, _ = k.shape
    pair = min(2, heads)
    rows = pair * HD
    by_rows = lambda width: pl.BlockSpec((rows, width), lambda g, info: (g, 0))
    by_head = lambda a, b: pl.BlockSpec((pair, a, b), lambda g, info: (g, 0, 0))
    return pl.pallas_call(
        functools.partial(unattend_kernel, n_head, chunks, row_len, piece, pair),
        grid_spec=pltpu.PrefetchScalarGridSpec(
            num_scalar_prefetch=1,
            grid=(heads // pair,),
            in_specs=[by_rows(piece)] * (chunks * n_head)
            + [by_head(row_len, HD)] * 2
            + [by_rows(row_len)] * 3
            + [by_head(1, row_len)] * 3
            + [whole((1, row_len)), whole((HALF, row_len)), whole((HALF, row_len)), by_rows(1)],
            out_specs=[pl.BlockSpec((3, rows, row_len), lambda g, info: (0, g, 0)), by_rows(1)],
            scratch_shapes=[
                pltpu.VMEM((rows, row_len), BF16),
                pltpu.VMEM((pair, 1, row_len), F32),
                pltpu.VMEM((rows, row_len), F32),
                pltpu.VMEM((rows, row_len), F32),
                pltpu.VMEM((rows, row_len), F32),
            ],
        ),
        out_shape=[shape((3, cols, row_len), BF16), shape((cols, 1), F32)],
        compiler_params=params(40),
        cost_estimate=cost(45e9, 12e6),
        name="unattend",
    )(info, *do_pieces, k, v, kt, qt, ot, inv, qf, kf, starts, cosine, sine, gain)


def norm(values):
    factor = lax.rsqrt(jnp.mean(values * values, axis=-1, keepdims=True) + EPSILON)
    return values * factor, factor


def norm_back(grad, unit, factor):
    return factor * (grad - unit * jnp.mean(grad * unit, axis=-1, keepdims=True))


def project_kernel(n_head, share, info, *refs):
    o_refs, w_refs = refs[:n_head], refs[n_head : 2 * n_head]
    x_refs = refs[2 * n_head : 3 * n_head]
    alpha_ref, y_ref, x_ref, h_ref, low_ref = refs[3 * n_head :]
    me = info[0]
    y = dot(o_refs[0][...], w_refs[0][...])
    for e in range(1, n_head):
        y += dot(o_refs[e][...], w_refs[e][...])
    for e in range(n_head):
        first = pl.multiple_of((me ^ e) * share, share)
        x_ref[:, pl.ds(first, share)] = x_refs[e][...]
    y_ref[...] = y
    h_zero = x_ref[...].astype(F32)
    h_one, _ = norm(h_zero + alpha_ref[...] * (norm(y)[0] - h_zero))
    h_ref[...] = h_one
    low_ref[...] = h_one.astype(BF16)


def project(o_pieces, w_pieces, x_pieces, alpha, info):
    n_head = len(o_pieces)
    cols, model = w_pieces[0].shape
    chunk_len, share = x_pieces[0].shape
    rows = chunk_len // n_head
    mine = lambda width: pl.BlockSpec((rows, width), lambda i, info: (info[0], 0))
    return pl.pallas_call(
        functools.partial(project_kernel, n_head, share),
        grid_spec=pltpu.PrefetchScalarGridSpec(
            num_scalar_prefetch=1,
            grid=(1,),
            in_specs=[mine(cols)]
            + [whole((rows, cols))] * (n_head - 1)
            + [whole((cols, model))] * n_head
            + [mine(share)] * n_head
            + [whole((1, model))],
            out_specs=[whole((rows, model))] * 4,
        ),
        out_shape=[
            shape((rows, model), F32),
            shape((rows, model), BF16),
            shape((rows, model), F32),
            shape((rows, model), BF16),
        ],
        compiler_params=params(32),
        cost_estimate=cost(2.0 * rows * model * model, 6e6),
        name="project",
    )(info, *o_pieces, *w_pieces, *x_pieces, alpha)


def feed_kernel(n_head, rows, refs_in, *refs):
    h_refs = (refs_in, *refs[: n_head - 1])
    refs = refs[n_head - 1 :]
    up_ref, gate_ref, down_ref, su_ref, sg_ref, m_ref, u_ref, g_ref, cat_ref = refs[:9]
    z_refs, acc = refs[9 : 9 + n_head], refs[9 + n_head]
    tile = pl.program_id(0)

    @pl.when(tile == 0)
    def _():
        for e in range(n_head):
            cat_ref[e * rows : (e + 1) * rows, :] = h_refs[e][...]

    up_raw = dot(cat_ref[...], up_ref[...])
    gate_raw = dot(cat_ref[...], gate_ref[...])
    u_ref[...] = up_raw.astype(BF16)
    g_ref[...] = gate_raw.astype(BF16)
    gate = gate_raw * sg_ref[...]
    mixed = (up_raw * su_ref[...] * (gate * jax.nn.sigmoid(gate))).astype(BF16)
    m_ref[...] = mixed
    term = dot(mixed, down_ref[...])

    @pl.when(tile == 0)
    def _():
        acc[...] = term

    @pl.when(tile > 0)
    def _():
        acc[...] += term

    @pl.when(tile == pl.num_programs(0) - 1)
    def _():
        for e in range(n_head):
            z_refs[e][...] = acc[e * rows : (e + 1) * rows, :].astype(BF16)


def feed(h_pieces, w_up, w_gate, w_down, scale_up, scale_gate):
    n_head = len(h_pieces)
    rows, model = h_pieces[0].shape
    hidden = w_up.shape[1]
    tile = min(256, hidden)
    count = n_head * rows
    by_col = lambda height: pl.BlockSpec((height, tile), lambda n: (0, n))
    outs = pl.pallas_call(
        functools.partial(feed_kernel, n_head, rows),
        grid=(hidden // tile,),
        in_specs=[whole((rows, model))] * n_head
        + [
            by_col(model),
            by_col(model),
            pl.BlockSpec((tile, model), lambda n: (n, 0)),
            by_col(1),
            by_col(1),
        ],
        out_specs=[by_col(count)] * 3 + [whole((count, model))] + [whole((rows, model))] * n_head,
        out_shape=[shape((count, hidden), BF16)] * 3
        + [shape((count, model), BF16)]
        + [shape((rows, model), BF16)] * n_head,
        scratch_shapes=[pltpu.VMEM((count, model), F32)],
        compiler_params=params(48),
        cost_estimate=cost(6.0 * count * model * hidden, 20e6),
        name="feed",
    )(*h_pieces, w_up, w_gate, w_down, scale_up, scale_gate)
    return outs[:4], list(outs[4:])


def middle_kernel(n_head, n_terms, share, info, *refs):
    z_refs, c_refs = refs[:n_terms], refs[n_terms : n_terms + n_head]
    h_ref, alpha_ref = refs[n_terms + n_head : n_terms + n_head + 2]
    refs = refs[n_terms + n_head + 2 :]
    out_refs = refs[:n_head]
    dz_ref, direct_ref, grad_ref, two_s, cot_s = refs[n_head:]
    me = info[0]
    z = z_refs[0][...].astype(F32)
    for r in z_refs[1:]:
        z += r[...].astype(F32)
    h_one, alpha = h_ref[...], alpha_ref[...]
    h_ffn, z_factor = norm(z)
    h_two, factor = norm(h_one + alpha * (h_ffn - h_one))
    two_s[...] = h_two.astype(BF16)
    for e in range(n_head):
        at = pl.ds(pl.multiple_of((me ^ e) * share, share), share)
        out_refs[e][...] = two_s[:, at]
        cot_s[:, at] = c_refs[e][...]
    grad = norm_back(cot_s[...].astype(F32), h_two, factor)
    grad_ref[...] = jnp.sum(grad * (h_ffn - h_one), axis=0, keepdims=True)
    direct_ref[...] = grad * (1.0 - alpha)
    dz_ref[...] = norm_back(grad * alpha, h_ffn, z_factor).astype(BF16)


def middle(z_terms, cot_pieces, h_one, alpha, info):
    n_head, n_terms = len(cot_pieces), len(z_terms)
    rows, model = h_one.shape
    share = cot_pieces[0].shape[1]
    mine = pl.BlockSpec((rows, share), lambda i, info: (info[0], 0))
    outs = pl.pallas_call(
        functools.partial(middle_kernel, n_head, n_terms, share),
        grid_spec=pltpu.PrefetchScalarGridSpec(
            num_scalar_prefetch=1,
            grid=(1,),
            in_specs=[whole((rows, model))] * n_terms
            + [mine]
            + [whole((rows, share))] * (n_head - 1)
            + [whole((rows, model)), whole((1, model))],
            out_specs=[whole((rows, share))] * n_head
            + [whole((rows, model))] * 2
            + [whole((1, model))],
            scratch_shapes=[pltpu.VMEM((rows, model), BF16), pltpu.VMEM((rows, model), BF16)],
        ),
        out_shape=[shape((rows, share), BF16)] * n_head
        + [shape((rows, model), BF16), shape((rows, model), F32), shape((1, model), F32)],
        compiler_params=params(32),
        cost_estimate=cost(rows * model * 60, rows * model * 24),
        name="middle",
    )(info, *z_terms, *cot_pieces, h_one, alpha)
    return list(outs[:n_head]), outs[n_head], outs[n_head + 1], outs[n_head + 2]


def unfeed_kernel(n_head, rows, first_ref, *refs):
    d_refs = (first_ref, *refs[: n_head - 1])
    refs = refs[n_head - 1 :]
    u_ref, g_ref, up_ref, gate_ref, down_ref, su_ref, sg_ref = refs[:7]
    du_ref, dg_ref, cat_ref, gsu_ref, gsg_ref = refs[7:12]
    out_refs, acc = refs[12 : 12 + n_head], refs[12 + n_head]
    tile = pl.program_id(0)

    @pl.when(tile == 0)
    def _():
        for e in range(n_head):
            cat_ref[e * rows : (e + 1) * rows, :] = d_refs[e][...]

    d_mixed = dot(cat_ref[...], down_ref[...], 1, 1)
    up_raw, gate_raw = u_ref[...].astype(F32), g_ref[...].astype(F32)
    gate = gate_raw * sg_ref[...]
    sigmoid = jax.nn.sigmoid(gate)
    d_up = d_mixed * (gate * sigmoid)
    d_gate = d_mixed * (up_raw * su_ref[...]) * sigmoid * (1.0 + gate * (1.0 - sigmoid))
    gsu_ref[...] = jnp.sum(d_up * up_raw, axis=0, keepdims=True)
    gsg_ref[...] = jnp.sum(d_gate * gate_raw, axis=0, keepdims=True)
    up_low = (d_up * su_ref[...]).astype(BF16)
    gate_low = (d_gate * sg_ref[...]).astype(BF16)
    du_ref[...] = up_low
    dg_ref[...] = gate_low
    term = dot(up_low, up_ref[...], 1, 1) + dot(gate_low, gate_ref[...], 1, 1)

    @pl.when(tile == 0)
    def _():
        acc[...] = term

    @pl.when(tile > 0)
    def _():
        acc[...] += term

    @pl.when(tile == pl.num_programs(0) - 1)
    def _():
        for e in range(n_head):
            out_refs[e][...] = acc[e * rows : (e + 1) * rows, :].astype(BF16)


def unfeed(d_pieces, u, g, w_up, w_gate, w_down, scale_up, scale_gate):
    n_head = len(d_pieces)
    rows, model = d_pieces[0].shape
    hidden = w_up.shape[1]
    tile = min(256, hidden)
    count = n_head * rows
    by_col = lambda height: pl.BlockSpec((height, tile), lambda n: (0, n))
    outs = pl.pallas_call(
        functools.partial(unfeed_kernel, n_head, rows),
        grid=(hidden // tile,),
        in_specs=[whole((rows, model))] * n_head
        + [
            by_col(count),
            by_col(count),
            by_col(model),
            by_col(model),
            pl.BlockSpec((tile, model), lambda n: (n, 0)),
            by_col(1),
            by_col(1),
        ],
        out_specs=[by_col(count)] * 2
        + [whole((count, model)), by_col(1), by_col(1)]
        + [whole((rows, model))] * n_head,
        out_shape=[shape((count, hidden), BF16)] * 2
        + [shape((count, model), BF16), shape((1, hidden), F32), shape((1, hidden), F32)]
        + [shape((rows, model), BF16)] * n_head,
        scratch_shapes=[pltpu.VMEM((count, model), F32)],
        compiler_params=params(48),
        cost_estimate=cost(6.0 * count * model * hidden, 20e6),
        name="unfeed",
    )(*d_pieces, u, g, w_up, w_gate, w_down, scale_up, scale_gate)
    return outs[:5], list(outs[5:])


def unproject_kernel(n_head, n_terms, cols, *refs):
    t_refs, w_refs = refs[:n_terms], refs[n_terms : n_terms + n_head]
    direct_ref, y_ref, x_ref, alpha_ref = refs[n_terms + n_head : n_terms + n_head + 4]
    refs = refs[n_terms + n_head + 4 :]
    do_refs = refs[:n_head]
    dy_ref, zero_ref, grad_ref = refs[n_head:]
    grad = direct_ref[...]
    for r in t_refs:
        grad += r[...].astype(F32)
    alpha = alpha_ref[...]
    h_zero = x_ref[...].astype(F32)
    h_attn, y_factor = norm(y_ref[...])
    h_one, factor = norm(h_zero + alpha * (h_attn - h_zero))
    grad = norm_back(grad, h_one, factor)
    grad_ref[...] = jnp.sum(grad * (h_attn - h_zero), axis=0, keepdims=True)
    zero_ref[...] = grad * (1.0 - alpha)
    dy = norm_back(grad * alpha, h_attn, y_factor).astype(BF16)
    dy_ref[...] = dy
    for e in range(n_head):
        do_refs[e][...] = dot(w_refs[e][...], dy, 1, 1).astype(BF16)


def unproject(terms, w_pieces, direct, y, x, alpha):
    n_head, n_terms = len(w_pieces), len(terms)
    rows, model = y.shape
    cols = w_pieces[0].shape[0]
    outs = pl.pallas_call(
        functools.partial(unproject_kernel, n_head, n_terms, cols),
        grid=(1,),
        in_specs=[whole((rows, model))] * n_terms
        + [whole((cols, model))] * n_head
        + [whole((rows, model))] * 3
        + [whole((1, model))],
        out_specs=[whole((cols, rows))] * n_head
        + [whole((rows, model))] * 2
        + [whole((1, model))],
        out_shape=[shape((cols, rows), BF16)] * n_head
        + [shape((rows, model), BF16), shape((rows, model), F32), shape((1, model), F32)],
        compiler_params=params(32),
        cost_estimate=cost(2.0 * rows * model * model, 8e6),
        name="unproject",
    )(*terms, *w_pieces, direct, y, x, alpha)
    return list(outs[:n_head]), outs[n_head], outs[n_head + 1], outs[n_head + 2]


def spread_kernel(n_head, share, info, d_ref, w_ref, direct_ref, *out_refs):
    me = info[0]
    block = pl.program_id(0)
    d_all = d_ref[...].T
    for e in range(n_head):
        at = pl.ds(pl.multiple_of((me ^ e) * share, share), share)
        term = dot(d_all, w_ref[:, at])

        @pl.when(block == me)
        def _():
            out_refs[e][...] = (term + direct_ref[:, at]).astype(BF16)

        @pl.when(block != me)
        def _():
            out_refs[e][...] = term.astype(BF16)


def spread(chunk, chunk_len, d_all, w_t, direct, info, n_head):
    rows3, model = w_t.shape
    share = model // n_head
    rows = chunk_len // n_head
    return pl.pallas_call(
        functools.partial(spread_kernel, n_head, share),
        grid_spec=pltpu.PrefetchScalarGridSpec(
            num_scalar_prefetch=1,
            grid=(n_head,),
            in_specs=[
                pl.BlockSpec((rows3, rows), lambda i, info: (0, chunk * n_head + i)),
                whole((rows3, model)),
                whole((rows, model)),
            ],
            out_specs=[pl.BlockSpec((rows, share), lambda i, info: (i, 0))] * n_head,
        ),
        out_shape=[shape((chunk_len, share), BF16)] * n_head,
        compiler_params=params(32),
        cost_estimate=cost(2.0 * chunk_len * model * rows3, 8e6),
        name="spread",
    )(info, d_all, w_t, direct)


def on_device(
    n_batch,
    n_head,
    hidden_in,
    cotangent,
    doc_ids,
    lengths,
    w_query,
    w_key,
    w_value,
    w_out,
    w_up,
    w_gate,
    w_down,
    scale_qk,
    scale_up,
    scale_gate,
    alpha_attn,
    alpha_ffn,
):
    _, row_len, share = hidden_in.shape
    model = share * n_head
    cols = w_query.shape[1]
    chunk_len = row_len // CHUNKS
    rows = chunk_len // n_head
    me = lax.axis_index("head")
    chunks = range(CHUNKS)
    x_own, cot_own = hidden_in[0], cotangent[0]

    docs = doc_ids[0]
    column = jnp.arange(row_len, dtype=jnp.int32)
    starts = sum(
        jnp.where(docs > d, jnp.sum((docs == d).astype(jnp.int32)), 0) for d in range(5)
    ).astype(jnp.int32)
    position = (column - starts).astype(F32)
    frequency = 10000.0 ** (-(jnp.arange(HALF, dtype=F32) * 2.0 / HD))
    angles = frequency[:, None] * position[None, :]
    cosine, sine = jnp.cos(angles), jnp.sin(angles)
    info = jnp.concatenate(
        [me[None].astype(jnp.int32), lengths.astype(jnp.int32), starts[::BLOCK] // BLOCK]
    )
    starts = starts[None, :]
    gain = scale_qk[:, None]
    up_scale, gate_scale = scale_up[None, :], scale_gate[None, :]
    attn_alpha, ffn_alpha = alpha_attn[None, :], alpha_ffn[None, :]

    def part(values, c):
        return lax.slice_in_dim(values, c * chunk_len, (c + 1) * chunk_len, axis=0)

    def block_of(values, e):
        return lax.dynamic_slice_in_dim(values, (me ^ e) * rows, rows, 0)

    x_pieces = [gather_pieces(part(x_own, c), n_head) for c in chunks]
    w_t = jnp.concatenate([w_query.T, w_key.T, w_value.T], axis=0)
    out_pieces = gather_pieces(w_out, n_head)

    buffers = []
    state = []
    for c in chunks:
        buffers, o_chunk = attend_chunk(
            c, x_pieces[c], w_t, cosine, sine, gain, starts, info, buffers, row_len
        )
        o_pieces = exchange_pieces(
            [o_chunk] + [block_of(o_chunk, e) for e in range(1, n_head)], n_head
        )
        y, x_rows, h_one, h_low = project(o_pieces, out_pieces, x_pieces[c], attn_alpha, info)
        o_pieces[0] = block_of(o_chunk, 0)
        state.append((o_pieces, y, x_rows, h_one, h_low))
    cot_pieces = []
    for c in chunks:
        cot = part(cot_own, c)
        cot_pieces.append(
            exchange_pieces([cot] + [block_of(cot, e) for e in range(1, n_head)], n_head)
        )
    after = []
    for c in chunks:
        o_pieces, y, x_rows, h_one, h_low = state[c]
        (mixed, up_raw, gate_raw, h_cat), z_pieces = feed(
            gather_pieces(h_low, n_head), w_up, w_gate, w_down, up_scale, gate_scale
        )
        z_terms = reduce_pieces(z_pieces, n_head)
        two_pieces, dz, direct, grad_alpha_ffn = middle(
            z_terms, cot_pieces[c], h_one, ffn_alpha, info
        )
        after.append((mixed, up_raw, gate_raw, h_cat, two_pieces, dz, direct, grad_alpha_ffn))

    ffn = []
    for c in chunks:
        mixed, up_raw, gate_raw, h_cat, two_pieces, dz, direct, _ = after[c]
        (du, dg, dz_cat, gsu, gsg), dh_pieces = unfeed(
            gather_pieces(dz, n_head), up_raw, gate_raw, w_up, w_gate, w_down, up_scale, gate_scale
        )
        ffn.append((mixed, h_cat, du, dg, dz_cat, gsu, gsg, dh_pieces))

    grad_down = sum(dot(f[0], f[4], 0, 0) for f in ffn).astype(BF16)
    grad_up = sum(dot(f[1], f[2], 0, 0) for f in ffn).astype(BF16)
    grad_gate = sum(dot(f[1], f[3], 0, 0) for f in ffn).astype(BF16)
    place = ring_place(lax.axis_index("batch"), n_batch)[None].astype(jnp.int32)
    grad_down = assemble(rings(grad_down, n_batch), place)
    grad_up = assemble(rings(grad_up, n_batch, (1,)), place)
    grad_gate = assemble(rings(grad_gate, n_batch, (-1,)), place)

    do_pieces, zeros, dys, alphas = [], [], [], []
    for c in chunks:
        terms = reduce_pieces(ffn[c][7], n_head)
        _, y, x_rows, _, _ = state[c]
        pieces, dy, zero, grad_alpha_attn = unproject(
            terms, out_pieces, after[c][6], y, x_rows, attn_alpha
        )
        do_pieces += exchange_pieces(pieces, n_head)
        zeros.append(zero)
        dys.append(dy)
        alphas.append(grad_alpha_attn)

    out_terms = [
        sum(dot(state[c][0][e], dys[c], 0, 0) for c in chunks).astype(BF16) for e in range(n_head)
    ]
    grad_out = total(reduce_pieces(out_terms, n_head))

    d_all, grad_gain = unattend(
        do_pieces, buffers, starts, cosine, sine, gain, info, n_head
    )
    d_all = d_all.reshape(3 * cols, row_len)

    grad_hidden = []
    for c in chunks:
        pieces = spread(c, chunk_len, d_all, w_t, zeros[c], info, n_head)
        terms = reduce_pieces(pieces, n_head)
        grad_hidden.append(sum(t.astype(F32) for t in terms))
    grad_hidden = jnp.concatenate(grad_hidden, axis=0)[None]

    def lanes(c):
        return lax.slice_in_dim(d_all, c * chunk_len, (c + 1) * chunk_len, axis=1)

    grad_t = jnp.concatenate(
        [sum(dot(lanes(c), x_pieces[c][e]) for c in chunks) for e in range(n_head)], axis=1
    ).astype(BF16)
    grad_attn = rings(jnp.concatenate([grad_t, grad_out], axis=0), n_batch)
    grad_query, grad_key, grad_value, grad_out = assemble_turned(
        grad_attn, place, info, cols, n_head
    )

    alpha_sums = jnp.concatenate([sum(alphas), sum(a[7] for a in after)], axis=0)
    alpha_sums = sum_small(sum_small(alpha_sums, "head", n_head), "batch", n_batch)
    alpha_own = lax.dynamic_slice_in_dim(alpha_sums, me * share, share, 1)
    scale_sums = jnp.concatenate([sum(f[5] for f in ffn), sum(f[6] for f in ffn)], axis=0)
    scale_sums = sum_small(scale_sums, "batch", n_batch)
    gain_sums = sum_small(grad_gain[:, 0], "batch", n_batch)

    hidden_out = []
    for c in chunks:
        pieces = exchange_pieces(after[c][4], n_head)
        stacked = jnp.stack(pieces)
        hidden_out += [
            lax.dynamic_index_in_dim(stacked, b ^ me, 0, keepdims=False) for b in range(n_head)
        ]
    hidden_out = jnp.concatenate(hidden_out, axis=0)[None]
    return (
        hidden_out,
        grad_hidden,
        grad_query,
        grad_key,
        grad_value,
        grad_out,
        grad_up,
        grad_gate,
        grad_down,
        gain_sums,
        scale_sums[0],
        scale_sums[1],
        alpha_own[0],
        alpha_own[1],
    )


def solution(mesh):
    split = P("batch", None, "head")
    by_col, by_row, by_head = P(None, "head"), P("head", None), P("head")
    return jax.shard_map(
        functools.partial(on_device, mesh.shape["batch"], mesh.shape["head"]),
        mesh=mesh,
        in_specs=(split, split, P("batch", None), P("batch"))
        + (by_col, by_col, by_col, by_row, by_col, by_col, by_row)
        + (by_head, by_head, by_head, P(), P()),
        out_specs=(split, split, by_col, by_col, by_col, by_row, by_col, by_col, by_row)
        + (by_head,) * 5,
        check_vma=False,
    )
```

```python
import functools
import math

import jax
import jax.numpy as jnp
from jax import lax
from jax.experimental import pallas as pl
from jax.experimental.pallas import tpu as pltpu
from jax.sharding import PartitionSpec as P

HD = 64
HALF = HD // 2
VALUE_ROWS = 80
EPSILON = 1e-06
BLOCK = 256
CHUNKS = 2
F32 = jnp.float32
BF16 = jnp.bfloat16
MIB = 1024 * 1024


def dot(left, right, left_dim=1, right_dim=0):
    return lax.dot_general(
        left, right, (((left_dim,), (right_dim,)), ((), ())), preferred_element_type=F32
    )


def shape(dims, dtype):
    return jax.ShapeDtypeStruct(dims, dtype)


def kept_shape(dims, dtype):
    return pltpu.HBM(dims, dtype)


def after(value, *others):
    others = [o for o in others if o is not None]
    return lax.optimization_barrier((value, *others))[0] if others else value


def whole(dims):
    return pl.BlockSpec(dims, lambda *_: (0,) * len(dims))


def params(mib):
    return pltpu.CompilerParams(vmem_limit_bytes=mib * MIB)


def cost(flops, moved):
    return pl.CostEstimate(flops=1, bytes_accessed=1, transcendentals=0)


class Order:
    def __init__(self):
        self.last = None

    def run(self, step, value, *rest, need=()):
        out = step(after(value, self.last, *need), *rest)
        self.last = jax.tree.leaves(out)[0]
        return out

    def land(self, values):
        return jax.tree.map(lambda v: after(v, self.last), values)


def swap(value, axis, mask, size):
    return lax.ppermute(value, axis, [(i, i ^ mask) for i in range(size)])


def gather_far(own, size):
    pieces = {0: own}
    bit = size // 2
    while bit > 1:
        pieces.update({e | bit: swap(p, "head", bit, size) for e, p in pieces.items()})
        bit //= 2
    return pieces


def gather_near(far, size):
    pieces = dict(far)
    pieces.update({e | 1: swap(p, "head", 1, size) for e, p in far.items()})
    return [pieces[e] for e in range(size)]


def exchange_pieces(pieces, size):
    return [pieces[0]] + [swap(pieces[e], "head", e, size) for e in range(1, size)]


def total(terms):
    if len(terms) == 1:
        return terms[0]
    return sum(t.astype(F32) for t in terms).astype(BF16)


def reduce_pieces(pieces, size):
    held = {e: [p] for e, p in enumerate(pieces)}
    bit = 1
    while bit < size:
        for e in [e for e in held if e & bit]:
            sent = total(held.pop(e))
            held[e ^ bit].append(swap(sent, "head", bit, size))
        bit *= 2
    return held[0], sent


def sum_small(value, axis, size):
    bit = 1
    while bit < size:
        value = value + swap(value, axis, bit, size)
        bit *= 2
    return value


class BatchSum:
    def __init__(self, values, size):
        self.size = size
        self.place = lax.axis_index("batch")
        bits = [1 << i for i in range(size.bit_length() - 1)]
        if size == 8:
            self.bits = bits[:1]
            self.todo = [("halve", 1), ("in", 0), ("across", 0), ("out", 0), ("join", 1)]
        else:
            self.bits = bits
            self.todo = [("halve", b) for b in bits] + [("join", b) for b in reversed(bits)]
        self.values, self.mine, self.flying, self.sent = values, None, None, None
        self.start()

    def start(self):
        kind, bit = self.todo[0]
        self.sent = self.values
        if kind == "halve":
            rows = self.values.shape[0] // 2
            own = (self.place & bit) // bit
            self.mine = lax.dynamic_slice_in_dim(self.values, own * rows, rows, 0)
            self.sent = lax.dynamic_slice_in_dim(self.values, (1 - own) * rows, rows, 0)
        if kind in ("halve", "join"):
            self.flying = swap(self.sent, "batch", bit, self.size)
        else:
            hops = {"in": [(0, 1), (3, 2)], "across": [(1, 2), (2, 1)], "out": [(1, 0), (2, 3)]}[kind]
            pairs = [(2 * a + i, 2 * b + i) for a, b in hops for i in range(2)]
            self.flying = lax.ppermute(self.sent, "batch", pairs)

    def advance(self, order=None):
        if not self.todo:
            return []
        got = order.land(self.flying) if order else self.flying
        kind, _ = self.todo.pop(0)
        if not self.todo:
            self.parts = [self.values, got]
            return []
        if kind == "halve":
            self.values = total([self.mine, got])
        elif kind == "join":
            self.values = jnp.concatenate([self.values, got], axis=0)
        elif kind == "out":
            row = self.place // 2
            self.values = jnp.where((row == 1) | (row == 2), self.values, got)
        else:
            self.values = total([self.values, got])
        self.start()
        return [self.sent]

    def finish(self):
        while self.todo:
            self.advance()
        return self.parts, self.bits


def store_blocks(place, summed, refs, out):
    (first, _), bits = summed
    count = 1 << len(bits)
    rows = 2 * first.shape[0] // count
    for p in range(count):
        at = 0
        for level, bit in enumerate(bits):
            other = p >> (len(bits) - 1 - level) & 1
            at = at + (((place // bit) % 2) ^ other) * ((count >> (level + 1)) * rows)
        ref, row = refs[p * 2 // count], (p % (count // 2)) * rows
        out[pl.ds(pl.multiple_of(at, rows), rows), :] = ref[row : row + rows, :].astype(out.dtype)


def assemble(summed, place):
    parts, _ = summed
    rows, width = parts[0].shape

    def body(place, own_ref, other_ref, out):
        store_blocks(place[0], summed, (own_ref, other_ref), out)

    return pl.pallas_call(
        body,
        grid_spec=pltpu.PrefetchScalarGridSpec(
            num_scalar_prefetch=1,
            grid=(1,),
            in_specs=[whole((rows, width))] * 2,
            out_specs=whole((2 * rows, width)),
        ),
        out_shape=shape((2 * rows, width), F32),
        compiler_params=params(24),
        cost_estimate=cost(0, rows * width * 12),
        name="assemble",
    )(place, *parts)


def assemble_turned(sums, place, info, cols, n_head, out_rows, small_rows):
    pairs = len(sums)
    width = cols // pairs
    model = sums[0][0][0].shape[1]
    share = model // n_head
    counts = [2 * parts[0].shape[0] for parts, _ in sums]

    def body(place, info, *refs):
        ins, outs, held = refs[: 2 * pairs], refs[2 * pairs : 2 * pairs + 5], refs[2 * pairs + 5 :]
        for g in range(pairs):
            store_blocks(place[0], sums[g], ins[2 * g : 2 * g + 2], held[g])
            for i in range(3):
                for e in range(n_head):
                    at = pl.ds(pl.multiple_of((info[0] ^ e) * share, share), share)
                    block = held[g][i * width : (i + 1) * width, e * share : (e + 1) * share]
                    outs[i][at, g * width : (g + 1) * width] = block.T
        outs[3][...] = held[pairs - 1][3 * width : 3 * width + out_rows, :]
        first = 3 * width + out_rows
        outs[4][...] = held[pairs - 1][first : first + small_rows, :]

    flat = [part for parts, _ in sums for part in parts]
    return pl.pallas_call(
        body,
        grid_spec=pltpu.PrefetchScalarGridSpec(
            num_scalar_prefetch=2,
            grid=(1,),
            in_specs=[whole(h.shape) for h in flat],
            out_specs=[whole((model, cols))] * 3 + [whole((out_rows, model)), whole((small_rows, model))],
            scratch_shapes=[pltpu.VMEM((n, model), F32) for n in counts],
        ),
        out_shape=[shape((model, cols), F32)] * 3
        + [shape((out_rows, model), F32), shape((small_rows, model), F32)],
        compiler_params=params(32),
        cost_estimate=cost(0, cols * model * 24),
        name="assemble_turned",
    )(place, info, *flat)


def visible(first_key, first_query, starts, length, rows, cols):
    key = first_key + lax.broadcasted_iota(jnp.int32, (rows, cols), 0)
    query = first_query + lax.broadcasted_iota(jnp.int32, (rows, cols), 1)
    last = jnp.minimum(query, length - 1)
    return (key >= starts) & ((key <= last) | (key == query))


def turn(w_query, w_key, w_value, pair):
    model, cols = w_query.shape

    def body(q_ref, k_ref, v_ref, out):
        for g in range(cols // pair):
            for i, ref in enumerate((q_ref, k_ref, v_ref)):
                first = (3 * g + i) * pair
                out[first : first + pair, :] = ref[:, g * pair : (g + 1) * pair].T

    return pl.pallas_call(
        body,
        in_specs=[whole((model, cols))] * 3,
        out_specs=whole((3 * cols, model)),
        grid=(1,),
        out_shape=shape((3 * cols, model), BF16),
        compiler_params=params(24),
        cost_estimate=cost(0, 12 * cols * model),
        name="turn",
    )(w_query, w_key, w_value)


def attend_kernel(
    chunk, n_head, heads, chunk_len, share, info, *refs
):
    refs = list(refs)
    x_refs = [refs.pop(0) for _ in range(n_head)]
    w_ref, cos_ref, sin_ref, gain_ref, start_ref = [refs.pop(0) for _ in range(5)]
    old_k, old_v = None, None
    if chunk:
        old_k, old_v = refs.pop(0), refs.pop(0)
        refs = refs[7:]
    k_ref, ve_ref, v_ref, kt_ref, qt_ref, ot_ref, inv_ref, qf_ref, kf_ref, o_ref = refs[:10]
    raw, acc = refs[10:]
    me, length = info[0], info[1]
    cols = heads * HD
    pair = min(2, heads)
    for e in range(n_head):
        first = pl.multiple_of((me ^ e) * share, share)
        for third in range(3):
            rows = slice(third * cols, (third + 1) * cols)
            term = dot(w_ref[rows, pl.ds(first, share)], x_refs[e][...], 1, 1)
            if e == 0:
                raw[rows, :] = term
            else:
                raw[rows, :] += term

    def raw_row(part, h):
        return ((h // pair * 3 + part) * pair + h % pair) * HD

    cosine, sine = cos_ref[...], sin_ref[...]
    for h in range(heads):
        own = slice(h * HD, (h + 1) * HD)
        for part, factor_ref in ((0, qf_ref), (1, kf_ref)):
            base = raw_row(part, h)
            a, b = raw[base : base + HALF, :], raw[base + HALF : base + HD, :]
            front, back = a * cosine - b * sine, b * cosine + a * sine
            mean = jnp.sum(front * front + back * back, axis=0, keepdims=True) / HD
            factor = lax.rsqrt(mean + EPSILON)
            factor_ref[h] = factor
            unit = jnp.concatenate([front, back], axis=0) * factor
            low = (unit * gain_ref[own, :]).astype(BF16)
            if part == 0:
                qt_ref[own, :] = low * BF16(1.0 / math.sqrt(HD))
            else:
                kt_ref[own, :] = low
                k_ref[h] = low.T
        value = raw[raw_row(2, h) : raw_row(2, h) + HD, :].astype(BF16)
        v_ref[h] = value.T
        ve_ref[h, :HD, :] = value
        ve_ref[h, HD:, :] = jnp.ones((VALUE_ROWS - HD, chunk_len), BF16)

    blocks = chunk_len // BLOCK
    before = chunk * blocks

    def step(local, key_first, k_of, v_of, starts):
        query = slice(local * BLOCK, (local + 1) * BLOCK)
        mask = visible(key_first, (before + local) * BLOCK, starts, length, BLOCK, BLOCK)
        for h in range(heads):
            scores = dot(k_of(h), qt_ref[h * HD : (h + 1) * HD, query])
            probs = jnp.where(mask, jnp.exp(scores), 0.0).astype(BF16)
            acc[h] += dot(v_of(h), probs)

    for local in range(blocks):
        query = slice(local * BLOCK, (local + 1) * BLOCK)
        starts = start_ref[:, query]
        lowest = info[2 + before + local]
        acc[...] = jnp.zeros_like(acc)
        if chunk:

            @pl.loop(lowest, before)
            def _(kb):
                at = pl.ds(pl.multiple_of(kb * BLOCK, BLOCK), BLOCK)
                step(
                    local, kb * BLOCK, lambda h: old_k[h, at, :], lambda h: old_v[h, :, at], starts
                )

        @pl.loop(jnp.maximum(lowest - before, 0), local + 1)
        def _(kb):
            at = pl.ds(pl.multiple_of(kb * BLOCK, BLOCK), BLOCK)
            step(
                local,
                (before + kb) * BLOCK,
                lambda h: k_ref[h, at, :],
                lambda h: ve_ref[h, :, at],
                starts,
            )

        for h in range(heads):
            inverse = 1.0 / acc[h, HD : HD + 1, :]
            inv_ref[h, :, query] = inverse
            out = acc[h, :HD, :] * inverse
            ot_ref[h * HD : (h + 1) * HD, query] = out.astype(BF16)
            o_ref[query, h * HD : (h + 1) * HD] = out.T.astype(BF16)


def attend_chunk(
    chunk, x_pieces, w_t, cosine, sine, gain, starts, info, buffers, row_len, chunk_len
):
    n_head = len(x_pieces)
    share = x_pieces[0].shape[1]
    cols = w_t.shape[0] // 3
    heads = cols // HD
    model = w_t.shape[1]
    body = functools.partial(attend_kernel, chunk, n_head, heads, chunk_len, share)
    by_lane = lambda rows: pl.BlockSpec((rows, chunk_len), lambda i, info: (0, chunk))
    specs = [whole((chunk_len, share))] * n_head + [
        whole((3 * cols, model)),
        by_lane(HALF),
        by_lane(HALF),
        whole((cols, 1)),
        by_lane(1),
    ]
    operands = [*x_pieces, w_t, cosine, sine, gain, starts]
    aliases = {}
    if chunk:
        aliases = {1 + len(operands) + i: i for i in range(9)}
        specs += [whole((heads, row_len, HD)), whole((heads, VALUE_ROWS, row_len))]
        specs += [pl.BlockSpec(memory_space=pl.ANY)] * 7
        operands += buffers
    lane3 = lambda rows: pl.BlockSpec((heads, rows, chunk_len), lambda i, info: (0, 0, chunk))
    row3 = pl.BlockSpec((heads, chunk_len, HD), lambda i, info: (0, chunk, 0))
    outs = pl.pallas_call(
        body,
        grid_spec=pltpu.PrefetchScalarGridSpec(
            num_scalar_prefetch=1,
            grid=(1,),
            in_specs=specs,
            out_specs=[
                row3,
                lane3(VALUE_ROWS),
                row3,
                by_lane(cols),
                by_lane(cols),
                by_lane(cols),
                lane3(1),
                lane3(1),
                lane3(1),
                whole((chunk_len, cols)),
            ],
            scratch_shapes=[
                pltpu.VMEM((3 * cols, chunk_len), F32),
                pltpu.VMEM((heads, VALUE_ROWS, BLOCK), F32),
            ],
        ),
        out_shape=[
            kept_shape((heads, row_len, HD), BF16),
            kept_shape((heads, VALUE_ROWS, row_len), BF16),
            kept_shape((heads, row_len, HD), BF16),
            kept_shape((cols, row_len), BF16),
            kept_shape((cols, row_len), BF16),
            kept_shape((cols, row_len), BF16),
            kept_shape((heads, 1, row_len), F32),
            kept_shape((heads, 1, row_len), F32),
            kept_shape((heads, 1, row_len), F32),
            shape((chunk_len, cols), BF16),
        ],
        input_output_aliases=aliases,
        compiler_params=params(40),
        cost_estimate=cost(16e9 / CHUNKS, 8e6),
        name="attend",
    )(info, *operands)
    return outs[:9], outs[9]


def unattend_kernel(n_head, chunks, row_len, piece, pair, info, *refs):
    refs = list(refs)
    d_refs = [refs.pop(0) for _ in range(chunks * n_head)]
    k_ref, v_ref, kt_ref, qt_ref, ot_ref, inv_ref, qf_ref, kf_ref = [refs.pop(0) for _ in range(8)]
    start_ref, cos_ref, sin_ref, gain_ref = [refs.pop(0) for _ in range(4)]
    out_ref, gain_out, do_s, inner_s, dq_s, dk_s, dv_s = refs
    me, length = info[0], info[1]
    for c in range(chunks):
        for e in range(n_head):
            first = c * n_head * piece + (me ^ e) * piece
            do_s[:, pl.ds(pl.multiple_of(first, piece), piece)] = d_refs[c * n_head + e][...]
    for h in range(pair):
        own = slice(h * HD, (h + 1) * HD)
        product = do_s[own, :].astype(F32) * ot_ref[own, :].astype(F32)
        inner_s[h] = jnp.sum(product, axis=0, keepdims=True)
    dq_s[...] = jnp.zeros_like(dq_s)
    dk_s[...] = jnp.zeros_like(dk_s)
    dv_s[...] = jnp.zeros_like(dv_s)

    @pl.loop(0, row_len // BLOCK)
    def _(qb):
        query = pl.ds(pl.multiple_of(qb * BLOCK, BLOCK), BLOCK)
        starts = start_ref[:, query]

        @pl.loop(info[2 + qb], qb + 1)
        def _(kb):
            key = pl.ds(pl.multiple_of(kb * BLOCK, BLOCK), BLOCK)
            mask = visible(kb * BLOCK, qb * BLOCK, starts, length, BLOCK, BLOCK)
            for h in range(pair):
                own = slice(h * HD, (h + 1) * HD)
                q_block, do_block = qt_ref[own, query], do_s[own, query]
                scores = dot(k_ref[h, key, :], q_block)
                probs = jnp.where(mask, jnp.exp(scores), 0.0) * inv_ref[h, :, query]
                d_probs = dot(v_ref[h, key, :], do_block)
                d_scores = (probs * (d_probs - inner_s[h, :, query])).astype(BF16)
                dv_s[own, key] += dot(do_block, probs.astype(BF16), 1, 1)
                dk_s[own, key] += dot(q_block, d_scores, 1, 1)
                dq_s[own, query] += dot(kt_ref[own, key], d_scores)

    for h in range(pair):
        own = slice(h * HD, (h + 1) * HD)
        gain = gain_ref[own, :]
        summed = jnp.zeros((HD, 1), F32)
        for part, low_ref, grad_ref, factor_ref in (
            (0, qt_ref, dq_s, qf_ref),
            (1, kt_ref, dk_s, kf_ref),
        ):
            scale = math.sqrt(HD) if part == 0 else 1.0
            unit = low_ref[own, :].astype(F32) * (scale / gain)
            grad = grad_ref[own, :]
            if part == 0:
                grad = grad * (1.0 / math.sqrt(HD))
            summed += jnp.sum(grad * unit, axis=1, keepdims=True)
            grad = grad * gain
            mean = jnp.sum(grad * unit, axis=0, keepdims=True) / HD
            grad = (grad - unit * mean) * factor_ref[h]
            front, back = grad[:HALF], grad[HALF:]
            cosine, sine = cos_ref[...], sin_ref[...]
            out_ref[part, h * HD : h * HD + HALF, :] = (front * cosine + back * sine).astype(BF16)
            out_ref[part, h * HD + HALF : (h + 1) * HD, :] = (
                back * cosine - front * sine
            ).astype(BF16)
        out_ref[2, own, :] = dv_s[own, :].astype(BF16)
        gain_out[own, :] = summed


def unattend(index, do_pieces, buffers, starts, cosine, sine, gain, info, n_head):
    k, _, v, kt, qt, ot, inv, qf, kf = buffers
    chunks = len(do_pieces) // n_head
    cols, piece = do_pieces[0].shape
    heads, row_len, _ = k.shape
    pair = min(2, heads)
    rows = pair * HD
    by_rows = lambda width: pl.BlockSpec((rows, width), lambda g, info: (index, 0))
    by_head = lambda a, b: pl.BlockSpec((pair, a, b), lambda g, info: (index, 0, 0))
    return pl.pallas_call(
        functools.partial(unattend_kernel, n_head, chunks, row_len, piece, pair),
        grid_spec=pltpu.PrefetchScalarGridSpec(
            num_scalar_prefetch=1,
            grid=(1,),
            in_specs=[by_rows(piece)] * (chunks * n_head)
            + [by_head(row_len, HD)] * 2
            + [by_rows(row_len)] * 3
            + [by_head(1, row_len)] * 3
            + [whole((1, row_len)), whole((HALF, row_len)), whole((HALF, row_len)), by_rows(1)],
            out_specs=[whole((3, rows, row_len)), whole((rows, 1))],
            scratch_shapes=[
                pltpu.VMEM((rows, row_len), BF16),
                pltpu.VMEM((pair, 1, row_len), F32),
                pltpu.VMEM((rows, row_len), F32),
                pltpu.VMEM((rows, row_len), F32),
                pltpu.VMEM((rows, row_len), F32),
            ],
        ),
        out_shape=[shape((3, rows, row_len), BF16), shape((rows, 1), F32)],
        compiler_params=params(32),
        cost_estimate=cost(22e9, 6e6),
        name="unattend",
    )(info, *do_pieces, k, v, kt, qt, ot, inv, qf, kf, starts, cosine, sine, gain)


def norm(values):
    factor = lax.rsqrt(jnp.mean(values * values, axis=-1, keepdims=True) + EPSILON)
    return values * factor, factor


def norm_back(grad, unit, factor):
    return factor * (grad - unit * jnp.mean(grad * unit, axis=-1, keepdims=True))


def project_kernel(n_head, share, kept, info, *refs):
    o_refs, w_refs = refs[:n_head], refs[n_head : 2 * n_head]
    x_refs = refs[2 * n_head : 3 * n_head]
    alpha_ref = refs[3 * n_head]
    cat_ref, y_ref, x_ref, h_ref, low_ref = refs[3 * n_head + 1 + kept :]
    me = info[0]
    cols = w_refs[0].shape[0]
    y = dot(o_refs[0][...], w_refs[0][...])
    for e in range(1, n_head):
        y += dot(o_refs[e][...], w_refs[e][...])
    for e in range(n_head):
        cat_ref[:, e * cols : (e + 1) * cols] = o_refs[e][...]
    for e in range(n_head):
        first = pl.multiple_of((me ^ e) * share, share)
        x_ref[:, pl.ds(first, share)] = x_refs[e][...]
    y_ref[...] = y
    h_zero = x_ref[...].astype(F32)
    h_one, _ = norm(h_zero + alpha_ref[...] * (norm(y)[0] - h_zero))
    h_ref[...] = h_one
    low_ref[...] = h_one.astype(BF16)


def project(chunk, kept, o_pieces, w_pieces, x_pieces, alpha, info, chunk_len):
    n_head = len(o_pieces)
    cols, model = w_pieces[0].shape
    share = x_pieces[0].shape[1]
    rows = chunk_len // n_head
    mine = lambda width: pl.BlockSpec((rows, width), lambda i, info: (info[0], 0))
    return pl.pallas_call(
        functools.partial(project_kernel, n_head, share, len(kept)),
        grid_spec=pltpu.PrefetchScalarGridSpec(
            num_scalar_prefetch=1,
            grid=(1,),
            in_specs=[mine(cols)]
            + [whole((rows, cols))] * (n_head - 1)
            + [whole((cols, model))] * n_head
            + [mine(share)] * n_head
            + [whole((1, model))]
            + [pl.BlockSpec(memory_space=pl.ANY)] * len(kept),
            out_specs=[pl.BlockSpec((rows, n_head * cols), lambda i, info: (chunk, 0))]
            + [whole((rows, model))] * 4,
        ),
        input_output_aliases={3 * n_head + 2 + i: i for i in range(len(kept))},
        out_shape=[
            kept_shape((CHUNKS * rows, n_head * cols), BF16),
            kept_shape((rows, model), F32),
            kept_shape((rows, model), BF16),
            kept_shape((rows, model), F32),
            shape((rows, model), BF16),
        ],
        compiler_params=params(32),
        cost_estimate=cost(2.0 * rows * model * model, 6e6),
        name="project",
    )(info, *o_pieces, *w_pieces, *x_pieces, alpha, *kept)


def feed_kernel(n_head, rows, kept, *refs):
    h_refs = refs[:n_head]
    refs = refs[n_head:]
    up_ref, gate_ref, down_ref, su_ref, sg_ref = refs[:5]
    m_ref, cat_ref, u_ref, g_ref = refs[5 + kept : 9 + kept]
    refs = refs[9 + kept :]
    z_refs, acc = refs[:n_head], refs[n_head]
    tile = pl.program_id(0)

    @pl.when(tile == 0)
    def _():
        for e in range(n_head):
            cat_ref[e * rows : (e + 1) * rows, :] = h_refs[e][...]

    up_raw = dot(cat_ref[...], up_ref[...])
    gate_raw = dot(cat_ref[...], gate_ref[...])
    u_ref[...] = up_raw.astype(BF16)
    g_ref[...] = gate_raw.astype(BF16)
    gate = gate_raw * sg_ref[...]
    mixed = (up_raw * su_ref[...] * (gate * jax.nn.sigmoid(gate))).astype(BF16)
    m_ref[...] = mixed
    term = dot(mixed, down_ref[...])

    @pl.when(tile == 0)
    def _():
        acc[...] = term

    @pl.when(tile > 0)
    def _():
        acc[...] += term

    @pl.when(tile == pl.num_programs(0) - 1)
    def _():
        for e in range(n_head):
            z_refs[e][...] = acc[e * rows : (e + 1) * rows, :].astype(BF16)


def feed(chunk, kept, h_pieces, w_up, w_gate, w_down, scale_up, scale_gate):
    n_head = len(h_pieces)
    rows, model = h_pieces[0].shape
    hidden = w_up.shape[1]
    tile = min(256, hidden)
    count = n_head * rows
    by_col = lambda height: pl.BlockSpec((height, tile), lambda n: (0, n))
    outs = pl.pallas_call(
        functools.partial(feed_kernel, n_head, rows, len(kept)),
        grid=(hidden // tile,),
        in_specs=[whole((rows, model))] * n_head
        + [
            by_col(model),
            by_col(model),
            pl.BlockSpec((tile, model), lambda n: (n, 0)),
            by_col(1),
            by_col(1),
        ]
        + [pl.BlockSpec(memory_space=pl.ANY)] * len(kept),
        out_specs=[
            pl.BlockSpec((count, tile), lambda n: (chunk, n)),
            pl.BlockSpec((count, model), lambda n: (chunk, 0)),
            by_col(count),
            by_col(count),
        ]
        + [whole((rows, model))] * n_head,
        out_shape=[
            kept_shape((CHUNKS * count, hidden), BF16),
            kept_shape((CHUNKS * count, model), BF16),
            kept_shape((count, hidden), BF16),
            kept_shape((count, hidden), BF16),
        ]
        + [shape((rows, model), BF16)] * n_head,
        input_output_aliases={n_head + 5 + i: i for i in range(len(kept))},
        scratch_shapes=[pltpu.VMEM((count, model), F32)],
        compiler_params=params(48),
        cost_estimate=cost(6.0 * count * model * hidden, 20e6),
        name="feed",
    )(*h_pieces, w_up, w_gate, w_down, scale_up, scale_gate, *kept)
    return outs[:2], outs[2:4], list(outs[4:])


def middle_kernel(n_head, n_terms, share, info, *refs):
    z_refs, c_refs = refs[:n_terms], refs[n_terms : n_terms + n_head]
    h_ref, alpha_ref = refs[n_terms + n_head : n_terms + n_head + 2]
    refs = refs[n_terms + n_head + 2 :]
    out_refs = refs[:n_head]
    dz_ref, direct_ref, grad_ref, two_s, cot_s = refs[n_head:]
    me = info[0]
    z = z_refs[0][...].astype(F32)
    for r in z_refs[1:]:
        z += r[...].astype(F32)
    h_one, alpha = h_ref[...], alpha_ref[...]
    h_ffn, z_factor = norm(z)
    h_two, factor = norm(h_one + alpha * (h_ffn - h_one))
    two_s[...] = h_two.astype(BF16)
    for e in range(n_head):
        at = pl.ds(pl.multiple_of((me ^ e) * share, share), share)
        out_refs[e][...] = two_s[:, at]
        cot_s[:, at] = c_refs[e][...]
    grad = norm_back(cot_s[...].astype(F32), h_two, factor)
    grad_ref[...] = jnp.sum(grad * (h_ffn - h_one), axis=0, keepdims=True)
    direct_ref[...] = grad * (1.0 - alpha)
    dz_ref[...] = norm_back(grad * alpha, h_ffn, z_factor).astype(BF16)


def middle(chunk, z_terms, cot_pieces, h_one, alpha, info):
    n_head, n_terms = len(cot_pieces), len(z_terms)
    rows, model = h_one.shape
    share = cot_pieces[0].shape[1]
    mine = pl.BlockSpec((rows, share), lambda i, info: (chunk * n_head + info[0], 0))
    theirs = pl.BlockSpec((rows, share), lambda i, info: (1 + chunk, 0))
    outs = pl.pallas_call(
        functools.partial(middle_kernel, n_head, n_terms, share),
        grid_spec=pltpu.PrefetchScalarGridSpec(
            num_scalar_prefetch=1,
            grid=(1,),
            in_specs=[whole((rows, model))] * n_terms
            + [mine]
            + [theirs] * (n_head - 1)
            + [whole((rows, model)), whole((1, model))],
            out_specs=[whole((rows, share))] * n_head
            + [whole((rows, model))] * 2
            + [whole((1, model))],
            scratch_shapes=[pltpu.VMEM((rows, model), BF16), pltpu.VMEM((rows, model), BF16)],
        ),
        out_shape=[shape((rows, share), BF16)] * n_head
        + [shape((rows, model), BF16), shape((rows, model), F32), shape((1, model), F32)],
        compiler_params=params(32),
        cost_estimate=cost(rows * model * 60, rows * model * 24),
        name="middle",
    )(info, *z_terms, *cot_pieces, h_one, alpha)
    return list(outs[:n_head]), outs[n_head], outs[n_head + 1], outs[n_head + 2]


def join(pieces):
    rows, width = pieces[0].shape

    def body(*refs):
        for i, ref in enumerate(refs[:-1]):
            refs[-1][i * rows : (i + 1) * rows, :] = ref[...]

    return pl.pallas_call(
        body,
        in_specs=[whole((rows, width))] * len(pieces),
        out_specs=whole((rows * len(pieces), width)),
        grid=(1,),
        out_shape=shape((rows * len(pieces), width), pieces[0].dtype),
        compiler_params=params(16),
        cost_estimate=cost(0, rows * width * 4 * len(pieces)),
        name="join",
    )(*pieces)


def weigh(d_pair, x_pieces, chunk_len):
    rows, row_len = d_pair.shape
    n_head = len(x_pieces[0])
    share = x_pieces[0][0].shape[1]
    flat = [p for chunk in x_pieces for p in chunk]

    def body(d_ref, *refs):
        for e in range(n_head):
            term = None
            for c in range(len(x_pieces)):
                d_part = d_ref[:, c * chunk_len : (c + 1) * chunk_len]
                new = dot(d_part, refs[c * n_head + e][...])
                term = new if term is None else term + new
            refs[-1][:, e * share : (e + 1) * share] = term.astype(BF16)

    return pl.pallas_call(
        body,
        in_specs=[whole((rows, row_len))] + [whole((chunk_len, share))] * len(flat),
        out_specs=whole((rows, n_head * share)),
        grid=(1,),
        out_shape=shape((rows, n_head * share), BF16),
        compiler_params=params(32),
        cost_estimate=cost(0, 1),
        name="weigh",
    )(d_pair, *flat)


def unfeed_kernel(n_head, rows, kept, cat_ref, *refs):
    u_ref, g_ref, up_ref, gate_ref, down_ref, su_ref, sg_ref = refs[:7]
    du_ref, dg_ref, gsu_ref, gsg_ref = refs[7 + kept : 11 + kept]
    refs = refs[11 + kept :]
    out_refs, acc = refs[:n_head], refs[n_head]
    tile = pl.program_id(0)
    d_mixed = dot(cat_ref[...], down_ref[...], 1, 1)
    up_raw, gate_raw = u_ref[...].astype(F32), g_ref[...].astype(F32)
    gate = gate_raw * sg_ref[...]
    sigmoid = jax.nn.sigmoid(gate)
    d_up = d_mixed * (gate * sigmoid)
    d_gate = d_mixed * (up_raw * su_ref[...]) * sigmoid * (1.0 + gate * (1.0 - sigmoid))
    gsu_ref[...] = jnp.sum(d_up * up_raw, axis=0, keepdims=True)
    gsg_ref[...] = jnp.sum(d_gate * gate_raw, axis=0, keepdims=True)
    up_low = (d_up * su_ref[...]).astype(BF16)
    gate_low = (d_gate * sg_ref[...]).astype(BF16)
    du_ref[...] = up_low
    dg_ref[...] = gate_low
    term = dot(up_low, up_ref[...], 1, 1) + dot(gate_low, gate_ref[...], 1, 1)

    @pl.when(tile == 0)
    def _():
        acc[...] = term

    @pl.when(tile > 0)
    def _():
        acc[...] += term

    @pl.when(tile == pl.num_programs(0) - 1)
    def _():
        for e in range(n_head):
            out_refs[e][...] = acc[e * rows : (e + 1) * rows, :].astype(BF16)


def unfeed(chunk, kept, dz, u, g, w_up, w_gate, w_down, scale_up, scale_gate, n_head):
    count, model = dz.shape
    rows = count // n_head
    hidden = w_up.shape[1]
    tile = min(256, hidden)
    by_col = lambda height: pl.BlockSpec((height, tile), lambda n: (0, n))
    outs = pl.pallas_call(
        functools.partial(unfeed_kernel, n_head, rows, len(kept)),
        grid=(hidden // tile,),
        in_specs=[
            whole((count, model)),
            by_col(count),
            by_col(count),
            by_col(model),
            by_col(model),
            pl.BlockSpec((tile, model), lambda n: (n, 0)),
            by_col(1),
            by_col(1),
        ]
        + [pl.BlockSpec(memory_space=pl.ANY)] * len(kept),
        out_specs=[pl.BlockSpec((count, tile), lambda n: (chunk, n))] * 2
        + [by_col(1), by_col(1)]
        + [whole((rows, model))] * n_head,
        out_shape=[kept_shape((CHUNKS * count, hidden), BF16)] * 2
        + [shape((1, hidden), F32), shape((1, hidden), F32)]
        + [shape((rows, model), BF16)] * n_head,
        input_output_aliases={8 + i: i for i in range(len(kept))},
        scratch_shapes=[pltpu.VMEM((count, model), F32)],
        compiler_params=params(48),
        cost_estimate=cost(6.0 * count * model * hidden, 20e6),
        name="unfeed",
    )(dz, u, g, w_up, w_gate, w_down, scale_up, scale_gate, *kept)
    return outs[:2], outs[2:4], list(outs[4:])


def unproject_kernel(n_head, n_terms, kept, *refs):
    t_refs, w_refs = refs[:n_terms], refs[n_terms : n_terms + n_head]
    direct_ref, y_ref, x_ref, alpha_ref = refs[n_terms + n_head : n_terms + n_head + 4]
    refs = refs[n_terms + n_head + 4 + kept :]
    dy_ref, refs = refs[0], refs[1:]
    do_refs = refs[:n_head]
    zero_ref, grad_ref = refs[n_head:]
    grad = direct_ref[...]
    for r in t_refs:
        grad += r[...].astype(F32)
    alpha = alpha_ref[...]
    h_zero = x_ref[...].astype(F32)
    h_attn, y_factor = norm(y_ref[...])
    h_one, factor = norm(h_zero + alpha * (h_attn - h_zero))
    grad = norm_back(grad, h_one, factor)
    grad_ref[...] = jnp.sum(grad * (h_attn - h_zero), axis=0, keepdims=True)
    zero_ref[...] = grad * (1.0 - alpha)
    dy = norm_back(grad * alpha, h_attn, y_factor).astype(BF16)
    dy_ref[...] = dy
    for e in range(n_head):
        do_refs[e][...] = dot(w_refs[e][...], dy, 1, 1).astype(BF16)


def unproject(chunk, kept, terms, w_pieces, direct, y, x, alpha):
    n_head, n_terms = len(w_pieces), len(terms)
    rows, model = y.shape
    cols = w_pieces[0].shape[0]
    outs = pl.pallas_call(
        functools.partial(unproject_kernel, n_head, n_terms, len(kept)),
        grid=(1,),
        in_specs=[whole((rows, model))] * n_terms
        + [whole((cols, model))] * n_head
        + [whole((rows, model))] * 3
        + [whole((1, model))]
        + [pl.BlockSpec(memory_space=pl.ANY)] * len(kept),
        out_specs=[pl.BlockSpec((rows, model), lambda i: (chunk, 0))]
        + [whole((cols, rows))] * n_head
        + [whole((rows, model)), whole((1, model))],
        input_output_aliases={n_terms + n_head + 4 + i: i for i in range(len(kept))},
        out_shape=[kept_shape((CHUNKS * rows, model), BF16)]
        + [shape((cols, rows), BF16)] * n_head
        + [shape((rows, model), F32), shape((1, model), F32)],
        compiler_params=params(32),
        cost_estimate=cost(2.0 * rows * model * model, 8e6),
        name="unproject",
    )(*terms, *w_pieces, direct, y, x, alpha, *kept)
    return outs[0], list(outs[1 : n_head + 1]), outs[n_head + 1], outs[n_head + 2]


def spread_kernel(n_head, share, pairs, info, *refs):
    d_refs, (w_ref, direct_ref), out_refs = refs[:pairs], refs[pairs : pairs + 2], refs[pairs + 2 :]
    me = info[0]
    block = pl.program_id(0)
    d_all = jnp.concatenate([r[...] for r in d_refs], axis=0).T
    for e in range(n_head):
        at = pl.ds(pl.multiple_of((me ^ e) * share, share), share)
        term = dot(d_all, w_ref[:, at])

        @pl.when(block == me)
        def _():
            out_refs[e][...] = (term + direct_ref[:, at]).astype(BF16)

        @pl.when(block != me)
        def _():
            out_refs[e][...] = term.astype(BF16)


def spread(chunk, chunk_len, d_all, w_t, direct, info, n_head):
    rows3, model = w_t.shape
    share = model // n_head
    rows = chunk_len // n_head
    return pl.pallas_call(
        functools.partial(spread_kernel, n_head, share, len(d_all)),
        grid_spec=pltpu.PrefetchScalarGridSpec(
            num_scalar_prefetch=1,
            grid=(n_head,),
            in_specs=[
                *[pl.BlockSpec((d.shape[0], rows), lambda i, info: (0, chunk * n_head + i)) for d in d_all],
                whole((rows3, model)),
                whole((rows, model)),
            ],
            out_specs=[pl.BlockSpec((rows, share), lambda i, info: (i, 0))] * n_head,
        ),
        out_shape=[shape((chunk_len, share), BF16)] * n_head,
        compiler_params=params(32),
        cost_estimate=cost(2.0 * chunk_len * model * rows3, 8e6),
        name="spread",
    )(info, *d_all, w_t, direct)


def on_device(
    n_batch,
    n_head,
    hidden_in,
    cotangent,
    doc_ids,
    lengths,
    w_query,
    w_key,
    w_value,
    w_out,
    w_up,
    w_gate,
    w_down,
    scale_qk,
    scale_up,
    scale_gate,
    alpha_attn,
    alpha_ffn,
):
    _, row_len, share = hidden_in.shape
    model = share * n_head
    cols = w_query.shape[1]
    chunk_len = row_len // CHUNKS
    rows = chunk_len // n_head
    me = lax.axis_index("head")
    chunks = range(CHUNKS)
    x_own, cot_own = hidden_in[0], cotangent[0]

    docs = doc_ids[0]
    column = jnp.arange(row_len, dtype=jnp.int32)
    starts = sum(
        jnp.where(docs > d, jnp.sum((docs == d).astype(jnp.int32)), 0) for d in range(5)
    ).astype(jnp.int32)
    position = (column - starts).astype(F32)
    frequency = 10000.0 ** (-(jnp.arange(HALF, dtype=F32) * 2.0 / HD))
    angles = frequency[:, None] * position[None, :]
    cosine, sine = jnp.cos(angles), jnp.sin(angles)
    info = jnp.concatenate(
        [me[None].astype(jnp.int32), lengths.astype(jnp.int32), starts[::BLOCK] // BLOCK]
    )
    starts = starts[None, :]
    gain = scale_qk[:, None]
    up_scale, gate_scale = scale_up[None, :], scale_gate[None, :]
    attn_alpha, ffn_alpha = alpha_attn[None, :], alpha_ffn[None, :]

    def part(values, c):
        return lax.slice_in_dim(values, c * chunk_len, (c + 1) * chunk_len, axis=0)

    def block_of(values, e):
        return lax.dynamic_slice_in_dim(values, (me ^ e) * rows, rows, 0)

    order = Order()
    pair = min(2, cols // HD) * HD
    pairs = cols // pair
    w_t = turn(w_query, w_key, w_value, pair)

    def block_parts(values):
        return [values] + [block_of(values, e) for e in range(1, n_head)]

    bit = lax.axis_index("batch") % 2
    half = model // 2
    out_half = lax.dynamic_slice_in_dim(w_out, bit * half, half, 1)
    out_half = jnp.concatenate(
        [out_half[:, i : i + share] for i in range(0, half, share)], axis=0
    )
    far = n_head // 2
    x_far = gather_far(part(x_own, 0), n_head)

    buffers, x_pieces, o_flying = [], [], []
    for c in chunks:
        near = x_far if c == 0 else {e: p[:chunk_len] for e, p in x_far.items()}
        x_pieces.append(gather_near(near, n_head))
        if c < CHUNKS - 1:
            following = part(x_own, c + 1)
            if c == 0:
                following = jnp.concatenate([following, out_half], axis=0)
            x_far = gather_far(after(following, x_far[far]), n_head)
        buffers, o_chunk = order.run(
            lambda w: attend_chunk(
                c, x_pieces[c], w, cosine, sine, gain, starts, info, buffers, row_len, chunk_len
            ),
            w_t,
            need=x_pieces[c],
        )
        order.last = o_chunk
        pieces = block_parts(o_chunk)
        if c == 0:
            cots = [block_parts(part(cot_own, i)) for i in chunks]
            pieces[1:] = [
                jnp.concatenate([p] + [cot[e] for cot in cots], axis=0)
                for e, p in enumerate(pieces)
                if e
            ]
        o_flying.append(exchange_pieces(pieces, n_head))
        if c == 0:
            x_far = order.land(x_far)
            out_far = {e: p[chunk_len:] for e, p in x_far.items()}
            out_far = {e: (v, swap(v, "batch", 1, n_batch)) for e, v in out_far.items() if e}

    def out_of(first, second):
        blocks = [
            v[i : i + cols] for v in (first, second) for i in range(0, first.shape[0], cols)
        ]
        return jnp.concatenate(blocks, axis=1)

    out_far = {
        e: jnp.where(bit == 0, out_of(v, w), out_of(w, v))
        for e, (v, w) in order.land(out_far).items()
    }
    out_far[0] = w_out
    out_pieces = gather_near(out_far, n_head)

    state, h_fars, joined = [], [], []
    for c in chunks:
        o_pieces = order.land(o_flying[c])
        joined, y, x_rows, h_one, h_low = order.run(
            lambda first: project(
                c,
                joined,
                [first] + o_pieces[1:],
                out_pieces,
                x_pieces[c],
                attn_alpha,
                info,
                chunk_len,
            ),
            o_pieces[0],
            need=o_pieces[1:],
        )
        joined = [joined]
        order.last = h_low
        state.append((y, x_rows, h_one))
        before = h_fars[-1][far] if c else None
        if c < CHUNKS - 1:
            before = o_flying[c + 1][far]
        h_fars.append(gather_far(after(h_low, before), n_head))
    cot_pieces = [cot_own] + o_flying[0][1:]

    fed, raws, z_all, z_flying, sent = [], [], [], [], None
    for c in chunks:
        h_pieces = gather_near(order.land(h_fars[c]), n_head)
        fed, raw, z_pieces = order.run(
            lambda first: feed(
                c,
                fed,
                [first] + h_pieces[1:],
                w_up,
                w_gate,
                w_down,
                up_scale,
                gate_scale,
            ),
            h_pieces[0],
            need=h_pieces[1:] + [sent],
        )
        order.last = z_pieces[0]
        raws.append(raw)
        z_all.append(z_pieces)
        if c < CHUNKS - 1:
            terms, sent = reduce_pieces(z_pieces, n_head)
            z_flying.append(terms)
    mixed, h_cat = fed

    mids, dz_fars = [], []
    for c in chunks:
        if c == CHUNKS - 1:
            terms, _ = reduce_pieces(order.land(z_all[c]) if c else z_all[c], n_head)
            z_flying.append(terms)
        terms = order.land(z_flying[c])
        mid = order.run(
            lambda first: middle(
                c, [first] + terms[1:], cot_pieces, state[c][2], ffn_alpha, info
            ),
            terms[0],
            need=terms[1:],
        )
        mids.append(mid)
        dz = mid[1]
        order.last = dz
        dz_fars.append(gather_far(after(dz, dz_fars[-1][far]) if c else dz, n_head))

    place = lax.axis_index("batch")[None].astype(jnp.int32)
    unfed, scale_sums, dh_all, dh_flying, dzs, sent = [], [], [], [], [], None
    for c in chunks:
        dz_pieces = gather_near(order.land(dz_fars[c]), n_head)
        dzs.append(
            order.run(lambda first: join([first] + dz_pieces[1:]), dz_pieces[0], need=dz_pieces[1:])
        )
        need = [sent]
        if c == CHUNKS - 1:
            grad_down = order.run(
                lambda first: sum(
                    dot(part(mixed, i), (dzs[:-1] + [first])[i], 0, 0) for i in chunks
                ).astype(BF16),
                dzs[c],
                need=[sent],
            )
            sum_down = BatchSum(grad_down, n_batch)
            need.append(sum_down.sent)
        unfed, sums, pieces = order.run(
            lambda first: unfeed(
                c, unfed, first, *raws[c], w_up, w_gate, w_down, up_scale, gate_scale, n_head
            ),
            dzs[c],
            need=need,
        )
        order.last = pieces[0]
        scale_sums.append(jnp.concatenate(sums, axis=0))
        dh_all.append(pieces)
        if c < CHUNKS - 1:
            terms, sent = reduce_pieces(pieces, n_head)
            dh_flying.append(terms)

    do_pieces, zeros, alphas, dys = [], [], [], []

    def back(c):
        y, x_rows, _ = state[c]
        terms = order.land(dh_flying[c])
        dy, d_pieces, zero, grad_alpha_attn = order.run(
            lambda first: unproject(
                c, dys, [first] + terms[1:], out_pieces, mids[c][2], y, x_rows, attn_alpha
            ),
            terms[0],
            need=terms[1:],
        )
        order.last = d_pieces[0]
        dys[:] = [dy]
        do_pieces.extend(exchange_pieces(d_pieces, n_head))
        zeros.append(zero)
        alphas.append(grad_alpha_attn)

    for c in chunks[:-1]:
        back(c)
    terms, sent = reduce_pieces(order.land(dh_all[-1]) if CHUNKS > 1 else dh_all[-1], n_head)
    dh_flying.append(terms)
    moved = sum_down.advance(order)
    grad_up = order.run(
        lambda h: dot(h, unfed[0], 0, 0).astype(BF16), h_cat, need=[sent] + moved
    )
    sum_up = BatchSum(grad_up, n_batch)
    grad_gate = order.run(
        lambda h: dot(h, unfed[1], 0, 0).astype(BF16), h_cat, need=[sum_up.sent]
    )
    back(CHUNKS - 1)
    sum_gate = BatchSum(after(grad_gate, sum_up.flying), n_batch)
    moved = sum_down.advance(order) + sum_up.advance(order) + [sum_gate.sent]
    do_pieces = order.land(do_pieces)

    alpha_sums = jnp.concatenate([sum(alphas), sum(m[3] for m in mids)], axis=0)
    alpha_sums = sum_small(alpha_sums, "head", n_head)
    d_all, gains, attn_sums = [], [], []
    sums = [sum_down, sum_up, sum_gate]
    for g in range(pairs):
        d_pair, grad_gain = order.run(
            lambda first: unattend(
                g, [first] + do_pieces[1:], buffers, starts, cosine, sine, gain, info, n_head
            ),
            do_pieces[0],
            need=do_pieces[1:] + moved,
        )
        order.last = d_pair
        moved = [m for b in sums for m in b.advance(order)]
        d_pair = d_pair.reshape(3 * pair, row_len)
        d_all.append(d_pair)
        gains.append(grad_gain[:, 0])
        if g == 0:
            out_terms = order.run(lambda o: dot(o, dys[0], 0, 0).astype(BF16), joined[0])
            out_terms = [out_terms[e * cols : (e + 1) * cols] for e in range(n_head)]
            out_flying, _ = reduce_pieces(out_terms, n_head)
            outgoing = order.land(
                [jnp.concatenate([m[0][e] for m in mids], axis=0) for e in range(n_head)]
            )
            hidden_flying = exchange_pieces(outgoing, n_head)
        grads = order.run(lambda d: weigh(d, x_pieces, chunk_len), d_pair, need=moved)
        if g == pairs - 1:
            small = jnp.concatenate(
                [alpha_sums]
                + [
                    jnp.pad(v, ((0, 0), (0, model - v.shape[1])))
                    for v in (sum(scale_sums), jnp.concatenate(gains)[None])
                ],
                axis=0,
            )
            unit = 32 if n_batch == 8 else 16 * n_batch
            rows_now = 3 * pair + cols + 5
            small = jnp.pad(small, ((0, 5 - small.shape[0] + -rows_now % unit), (0, 0)))
            grads = jnp.concatenate(
                [grads, total(order.land(out_flying)), small.astype(BF16)], axis=0
            )
        attn_sums.append(BatchSum(grads, n_batch))
        moved = [attn_sums[-1].sent]
    sums += attn_sums

    grad_hidden = []
    for c in chunks:
        d_pieces = order.run(
            lambda w: spread(c, chunk_len, d_all, w, zeros[c], info, n_head), w_t, need=moved
        )
        moved = [m for b in sums for m in b.advance(order)]
        terms, _ = reduce_pieces(d_pieces, n_head)
        grad_hidden.append(sum(t.astype(F32) for t in terms))
    grad_hidden = jnp.concatenate(grad_hidden, axis=0)[None]
    while any(b.todo for b in sums):
        for b in sums:
            b.advance()

    grad_down = assemble(sum_down.finish(), place)
    grad_up = assemble(sum_up.finish(), place)
    grad_gate = assemble(sum_gate.finish(), place)
    grad_query, grad_key, grad_value, grad_out, small = assemble_turned(
        [b.finish() for b in attn_sums], place, info, cols, n_head, cols, small.shape[0]
    )
    alpha_own = lax.dynamic_slice_in_dim(small[:2], me * share, share, 1)
    hidden_units = w_up.shape[1]

    stacked = jnp.stack(hidden_flying)
    hidden_out = jnp.concatenate(
        [
            lax.dynamic_index_in_dim(stacked, b ^ me, 0, keepdims=False)[c * rows : (c + 1) * rows]
            for c in chunks
            for b in range(n_head)
        ],
        axis=0,
    )[None]
    return (
        hidden_out,
        grad_hidden,
        grad_query,
        grad_key,
        grad_value,
        grad_out,
        grad_up,
        grad_gate,
        grad_down,
        small[4, :cols],
        small[2, :hidden_units],
        small[3, :hidden_units],
        alpha_own[0],
        alpha_own[1],
    )


def solution(mesh):
    split = P("batch", None, "head")
    by_col, by_row, by_head = P(None, "head"), P("head", None), P("head")
    return jax.shard_map(
        functools.partial(on_device, mesh.shape["batch"], mesh.shape["head"]),
        mesh=mesh,
        in_specs=(split, split, P("batch", None), P("batch"))
        + (by_col, by_col, by_col, by_row, by_col, by_col, by_row)
        + (by_head, by_head, by_head, P(), P()),
        out_specs=(split, split, by_col, by_col, by_col, by_row, by_col, by_col, by_row)
        + (by_head,) * 5,
        check_vma=False,
    )
```

```python
import functools
import math

import jax
import jax.numpy as jnp
from jax import lax
from jax.experimental import pallas as pl
from jax.experimental.pallas import tpu as pltpu
from jax.sharding import PartitionSpec as P

HD = 64
HALF = HD // 2
VALUE_ROWS = 80
EPSILON = 1e-06
BLOCK = 256
CHUNKS = 2
F32 = jnp.float32
BF16 = jnp.bfloat16
MIB = 1024 * 1024


def dot(left, right, left_dim=1, right_dim=0):
    return lax.dot_general(
        left, right, (((left_dim,), (right_dim,)), ((), ())), preferred_element_type=F32
    )


def shape(dims, dtype):
    return jax.ShapeDtypeStruct(dims, dtype)


def kept_shape(dims, dtype):
    return pltpu.HBM(dims, dtype)


def held(array):
    return pltpu.with_memory_space_constraint(array, pltpu.HBM)


def after(value, *others):
    others = [o for o in others if o is not None]
    return lax.optimization_barrier((value, *others))[0] if others else value


def whole(dims):
    return pl.BlockSpec(dims, lambda *_: (0,) * len(dims))


def term_spec(term):
    if term.ndim == 3:
        return pl.BlockSpec((None, *term.shape[1:]), lambda *_: (0, 0, 0))
    return whole(term.shape)


def params(mib):
    return pltpu.CompilerParams(vmem_limit_bytes=mib * MIB)


def cost(flops, moved):
    return pl.CostEstimate(flops=int(flops), bytes_accessed=int(moved), transcendentals=0)


class Order:
    def __init__(self):
        self.last = None

    def run(self, step, value, need=(), beside=()):
        out = step(after(value, self.last, *need))
        out, beside = lax.optimization_barrier((out, beside))
        self.last = jax.tree.leaves(out)[0]
        return out, beside


def swap(value, axis, mask, size):
    return lax.ppermute(value, axis, [(i, i ^ mask) for i in range(size)])


def gather_far(own, size):
    pieces = {0: own}
    bit = size // 2
    while bit > 1:
        pieces.update({e | bit: swap(p, "head", bit, size) for e, p in pieces.items()})
        bit //= 2
    return pieces


def gather_near(far, size):
    pieces = dict(far)
    pieces.update({e | 1: swap(p, "head", 1, size) for e, p in far.items()})
    return [pieces[e] for e in range(size)]


class Exchange:
    def __init__(self, near, far, size):
        self.size = size
        if size == 4:
            self.flying = [swap(near, "head", 1, size), swap(far, "head", 2, size)]
        else:
            blocks = [near, *far]
            self.flying = [swap(p, "head", e, size) for e, p in enumerate(blocks, 1)]

    def finish(self, flying):
        if self.size != 4:
            return flying
        near, far = flying
        return [near, far[0], swap(far[1], "head", 1, self.size)]


def total(terms):
    if len(terms) == 1:
        return terms[0]
    return sum(t.astype(F32) for t in terms).astype(BF16)


def reduce_near(odd, size):
    return jax.tree.map(lambda p: swap(p, "head", 1, size), odd)


def reduce_far(even, near, size):
    held = {2 * i: [p, near[i]] for i, p in enumerate(even)}
    bit, sent = 2, None
    while bit < size:
        for e in [e for e in held if e & bit]:
            sent = total(held.pop(e))
            got = swap(sent, "head", bit, size)
            held[e ^ bit].append(got)
        bit *= 2
    return held[0], sent


def term_sum(terms):
    return sum((t[0] if t.ndim == 3 else t).astype(F32) for t in terms)


def sum_small(value, axis, size):
    bit = 1
    while bit < size:
        value = value + swap(value, axis, bit, size)
        bit *= 2
    return value


def halve(values, bit, place):
    rows = values.shape[0] // 2
    own = (place & bit) // bit
    return tuple(
        lax.dynamic_slice_in_dim(values, part * rows, rows, 0) for part in (own, 1 - own)
    )


class BatchSum:
    def __init__(self, values, size, direct=False, before=()):
        self.size = size
        self.place = lax.axis_index("batch")
        self.bits = [1 << i for i in range(size.bit_length() - 1)]
        self.todo = [("halve", b) for b in self.bits] + [("join", b) for b in reversed(self.bits)]
        if direct and size <= 8:
            self.bits = self.bits[:1] + self.bits[:0:-1]
            self.todo = [("halve", 1), ("scatter", 0), ("gather", 0), ("join", 1)]
        self.values, self.mine, self.flying, self.sent = values, None, None, None
        self.before = list(before)
        self.start()

    def start(self):
        kind, bit = self.todo[0]
        self.sent = self.values
        if kind == "halve":
            self.mine, self.sent = halve(self.values, bit, self.place)
        others = range(1, self.size // 2)
        if kind == "scatter":
            rows = self.values.shape[0] * 2 // self.size
            own = self.place // 2
            blocks = [
                lax.dynamic_slice_in_dim(self.values, (own ^ d) * rows, rows, 0)
                for d in range(self.size // 2)
            ]
            self.mine, self.sent = blocks[0], blocks[-1]
            self.flying = [swap(blocks[d], "batch", 2 * d, self.size) for d in others]
        elif kind == "gather":
            self.flying = [swap(self.values, "batch", 2 * d, self.size) for d in others]
        else:
            self.flying = swap(self.sent, "batch", bit, self.size)

    def advance(self, got):
        kind, _ = self.todo.pop(0)
        if not self.todo:
            self.parts = [self.values, got]
        elif kind == "halve":
            self.values = total([self.mine, got])
        elif kind == "scatter":
            self.values = total([self.mine] + got)
        else:
            got = got if kind == "gather" else [got]
            self.values = jnp.concatenate([self.values] + got, axis=0)
        if self.before:
            self.values = jnp.concatenate(self.before + [self.values], axis=0)
            self.before = []
        if self.todo:
            self.start()

    def finish(self):
        while self.todo:
            self.advance(self.flying)
        return self.parts, self.bits


def store_blocks(place, summed, refs, out):
    (first, _), bits = summed
    count = 1 << len(bits)
    rows = 2 * first.shape[0] // count
    for p in range(count):
        at = 0
        for level, bit in enumerate(bits):
            other = p >> (len(bits) - 1 - level) & 1
            at = at + (((place // bit) % 2) ^ other) * ((count >> (level + 1)) * rows)
        ref, row = refs[p * 2 // count], (p % (count // 2)) * rows
        out[pl.ds(pl.multiple_of(at, rows), rows), :] = ref[row : row + rows, :].astype(out.dtype)


def segments(first, count, ranges):
    half, skip = sum(ranges) // 2, 0
    found = []
    for size in ranges:
        part = size // 2
        for side in range(2):
            low, high = max(first, 0), min(first + count, part)
            if low < high:
                found.append((side * half + skip + low, low - first, high - low))
            first -= part
        skip += part
    return found


def assemble(summed, place):
    parts, _ = summed
    rows, width = parts[0].shape

    def body(place, own_ref, other_ref, out):
        store_blocks(place[0], summed, (own_ref, other_ref), out)

    return pl.pallas_call(
        body,
        grid_spec=pltpu.PrefetchScalarGridSpec(
            num_scalar_prefetch=1,
            grid=(1,),
            in_specs=[whole((rows, width))] * 2,
            out_specs=whole((2 * rows, width)),
        ),
        out_shape=shape((2 * rows, width), F32),
        compiler_params=params(24),
        cost_estimate=cost(0, rows * width * 12),
        name="assemble",
    )(place, *parts)


def assemble_turned(summed, place, info, cols, n_head, pairs, ranges):
    parts, _ = summed
    width = cols // pairs
    rows, model = parts[0].shape
    share = model // n_head

    def body(place, info, own_ref, other_ref, q_out, k_out, v_out, o_out, small_out, room):
        store_blocks(place[0], summed, (own_ref, other_ref), room)
        for g in range(pairs):
            for i, out in enumerate((q_out, k_out, v_out)):
                for row, offset, count in segments((3 * g + i) * width, width, ranges):
                    lanes = slice(g * width + offset, g * width + offset + count)
                    for e in range(n_head):
                        at = pl.ds(pl.multiple_of((info[0] ^ e) * share, share), share)
                        out[at, lanes] = room[row : row + count, e * share : (e + 1) * share].T
        for out, first, rows in ((o_out, 3 * cols, cols), (small_out, 4 * cols, 8)):
            for row, offset, count in segments(first, rows, ranges):
                out[offset : offset + count, :] = room[row : row + count, :]

    return pl.pallas_call(
        body,
        grid_spec=pltpu.PrefetchScalarGridSpec(
            num_scalar_prefetch=2,
            grid=(1,),
            in_specs=[whole((rows, model))] * 2,
            out_specs=[whole((model, cols))] * 3 + [whole((cols, model)), whole((8, model))],
            scratch_shapes=[pltpu.VMEM((2 * rows, model), F32)],
        ),
        out_shape=[shape((model, cols), F32)] * 3 + [shape((n, model), F32) for n in (cols, 8)],
        compiler_params=params(32),
        cost_estimate=cost(0, cols * model * 24),
        name="assemble_turned",
    )(place, info, *parts)


def visible(first_key, first_query, starts, length, rows, cols):
    key = first_key + lax.broadcasted_iota(jnp.int32, (rows, cols), 0)
    query = first_query + lax.broadcasted_iota(jnp.int32, (rows, cols), 1)
    last = jnp.minimum(query, length - 1)
    return (key >= starts) & ((key <= last) | (key == query))


def prepare(w_query, w_key, w_value, w_out, cotangent, own, pair, n_head):
    model, cols = w_query.shape
    row_len, share = cotangent.shape
    rows = row_len // CHUNKS // n_head

    def body(own, q_ref, k_ref, v_ref, o_ref, c_ref, out, half, near, far_blocks):
        for g in range(cols // pair):
            for i, ref in enumerate((q_ref, k_ref, v_ref)):
                first = (3 * g + i) * pair
                out[first : first + pair, :] = ref[:, g * pair : (g + 1) * pair].T
        half[...] = o_ref[:, pl.ds(pl.multiple_of(own[1] * (model // 2), model // 2), model // 2)]
        for e in range(1, n_head):
            for c in range(CHUNKS):
                at = (c * n_head + (own[0] ^ e)) * rows
                block = c_ref[pl.ds(pl.multiple_of(at, rows), rows), :]
                if e == 1:
                    near[c * rows : (c + 1) * rows, :] = block
                else:
                    far_blocks[e - 2, c * rows : (c + 1) * rows, :] = block

    outs = pl.pallas_call(
        body,
        grid_spec=pltpu.PrefetchScalarGridSpec(
            num_scalar_prefetch=1,
            grid=(1,),
            in_specs=[whole((model, cols))] * 3 + [whole((cols, model)), whole((row_len, share))],
            out_specs=[
                whole((3 * cols, model)),
                whole((cols, model // 2)),
                whole((CHUNKS * rows, share)),
                whole((n_head - 2, CHUNKS * rows, share)),
            ],
        ),
        out_shape=[
            shape((3 * cols, model), BF16),
            shape((cols, model // 2), BF16),
            shape((CHUNKS * rows, share), BF16),
            shape((n_head - 2, CHUNKS * rows, share), BF16),
        ],
        compiler_params=params(24),
        cost_estimate=cost(0, 12 * cols * model),
        name="prepare",
    )(own, w_query, w_key, w_value, w_out, cotangent)
    return outs


def attend_kernel(
    chunk, n_head, heads, chunk_len, share, info, *refs
):
    refs = list(refs)
    x_refs = [refs.pop(0) for _ in range(n_head)]
    w_ref, cos_ref, sin_ref, gain_ref, start_ref = [refs.pop(0) for _ in range(5)]
    old_k, old_v = None, None
    if chunk:
        old_k, old_v = refs.pop(0), refs.pop(0)
        refs = refs[7:]
    k_ref, ve_ref, v_ref, kt_ref, qt_ref, ot_ref, inv_ref, qf_ref, kf_ref, o_ref = refs[:10]
    near_ref, far_ref, raw, acc = refs[10:]
    me, length = info[0], info[1]
    cols = heads * HD
    pair = min(2, heads)
    for e in range(n_head):
        first = pl.multiple_of((me ^ e) * share, share)
        for third in range(3):
            rows = slice(third * cols, (third + 1) * cols)
            term = dot(w_ref[rows, pl.ds(first, share)], x_refs[e][...], 1, 1)
            if e == 0:
                raw[rows, :] = term
            else:
                raw[rows, :] += term

    def raw_row(part, h):
        return ((h // pair * 3 + part) * pair + h % pair) * HD

    cosine, sine = cos_ref[...], sin_ref[...]
    for h in range(heads):
        own = slice(h * HD, (h + 1) * HD)
        for part, factor_ref in ((0, qf_ref), (1, kf_ref)):
            base = raw_row(part, h)
            a, b = raw[base : base + HALF, :], raw[base + HALF : base + HD, :]
            front, back = a * cosine - b * sine, b * cosine + a * sine
            mean = jnp.sum(front * front + back * back, axis=0, keepdims=True) / HD
            factor = lax.rsqrt(mean + EPSILON)
            factor_ref[h] = factor
            unit = jnp.concatenate([front, back], axis=0) * factor
            low = (unit * gain_ref[own, :]).astype(BF16)
            if part == 0:
                qt_ref[own, :] = low * BF16(1.0 / math.sqrt(HD))
            else:
                kt_ref[own, :] = low
                k_ref[h] = low.T
        value = raw[raw_row(2, h) : raw_row(2, h) + HD, :].astype(BF16)
        v_ref[h] = value.T
        ve_ref[h, :HD, :] = value
        ve_ref[h, HD:, :] = jnp.ones((VALUE_ROWS - HD, chunk_len), BF16)

    blocks = chunk_len // BLOCK
    before = chunk * blocks

    def step(local, key_first, k_of, v_of, starts):
        query = slice(local * BLOCK, (local + 1) * BLOCK)
        mask = visible(key_first, (before + local) * BLOCK, starts, length, BLOCK, BLOCK)
        for h in range(heads):
            scores = dot(k_of(h), qt_ref[h * HD : (h + 1) * HD, query])
            probs = jnp.where(mask, jnp.exp(scores), 0.0).astype(BF16)
            acc[h] += dot(v_of(h), probs)

    for local in range(blocks):
        query = slice(local * BLOCK, (local + 1) * BLOCK)
        starts = start_ref[:, query]
        lowest = info[2 + before + local]
        acc[...] = jnp.zeros_like(acc)
        if chunk:

            @pl.loop(lowest, before)
            def _(kb):
                at = pl.ds(pl.multiple_of(kb * BLOCK, BLOCK), BLOCK)
                step(
                    local, kb * BLOCK, lambda h: old_k[h, at, :], lambda h: old_v[h, :, at], starts
                )

        @pl.loop(jnp.maximum(lowest - before, 0), local + 1)
        def _(kb):
            at = pl.ds(pl.multiple_of(kb * BLOCK, BLOCK), BLOCK)
            step(
                local,
                (before + kb) * BLOCK,
                lambda h: k_ref[h, at, :],
                lambda h: ve_ref[h, :, at],
                starts,
            )

        for h in range(heads):
            inverse = 1.0 / acc[h, HD : HD + 1, :]
            inv_ref[h, :, query] = inverse
            out = acc[h, :HD, :] * inverse
            ot_ref[h * HD : (h + 1) * HD, query] = out.astype(BF16)
            o_ref[query, h * HD : (h + 1) * HD] = out.T.astype(BF16)
    rows = chunk_len // n_head
    for e in range(1, n_head):
        block = o_ref[pl.ds(pl.multiple_of((me ^ e) * rows, rows), rows), :]
        if e == 1:
            near_ref[...] = block
        else:
            far_ref[e - 2] = block


def attend_chunk(
    chunk, x_pieces, w_t, cosine, sine, gain, starts, info, buffers, row_len, chunk_len
):
    n_head = len(x_pieces)
    share = x_pieces[0].shape[1]
    cols = w_t.shape[0] // 3
    heads = cols // HD
    model = w_t.shape[1]
    body = functools.partial(attend_kernel, chunk, n_head, heads, chunk_len, share)
    by_lane = lambda rows: pl.BlockSpec((rows, chunk_len), lambda i, info: (0, chunk))
    specs = [whole((chunk_len, share))] * n_head + [
        whole((3 * cols, model)),
        by_lane(HALF),
        by_lane(HALF),
        whole((cols, 1)),
        by_lane(1),
    ]
    operands = [*x_pieces, w_t, cosine, sine, gain, starts]
    aliases = {}
    if chunk:
        aliases = {1 + len(operands) + i: i for i in range(9)}
        specs += [whole((heads, row_len, HD)), whole((heads, VALUE_ROWS, row_len))]
        specs += [pl.BlockSpec(memory_space=pl.ANY)] * 7
        operands += buffers
    lane3 = lambda rows: pl.BlockSpec((heads, rows, chunk_len), lambda i, info: (0, 0, chunk))
    row3 = pl.BlockSpec((heads, chunk_len, HD), lambda i, info: (0, chunk, 0))
    outs = pl.pallas_call(
        body,
        grid_spec=pltpu.PrefetchScalarGridSpec(
            num_scalar_prefetch=1,
            grid=(1,),
            in_specs=specs,
            out_specs=[
                row3,
                lane3(VALUE_ROWS),
                row3,
                by_lane(cols),
                by_lane(cols),
                by_lane(cols),
                lane3(1),
                lane3(1),
                lane3(1),
                whole((chunk_len, cols)),
            ]
            + [
                whole((chunk_len // n_head, cols)),
                whole((n_head - 2, chunk_len // n_head, cols)),
            ],
            scratch_shapes=[
                pltpu.VMEM((3 * cols, chunk_len), F32),
                pltpu.VMEM((heads, VALUE_ROWS, BLOCK), F32),
            ],
        ),
        out_shape=[
            kept_shape((heads, row_len, HD), BF16),
            kept_shape((heads, VALUE_ROWS, row_len), BF16),
            kept_shape((heads, row_len, HD), BF16),
            kept_shape((cols, row_len), BF16),
            kept_shape((cols, row_len), BF16),
            kept_shape((cols, row_len), BF16),
            kept_shape((heads, 1, row_len), F32),
            kept_shape((heads, 1, row_len), F32),
            kept_shape((heads, 1, row_len), F32),
            shape((chunk_len, cols), BF16),
        ]
        + [
            shape((chunk_len // n_head, cols), BF16),
            shape((n_head - 2, chunk_len // n_head, cols), BF16),
        ],
        input_output_aliases=aliases,
        compiler_params=params(40),
        cost_estimate=cost(16e9 / CHUNKS, 8e6),
        name="attend",
    )(info, *operands)
    return outs[:9], list(outs[9:])


def unattend_kernel(n_head, chunks, row_len, piece, pair, info, *refs):
    refs = list(refs)
    d_refs = [refs.pop(0) for _ in range(chunks * n_head)]
    k_ref, v_ref, kt_ref, qt_ref, ot_ref, inv_ref, qf_ref, kf_ref = [refs.pop(0) for _ in range(8)]
    start_ref, cos_ref, sin_ref, gain_ref = [refs.pop(0) for _ in range(4)]
    out_ref, gain_out, do_s, inner_s, dq_s, dk_s, dv_s = refs
    me, length = info[0], info[1]
    for c in range(chunks):
        for e in range(n_head):
            first = c * n_head * piece + (me ^ e) * piece
            do_s[:, pl.ds(pl.multiple_of(first, piece), piece)] = d_refs[c * n_head + e][...]
    for h in range(pair):
        own = slice(h * HD, (h + 1) * HD)
        product = do_s[own, :].astype(F32) * ot_ref[own, :].astype(F32)
        inner_s[h] = jnp.sum(product, axis=0, keepdims=True)
    dq_s[...] = jnp.zeros_like(dq_s)
    dk_s[...] = jnp.zeros_like(dk_s)
    dv_s[...] = jnp.zeros_like(dv_s)

    @pl.loop(0, row_len // BLOCK)
    def _(qb):
        query = pl.ds(pl.multiple_of(qb * BLOCK, BLOCK), BLOCK)
        starts = start_ref[:, query]

        @pl.loop(info[2 + qb], qb + 1)
        def _(kb):
            key = pl.ds(pl.multiple_of(kb * BLOCK, BLOCK), BLOCK)
            mask = visible(kb * BLOCK, qb * BLOCK, starts, length, BLOCK, BLOCK)
            for h in range(pair):
                own = slice(h * HD, (h + 1) * HD)
                q_block, do_block = qt_ref[own, query], do_s[own, query]
                scores = dot(k_ref[h, key, :], q_block)
                probs = jnp.where(mask, jnp.exp(scores), 0.0) * inv_ref[h, :, query]
                d_probs = dot(v_ref[h, key, :], do_block)
                d_scores = (probs * (d_probs - inner_s[h, :, query])).astype(BF16)
                dv_s[own, key] += dot(do_block, probs.astype(BF16), 1, 1)
                dk_s[own, key] += dot(q_block, d_scores, 1, 1)
                dq_s[own, query] += dot(kt_ref[own, key], d_scores)

    for h in range(pair):
        own = slice(h * HD, (h + 1) * HD)
        gain = gain_ref[own, :]
        summed = jnp.zeros((HD, 1), F32)
        for part, low_ref, grad_ref, factor_ref in (
            (0, qt_ref, dq_s, qf_ref),
            (1, kt_ref, dk_s, kf_ref),
        ):
            scale = math.sqrt(HD) if part == 0 else 1.0
            unit = low_ref[own, :].astype(F32) * (scale / gain)
            grad = grad_ref[own, :]
            if part == 0:
                grad = grad * (1.0 / math.sqrt(HD))
            summed += jnp.sum(grad * unit, axis=1, keepdims=True)
            grad = grad * gain
            mean = jnp.sum(grad * unit, axis=0, keepdims=True) / HD
            grad = (grad - unit * mean) * factor_ref[h]
            front, back = grad[:HALF], grad[HALF:]
            cosine, sine = cos_ref[...], sin_ref[...]
            out_ref[part, h * HD : h * HD + HALF, :] = (front * cosine + back * sine).astype(BF16)
            out_ref[part, h * HD + HALF : (h + 1) * HD, :] = (
                back * cosine - front * sine
            ).astype(BF16)
        out_ref[2, own, :] = dv_s[own, :].astype(BF16)
        gain_out[own, :] = summed


def unattend(index, do_pieces, buffers, starts, cosine, sine, gain, info, n_head):
    k, _, v, kt, qt, ot, inv, qf, kf = buffers
    chunks = len(do_pieces) // n_head
    cols, piece = do_pieces[0].shape
    heads, row_len, _ = k.shape
    pair = min(2, heads)
    rows = pair * HD
    by_rows = lambda width: pl.BlockSpec((rows, width), lambda g, info: (index, 0))
    by_head = lambda a, b: pl.BlockSpec((pair, a, b), lambda g, info: (index, 0, 0))
    return pl.pallas_call(
        functools.partial(unattend_kernel, n_head, chunks, row_len, piece, pair),
        grid_spec=pltpu.PrefetchScalarGridSpec(
            num_scalar_prefetch=1,
            grid=(1,),
            in_specs=[by_rows(piece)] * (chunks * n_head)
            + [by_head(row_len, HD)] * 2
            + [by_rows(row_len)] * 3
            + [by_head(1, row_len)] * 3
            + [whole((1, row_len)), whole((HALF, row_len)), whole((HALF, row_len)), by_rows(1)],
            out_specs=[whole((3, rows, row_len)), whole((rows, 1))],
            scratch_shapes=[
                pltpu.VMEM((rows, row_len), BF16),
                pltpu.VMEM((pair, 1, row_len), F32),
                pltpu.VMEM((rows, row_len), F32),
                pltpu.VMEM((rows, row_len), F32),
                pltpu.VMEM((rows, row_len), F32),
            ],
        ),
        out_shape=[kept_shape((3, rows, row_len), BF16), shape((rows, 1), F32)],
        compiler_params=params(32),
        cost_estimate=cost(22e9, 6e6),
        name="unattend",
    )(info, *do_pieces, k, v, kt, qt, ot, inv, qf, kf, starts, cosine, sine, gain)


def norm(values):
    factor = lax.rsqrt(jnp.mean(values * values, axis=-1, keepdims=True) + EPSILON)
    return values * factor, factor


def norm_back(grad, unit, factor):
    return factor * (grad - unit * jnp.mean(grad * unit, axis=-1, keepdims=True))


def project_kernel(n_head, share, kept, info, *refs):
    o_refs, w_refs = refs[:n_head], refs[n_head : 2 * n_head]
    x_refs = refs[2 * n_head : 3 * n_head]
    alpha_ref = refs[3 * n_head]
    cat_ref, y_ref, x_ref, h_ref, low_ref = refs[3 * n_head + 1 + kept :]
    me = info[0]
    cols = w_refs[0].shape[0]
    y = dot(o_refs[0][...], w_refs[0][...])
    for e in range(1, n_head):
        y += dot(o_refs[e][...], w_refs[e][...])
    for e in range(n_head):
        cat_ref[:, e * cols : (e + 1) * cols] = o_refs[e][...]
    for e in range(n_head):
        first = pl.multiple_of((me ^ e) * share, share)
        x_ref[:, pl.ds(first, share)] = x_refs[e][...]
    y_ref[...] = y
    h_zero = x_ref[...].astype(F32)
    h_one, _ = norm(h_zero + alpha_ref[...] * (norm(y)[0] - h_zero))
    h_ref[...] = h_one
    low_ref[...] = h_one.astype(BF16)


def project(chunk, kept, o_pieces, w_pieces, x_pieces, alpha, info, chunk_len):
    n_head = len(o_pieces)
    cols, model = w_pieces[0].shape
    share = x_pieces[0].shape[1]
    rows = chunk_len // n_head
    mine = lambda width: pl.BlockSpec((rows, width), lambda i, info: (info[0], 0))
    return pl.pallas_call(
        functools.partial(project_kernel, n_head, share, len(kept)),
        grid_spec=pltpu.PrefetchScalarGridSpec(
            num_scalar_prefetch=1,
            grid=(1,),
            in_specs=[mine(cols)]
            + [whole((rows, cols))] * (n_head - 1)
            + [whole((cols, model))] * n_head
            + [mine(share)] * n_head
            + [whole((1, model))]
            + [pl.BlockSpec(memory_space=pl.ANY)] * len(kept),
            out_specs=[pl.BlockSpec((rows, n_head * cols), lambda i, info: (chunk, 0))]
            + [whole((rows, model))] * 4,
        ),
        input_output_aliases={3 * n_head + 2 + i: i for i in range(len(kept))},
        out_shape=[
            kept_shape((CHUNKS * rows, n_head * cols), BF16),
            kept_shape((rows, model), F32),
            kept_shape((rows, model), BF16),
            kept_shape((rows, model), F32),
            shape((rows, model), BF16),
        ],
        compiler_params=params(32),
        cost_estimate=cost(2.0 * rows * model * model, 6e6),
        name="project",
    )(info, *o_pieces, *w_pieces, *x_pieces, alpha, *kept)


def feed_kernel(n_head, rows, *refs):
    h_refs = refs[:n_head]
    refs = refs[n_head:]
    up_ref, gate_ref, down_ref, su_ref, sg_ref = refs[:5]
    m_ref, cat_ref, u_ref, g_ref = refs[5:9]
    refs = refs[9:]
    z_refs, acc = refs[:n_head], refs[n_head]
    tile = pl.program_id(0)

    @pl.when(tile == 0)
    def _():
        for e in range(n_head):
            cat_ref[e * rows : (e + 1) * rows, :] = h_refs[e][...]

    up_raw = dot(cat_ref[...], up_ref[...])
    gate_raw = dot(cat_ref[...], gate_ref[...])
    u_ref[...] = up_raw.astype(BF16)
    g_ref[...] = gate_raw.astype(BF16)
    gate = gate_raw * sg_ref[...]
    mixed = (up_raw * su_ref[...] * (gate * jax.nn.sigmoid(gate))).astype(BF16)
    m_ref[...] = mixed
    term = dot(mixed, down_ref[...])
    last = pl.num_programs(0) - 1

    @pl.when(tile == 0)
    def _():
        acc[...] = term

    @pl.when((tile > 0) & (tile < last))
    def _():
        acc[...] += term

    @pl.when(tile == last)
    def _():
        for e in range(n_head):
            piece = slice(e * rows, (e + 1) * rows)
            z_refs[e][...] = (acc[piece, :] + term[piece, :]).astype(BF16)


def feed(h_pieces, w_up, w_gate, w_down, scale_up, scale_gate):
    n_head = len(h_pieces)
    rows, model = h_pieces[0].shape
    hidden = w_up.shape[1]
    tile = min(256, hidden // 2)
    count = n_head * rows
    by_col = lambda height: pl.BlockSpec((height, tile), lambda n: (0, n))
    outs = pl.pallas_call(
        functools.partial(feed_kernel, n_head, rows),
        grid=(hidden // tile,),
        in_specs=[whole((rows, model))] * n_head
        + [
            by_col(model),
            by_col(model),
            pl.BlockSpec((tile, model), lambda n: (n, 0)),
            by_col(1),
            by_col(1),
        ],
        out_specs=[by_col(count), whole((count, model)), by_col(count), by_col(count)]
        + [whole((rows, model))] * n_head,
        out_shape=[
            kept_shape((count, hidden), BF16),
            kept_shape((count, model), BF16),
            kept_shape((count, hidden), BF16),
            kept_shape((count, hidden), BF16),
        ]
        + [shape((rows, model), BF16)] * n_head,
        scratch_shapes=[pltpu.VMEM((count, model), F32)],
        compiler_params=params(48),
        cost_estimate=cost(6.0 * count * model * hidden, 20e6),
        name="feed",
    )(*h_pieces, w_up, w_gate, w_down, scale_up, scale_gate)
    return outs[:2], outs[2:4], list(outs[4::2]), list(outs[5::2])


def middle_kernel(n_head, n_terms, share, kept, info, *refs):
    z_refs, c_refs = refs[:n_terms], refs[n_terms : n_terms + n_head]
    h_ref, alpha_ref = refs[n_terms + n_head : n_terms + n_head + 2]
    refs = refs[n_terms + n_head + 2 + kept :]
    own_ref, near_ref, far_ref, dz_ref, direct_ref, grad_ref, two_s, cot_s = refs
    me = info[0]
    z = z_refs[0][...].astype(F32)
    for r in z_refs[1:]:
        z += r[...].astype(F32)
    h_one, alpha = h_ref[...], alpha_ref[...]
    h_ffn, z_factor = norm(z)
    h_two, factor = norm(h_one + alpha * (h_ffn - h_one))
    two_s[...] = h_two.astype(BF16)
    for e in range(n_head):
        at = pl.ds(pl.multiple_of((me ^ e) * share, share), share)
        if e < 2:
            (own_ref, near_ref)[e][...] = two_s[:, at]
        else:
            far_ref[e - 2] = two_s[:, at]
        cot_s[:, at] = c_refs[e][...]
    grad = norm_back(cot_s[...].astype(F32), h_two, factor)
    grad_ref[...] = jnp.sum(grad * (h_ffn - h_one), axis=0, keepdims=True)
    direct_ref[...] = grad * (1.0 - alpha)
    dz_ref[...] = norm_back(grad * alpha, h_ffn, z_factor).astype(BF16)


def middle(chunk, kept, z_terms, cot_pieces, h_one, alpha, info):
    n_head, n_terms = len(cot_pieces), len(z_terms)
    rows, model = h_one.shape
    share = cot_pieces[0].shape[1]
    mine = pl.BlockSpec((rows, share), lambda i, info: (chunk * n_head + info[0], 0))
    theirs = pl.BlockSpec((rows, share), lambda i, info: (chunk, 0))
    outs = pl.pallas_call(
        functools.partial(middle_kernel, n_head, n_terms, share, len(kept)),
        grid_spec=pltpu.PrefetchScalarGridSpec(
            num_scalar_prefetch=1,
            grid=(1,),
            in_specs=[term_spec(t) for t in z_terms]
            + [mine]
            + [theirs] * (n_head - 1)
            + [whole((rows, model)), whole((1, model))]
            + [pl.BlockSpec(memory_space=pl.ANY)] * len(kept),
            out_specs=[theirs] * 2
            + [pl.BlockSpec((n_head - 2, rows, share), lambda i, info: (0, chunk, 0))]
            + [whole((rows, model))] * 2
            + [whole((1, model))],
            scratch_shapes=[pltpu.VMEM((rows, model), BF16), pltpu.VMEM((rows, model), BF16)],
        ),
        input_output_aliases={n_terms + n_head + 3 + i: i for i in range(len(kept))},
        out_shape=[kept_shape((CHUNKS * rows, share), BF16)] * 2
        + [kept_shape((n_head - 2, CHUNKS * rows, share), BF16)]
        + [shape((rows, model), BF16), kept_shape((rows, model), F32), shape((1, model), F32)],
        compiler_params=params(32),
        cost_estimate=cost(rows * model * 60, rows * model * 24),
        name="middle",
    )(info, *z_terms, *cot_pieces, held(h_one), alpha, *kept)
    return list(outs[:3]), *outs[3:]


def join(pieces):
    rows, width = pieces[0].shape

    def body(*refs):
        for i, ref in enumerate(refs[:-1]):
            refs[-1][i * rows : (i + 1) * rows, :] = ref[...]

    return pl.pallas_call(
        body,
        in_specs=[whole((rows, width))] * len(pieces),
        out_specs=whole((rows * len(pieces), width)),
        grid=(1,),
        out_shape=shape((rows * len(pieces), width), pieces[0].dtype),
        compiler_params=params(16),
        cost_estimate=cost(0, rows * width * 4 * len(pieces)),
        name="join",
    )(*pieces)


def weigh_feed(mixed, joined, dz, du, dg):
    count, hidden = mixed.shape
    model = joined.shape[1]
    tile = min(256, hidden // 2)

    def body(m_ref, h_ref, z_ref, u_ref, g_ref, down, up, gate):
        down[...] = dot(m_ref[...], z_ref[...], 0, 0)
        up[...] = dot(h_ref[...], u_ref[...], 0, 0)
        gate[...] = dot(h_ref[...], g_ref[...], 0, 0)

    by_col = lambda height: pl.BlockSpec((height, tile), lambda n: (0, n))
    return pl.pallas_call(
        body,
        in_specs=[
            by_col(count),
            whole((count, model)),
            whole((count, model)),
            by_col(count),
            by_col(count),
        ],
        out_specs=[pl.BlockSpec((tile, model), lambda n: (n, 0)), by_col(model), by_col(model)],
        grid=(hidden // tile,),
        out_shape=[kept_shape((hidden, model), F32)] + [kept_shape((model, hidden), F32)] * 2,
        compiler_params=params(48),
        cost_estimate=cost(6.0 * count * hidden * model, 20e6),
        name="weigh_feed",
    )(mixed, joined, dz, du, dg)


def weigh(d_pair, x_pieces, chunk_len):
    rows, row_len = d_pair.shape
    n_head = len(x_pieces[0])
    share = x_pieces[0][0].shape[1]
    flat = [p for chunk in x_pieces for p in chunk]

    def body(d_ref, *refs):
        for e in range(n_head):
            term = None
            for c in range(len(x_pieces)):
                d_part = d_ref[:, c * chunk_len : (c + 1) * chunk_len]
                new = dot(d_part, refs[c * n_head + e][...])
                term = new if term is None else term + new
            refs[-1][:, e * share : (e + 1) * share] = term.astype(BF16)

    return pl.pallas_call(
        body,
        in_specs=[whole((rows, row_len))] + [whole((chunk_len, share))] * len(flat),
        out_specs=whole((rows, n_head * share)),
        grid=(1,),
        out_shape=shape((rows, n_head * share), BF16),
        compiler_params=params(32),
        cost_estimate=cost(0, 1),
        name="weigh",
    )(d_pair, *flat)


def unfeed_kernel(n_head, n_in, rows, *refs):
    d_refs, refs = refs[:n_in], refs[n_in:]
    u_ref, g_ref, up_ref, gate_ref, down_ref, su_ref, sg_ref = refs[:7]
    du_ref, dg_ref, gsu_ref, gsg_ref = refs[7:11]
    out_refs = refs[11 : 11 + n_head]
    cat_ref = refs[11 + n_head] if n_in > 1 else d_refs[0]
    acc = refs[-1]
    tile = pl.program_id(0)

    if n_in > 1:

        @pl.when(tile == 0)
        def _():
            for e in range(n_in):
                cat_ref[e * rows : (e + 1) * rows, :] = d_refs[e][...]

    d_mixed = dot(cat_ref[...], down_ref[...], 1, 1)
    up_raw, gate_raw = u_ref[...].astype(F32), g_ref[...].astype(F32)
    gate = gate_raw * sg_ref[...]
    sigmoid = jax.nn.sigmoid(gate)
    silu = gate * sigmoid
    d_up = d_mixed * silu
    d_gate = d_mixed * (up_raw * su_ref[...]) * (sigmoid + silu * (1.0 - sigmoid))
    gsu_ref[...] = jnp.sum(d_up * up_raw, axis=0, keepdims=True)
    gsg_ref[...] = jnp.sum(d_gate * gate_raw, axis=0, keepdims=True)
    up_low = (d_up * su_ref[...]).astype(BF16)
    gate_low = (d_gate * sg_ref[...]).astype(BF16)
    du_ref[...] = up_low
    dg_ref[...] = gate_low
    term = dot(up_low, up_ref[...], 1, 1) + dot(gate_low, gate_ref[...], 1, 1)
    last = pl.num_programs(0) - 1

    @pl.when(tile == 0)
    def _():
        acc[...] = term

    @pl.when((tile > 0) & (tile < last))
    def _():
        acc[...] += term

    @pl.when(tile == last)
    def _():
        for e in range(n_head):
            piece = slice(e * rows, (e + 1) * rows)
            out_refs[e][...] = (acc[piece, :] + term[piece, :]).astype(BF16)


def unfeed(dz_pieces, u, g, w_up, w_gate, w_down, scale_up, scale_gate, n_head):
    n_in = len(dz_pieces)
    model = dz_pieces[0].shape[1]
    count, hidden = u.shape
    rows = count // n_head
    tile = min(256, hidden // 2)
    by_col = lambda height: pl.BlockSpec((height, tile), lambda n: (0, n))
    outs = pl.pallas_call(
        functools.partial(unfeed_kernel, n_head, n_in, rows),
        grid=(hidden // tile,),
        in_specs=[whole(dz_pieces[0].shape)] * n_in
        + [
            by_col(count),
            by_col(count),
            by_col(model),
            by_col(model),
            pl.BlockSpec((tile, model), lambda n: (n, 0)),
            by_col(1),
            by_col(1),
        ],
        out_specs=[by_col(count)] * 2
        + [by_col(1), by_col(1)]
        + [whole((rows, model))] * n_head
        + [whole((count, model))] * (n_in > 1),
        out_shape=[kept_shape((count, hidden), BF16)] * 2
        + [shape((1, hidden), F32), shape((1, hidden), F32)]
        + [shape((rows, model), BF16)] * n_head
        + [shape((count, model), BF16)] * (n_in > 1),
        scratch_shapes=[pltpu.VMEM((count, model), F32)],
        compiler_params=params(48),
        cost_estimate=cost(6.0 * count * model * hidden, 20e6),
        name="unfeed",
    )(*dz_pieces, u, g, w_up, w_gate, w_down, scale_up, scale_gate)
    pieces = outs[4 : 4 + n_head]
    return outs[:2], outs[2:4], list(pieces[::2]), list(pieces[1::2]), outs[-1]


def unproject_kernel(n_head, n_terms, kept, *refs):
    t_refs, w_refs = refs[:n_terms], refs[n_terms : n_terms + n_head]
    direct_ref, y_ref, x_ref, alpha_ref = refs[n_terms + n_head : n_terms + n_head + 4]
    refs = refs[n_terms + n_head + 4 + kept :]
    dy_ref, refs = refs[0], refs[1:]
    own_ref, near_ref, far_ref, zero_ref, grad_ref = refs
    grad = direct_ref[...]
    for r in t_refs:
        grad += r[...].astype(F32)
    alpha = alpha_ref[...]
    h_zero = x_ref[...].astype(F32)
    h_attn, y_factor = norm(y_ref[...])
    h_one, factor = norm(h_zero + alpha * (h_attn - h_zero))
    grad = norm_back(grad, h_one, factor)
    grad_ref[...] = jnp.sum(grad * (h_attn - h_zero), axis=0, keepdims=True)
    zero_ref[...] = grad * (1.0 - alpha)
    dy = norm_back(grad * alpha, h_attn, y_factor).astype(BF16)
    dy_ref[...] = dy
    for e in range(n_head):
        value = dot(w_refs[e][...], dy, 1, 1).astype(BF16)
        if e < 2:
            (own_ref, near_ref)[e][...] = value
        else:
            far_ref[e - 2] = value


def unproject(chunk, kept, terms, w_pieces, direct, y, x, alpha):
    n_head, n_terms = len(w_pieces), len(terms)
    rows, model = y.shape
    cols = w_pieces[0].shape[0]
    outs = pl.pallas_call(
        functools.partial(unproject_kernel, n_head, n_terms, len(kept)),
        grid=(1,),
        in_specs=[term_spec(t) for t in terms]
        + [whole((cols, model))] * n_head
        + [whole((rows, model))] * 3
        + [whole((1, model))]
        + [pl.BlockSpec(memory_space=pl.ANY)] * len(kept),
        out_specs=[pl.BlockSpec((rows, model), lambda i: (chunk, 0))]
        + [whole((cols, rows))] * 2
        + [whole((n_head - 2, cols, rows))]
        + [whole((rows, model)), whole((1, model))],
        input_output_aliases={n_terms + n_head + 4 + i: i for i in range(len(kept))},
        out_shape=[kept_shape((CHUNKS * rows, model), BF16)]
        + [shape((cols, rows), BF16)] * 2
        + [shape((n_head - 2, cols, rows), BF16)]
        + [kept_shape((rows, model), F32), shape((1, model), F32)],
        compiler_params=params(32),
        cost_estimate=cost(2.0 * rows * model * model, 8e6),
        name="unproject",
    )(*terms, *w_pieces, held(direct), held(y), held(x), alpha, *kept)
    return outs[0], list(outs[1:4]), outs[4], outs[5]


def spread_kernel(n_head, share, pairs, info, *refs):
    d_refs, (w_ref, direct_ref), out_refs = refs[:pairs], refs[pairs : pairs + 2], refs[pairs + 2 :]
    me = info[0]
    block = pl.program_id(0)
    d_all = jnp.concatenate([r[...] for r in d_refs], axis=0).T
    for e in range(n_head):
        at = pl.ds(pl.multiple_of((me ^ e) * share, share), share)
        term = dot(d_all, w_ref[:, at])

        ref = out_refs[n_head // 2].at[e // 2] if e % 2 else out_refs[e // 2]

        @pl.when(block == me)
        def _():
            ref[...] = (term + direct_ref[:, at]).astype(BF16)

        @pl.when(block != me)
        def _():
            ref[...] = term.astype(BF16)


def spread(chunk, chunk_len, d_all, w_t, direct, info, n_head):
    rows3, model = w_t.shape
    share = model // n_head
    rows = chunk_len // n_head
    return pl.pallas_call(
        functools.partial(spread_kernel, n_head, share, len(d_all)),
        grid_spec=pltpu.PrefetchScalarGridSpec(
            num_scalar_prefetch=1,
            grid=(n_head,),
            in_specs=[
                *[pl.BlockSpec((d.shape[0], rows), lambda i, info: (0, chunk * n_head + i)) for d in d_all],
                whole((rows3, model)),
                whole((rows, model)),
            ],
            out_specs=[pl.BlockSpec((rows, share), lambda i, info: (i, 0))] * (n_head // 2)
            + [pl.BlockSpec((n_head // 2, rows, share), lambda i, info: (0, i, 0))],
        ),
        out_shape=[shape((chunk_len, share), BF16)] * (n_head // 2)
        + [shape((n_head // 2, chunk_len, share), BF16)],
        compiler_params=params(32),
        cost_estimate=cost(2.0 * chunk_len * model * rows3, 8e6),
        name="spread",
    )(info, *d_all, w_t, direct)


def settle(own, pieces, info):
    pieces = [own] + pieces
    n_head = len(pieces)
    count, share = own.shape
    rows = count // CHUNKS

    def body(info, *refs):
        for e in range(n_head):
            for c in range(CHUNKS):
                at = (c * n_head + (info[0] ^ e)) * rows
                refs[-1][pl.ds(pl.multiple_of(at, rows), rows), :] = refs[e][
                    c * rows : (c + 1) * rows, :
                ]

    return pl.pallas_call(
        body,
        grid_spec=pltpu.PrefetchScalarGridSpec(
            num_scalar_prefetch=1,
            grid=(1,),
            in_specs=[whole((count, share))] * n_head,
            out_specs=whole((n_head * count, share)),
        ),
        out_shape=shape((n_head * count, share), BF16),
        compiler_params=params(16),
        cost_estimate=cost(0, n_head * count * share * 4),
        name="settle",
    )(info, *pieces)


def on_device(
    n_batch,
    n_head,
    hidden_in,
    cotangent,
    doc_ids,
    lengths,
    w_query,
    w_key,
    w_value,
    w_out,
    w_up,
    w_gate,
    w_down,
    scale_qk,
    scale_up,
    scale_gate,
    alpha_attn,
    alpha_ffn,
):
    _, row_len, share = hidden_in.shape
    model = share * n_head
    cols = w_query.shape[1]
    chunk_len = row_len // CHUNKS
    rows = chunk_len // n_head
    me = lax.axis_index("head")
    chunks = range(CHUNKS)
    x_own, cot_own = hidden_in[0], cotangent[0]

    docs = doc_ids[0]
    column = jnp.arange(row_len, dtype=jnp.int32)
    starts = sum(
        jnp.where(docs > d, jnp.sum((docs == d).astype(jnp.int32)), 0) for d in range(5)
    ).astype(jnp.int32)
    position = (column - starts).astype(F32)
    frequency = 10000.0 ** (-(jnp.arange(HALF, dtype=F32) * 2.0 / HD))
    angles = frequency[:, None] * position[None, :]
    cosine, sine = jnp.cos(angles), jnp.sin(angles)
    info = jnp.concatenate(
        [me[None].astype(jnp.int32), lengths.astype(jnp.int32), starts[::BLOCK] // BLOCK]
    )
    starts = starts[None, :]
    gain = scale_qk[:, None]
    up_scale, gate_scale = scale_up[None, :], scale_gate[None, :]
    attn_alpha, ffn_alpha = alpha_attn[None, :], alpha_ffn[None, :]

    def part(values, c):
        return lax.slice_in_dim(values, c * chunk_len, (c + 1) * chunk_len, axis=0)

    def block_of(values, e):
        return lax.dynamic_slice_in_dim(values, (me ^ e) * rows, rows, 0)

    order = Order()
    pair = min(2, cols // HD) * HD
    pairs = cols // pair
    far = n_head // 2
    place = lax.axis_index("batch")[None].astype(jnp.int32)

    bit = lax.axis_index("batch") % 2
    own = jnp.stack([me, bit]).astype(jnp.int32)

    x_far = gather_far(part(x_own, 0), n_head)
    (w_t, out_half, cot_near, cot_far), x_far = order.run(
        lambda w: prepare(w, w_key, w_value, w_out, cot_own, own, pair, n_head),
        w_query,
        beside=x_far,
    )
    buffers, x_pieces, o_own, o_moving = [], [], [], []
    for c in chunks:
        x_pieces.append(gather_near(x_far, n_head))
        beside = []
        if c == 0:
            halves = {
                e: swap(after(out_half, order.last), "head", e, n_head) for e in range(2, n_head, 2)
            }
            beside = [halves]
        else:
            cot_moving = Exchange(after(cot_near, order.last), after(cot_far, order.last), n_head)
            beside = [o_moving[0].flying, cot_moving.flying, out_far]
        if c < CHUNKS - 1:
            beside.append(gather_far(after(part(x_own, c + 1), order.last), n_head))
        (buffers, (o_chunk, near, far_blocks)), beside = order.run(
            lambda w: attend_chunk(
                c, x_pieces[c], w, cosine, sine, gain, starts, info, buffers, row_len, chunk_len
            ),
            w_t,
            need=x_pieces[c],
            beside=beside,
        )
        o_own.append(o_chunk)
        o_moving.append(Exchange(near, far_blocks, n_head))
        if c < CHUNKS - 1:
            x_far = beside[-1]
        if c == 0:
            out_far = {e: (v, swap(v, "batch", 1, n_batch)) for e, v in beside[0].items()}
        else:
            o_first = o_moving[0].finish(beside[0])
            cot_blocks = cot_moving.finish(beside[1])
            out_far = beside[2]

    out_far = {
        e: jnp.where(
            bit == 0, jnp.concatenate([v, w], axis=1), jnp.concatenate([w, v], axis=1)
        )
        for e, (v, w) in out_far.items()
    }
    out_far[0] = w_out
    out_pieces = gather_near(out_far, n_head)

    state, joined, h_far, h_fars = [], [], None, []
    o_came = o_first
    for c in chunks:
        o_pieces = [o_own[c]] + o_came
        beside = [h_far, o_moving[c + 1].flying if c < CHUNKS - 1 else None]
        (joined, y, x_rows, h_one, h_low), beside = order.run(
            lambda first: project(
                c,
                joined,
                [first] + o_pieces[1:],
                out_pieces,
                x_pieces[c],
                attn_alpha,
                info,
                chunk_len,
            ),
            o_pieces[0],
            need=o_pieces[1:] + out_pieces,
            beside=beside,
        )
        joined = [joined]
        if c < CHUNKS - 1:
            o_came = o_moving[c + 1].finish(beside[1])
        if c:
            h_fars = [beside[0]]
        state.append((y, x_rows, h_one))
        h_far = gather_far(h_low, n_head)
    cot_pieces = [cot_own] + cot_blocks

    fed, raws, z_terms, sent = [], [], None, None
    for c in chunks:
        h_pieces = gather_near(h_fars[c] if c < len(h_fars) else h_far, n_head)
        beside = [h_far if c < CHUNKS - 1 else None, z_terms]
        (kept, raw, z_even, z_odd), (h_next, z_done) = order.run(
            lambda first: feed(
                [first] + h_pieces[1:], w_up, w_gate, w_down, up_scale, gate_scale
            ),
            h_pieces[0],
            need=h_pieces[1:] + [sent],
            beside=beside,
        )
        if c < CHUNKS - 1:
            h_far = h_next
        fed.append(kept)
        raws.append(raw)
        z_near = reduce_near(z_odd, n_head)
        if c < CHUNKS - 1:
            z_terms, sent = reduce_far(z_even, z_near, n_head)

    two = []

    def mid_step(c, terms, beside, need=()):
        nonlocal two
        (two, dz, direct, alpha_sum), beside = order.run(
            lambda first: middle(
                c, two, [first] + terms[1:], cot_pieces, state[c][2], ffn_alpha, info
            ),
            terms[0],
            need=terms[1:] + list(need),
            beside=beside,
        )
        return dz, direct, alpha_sum, beside

    def unfeed_step(c, dz_pieces, beside, need=()):
        return order.run(
            lambda first: unfeed(
                [first] + dz_pieces[1:],
                *raws[c],
                w_up,
                w_gate,
                w_down,
                up_scale,
                gate_scale,
                n_head,
            ),
            dz_pieces[0],
            need=dz_pieces[1:] + list(need),
            beside=beside,
        )

    dz, direct, alpha_sum, z_near = mid_step(0, z_done, z_near)
    directs, ffn_alphas = [direct], [alpha_sum]
    dz_far = gather_far(dz, n_head)
    z_even = [z_even[0]] + [after(p, dz_far[far]) for p in z_even[1:]]
    z_terms, sent = reduce_far(z_even, z_near, n_head)
    dz_pieces = gather_near(dz_far, n_head)
    (low_first, scales_first, dh_even, dh_odd, dz_first), z_terms = unfeed_step(
        0, dz_pieces, z_terms, need=[sent]
    )
    dh_near = reduce_near(dh_odd, n_head)
    dz, direct, alpha_sum, dh_near = mid_step(1, z_terms, dh_near)
    directs.append(direct)
    ffn_alphas.append(alpha_sum)
    dz_far = gather_far(dz, n_head)
    firsts, dz_far = order.run(
        lambda v: weigh_feed(v, fed[0][1], dz_first, *low_first), fed[0][0], beside=dz_far
    )
    dz_pieces = gather_near(dz_far, n_head)
    dh_even = [dh_even[0]] + [after(p, dz_far[far]) for p in dh_even[1:]]
    dh_terms, sent = reduce_far(dh_even, dh_near, n_head)
    dz_last, _ = order.run(
        lambda first: join([first] + dz_pieces[1:]), dz_pieces[0], need=dz_pieces[1:] + [sent]
    )
    grad_down, _ = order.run(
        lambda v: (firsts[0] + dot(fed[1][0], v, 0, 0)).astype(BF16), dz_last
    )
    sum_down = BatchSum(grad_down, n_batch)
    (low_last, scales_last, dh_even, dh_odd, _), dh_terms = unfeed_step(
        1, [dz_last], dh_terms, need=[sum_down.sent]
    )
    scale_sums = [jnp.concatenate(s, axis=0) for s in (scales_first, scales_last)]
    dh_near = reduce_near(dh_odd, n_head)

    zeros, alphas, dys = [], [], []

    def back(c, terms, beside, need=()):
        y, x_rows, _ = state[c]
        (dy, d_pieces, zero, grad_alpha_attn), beside = order.run(
            lambda first: unproject(
                c, dys, [first] + terms[1:], out_pieces, directs[c], y, x_rows, attn_alpha
            ),
            terms[0],
            need=terms[1:] + list(need),
            beside=beside,
        )
        dys[:] = [dy]
        zeros.append(zero)
        alphas.append(grad_alpha_attn)
        return d_pieces[0], Exchange(d_pieces[1], d_pieces[2], n_head), beside

    def beside_sums(step, value, sums, beside=(), need=()):
        out, (got, beside) = order.run(
            step, value, need=need, beside=([b.flying for b in sums], beside)
        )
        for b, v in zip(sums, got, strict=True):
            b.advance(v)
        return out, beside

    grad_up, dh_near = beside_sums(
        lambda v: (firsts[1] + dot(fed[1][1], v, 0, 0)).astype(BF16),
        low_last[0],
        [sum_down],
        dh_near,
    )
    sum_up = BatchSum(grad_up, n_batch)
    dh_first, (dh_terms, sent) = dh_terms, reduce_far(dh_even, dh_near, n_head)
    grad_gate, _ = order.run(
        lambda v: (firsts[2] + dot(fed[1][1], v, 0, 0)).astype(BF16),
        low_last[1],
        need=[sent, sum_down.sent, sum_up.sent],
    )
    do_own, do_first, (dh_terms, got) = back(0, dh_first, (dh_terms, sum_down.flying))
    sum_down.advance(got)
    do_pieces = [do_own]
    do_own, do_last, do_came = back(1, dh_terms, do_first.flying, need=[sum_down.sent])
    do_pieces += do_first.finish(do_came)
    out_terms, do_came = beside_sums(
        lambda o: dot(o, dys[0], 0, 0).astype(BF16),
        joined[0],
        [sum_down, sum_up],
        do_last.flying,
    )
    sum_gate = BatchSum(after(grad_gate, order.last), n_batch)
    do_pieces += [do_own] + do_last.finish(do_came)
    alpha_sums = jnp.concatenate([sum(alphas), sum(ffn_alphas)], axis=0)
    alpha_rows = jnp.pad(alpha_sums.astype(BF16), ((0, 14), (0, 0)))
    out_blocks = [
        jnp.concatenate([out_terms[e * cols : (e + 1) * cols], alpha_rows], axis=0)
        for e in range(n_head)
    ]
    out_near = reduce_near(out_blocks[1::2], n_head)
    d_all, gains = [], []

    def attention_back(g, sums, beside, need=()):
        (d_pair, grad_gain), beside = beside_sums(
            lambda first: unattend(
                g, [first] + do_pieces[1:], buffers, starts, cosine, sine, gain, info, n_head
            ),
            do_pieces[0],
            sums,
            beside,
            need=do_pieces[1:] + list(need),
        )
        d_pair = d_pair.reshape(3 * pair, row_len)
        d_all.append(d_pair)
        gains.append(grad_gain[:, 0])
        return d_pair, beside

    big = [sum_down, sum_up, sum_gate]
    grads = []
    if pairs > 1:
        d_pair, out_near = attention_back(
            0, [sum_down, sum_up], out_near, need=[b.sent for b in big]
        )
        out_flying, out_sent = reduce_far(out_blocks[::2], out_near, n_head)
        grad_pair, _ = beside_sums(
            lambda d: weigh(d, x_pieces, chunk_len),
            d_pair,
            [sum_gate],
            need=[sum_down.sent, sum_up.sent, out_sent],
        )
        grads.append(grad_pair)
    else:
        out_flying, _ = reduce_far(out_blocks[::2], out_near, n_head)
    ahead = [BatchSum(g, n_batch) for g in grads] if n_batch == 8 else []
    d_pair, out_flying = attention_back(
        pairs - 1, big + ahead, out_flying, need=[sum_gate.sent] + [b.sent for b in ahead]
    )
    out_sum = term_sum(out_flying)
    grad_pair, _ = order.run(
        lambda d: weigh(d, x_pieces, chunk_len), d_pair, need=[sum_down.sent, sum_up.sent, sum_gate.sent]
    )
    small = jnp.concatenate(
        [out_sum[cols : cols + 2]]
        + [
            jnp.pad(v, ((0, 0), (0, model - v.shape[1])))
            for v in (sum(scale_sums), jnp.concatenate(gains)[None])
        ],
        axis=0,
    )
    small = jnp.pad(small, ((0, -(4 * cols + 5) % (16 * n_batch)), (0, 0)))
    if ahead:
        grads = []
    grads += [grad_pair, out_sum[:cols].astype(BF16), small.astype(BF16)]
    grads = jnp.concatenate(grads, axis=0)
    ranges = [2 * b.values.shape[0] for b in ahead] + [grads.shape[0]]
    sum_attn = BatchSum(grads, n_batch, direct=True, before=[b.values for b in ahead])

    def spread_step(c, sums, beside=(), need=()):
        return beside_sums(
            lambda w: spread(c, chunk_len, d_all, w, zeros[c], info, n_head),
            w_t,
            sums,
            beside,
            need=need,
        )

    def land(sums, beside=()):
        got, beside = lax.optimization_barrier(([b.flying for b in sums], beside))
        for b, v in zip(sums, got, strict=True):
            b.advance(v)
        return beside

    two_moving = Exchange(after(two[1], order.last), after(two[2], order.last), n_head)
    d_first, two_came = spread_step(
        0, [sum_up, sum_gate, sum_down], two_moving.flying, need=[sum_attn.sent]
    )
    two_pieces = two_moving.finish(two_came)
    dx_near = reduce_near(d_first[-1], n_head)
    d_last, dx_near = spread_step(
        1, [sum_attn, sum_up, sum_gate], dx_near, need=[sum_up.sent, sum_gate.sent]
    )
    dx_first, _ = reduce_far(d_first[:-1], dx_near, n_head)
    down_done = assemble(sum_down.finish(), place)
    land([sum_attn, sum_up, sum_gate])
    dx_first = land([sum_attn, sum_gate], dx_first)
    dx_near = reduce_near(after(d_last[-1], sum_attn.sent), n_head)
    dx_last, _ = reduce_far(d_last[:-1], dx_near, n_head)
    while len(sum_attn.todo) > 1:
        land([sum_attn])
    hidden_out = settle(two[0], two_pieces, info)
    grad_down = down_done
    grad_up = assemble(sum_up.finish(), place)
    grad_gate = assemble(sum_gate.finish(), place)
    grad_query, grad_key, grad_value, grad_out, small = assemble_turned(
        sum_attn.finish(), place, info, cols, n_head, pairs, ranges
    )
    grad_hidden = jnp.concatenate([term_sum(dx_first), term_sum(dx_last)], axis=0)[None]
    alpha_own = lax.dynamic_slice_in_dim(small[:2], me * share, share, 1)
    hidden_units = w_up.shape[1]

    return (
        hidden_out[None],
        grad_hidden,
        grad_query,
        grad_key,
        grad_value,
        grad_out,
        grad_up,
        grad_gate,
        grad_down,
        small[4, :cols],
        small[2, :hidden_units],
        small[3, :hidden_units],
        alpha_own[0],
        alpha_own[1],
    )


def solution(mesh):
    split = P("batch", None, "head")
    by_col, by_row, by_head = P(None, "head"), P("head", None), P("head")
    return jax.shard_map(
        functools.partial(on_device, mesh.shape["batch"], mesh.shape["head"]),
        mesh=mesh,
        in_specs=(split, split, P("batch", None), P("batch"))
        + (by_col, by_col, by_col, by_row, by_col, by_col, by_row)
        + (by_head, by_head, by_head, P(), P()),
        out_specs=(split, split, by_col, by_col, by_col, by_row, by_col, by_col, by_row)
        + (by_head,) * 5,
        check_vma=False,
    )
```

```python
import functools
import math

import jax
import jax.numpy as jnp
from jax import lax
from jax.experimental import pallas as pl
from jax.experimental.pallas import tpu as pltpu
from jax.sharding import PartitionSpec as P

HD = 64
HALF = HD // 2
VALUE_ROWS = 80
EPSILON = 1e-06
BLOCK = 256
QUERIES = 512
KEYS = 512
CHUNKS = 2
F32 = jnp.float32
BF16 = jnp.bfloat16
MIB = 1024 * 1024


def dot(left, right, left_dim=1, right_dim=0):
    return lax.dot_general(
        left, right, (((left_dim,), (right_dim,)), ((), ())), preferred_element_type=F32
    )


def shape(dims, dtype):
    return jax.ShapeDtypeStruct(dims, dtype)


def kept_shape(dims, dtype):
    return pltpu.HBM(dims, dtype)


def held(array):
    return pltpu.with_memory_space_constraint(array, pltpu.HBM)


def after(value, *others):
    others = [o for o in others if o is not None]
    return lax.optimization_barrier((value, *others))[0] if others else value


def whole(dims):
    return pl.BlockSpec(dims, lambda *_: (0,) * len(dims))


def term_spec(term):
    if term.ndim == 3:
        return pl.BlockSpec((None, *term.shape[1:]), lambda *_: (0, 0, 0))
    return whole(term.shape)


def params(mib):
    return pltpu.CompilerParams(vmem_limit_bytes=mib * MIB)


def cost(flops, moved):
    return pl.CostEstimate(flops=int(flops), bytes_accessed=int(moved), transcendentals=0)


class Order:
    def __init__(self):
        self.last = None

    def run(self, step, value, need=(), beside=()):
        out = step(after(value, self.last, *need))
        out, beside = lax.optimization_barrier((out, beside))
        self.last = jax.tree.leaves(out)[0]
        return out, beside


def swap(value, axis, mask, size):
    return lax.ppermute(value, axis, [(i, i ^ mask) for i in range(size)])


def gather_far(own, size):
    pieces = {0: own}
    bit = size // 2
    while bit > 1:
        pieces.update({e | bit: swap(p, "head", bit, size) for e, p in pieces.items()})
        bit //= 2
    return pieces


def gather_near(far, size):
    pieces = dict(far)
    pieces.update({e | 1: swap(p, "head", 1, size) for e, p in far.items()})
    return [pieces[e] for e in range(size)]


class Exchange:
    def __init__(self, near, far, size):
        self.size = size
        if size == 4:
            self.flying = [swap(near, "head", 1, size), swap(far, "head", 2, size)]
        else:
            blocks = [near, *far]
            self.flying = [swap(p, "head", e, size) for e, p in enumerate(blocks, 1)]

    def finish(self, flying):
        if self.size != 4:
            return flying
        near, far = flying
        return [near, far[0], swap(far[1], "head", 1, self.size)]


def total(terms):
    if len(terms) == 1:
        return terms[0]
    return sum(t.astype(F32) for t in terms).astype(BF16)


def reduce_near(odd, size):
    return jax.tree.map(lambda p: swap(p, "head", 1, size), odd)


def reduce_far(even, near, size):
    held = {2 * i: [p, near[i]] for i, p in enumerate(even)}
    bit, sent = 2, None
    while bit < size:
        for e in [e for e in held if e & bit]:
            sent = total(held.pop(e))
            got = swap(sent, "head", bit, size)
            held[e ^ bit].append(got)
        bit *= 2
    return held[0], sent


def term_sum(terms):
    return sum((t[0] if t.ndim == 3 else t).astype(F32) for t in terms)


def sum_small(value, axis, size):
    bit = 1
    while bit < size:
        value = value + swap(value, axis, bit, size)
        bit *= 2
    return value


def halve(values, bit, place):
    rows = values.shape[0] // 2
    own = (place & bit) // bit
    return tuple(
        lax.dynamic_slice_in_dim(values, part * rows, rows, 0) for part in (own, 1 - own)
    )


class BatchSum:
    def __init__(self, values, size, direct=False, before=()):
        self.size = size
        self.place = lax.axis_index("batch")
        self.bits = [1 << i for i in range(size.bit_length() - 1)]
        self.todo = [("halve", b) for b in self.bits] + [("join", b) for b in reversed(self.bits)]
        if direct and size <= 8:
            self.bits = self.bits[:1] + self.bits[:0:-1]
            self.todo = [("halve", 1), ("scatter", 0), ("gather", 0), ("join", 1)]
        self.values, self.mine, self.flying, self.sent = values, None, None, None
        self.before = list(before)
        self.start()

    def start(self):
        kind, bit = self.todo[0]
        self.sent = self.values
        if kind == "halve":
            self.mine, self.sent = halve(self.values, bit, self.place)
        others = range(1, self.size // 2)
        if kind == "scatter":
            rows = self.values.shape[0] * 2 // self.size
            own = self.place // 2
            blocks = [
                lax.dynamic_slice_in_dim(self.values, (own ^ d) * rows, rows, 0)
                for d in range(self.size // 2)
            ]
            self.mine, self.sent = blocks[0], blocks[-1]
            self.flying = [swap(blocks[d], "batch", 2 * d, self.size) for d in others]
        elif kind == "gather":
            self.flying = [swap(self.values, "batch", 2 * d, self.size) for d in others]
        else:
            self.flying = swap(self.sent, "batch", bit, self.size)

    def advance(self, got):
        kind, _ = self.todo.pop(0)
        if not self.todo:
            self.parts = [self.values, got]
        elif kind == "halve":
            self.values = total([self.mine, got])
        elif kind == "scatter":
            self.values = total([self.mine] + got)
        else:
            got = got if kind == "gather" else [got]
            self.values = jnp.concatenate([self.values] + got, axis=0)
        if self.before:
            self.values = jnp.concatenate(self.before + [self.values], axis=0)
            self.before = []
        if self.todo:
            self.start()

    def finish(self):
        while self.todo:
            self.advance(self.flying)
        return self.parts, self.bits


def store_blocks(place, summed, refs, out):
    (first, _), bits = summed
    count = 1 << len(bits)
    rows = 2 * first.shape[0] // count
    for p in range(count):
        at = 0
        for level, bit in enumerate(bits):
            other = p >> (len(bits) - 1 - level) & 1
            at = at + (((place // bit) % 2) ^ other) * ((count >> (level + 1)) * rows)
        ref, row = refs[p * 2 // count], (p % (count // 2)) * rows
        out[pl.ds(pl.multiple_of(at, rows), rows), :] = ref[row : row + rows, :].astype(out.dtype)


def segments(first, count, ranges):
    half, skip = sum(ranges) // 2, 0
    found = []
    for size in ranges:
        part = size // 2
        for side in range(2):
            low, high = max(first, 0), min(first + count, part)
            if low < high:
                found.append((side * half + skip + low, low - first, high - low))
            first -= part
        skip += part
    return found


def assemble(summed, place):
    parts, _ = summed
    rows, width = parts[0].shape

    def body(place, own_ref, other_ref, out):
        store_blocks(place[0], summed, (own_ref, other_ref), out)

    return pl.pallas_call(
        body,
        grid_spec=pltpu.PrefetchScalarGridSpec(
            num_scalar_prefetch=1,
            grid=(1,),
            in_specs=[whole((rows, width))] * 2,
            out_specs=whole((2 * rows, width)),
        ),
        out_shape=shape((2 * rows, width), F32),
        compiler_params=params(24),
        cost_estimate=cost(0, rows * width * 12),
        name="assemble",
    )(place, *parts)


def assemble_turned(summed, place, info, cols, n_head, pairs, ranges):
    parts, _ = summed
    width = cols // pairs
    rows, model = parts[0].shape
    share = model // n_head

    def body(place, info, own_ref, other_ref, q_out, k_out, v_out, o_out, small_out, room):
        store_blocks(place[0], summed, (own_ref, other_ref), room)
        for g in range(pairs):
            for i, out in enumerate((q_out, k_out, v_out)):
                for row, offset, count in segments((3 * g + i) * width, width, ranges):
                    lanes = slice(g * width + offset, g * width + offset + count)
                    for e in range(n_head):
                        at = pl.ds(pl.multiple_of((info[0] ^ e) * share, share), share)
                        out[at, lanes] = room[row : row + count, e * share : (e + 1) * share].T
        for out, first, rows in ((o_out, 3 * cols, cols), (small_out, 4 * cols, 8)):
            for row, offset, count in segments(first, rows, ranges):
                out[offset : offset + count, :] = room[row : row + count, :]

    return pl.pallas_call(
        body,
        grid_spec=pltpu.PrefetchScalarGridSpec(
            num_scalar_prefetch=2,
            grid=(1,),
            in_specs=[whole((rows, model))] * 2,
            out_specs=[whole((model, cols))] * 3 + [whole((cols, model)), whole((8, model))],
            scratch_shapes=[pltpu.VMEM((2 * rows, model), F32)],
        ),
        out_shape=[shape((model, cols), F32)] * 3 + [shape((n, model), F32) for n in (cols, 8)],
        compiler_params=params(32),
        cost_estimate=cost(0, cols * model * 24),
        name="assemble_turned",
    )(place, info, *parts)


def visible(first_key, first_query, starts, length, rows, cols):
    key = first_key + lax.broadcasted_iota(jnp.int32, (rows, cols), 0)
    query = first_query + lax.broadcasted_iota(jnp.int32, (rows, cols), 1)
    last = jnp.minimum(query, length - 1)
    return (key >= starts) & ((key <= last) | (key == query))


def prepare(w_query, w_key, w_value, w_out, cotangent, own, pair, n_head):
    model, cols = w_query.shape
    row_len, share = cotangent.shape
    rows = row_len // CHUNKS // n_head

    def body(own, q_ref, k_ref, v_ref, o_ref, c_ref, out, half, near, far_blocks):
        for g in range(cols // pair):
            for i, ref in enumerate((q_ref, k_ref, v_ref)):
                first = (3 * g + i) * pair
                out[first : first + pair, :] = ref[:, g * pair : (g + 1) * pair].T
        half[...] = o_ref[:, pl.ds(pl.multiple_of(own[1] * (model // 2), model // 2), model // 2)]
        for e in range(1, n_head):
            for c in range(CHUNKS):
                at = (c * n_head + (own[0] ^ e)) * rows
                block = c_ref[pl.ds(pl.multiple_of(at, rows), rows), :]
                if e == 1:
                    near[c * rows : (c + 1) * rows, :] = block
                else:
                    far_blocks[e - 2, c * rows : (c + 1) * rows, :] = block

    outs = pl.pallas_call(
        body,
        grid_spec=pltpu.PrefetchScalarGridSpec(
            num_scalar_prefetch=1,
            grid=(1,),
            in_specs=[whole((model, cols))] * 3 + [whole((cols, model)), whole((row_len, share))],
            out_specs=[
                whole((3 * cols, model)),
                whole((cols, model // 2)),
                whole((CHUNKS * rows, share)),
                whole((n_head - 2, CHUNKS * rows, share)),
            ],
        ),
        out_shape=[
            shape((3 * cols, model), BF16),
            shape((cols, model // 2), BF16),
            shape((CHUNKS * rows, share), BF16),
            shape((n_head - 2, CHUNKS * rows, share), BF16),
        ],
        compiler_params=params(24),
        cost_estimate=cost(0, 12 * cols * model),
        name="prepare",
    )(own, w_query, w_key, w_value, w_out, cotangent)
    return outs


def attend_kernel(
    chunk, n_head, heads, chunk_len, share, info, *refs
):
    refs = list(refs)
    x_refs = [refs.pop(0) for _ in range(n_head)]
    w_ref, cos_ref, sin_ref, gain_ref, start_ref = [refs.pop(0) for _ in range(5)]
    old_k, old_v = None, None
    if chunk:
        old_k, old_v = refs.pop(0), refs.pop(0)
        refs = refs[7:]
    k_ref, ve_ref, v_ref, kt_ref, qt_ref, ot_ref, inv_ref, qf_ref, kf_ref, o_ref = refs[:10]
    near_ref, far_ref, raw, acc = refs[10:]
    me, length = info[0], info[1]
    cols = heads * HD
    pair = min(2, heads)
    for e in range(n_head):
        first = pl.multiple_of((me ^ e) * share, share)
        for third in range(3):
            rows = slice(third * cols, (third + 1) * cols)
            term = dot(w_ref[rows, pl.ds(first, share)], x_refs[e][...], 1, 1)
            if e == 0:
                raw[rows, :] = term
            else:
                raw[rows, :] += term

    def raw_row(part, h):
        return ((h // pair * 3 + part) * pair + h % pair) * HD

    cosine, sine = cos_ref[...], sin_ref[...]
    for h in range(heads):
        own = slice(h * HD, (h + 1) * HD)
        for part, factor_ref in ((0, qf_ref), (1, kf_ref)):
            base = raw_row(part, h)
            a, b = raw[base : base + HALF, :], raw[base + HALF : base + HD, :]
            front, back = a * cosine - b * sine, b * cosine + a * sine
            mean = jnp.sum(front * front + back * back, axis=0, keepdims=True) / HD
            factor = lax.rsqrt(mean + EPSILON)
            factor_ref[h] = factor
            unit = jnp.concatenate([front, back], axis=0) * factor
            low = (unit * gain_ref[own, :]).astype(BF16)
            if part == 0:
                qt_ref[own, :] = low * BF16(1.0 / math.sqrt(HD))
            else:
                kt_ref[own, :] = low
                k_ref[h] = low.T
        value = raw[raw_row(2, h) : raw_row(2, h) + HD, :].astype(BF16)
        v_ref[h] = value.T
        ve_ref[h, :HD, :] = value
        ve_ref[h, HD:, :] = jnp.ones((VALUE_ROWS - HD, chunk_len), BF16)

    before = chunk * (chunk_len // KEYS)

    def step(local, key_first, k_of, v_of, starts):
        query = slice(local * QUERIES, (local + 1) * QUERIES)
        first = chunk * chunk_len + local * QUERIES
        mask = visible(key_first, first, starts, length, KEYS, QUERIES)
        for h in range(heads):
            scores = dot(k_of(h), qt_ref[h * HD : (h + 1) * HD, query])
            probs = jnp.where(mask, jnp.exp(scores), 0.0).astype(BF16)
            acc[h] += dot(v_of(h), probs)

    for local in range(chunk_len // QUERIES):
        query = slice(local * QUERIES, (local + 1) * QUERIES)
        starts = start_ref[:, query]
        lowest = info[2 + (chunk * chunk_len + local * QUERIES) // BLOCK] * BLOCK // KEYS
        acc[...] = jnp.zeros_like(acc)
        if chunk:

            @pl.loop(lowest, before)
            def _(kb):
                at = pl.ds(pl.multiple_of(kb * KEYS, KEYS), KEYS)
                step(
                    local, kb * KEYS, lambda h: old_k[h, at, :], lambda h: old_v[h, :, at], starts
                )

        @pl.loop(jnp.maximum(lowest - before, 0), (local + 1) * QUERIES // KEYS)
        def _(kb):
            at = pl.ds(pl.multiple_of(kb * KEYS, KEYS), KEYS)
            step(
                local,
                (before + kb) * KEYS,
                lambda h: k_ref[h, at, :],
                lambda h: ve_ref[h, :, at],
                starts,
            )

        for h in range(heads):
            inverse = 1.0 / acc[h, HD : HD + 1, :]
            inv_ref[h, :, query] = inverse
            out = acc[h, :HD, :] * inverse
            ot_ref[h * HD : (h + 1) * HD, query] = out.astype(BF16)
            o_ref[query, h * HD : (h + 1) * HD] = out.T.astype(BF16)
    rows = chunk_len // n_head
    for e in range(1, n_head):
        block = o_ref[pl.ds(pl.multiple_of((me ^ e) * rows, rows), rows), :]
        if e == 1:
            near_ref[...] = block
        else:
            far_ref[e - 2] = block


def attend_chunk(
    chunk, x_pieces, w_t, cosine, sine, gain, starts, info, buffers, row_len, chunk_len
):
    n_head = len(x_pieces)
    share = x_pieces[0].shape[1]
    cols = w_t.shape[0] // 3
    heads = cols // HD
    model = w_t.shape[1]
    body = functools.partial(attend_kernel, chunk, n_head, heads, chunk_len, share)
    by_lane = lambda rows: pl.BlockSpec((rows, chunk_len), lambda i, info: (0, chunk))
    specs = [whole((chunk_len, share))] * n_head + [
        whole((3 * cols, model)),
        by_lane(HALF),
        by_lane(HALF),
        whole((cols, 1)),
        by_lane(1),
    ]
    operands = [*x_pieces, w_t, cosine, sine, gain, starts]
    aliases = {}
    if chunk:
        aliases = {1 + len(operands) + i: i for i in range(9)}
        specs += [whole((heads, row_len, HD)), whole((heads, VALUE_ROWS, row_len))]
        specs += [pl.BlockSpec(memory_space=pl.ANY)] * 7
        operands += buffers
    lane3 = lambda rows: pl.BlockSpec((heads, rows, chunk_len), lambda i, info: (0, 0, chunk))
    row3 = pl.BlockSpec((heads, chunk_len, HD), lambda i, info: (0, chunk, 0))
    outs = pl.pallas_call(
        body,
        grid_spec=pltpu.PrefetchScalarGridSpec(
            num_scalar_prefetch=1,
            grid=(1,),
            in_specs=specs,
            out_specs=[
                row3,
                lane3(VALUE_ROWS),
                row3,
                by_lane(cols),
                by_lane(cols),
                by_lane(cols),
                lane3(1),
                lane3(1),
                lane3(1),
                whole((chunk_len, cols)),
            ]
            + [
                whole((chunk_len // n_head, cols)),
                whole((n_head - 2, chunk_len // n_head, cols)),
            ],
            scratch_shapes=[
                pltpu.VMEM((3 * cols, chunk_len), F32),
                pltpu.VMEM((heads, VALUE_ROWS, QUERIES), F32),
            ],
        ),
        out_shape=[
            kept_shape((heads, row_len, HD), BF16),
            kept_shape((heads, VALUE_ROWS, row_len), BF16),
            kept_shape((heads, row_len, HD), BF16),
            kept_shape((cols, row_len), BF16),
            kept_shape((cols, row_len), BF16),
            kept_shape((cols, row_len), BF16),
            kept_shape((heads, 1, row_len), F32),
            kept_shape((heads, 1, row_len), F32),
            kept_shape((heads, 1, row_len), F32),
            kept_shape((chunk_len, cols), BF16),
        ]
        + [
            kept_shape((chunk_len // n_head, cols), BF16),
            kept_shape((n_head - 2, chunk_len // n_head, cols), BF16),
        ],
        input_output_aliases=aliases,
        compiler_params=params(40),
        cost_estimate=cost(16e9 / CHUNKS, 8e6),
        name="attend",
    )(info, *operands)
    return outs[:9], list(outs[9:])


def unattend_kernel(n_head, chunks, row_len, piece, pair, info, *refs):
    refs = list(refs)
    d_refs = [refs.pop(0) for _ in range(chunks * n_head)]
    k_ref, v_ref, kt_ref, qt_ref, ot_ref, inv_ref, qf_ref, kf_ref = [refs.pop(0) for _ in range(8)]
    start_ref, cos_ref, sin_ref, gain_ref = [refs.pop(0) for _ in range(4)]
    out_ref, gain_out, do_s, inner_s, dq_s, dk_s, dv_s = refs
    me, length = info[0], info[1]
    for c in range(chunks):
        for e in range(n_head):
            first = c * n_head * piece + (me ^ e) * piece
            do_s[:, pl.ds(pl.multiple_of(first, piece), piece)] = d_refs[c * n_head + e][...]
    for h in range(pair):
        own = slice(h * HD, (h + 1) * HD)
        product = do_s[own, :].astype(F32) * ot_ref[own, :].astype(F32)
        inner_s[h] = jnp.sum(product, axis=0, keepdims=True)
    dq_s[...] = jnp.zeros_like(dq_s)
    dk_s[...] = jnp.zeros_like(dk_s)
    dv_s[...] = jnp.zeros_like(dv_s)

    ratio = QUERIES // BLOCK

    @pl.loop(0, row_len // QUERIES)
    def _(qb):
        query = pl.ds(pl.multiple_of(qb * QUERIES, QUERIES), QUERIES)
        starts = start_ref[:, query]

        @pl.loop(info[2 + qb * ratio], (qb + 1) * ratio)
        def _(kb):
            key = pl.ds(pl.multiple_of(kb * BLOCK, BLOCK), BLOCK)
            mask = visible(kb * BLOCK, qb * QUERIES, starts, length, BLOCK, QUERIES)
            for h in range(pair):
                own = slice(h * HD, (h + 1) * HD)
                q_block, do_block = qt_ref[own, query], do_s[own, query]
                scores = dot(k_ref[h, key, :], q_block)
                probs = jnp.where(mask, jnp.exp(scores), 0.0) * inv_ref[h, :, query]
                d_probs = dot(v_ref[h, key, :], do_block)
                d_scores = (probs * (d_probs - inner_s[h, :, query])).astype(BF16)
                dv_s[own, key] += dot(do_block, probs.astype(BF16), 1, 1)
                dk_s[own, key] += dot(q_block, d_scores, 1, 1)
                dq_s[own, query] += dot(kt_ref[own, key], d_scores)

    for h in range(pair):
        own = slice(h * HD, (h + 1) * HD)
        gain = gain_ref[own, :]
        summed = jnp.zeros((HD, 1), F32)
        for part, low_ref, grad_ref, factor_ref in (
            (0, qt_ref, dq_s, qf_ref),
            (1, kt_ref, dk_s, kf_ref),
        ):
            scale = math.sqrt(HD) if part == 0 else 1.0
            unit = low_ref[own, :].astype(F32) * (scale / gain)
            grad = grad_ref[own, :]
            if part == 0:
                grad = grad * (1.0 / math.sqrt(HD))
            summed += jnp.sum(grad * unit, axis=1, keepdims=True)
            grad = grad * gain
            mean = jnp.sum(grad * unit, axis=0, keepdims=True) / HD
            grad = (grad - unit * mean) * factor_ref[h]
            front, back = grad[:HALF], grad[HALF:]
            cosine, sine = cos_ref[...], sin_ref[...]
            out_ref[part, h * HD : h * HD + HALF, :] = (front * cosine + back * sine).astype(BF16)
            out_ref[part, h * HD + HALF : (h + 1) * HD, :] = (
                back * cosine - front * sine
            ).astype(BF16)
        out_ref[2, own, :] = dv_s[own, :].astype(BF16)
        gain_out[own, :] = summed


def unattend(index, do_pieces, buffers, starts, cosine, sine, gain, info, n_head):
    k, _, v, kt, qt, ot, inv, qf, kf = buffers
    chunks = len(do_pieces) // n_head
    cols, piece = do_pieces[0].shape
    heads, row_len, _ = k.shape
    pair = min(2, heads)
    rows = pair * HD
    by_rows = lambda width: pl.BlockSpec((rows, width), lambda g, info: (index, 0))
    by_head = lambda a, b: pl.BlockSpec((pair, a, b), lambda g, info: (index, 0, 0))
    return pl.pallas_call(
        functools.partial(unattend_kernel, n_head, chunks, row_len, piece, pair),
        grid_spec=pltpu.PrefetchScalarGridSpec(
            num_scalar_prefetch=1,
            grid=(1,),
            in_specs=[by_rows(piece)] * (chunks * n_head)
            + [by_head(row_len, HD)] * 2
            + [by_rows(row_len)] * 3
            + [by_head(1, row_len)] * 3
            + [whole((1, row_len)), whole((HALF, row_len)), whole((HALF, row_len)), by_rows(1)],
            out_specs=[whole((3, rows, row_len)), whole((rows, 1))],
            scratch_shapes=[
                pltpu.VMEM((rows, row_len), BF16),
                pltpu.VMEM((pair, 1, row_len), F32),
                pltpu.VMEM((rows, row_len), F32),
                pltpu.VMEM((rows, row_len), F32),
                pltpu.VMEM((rows, row_len), F32),
            ],
        ),
        out_shape=[kept_shape((3, rows, row_len), BF16), shape((rows, 1), F32)],
        compiler_params=params(32),
        cost_estimate=cost(22e9, 6e6),
        name="unattend",
    )(info, *do_pieces, k, v, kt, qt, ot, inv, qf, kf, starts, cosine, sine, gain)


def norm(values):
    factor = lax.rsqrt(jnp.mean(values * values, axis=-1, keepdims=True) + EPSILON)
    return values * factor, factor


def norm_back(grad, unit, factor):
    return factor * (grad - unit * jnp.mean(grad * unit, axis=-1, keepdims=True))


def project_kernel(n_head, share, kept, info, *refs):
    o_refs, w_refs = refs[:n_head], refs[n_head : 2 * n_head]
    x_refs = refs[2 * n_head : 3 * n_head]
    alpha_ref = refs[3 * n_head]
    cat_ref, y_ref, x_ref, h_ref, low_ref = refs[3 * n_head + 1 + kept :]
    me = info[0]
    cols = w_refs[0].shape[0]
    y = dot(o_refs[0][...], w_refs[0][...])
    for e in range(1, n_head):
        y += dot(o_refs[e][...], w_refs[e][...])
    for e in range(n_head):
        cat_ref[:, e * cols : (e + 1) * cols] = o_refs[e][...]
    for e in range(n_head):
        first = pl.multiple_of((me ^ e) * share, share)
        x_ref[:, pl.ds(first, share)] = x_refs[e][...]
    y_ref[...] = y
    h_zero = x_ref[...].astype(F32)
    h_one, _ = norm(h_zero + alpha_ref[...] * (norm(y)[0] - h_zero))
    h_ref[...] = h_one
    low_ref[...] = h_one.astype(BF16)


def project(chunk, kept, o_pieces, w_pieces, x_pieces, alpha, info, chunk_len):
    n_head = len(o_pieces)
    cols, model = w_pieces[0].shape
    share = x_pieces[0].shape[1]
    rows = chunk_len // n_head
    mine = lambda width: pl.BlockSpec((rows, width), lambda i, info: (info[0], 0))
    return pl.pallas_call(
        functools.partial(project_kernel, n_head, share, len(kept)),
        grid_spec=pltpu.PrefetchScalarGridSpec(
            num_scalar_prefetch=1,
            grid=(1,),
            in_specs=[mine(cols)]
            + [whole((rows, cols))] * (n_head - 1)
            + [whole((cols, model))] * n_head
            + [mine(share)] * n_head
            + [whole((1, model))]
            + [pl.BlockSpec(memory_space=pl.ANY)] * len(kept),
            out_specs=[pl.BlockSpec((rows, n_head * cols), lambda i, info: (chunk, 0))]
            + [whole((rows, model))] * 4,
        ),
        input_output_aliases={3 * n_head + 2 + i: i for i in range(len(kept))},
        out_shape=[
            kept_shape((CHUNKS * rows, n_head * cols), BF16),
            kept_shape((rows, model), F32),
            kept_shape((rows, model), BF16),
            kept_shape((rows, model), F32),
            shape((rows, model), BF16),
        ],
        compiler_params=params(32),
        cost_estimate=cost(2.0 * rows * model * model, 6e6),
        name="project",
    )(info, *o_pieces, *w_pieces, *x_pieces, alpha, *kept)


def feed_kernel(n_head, rows, *refs):
    h_refs = refs[:n_head]
    up_ref, gate_ref, down_hbm, su_ref, sg_ref = refs[n_head : n_head + 5]
    m_ref, cat_hbm, u_ref, g_ref = refs[n_head + 5 : n_head + 9]
    z_refs = refs[n_head + 9 : 2 * n_head + 9]
    cat, mixed_s, down, cat_sem, down_sem = refs[2 * n_head + 9 :]
    tile = pl.program_id(0)
    keep = pltpu.make_async_copy(cat, cat_hbm, cat_sem)
    fetch = pltpu.make_async_copy(down_hbm, down, down_sem)

    @pl.when(tile == 0)
    def _():
        fetch.start()
        for e in range(n_head):
            cat[e * rows : (e + 1) * rows, :] = h_refs[e][...]
        keep.start()

    up_raw = dot(cat[...], up_ref[...])
    gate_raw = dot(cat[...], gate_ref[...])
    u_ref[...] = up_raw.astype(BF16)
    g_ref[...] = gate_raw.astype(BF16)
    gate = gate_raw * sg_ref[...]
    mixed = (up_raw * su_ref[...] * (gate * jax.nn.sigmoid(gate))).astype(BF16)
    m_ref[...] = mixed
    width = m_ref.shape[1]
    mixed_s[:, pl.ds(pl.multiple_of(tile * width, width), width)] = mixed

    @pl.when(tile == pl.num_programs(0) - 1)
    def _():
        fetch.wait()
        z = dot(mixed_s[...], down[...])
        for e in range(n_head):
            z_refs[e][...] = z[e * rows : (e + 1) * rows, :].astype(BF16)
        keep.wait()


def feed(h_pieces, w_up, w_gate, w_down, scale_up, scale_gate):
    n_head = len(h_pieces)
    rows, model = h_pieces[0].shape
    hidden = w_up.shape[1]
    tile = min(256, hidden // 2)
    count = n_head * rows
    by_col = lambda height: pl.BlockSpec((height, tile), lambda n: (0, n))
    anywhere = pl.BlockSpec(memory_space=pl.ANY)
    outs = pl.pallas_call(
        functools.partial(feed_kernel, n_head, rows),
        grid=(hidden // tile,),
        in_specs=[whole((rows, model))] * n_head
        + [by_col(model), by_col(model), anywhere, by_col(1), by_col(1)],
        out_specs=[by_col(count), anywhere, by_col(count), by_col(count)]
        + [whole((rows, model))] * n_head,
        out_shape=[
            kept_shape((count, hidden), BF16),
            kept_shape((count, model), BF16),
            kept_shape((count, hidden), BF16),
            kept_shape((count, hidden), BF16),
        ]
        + [shape((rows, model), BF16)] * n_head,
        scratch_shapes=[
            pltpu.VMEM((count, model), BF16),
            pltpu.VMEM((count, hidden), BF16),
            pltpu.VMEM((hidden, model), BF16),
            pltpu.SemaphoreType.DMA,
            pltpu.SemaphoreType.DMA,
        ],
        compiler_params=params(48),
        cost_estimate=cost(6.0 * count * model * hidden, 20e6),
        name="feed",
    )(*h_pieces, w_up, w_gate, held(w_down), scale_up, scale_gate)
    return outs[:2], outs[2:4], list(outs[4::2]), list(outs[5::2])


def middle_kernel(n_head, n_terms, share, kept, info, *refs):
    z_refs, c_refs = refs[:n_terms], refs[n_terms : n_terms + n_head]
    h_ref, alpha_ref = refs[n_terms + n_head : n_terms + n_head + 2]
    refs = refs[n_terms + n_head + 2 + kept :]
    own_ref, near_ref, far_ref, dz_ref, direct_ref, grad_ref, two_s, cot_s = refs
    me = info[0]
    z = z_refs[0][...].astype(F32)
    for r in z_refs[1:]:
        z += r[...].astype(F32)
    h_one, alpha = h_ref[...], alpha_ref[...]
    h_ffn, z_factor = norm(z)
    h_two, factor = norm(h_one + alpha * (h_ffn - h_one))
    two_s[...] = h_two.astype(BF16)
    for e in range(n_head):
        at = pl.ds(pl.multiple_of((me ^ e) * share, share), share)
        if e < 2:
            (own_ref, near_ref)[e][...] = two_s[:, at]
        else:
            far_ref[e - 2] = two_s[:, at]
        cot_s[:, at] = c_refs[e][...]
    grad = norm_back(cot_s[...].astype(F32), h_two, factor)
    grad_ref[...] = jnp.sum(grad * (h_ffn - h_one), axis=0, keepdims=True)
    direct_ref[...] = grad * (1.0 - alpha)
    dz_ref[...] = norm_back(grad * alpha, h_ffn, z_factor).astype(BF16)


def middle(chunk, kept, z_terms, cot_pieces, h_one, alpha, info):
    n_head, n_terms = len(cot_pieces), len(z_terms)
    rows, model = h_one.shape
    share = cot_pieces[0].shape[1]
    mine = pl.BlockSpec((rows, share), lambda i, info: (chunk * n_head + info[0], 0))
    theirs = pl.BlockSpec((rows, share), lambda i, info: (chunk, 0))
    outs = pl.pallas_call(
        functools.partial(middle_kernel, n_head, n_terms, share, len(kept)),
        grid_spec=pltpu.PrefetchScalarGridSpec(
            num_scalar_prefetch=1,
            grid=(1,),
            in_specs=[term_spec(t) for t in z_terms]
            + [mine]
            + [theirs] * (n_head - 1)
            + [whole((rows, model)), whole((1, model))]
            + [pl.BlockSpec(memory_space=pl.ANY)] * len(kept),
            out_specs=[theirs] * 2
            + [pl.BlockSpec((n_head - 2, rows, share), lambda i, info: (0, chunk, 0))]
            + [whole((rows, model))] * 2
            + [whole((1, model))],
            scratch_shapes=[pltpu.VMEM((rows, model), BF16), pltpu.VMEM((rows, model), BF16)],
        ),
        input_output_aliases={n_terms + n_head + 3 + i: i for i in range(len(kept))},
        out_shape=[kept_shape((CHUNKS * rows, share), BF16)] * 2
        + [kept_shape((n_head - 2, CHUNKS * rows, share), BF16)]
        + [shape((rows, model), BF16), kept_shape((rows, model), F32), shape((1, model), F32)],
        compiler_params=params(32),
        cost_estimate=cost(rows * model * 60, rows * model * 24),
        name="middle",
    )(info, *z_terms, *cot_pieces, held(h_one), alpha, *kept)
    return list(outs[:3]), *outs[3:]


def join(pieces):
    rows, width = pieces[0].shape

    def body(*refs):
        for i, ref in enumerate(refs[:-1]):
            refs[-1][i * rows : (i + 1) * rows, :] = ref[...]

    return pl.pallas_call(
        body,
        in_specs=[whole((rows, width))] * len(pieces),
        out_specs=whole((rows * len(pieces), width)),
        grid=(1,),
        out_shape=shape((rows * len(pieces), width), pieces[0].dtype),
        compiler_params=params(16),
        cost_estimate=cost(0, rows * width * 4 * len(pieces)),
        name="join",
    )(*pieces)


def weigh_feed(mixed, joined, dz, du, dg):
    count, hidden = mixed.shape
    model = joined.shape[1]
    tile = min(256, hidden // 2)

    def body(m_ref, h_ref, z_ref, u_ref, g_ref, down, up, gate):
        down[...] = dot(m_ref[...], z_ref[...], 0, 0)
        up[...] = dot(h_ref[...], u_ref[...], 0, 0)
        gate[...] = dot(h_ref[...], g_ref[...], 0, 0)

    by_col = lambda height: pl.BlockSpec((height, tile), lambda n: (0, n))
    return pl.pallas_call(
        body,
        in_specs=[
            by_col(count),
            whole((count, model)),
            whole((count, model)),
            by_col(count),
            by_col(count),
        ],
        out_specs=[pl.BlockSpec((tile, model), lambda n: (n, 0)), by_col(model), by_col(model)],
        grid=(hidden // tile,),
        out_shape=[kept_shape((hidden, model), F32)] + [kept_shape((model, hidden), F32)] * 2,
        compiler_params=params(48),
        cost_estimate=cost(6.0 * count * hidden * model, 20e6),
        name="weigh_feed",
    )(mixed, joined, dz, du, dg)


def weigh(d_pair, x_pieces, chunk_len):
    rows, row_len = d_pair.shape
    n_head = len(x_pieces[0])
    share = x_pieces[0][0].shape[1]
    flat = [p for chunk in x_pieces for p in chunk]

    def body(d_ref, *refs):
        for e in range(n_head):
            term = None
            for c in range(len(x_pieces)):
                d_part = d_ref[:, c * chunk_len : (c + 1) * chunk_len]
                new = dot(d_part, refs[c * n_head + e][...])
                term = new if term is None else term + new
            refs[-1][:, e * share : (e + 1) * share] = term.astype(BF16)

    return pl.pallas_call(
        body,
        in_specs=[whole((rows, row_len))] + [whole((chunk_len, share))] * len(flat),
        out_specs=whole((rows, n_head * share)),
        grid=(1,),
        out_shape=shape((rows, n_head * share), BF16),
        compiler_params=params(32),
        cost_estimate=cost(0, 1),
        name="weigh",
    )(d_pair, *flat)


def unfeed_kernel(n_head, n_in, rows, *refs):
    d_refs, refs = refs[:n_in], refs[n_in:]
    u_ref, g_ref, up_hbm, gate_hbm, down_ref, su_ref, sg_ref = refs[:7]
    du_ref, dg_ref, gsu_ref, gsg_ref = refs[7:11]
    out_refs = refs[11 : 11 + n_head]
    cat_hbm = refs[11 + n_head] if n_in > 1 else None
    refs = refs[11 + n_head + (n_in > 1) :]
    du_s, dg_s, up, gate_w, sems = refs[:5]
    cat = refs[5] if n_in > 1 else d_refs[0]
    tile = pl.program_id(0)
    fetch_up = pltpu.make_async_copy(up_hbm, up, sems.at[0])
    fetch_gate = pltpu.make_async_copy(gate_hbm, gate_w, sems.at[1])
    keep = pltpu.make_async_copy(cat, cat_hbm, sems.at[2]) if n_in > 1 else None

    @pl.when(tile == 0)
    def _():
        fetch_up.start()
        fetch_gate.start()
        if n_in > 1:
            for e in range(n_in):
                cat[e * rows : (e + 1) * rows, :] = d_refs[e][...]
            keep.start()

    d_mixed = dot(cat[...], down_ref[...], 1, 1)
    up_raw, gate_raw = u_ref[...].astype(F32), g_ref[...].astype(F32)
    gate = gate_raw * sg_ref[...]
    sigmoid = jax.nn.sigmoid(gate)
    silu = gate * sigmoid
    d_up = d_mixed * silu
    d_gate = d_mixed * (up_raw * su_ref[...]) * (sigmoid + silu * (1.0 - sigmoid))
    gsu_ref[...] = jnp.sum(d_up * up_raw, axis=0, keepdims=True)
    gsg_ref[...] = jnp.sum(d_gate * gate_raw, axis=0, keepdims=True)
    up_low = (d_up * su_ref[...]).astype(BF16)
    gate_low = (d_gate * sg_ref[...]).astype(BF16)
    du_ref[...] = up_low
    dg_ref[...] = gate_low
    width = du_ref.shape[1]
    at = pl.ds(pl.multiple_of(tile * width, width), width)
    du_s[:, at] = up_low
    dg_s[:, at] = gate_low

    @pl.when(tile == pl.num_programs(0) - 1)
    def _():
        fetch_up.wait()
        fetch_gate.wait()
        dh = dot(du_s[...], up[...], 1, 1) + dot(dg_s[...], gate_w[...], 1, 1)
        for e in range(n_head):
            out_refs[e][...] = dh[e * rows : (e + 1) * rows, :].astype(BF16)
        if n_in > 1:
            keep.wait()


def unfeed(dz_pieces, u, g, w_up, w_gate, w_down, scale_up, scale_gate, n_head):
    n_in = len(dz_pieces)
    model = dz_pieces[0].shape[1]
    count, hidden = u.shape
    rows = count // n_head
    tile = min(256, hidden // 2)
    by_col = lambda height: pl.BlockSpec((height, tile), lambda n: (0, n))
    anywhere = pl.BlockSpec(memory_space=pl.ANY)
    outs = pl.pallas_call(
        functools.partial(unfeed_kernel, n_head, n_in, rows),
        grid=(hidden // tile,),
        in_specs=[whole(dz_pieces[0].shape)] * n_in
        + [
            by_col(count),
            by_col(count),
            anywhere,
            anywhere,
            pl.BlockSpec((tile, model), lambda n: (n, 0)),
            by_col(1),
            by_col(1),
        ],
        out_specs=[by_col(count)] * 2
        + [by_col(1), by_col(1)]
        + [whole((rows, model))] * n_head
        + [anywhere] * (n_in > 1),
        out_shape=[kept_shape((count, hidden), BF16)] * 2
        + [shape((1, hidden), F32), shape((1, hidden), F32)]
        + [shape((rows, model), BF16)] * n_head
        + [kept_shape((count, model), BF16)] * (n_in > 1),
        scratch_shapes=[
            pltpu.VMEM((count, hidden), BF16),
            pltpu.VMEM((count, hidden), BF16),
            pltpu.VMEM((model, hidden), BF16),
            pltpu.VMEM((model, hidden), BF16),
            pltpu.SemaphoreType.DMA((3,)),
        ]
        + [pltpu.VMEM((count, model), BF16)] * (n_in > 1),
        compiler_params=params(48),
        cost_estimate=cost(6.0 * count * model * hidden, 20e6),
        name="unfeed",
    )(*dz_pieces, u, g, held(w_up), held(w_gate), w_down, scale_up, scale_gate)
    pieces = outs[4 : 4 + n_head]
    return outs[:2], outs[2:4], list(pieces[::2]), list(pieces[1::2]), outs[-1]


def unproject_kernel(n_head, n_terms, kept, *refs):
    t_refs, w_refs = refs[:n_terms], refs[n_terms : n_terms + n_head]
    direct_ref, y_ref, x_ref, alpha_ref = refs[n_terms + n_head : n_terms + n_head + 4]
    refs = refs[n_terms + n_head + 4 + kept :]
    dy_ref, refs = refs[0], refs[1:]
    own_ref, near_ref, far_ref, zero_ref, grad_ref = refs
    grad = direct_ref[...]
    for r in t_refs:
        grad += r[...].astype(F32)
    alpha = alpha_ref[...]
    h_zero = x_ref[...].astype(F32)
    h_attn, y_factor = norm(y_ref[...])
    h_one, factor = norm(h_zero + alpha * (h_attn - h_zero))
    grad = norm_back(grad, h_one, factor)
    grad_ref[...] = jnp.sum(grad * (h_attn - h_zero), axis=0, keepdims=True)
    zero_ref[...] = grad * (1.0 - alpha)
    dy = norm_back(grad * alpha, h_attn, y_factor).astype(BF16)
    dy_ref[...] = dy
    for e in range(n_head):
        value = dot(w_refs[e][...], dy, 1, 1).astype(BF16)
        if e < 2:
            (own_ref, near_ref)[e][...] = value
        else:
            far_ref[e - 2] = value


def unproject(chunk, kept, terms, w_pieces, direct, y, x, alpha):
    n_head, n_terms = len(w_pieces), len(terms)
    rows, model = y.shape
    cols = w_pieces[0].shape[0]
    outs = pl.pallas_call(
        functools.partial(unproject_kernel, n_head, n_terms, len(kept)),
        grid=(1,),
        in_specs=[term_spec(t) for t in terms]
        + [whole((cols, model))] * n_head
        + [whole((rows, model))] * 3
        + [whole((1, model))]
        + [pl.BlockSpec(memory_space=pl.ANY)] * len(kept),
        out_specs=[pl.BlockSpec((rows, model), lambda i: (chunk, 0))]
        + [whole((cols, rows))] * 2
        + [whole((n_head - 2, cols, rows))]
        + [whole((rows, model)), whole((1, model))],
        input_output_aliases={n_terms + n_head + 4 + i: i for i in range(len(kept))},
        out_shape=[kept_shape((CHUNKS * rows, model), BF16)]
        + [shape((cols, rows), BF16)] * 2
        + [shape((n_head - 2, cols, rows), BF16)]
        + [kept_shape((rows, model), F32), shape((1, model), F32)],
        compiler_params=params(32),
        cost_estimate=cost(2.0 * rows * model * model, 8e6),
        name="unproject",
    )(*terms, *w_pieces, held(direct), held(y), held(x), alpha, *kept)
    return outs[0], list(outs[1:4]), outs[4], outs[5]


def spread_kernel(n_head, share, pairs, info, *refs):
    d_refs, (w_ref, direct_ref), out_refs = refs[:pairs], refs[pairs : pairs + 2], refs[pairs + 2 :]
    me = info[0]
    block = pl.program_id(0)
    d_all = jnp.concatenate([r[...] for r in d_refs], axis=0).T
    for e in range(n_head):
        at = pl.ds(pl.multiple_of((me ^ e) * share, share), share)
        term = dot(d_all, w_ref[:, at])

        ref = out_refs[n_head // 2].at[e // 2] if e % 2 else out_refs[e // 2]

        @pl.when(block == me)
        def _():
            ref[...] = (term + direct_ref[:, at]).astype(BF16)

        @pl.when(block != me)
        def _():
            ref[...] = term.astype(BF16)


def spread(chunk, chunk_len, d_all, w_t, direct, info, n_head):
    rows3, model = w_t.shape
    share = model // n_head
    rows = chunk_len // n_head
    return pl.pallas_call(
        functools.partial(spread_kernel, n_head, share, len(d_all)),
        grid_spec=pltpu.PrefetchScalarGridSpec(
            num_scalar_prefetch=1,
            grid=(n_head,),
            in_specs=[
                *[pl.BlockSpec((d.shape[0], rows), lambda i, info: (0, chunk * n_head + i)) for d in d_all],
                whole((rows3, model)),
                whole((rows, model)),
            ],
            out_specs=[pl.BlockSpec((rows, share), lambda i, info: (i, 0))] * (n_head // 2)
            + [pl.BlockSpec((n_head // 2, rows, share), lambda i, info: (0, i, 0))],
        ),
        out_shape=[shape((chunk_len, share), BF16)] * (n_head // 2)
        + [shape((n_head // 2, chunk_len, share), BF16)],
        compiler_params=params(32),
        cost_estimate=cost(2.0 * chunk_len * model * rows3, 8e6),
        name="spread",
    )(info, *d_all, w_t, direct)


def settle(own, pieces, info):
    pieces = [own] + pieces
    n_head = len(pieces)
    count, share = own.shape
    rows = count // CHUNKS

    def body(info, *refs):
        for e in range(n_head):
            for c in range(CHUNKS):
                at = (c * n_head + (info[0] ^ e)) * rows
                refs[-1][pl.ds(pl.multiple_of(at, rows), rows), :] = refs[e][
                    c * rows : (c + 1) * rows, :
                ]

    return pl.pallas_call(
        body,
        grid_spec=pltpu.PrefetchScalarGridSpec(
            num_scalar_prefetch=1,
            grid=(1,),
            in_specs=[whole((count, share))] * n_head,
            out_specs=whole((n_head * count, share)),
        ),
        out_shape=shape((n_head * count, share), BF16),
        compiler_params=params(16),
        cost_estimate=cost(0, n_head * count * share * 4),
        name="settle",
    )(info, *pieces)


def on_device(
    n_batch,
    n_head,
    hidden_in,
    cotangent,
    doc_ids,
    lengths,
    w_query,
    w_key,
    w_value,
    w_out,
    w_up,
    w_gate,
    w_down,
    scale_qk,
    scale_up,
    scale_gate,
    alpha_attn,
    alpha_ffn,
):
    _, row_len, share = hidden_in.shape
    model = share * n_head
    cols = w_query.shape[1]
    chunk_len = row_len // CHUNKS
    rows = chunk_len // n_head
    me = lax.axis_index("head")
    chunks = range(CHUNKS)
    x_own, cot_own = hidden_in[0], cotangent[0]

    docs = doc_ids[0]
    column = jnp.arange(row_len, dtype=jnp.int32)
    starts = sum(
        jnp.where(docs > d, jnp.sum((docs == d).astype(jnp.int32)), 0) for d in range(5)
    ).astype(jnp.int32)
    position = (column - starts).astype(F32)
    frequency = 10000.0 ** (-(jnp.arange(HALF, dtype=F32) * 2.0 / HD))
    angles = frequency[:, None] * position[None, :]
    cosine, sine = jnp.cos(angles), jnp.sin(angles)
    info = jnp.concatenate(
        [me[None].astype(jnp.int32), lengths.astype(jnp.int32), starts[::BLOCK] // BLOCK]
    )
    starts = starts[None, :]
    gain = scale_qk[:, None]
    up_scale, gate_scale = scale_up[None, :], scale_gate[None, :]
    attn_alpha, ffn_alpha = alpha_attn[None, :], alpha_ffn[None, :]

    def part(values, c):
        return lax.slice_in_dim(values, c * chunk_len, (c + 1) * chunk_len, axis=0)

    def block_of(values, e):
        return lax.dynamic_slice_in_dim(values, (me ^ e) * rows, rows, 0)

    order = Order()
    pair = min(2, cols // HD) * HD
    pairs = cols // pair
    far = n_head // 2
    place = lax.axis_index("batch")[None].astype(jnp.int32)

    bit = lax.axis_index("batch") % 2
    own = jnp.stack([me, bit]).astype(jnp.int32)

    x_far = gather_far(part(x_own, 0), n_head)
    (w_t, out_half, cot_near, cot_far), x_far = order.run(
        lambda w: prepare(w, w_key, w_value, w_out, cot_own, own, pair, n_head),
        w_query,
        beside=x_far,
    )
    buffers, x_pieces, o_own, o_moving = [], [], [], []
    for c in chunks:
        x_pieces.append(gather_near(x_far, n_head))
        beside = []
        if c == 0:
            halves = {
                e: swap(after(out_half, order.last), "head", e, n_head) for e in range(2, n_head, 2)
            }
            beside = [halves]
        else:
            cot_moving = Exchange(after(cot_near, order.last), after(cot_far, order.last), n_head)
            beside = [o_moving[0].flying, cot_moving.flying, out_far]
        if c < CHUNKS - 1:
            beside.append(gather_far(after(part(x_own, c + 1), order.last), n_head))
        (buffers, (o_chunk, near, far_blocks)), beside = order.run(
            lambda w: attend_chunk(
                c, x_pieces[c], w, cosine, sine, gain, starts, info, buffers, row_len, chunk_len
            ),
            w_t,
            need=x_pieces[c],
            beside=beside,
        )
        o_own.append(o_chunk)
        o_moving.append(Exchange(near, far_blocks, n_head))
        if c < CHUNKS - 1:
            x_far = beside[-1]
        if c == 0:
            out_far = {e: (v, swap(v, "batch", 1, n_batch)) for e, v in beside[0].items()}
        else:
            o_first = o_moving[0].finish(beside[0])
            cot_blocks = cot_moving.finish(beside[1])
            out_far = beside[2]

    out_far = {
        e: jnp.where(
            bit == 0, jnp.concatenate([v, w], axis=1), jnp.concatenate([w, v], axis=1)
        )
        for e, (v, w) in out_far.items()
    }
    out_far[0] = w_out
    out_pieces = gather_near(out_far, n_head)

    state, joined, h_far, h_fars = [], [], None, []
    o_came = o_first
    for c in chunks:
        o_pieces = [o_own[c]] + o_came
        beside = [h_far, o_moving[c + 1].flying if c < CHUNKS - 1 else None]
        (joined, y, x_rows, h_one, h_low), beside = order.run(
            lambda first: project(
                c,
                joined,
                [first] + o_pieces[1:],
                out_pieces,
                x_pieces[c],
                attn_alpha,
                info,
                chunk_len,
            ),
            o_pieces[0],
            need=o_pieces[1:] + out_pieces,
            beside=beside,
        )
        joined = [joined]
        if c < CHUNKS - 1:
            o_came = o_moving[c + 1].finish(beside[1])
        if c:
            h_fars = [beside[0]]
        state.append((y, x_rows, h_one))
        h_far = gather_far(h_low, n_head)
    cot_pieces = [cot_own] + cot_blocks

    fed, raws, z_terms, sent = [], [], None, None
    for c in chunks:
        h_pieces = gather_near(h_fars[c] if c < len(h_fars) else h_far, n_head)
        beside = [h_far if c < CHUNKS - 1 else None, z_terms]
        (kept, raw, z_even, z_odd), (h_next, z_done) = order.run(
            lambda first: feed(
                [first] + h_pieces[1:], w_up, w_gate, w_down, up_scale, gate_scale
            ),
            h_pieces[0],
            need=h_pieces[1:] + [sent],
            beside=beside,
        )
        if c < CHUNKS - 1:
            h_far = h_next
        fed.append(kept)
        raws.append(raw)
        z_near = reduce_near(z_odd, n_head)
        if c < CHUNKS - 1:
            z_terms, sent = reduce_far(z_even, z_near, n_head)

    two = []

    def mid_step(c, terms, beside, need=()):
        nonlocal two
        (two, dz, direct, alpha_sum), beside = order.run(
            lambda first: middle(
                c, two, [first] + terms[1:], cot_pieces, state[c][2], ffn_alpha, info
            ),
            terms[0],
            need=terms[1:] + list(need),
            beside=beside,
        )
        return dz, direct, alpha_sum, beside

    def unfeed_step(c, dz_pieces, beside, need=()):
        return order.run(
            lambda first: unfeed(
                [first] + dz_pieces[1:],
                *raws[c],
                w_up,
                w_gate,
                w_down,
                up_scale,
                gate_scale,
                n_head,
            ),
            dz_pieces[0],
            need=dz_pieces[1:] + list(need),
            beside=beside,
        )

    dz, direct, alpha_sum, z_near = mid_step(0, z_done, z_near)
    directs, ffn_alphas = [direct], [alpha_sum]
    dz_far = gather_far(dz, n_head)
    z_even = [z_even[0]] + [after(p, dz_far[far]) for p in z_even[1:]]
    z_terms, sent = reduce_far(z_even, z_near, n_head)
    dz_pieces = gather_near(dz_far, n_head)
    (low_first, scales_first, dh_even, dh_odd, dz_first), z_terms = unfeed_step(
        0, dz_pieces, z_terms, need=[sent]
    )
    dh_near = reduce_near(dh_odd, n_head)
    dz, direct, alpha_sum, dh_near = mid_step(1, z_terms, dh_near)
    directs.append(direct)
    ffn_alphas.append(alpha_sum)
    dz_far = gather_far(dz, n_head)
    firsts, dz_far = order.run(
        lambda v: weigh_feed(v, fed[0][1], dz_first, *low_first), fed[0][0], beside=dz_far
    )
    dz_pieces = gather_near(dz_far, n_head)
    dh_even = [dh_even[0]] + [after(p, dz_far[far]) for p in dh_even[1:]]
    dh_terms, sent = reduce_far(dh_even, dh_near, n_head)
    dz_last, _ = order.run(
        lambda first: join([first] + dz_pieces[1:]), dz_pieces[0], need=dz_pieces[1:] + [sent]
    )
    grad_down, _ = order.run(
        lambda v: (firsts[0] + dot(fed[1][0], v, 0, 0)).astype(BF16), dz_last
    )
    sum_down = BatchSum(grad_down, n_batch)
    (low_last, scales_last, dh_even, dh_odd, _), dh_terms = unfeed_step(
        1, [dz_last], dh_terms, need=[sum_down.sent]
    )
    scale_sums = [jnp.concatenate(s, axis=0) for s in (scales_first, scales_last)]
    dh_near = reduce_near(dh_odd, n_head)

    zeros, alphas, dys = [], [], []

    def back(c, terms, beside, need=()):
        y, x_rows, _ = state[c]
        (dy, d_pieces, zero, grad_alpha_attn), beside = order.run(
            lambda first: unproject(
                c, dys, [first] + terms[1:], out_pieces, directs[c], y, x_rows, attn_alpha
            ),
            terms[0],
            need=terms[1:] + list(need),
            beside=beside,
        )
        dys[:] = [dy]
        zeros.append(zero)
        alphas.append(grad_alpha_attn)
        return d_pieces[0], Exchange(d_pieces[1], d_pieces[2], n_head), beside

    def beside_sums(step, value, sums, beside=(), need=()):
        out, (got, beside) = order.run(
            step, value, need=need, beside=([b.flying for b in sums], beside)
        )
        for b, v in zip(sums, got, strict=True):
            b.advance(v)
        return out, beside

    grad_up, dh_near = beside_sums(
        lambda v: (firsts[1] + dot(fed[1][1], v, 0, 0)).astype(BF16),
        low_last[0],
        [sum_down],
        dh_near,
    )
    sum_up = BatchSum(grad_up, n_batch)
    dh_first, (dh_terms, sent) = dh_terms, reduce_far(dh_even, dh_near, n_head)
    grad_gate, _ = order.run(
        lambda v: (firsts[2] + dot(fed[1][1], v, 0, 0)).astype(BF16),
        low_last[1],
        need=[sent, sum_down.sent, sum_up.sent],
    )
    do_own, do_first, (dh_terms, got) = back(0, dh_first, (dh_terms, sum_down.flying))
    sum_down.advance(got)
    do_pieces = [do_own]
    do_own, do_last, do_came = back(1, dh_terms, do_first.flying, need=[sum_down.sent])
    do_pieces += do_first.finish(do_came)
    out_terms, do_came = beside_sums(
        lambda o: dot(o, dys[0], 0, 0).astype(BF16),
        joined[0],
        [sum_down, sum_up],
        do_last.flying,
    )
    sum_gate = BatchSum(after(grad_gate, order.last), n_batch)
    do_pieces += [do_own] + do_last.finish(do_came)
    alpha_sums = jnp.concatenate([sum(alphas), sum(ffn_alphas)], axis=0)
    alpha_rows = jnp.pad(alpha_sums.astype(BF16), ((0, 14), (0, 0)))
    out_blocks = [
        jnp.concatenate([out_terms[e * cols : (e + 1) * cols], alpha_rows], axis=0)
        for e in range(n_head)
    ]
    out_near = reduce_near(out_blocks[1::2], n_head)
    d_all, gains = [], []

    def attention_back(g, sums, beside, need=()):
        (d_pair, grad_gain), beside = beside_sums(
            lambda first: unattend(
                g, [first] + do_pieces[1:], buffers, starts, cosine, sine, gain, info, n_head
            ),
            do_pieces[0],
            sums,
            beside,
            need=do_pieces[1:] + list(need),
        )
        d_pair = d_pair.reshape(3 * pair, row_len)
        d_all.append(d_pair)
        gains.append(grad_gain[:, 0])
        return d_pair, beside

    big = [sum_down, sum_up, sum_gate]
    grads = []
    if pairs > 1:
        d_pair, out_near = attention_back(
            0, [sum_down, sum_up], out_near, need=[b.sent for b in big]
        )
        out_flying, out_sent = reduce_far(out_blocks[::2], out_near, n_head)
        grad_pair, _ = beside_sums(
            lambda d: weigh(d, x_pieces, chunk_len),
            d_pair,
            [sum_gate],
            need=[sum_down.sent, sum_up.sent, out_sent],
        )
        grads.append(grad_pair)
    else:
        out_flying, _ = reduce_far(out_blocks[::2], out_near, n_head)
    ahead = [BatchSum(g, n_batch) for g in grads] if n_batch == 8 else []
    d_pair, out_flying = attention_back(
        pairs - 1, big + ahead, out_flying, need=[sum_gate.sent] + [b.sent for b in ahead]
    )
    out_sum = term_sum(out_flying)
    grad_pair, _ = order.run(
        lambda d: weigh(d, x_pieces, chunk_len), d_pair, need=[sum_down.sent, sum_up.sent, sum_gate.sent]
    )
    small = jnp.concatenate(
        [out_sum[cols : cols + 2]]
        + [
            jnp.pad(v, ((0, 0), (0, model - v.shape[1])))
            for v in (sum(scale_sums), jnp.concatenate(gains)[None])
        ],
        axis=0,
    )
    small = jnp.pad(small, ((0, -(4 * cols + 5) % (16 * n_batch)), (0, 0)))
    if ahead:
        grads = []
    grads += [grad_pair, out_sum[:cols].astype(BF16), small.astype(BF16)]
    grads = jnp.concatenate(grads, axis=0)
    ranges = [2 * b.values.shape[0] for b in ahead] + [grads.shape[0]]
    sum_attn = BatchSum(grads, n_batch, direct=True, before=[b.values for b in ahead])

    def spread_step(c, sums, beside=(), need=()):
        return beside_sums(
            lambda w: spread(c, chunk_len, d_all, w, zeros[c], info, n_head),
            w_t,
            sums,
            beside,
            need=need,
        )

    def land(sums, beside=()):
        got, beside = lax.optimization_barrier(([b.flying for b in sums], beside))
        for i, (b, v) in enumerate(zip(sums, got, strict=True)):
            b.advance(after(v, sums[0].sent) if i else v)
        return jax.tree.map(lambda v: after(v, sums[0].sent), beside)

    two_moving = Exchange(after(two[1], order.last), after(two[2], order.last), n_head)
    d_first, two_came = spread_step(
        0, [sum_up, sum_gate, sum_down], two_moving.flying, need=[sum_attn.sent]
    )
    two_pieces = two_moving.finish(two_came)
    dx_near = reduce_near(d_first[-1], n_head)
    d_last, dx_near = spread_step(
        1, [sum_attn, sum_up, sum_gate], dx_near, need=[sum_up.sent, sum_gate.sent]
    )
    dx_first, _ = reduce_far(d_first[:-1], dx_near, n_head)
    down_done = assemble(sum_down.finish(), place)
    land([sum_attn, sum_up, sum_gate])
    dx_first = land([sum_attn, sum_gate], dx_first)
    dx_near = reduce_near(after(d_last[-1], sum_attn.sent), n_head)
    dx_last, _ = reduce_far(d_last[:-1], dx_near, n_head)
    while len(sum_attn.todo) > 1:
        land([sum_attn])
    hidden_out = settle(two[0], two_pieces, info)
    grad_down = down_done
    grad_up = assemble(sum_up.finish(), place)
    grad_gate = assemble(sum_gate.finish(), place)
    grad_query, grad_key, grad_value, grad_out, small = assemble_turned(
        sum_attn.finish(), place, info, cols, n_head, pairs, ranges
    )
    grad_hidden = jnp.concatenate([term_sum(dx_first), term_sum(dx_last)], axis=0)[None]
    alpha_own = lax.dynamic_slice_in_dim(small[:2], me * share, share, 1)
    hidden_units = w_up.shape[1]

    return (
        hidden_out[None],
        grad_hidden,
        grad_query,
        grad_key,
        grad_value,
        grad_out,
        grad_up,
        grad_gate,
        grad_down,
        small[4, :cols],
        small[2, :hidden_units],
        small[3, :hidden_units],
        alpha_own[0],
        alpha_own[1],
    )


def solution(mesh):
    split = P("batch", None, "head")
    by_col, by_row, by_head = P(None, "head"), P("head", None), P("head")
    return jax.shard_map(
        functools.partial(on_device, mesh.shape["batch"], mesh.shape["head"]),
        mesh=mesh,
        in_specs=(split, split, P("batch", None), P("batch"))
        + (by_col, by_col, by_col, by_row, by_col, by_col, by_row)
        + (by_head, by_head, by_head, P(), P()),
        out_specs=(split, split, by_col, by_col, by_col, by_row, by_col, by_col, by_row)
        + (by_head,) * 5,
        check_vma=False,
    )
```

```python
import functools
import math

import jax
import jax.numpy as jnp
from jax import lax
from jax.experimental import pallas as pl
from jax.experimental.pallas import tpu as pltpu
from jax.sharding import PartitionSpec as P

HD = 64
HALF = HD // 2
VALUE_ROWS = 80
EPSILON = 1e-06
BLOCK = 256
QUERIES = 512
KEYS = 512
CHUNKS = 2
F32 = jnp.float32
BF16 = jnp.bfloat16
MIB = 1024 * 1024


def dot(left, right, left_dim=1, right_dim=0):
    return lax.dot_general(
        left, right, (((left_dim,), (right_dim,)), ((), ())), preferred_element_type=F32
    )


def shape(dims, dtype):
    return jax.ShapeDtypeStruct(dims, dtype)


def kept_shape(dims, dtype):
    return pltpu.HBM(dims, dtype)


def held(array):
    return pltpu.with_memory_space_constraint(array, pltpu.HBM)


def after(value, *others):
    others = [o for o in others if o is not None]
    return lax.optimization_barrier((value, *others))[0] if others else value


def whole(dims):
    return pl.BlockSpec(dims, lambda *_: (0,) * len(dims))


def term_spec(term):
    if term.ndim == 3:
        return pl.BlockSpec((None, *term.shape[1:]), lambda *_: (0, 0, 0))
    return whole(term.shape)


def params(mib):
    return pltpu.CompilerParams(vmem_limit_bytes=mib * MIB)


def cost(flops, moved):
    return pl.CostEstimate(flops=int(flops), bytes_accessed=int(moved), transcendentals=0)


class Order:
    def __init__(self):
        self.last = None

    def run(self, step, value, need=(), beside=()):
        out = step(after(value, self.last, *need))
        out, beside = lax.optimization_barrier((out, beside))
        self.last = jax.tree.leaves(out)[0]
        return out, beside


def swap(value, axis, mask, size):
    return lax.ppermute(value, axis, [(i, i ^ mask) for i in range(size)])


def gather_far(own, size):
    pieces = {0: own}
    bit = size // 2
    while bit > 1:
        pieces.update({e | bit: swap(p, "head", bit, size) for e, p in pieces.items()})
        bit //= 2
    return pieces


def gather_near(far, size):
    pieces = dict(far)
    pieces.update({e | 1: swap(p, "head", 1, size) for e, p in far.items()})
    return [pieces[e] for e in range(size)]


class Exchange:
    def __init__(self, near, far, size):
        self.size = size
        if size == 4:
            self.flying = [swap(near, "head", 1, size), swap(far, "head", 2, size)]
        else:
            blocks = [near, *far]
            self.flying = [swap(p, "head", e, size) for e, p in enumerate(blocks, 1)]

    def finish(self, flying):
        if self.size != 4:
            return flying
        near, far = flying
        return [near, far[0], swap(far[1], "head", 1, self.size)]


def total(terms):
    if len(terms) == 1:
        return terms[0]
    return sum(t.astype(F32) for t in terms).astype(BF16)


def reduce_near(odd, size):
    return jax.tree.map(lambda p: swap(p, "head", 1, size), odd)


def reduce_far(even, near, size):
    held = {2 * i: [p, near[i]] for i, p in enumerate(even)}
    bit, sent = 2, None
    while bit < size:
        for e in [e for e in held if e & bit]:
            sent = total(held.pop(e))
            got = swap(sent, "head", bit, size)
            held[e ^ bit].append(got)
        bit *= 2
    return held[0], sent


def term_sum(terms):
    return sum((t[0] if t.ndim == 3 else t).astype(F32) for t in terms)


def sum_small(value, axis, size):
    bit = 1
    while bit < size:
        value = value + swap(value, axis, bit, size)
        bit *= 2
    return value


def halve(values, bit, place):
    rows = values.shape[0] // 2
    own = (place & bit) // bit
    return tuple(
        lax.dynamic_slice_in_dim(values, part * rows, rows, 0) for part in (own, 1 - own)
    )


class BatchSum:
    def __init__(self, values, size, direct=False, before=()):
        self.size = size
        self.place = lax.axis_index("batch")
        self.bits = [1 << i for i in range(size.bit_length() - 1)]
        self.todo = [("halve", b) for b in self.bits] + [("join", b) for b in reversed(self.bits)]
        if direct and size <= 8:
            self.bits = self.bits[:1] + self.bits[:0:-1]
            self.todo = [("halve", 1), ("scatter", 0), ("gather", 0), ("join", 1)]
        self.values, self.mine, self.flying, self.sent = values, None, None, None
        self.before = list(before)
        self.start()

    def start(self):
        kind, bit = self.todo[0]
        self.sent = self.values
        if kind == "halve":
            self.mine, self.sent = halve(self.values, bit, self.place)
        others = range(1, self.size // 2)
        if kind == "scatter":
            rows = self.values.shape[0] * 2 // self.size
            own = self.place // 2
            blocks = [
                lax.dynamic_slice_in_dim(self.values, (own ^ d) * rows, rows, 0)
                for d in range(self.size // 2)
            ]
            self.mine, self.sent = blocks[0], blocks[-1]
            self.flying = [swap(blocks[d], "batch", 2 * d, self.size) for d in others]
        elif kind == "gather":
            self.flying = [swap(self.values, "batch", 2 * d, self.size) for d in others]
        else:
            self.flying = swap(self.sent, "batch", bit, self.size)

    def advance(self, got):
        kind, _ = self.todo.pop(0)
        if not self.todo:
            self.parts = [self.values, got]
        elif kind == "halve":
            self.values = total([self.mine, got])
        elif kind == "scatter":
            self.values = total([self.mine] + got)
        else:
            got = got if kind == "gather" else [got]
            self.values = jnp.concatenate([self.values] + got, axis=0)
        if self.before:
            self.values = jnp.concatenate(self.before + [self.values], axis=0)
            self.before = []
        if self.todo:
            self.start()

    def finish(self):
        while self.todo:
            self.advance(self.flying)
        return self.parts, self.bits


def store_blocks(place, summed, refs, out):
    (first, _), bits = summed
    count = 1 << len(bits)
    rows = 2 * first.shape[0] // count
    for p in range(count):
        at = 0
        for level, bit in enumerate(bits):
            other = p >> (len(bits) - 1 - level) & 1
            at = at + (((place // bit) % 2) ^ other) * ((count >> (level + 1)) * rows)
        ref, row = refs[p * 2 // count], (p % (count // 2)) * rows
        out[pl.ds(pl.multiple_of(at, rows), rows), :] = ref[row : row + rows, :].astype(out.dtype)


def segments(first, count, ranges):
    half, skip = sum(ranges) // 2, 0
    found = []
    for size in ranges:
        part = size // 2
        for side in range(2):
            low, high = max(first, 0), min(first + count, part)
            if low < high:
                found.append((side * half + skip + low, low - first, high - low))
            first -= part
        skip += part
    return found


def assemble(summed, place):
    parts, _ = summed
    rows, width = parts[0].shape

    def body(place, own_ref, other_ref, out):
        store_blocks(place[0], summed, (own_ref, other_ref), out)

    return pl.pallas_call(
        body,
        grid_spec=pltpu.PrefetchScalarGridSpec(
            num_scalar_prefetch=1,
            grid=(1,),
            in_specs=[whole((rows, width))] * 2,
            out_specs=whole((2 * rows, width)),
        ),
        out_shape=shape((2 * rows, width), F32),
        compiler_params=params(24),
        cost_estimate=cost(0, rows * width * 12),
        name="assemble",
    )(place, *parts)


def assemble_turned(summed, place, info, cols, n_head, pairs, ranges):
    parts, _ = summed
    width = cols // pairs
    rows, model = parts[0].shape
    share = model // n_head

    def body(place, info, own_ref, other_ref, q_out, k_out, v_out, o_out, room):
        store_blocks(place[0], summed, (own_ref, other_ref), room)
        for g in range(pairs):
            for i, out in enumerate((q_out, k_out, v_out)):
                for row, offset, count in segments((3 * g + i) * width, width, ranges):
                    lanes = slice(g * width + offset, g * width + offset + count)
                    for e in range(n_head):
                        at = pl.ds(pl.multiple_of((info[0] ^ e) * share, share), share)
                        out[at, lanes] = room[row : row + count, e * share : (e + 1) * share].T
        for row, offset, count in segments(3 * cols, cols, ranges):
            o_out[offset : offset + count, :] = room[row : row + count, :]

    return pl.pallas_call(
        body,
        grid_spec=pltpu.PrefetchScalarGridSpec(
            num_scalar_prefetch=2,
            grid=(1,),
            in_specs=[whole((rows, model))] * 2,
            out_specs=[whole((model, cols))] * 3 + [whole((cols, model))],
            scratch_shapes=[pltpu.VMEM((2 * rows, model), F32)],
        ),
        out_shape=[shape((model, cols), F32)] * 3 + [shape((cols, model), F32)],
        compiler_params=params(32),
        cost_estimate=cost(0, cols * model * 24),
        name="assemble_turned",
    )(place, info, *parts)


def visible(first_key, first_query, starts, length, rows, cols):
    key = first_key + lax.broadcasted_iota(jnp.int32, (rows, cols), 0)
    query = first_query + lax.broadcasted_iota(jnp.int32, (rows, cols), 1)
    last = jnp.minimum(query, length - 1)
    return (key >= starts) & ((key <= last) | (key == query))


def prepare(w_query, w_key, w_value, w_out, cotangent, own, pair, n_head):
    model, cols = w_query.shape
    row_len, share = cotangent.shape
    rows = row_len // CHUNKS // n_head

    def body(own, q_ref, k_ref, v_ref, o_ref, c_ref, out, half, near, far_blocks):
        for g in range(cols // pair):
            for i, ref in enumerate((q_ref, k_ref, v_ref)):
                first = (3 * g + i) * pair
                out[first : first + pair, :] = ref[:, g * pair : (g + 1) * pair].T
        half[...] = o_ref[:, pl.ds(pl.multiple_of(own[1] * (model // 2), model // 2), model // 2)]
        for e in range(1, n_head):
            for c in range(CHUNKS):
                at = (c * n_head + (own[0] ^ e)) * rows
                block = c_ref[pl.ds(pl.multiple_of(at, rows), rows), :]
                if e == 1:
                    near[c * rows : (c + 1) * rows, :] = block
                else:
                    far_blocks[e - 2, c * rows : (c + 1) * rows, :] = block

    outs = pl.pallas_call(
        body,
        grid_spec=pltpu.PrefetchScalarGridSpec(
            num_scalar_prefetch=1,
            grid=(1,),
            in_specs=[whole((model, cols))] * 3 + [whole((cols, model)), whole((row_len, share))],
            out_specs=[
                whole((3 * cols, model)),
                whole((cols, model // 2)),
                whole((CHUNKS * rows, share)),
                whole((n_head - 2, CHUNKS * rows, share)),
            ],
        ),
        out_shape=[
            shape((3 * cols, model), BF16),
            shape((cols, model // 2), BF16),
            shape((CHUNKS * rows, share), BF16),
            shape((n_head - 2, CHUNKS * rows, share), BF16),
        ],
        compiler_params=params(24),
        cost_estimate=cost(0, 12 * cols * model),
        name="prepare",
    )(own, w_query, w_key, w_value, w_out, cotangent)
    return outs


def attend_kernel(
    chunk, n_head, heads, chunk_len, share, info, *refs
):
    refs = list(refs)
    x_refs = [refs.pop(0) for _ in range(n_head)]
    w_ref, cos_ref, sin_ref, gain_ref, start_ref = [refs.pop(0) for _ in range(5)]
    old_k, old_v = None, None
    if chunk:
        old_k, old_v = refs.pop(0), refs.pop(0)
        refs = refs[7:]
    k_ref, ve_ref, v_ref, kt_ref, qt_ref, ot_ref, inv_ref, qf_ref, kf_ref, o_ref = refs[:10]
    near_ref, far_ref, raw, acc = refs[10:]
    me, length = info[0], info[1]
    cols = heads * HD
    pair = min(2, heads)
    for e in range(n_head):
        first = pl.multiple_of((me ^ e) * share, share)
        for third in range(3):
            rows = slice(third * cols, (third + 1) * cols)
            term = dot(w_ref[rows, pl.ds(first, share)], x_refs[e][...], 1, 1)
            if e == 0:
                raw[rows, :] = term
            else:
                raw[rows, :] += term

    def raw_row(part, h):
        return ((h // pair * 3 + part) * pair + h % pair) * HD

    cosine, sine = cos_ref[...], sin_ref[...]
    for h in range(heads):
        own = slice(h * HD, (h + 1) * HD)
        for part, factor_ref in ((0, qf_ref), (1, kf_ref)):
            base = raw_row(part, h)
            a, b = raw[base : base + HALF, :], raw[base + HALF : base + HD, :]
            front, back = a * cosine - b * sine, b * cosine + a * sine
            mean = jnp.sum(front * front + back * back, axis=0, keepdims=True) / HD
            factor = lax.rsqrt(mean + EPSILON)
            factor_ref[h] = factor
            unit = jnp.concatenate([front, back], axis=0) * factor
            low = (unit * gain_ref[own, :]).astype(BF16)
            if part == 0:
                qt_ref[own, :] = low * BF16(1.0 / math.sqrt(HD))
            else:
                kt_ref[own, :] = low
                k_ref[h] = low.T
        value = raw[raw_row(2, h) : raw_row(2, h) + HD, :].astype(BF16)
        v_ref[h] = value.T
        ve_ref[h, :HD, :] = value
        ve_ref[h, HD:, :] = jnp.ones((VALUE_ROWS - HD, chunk_len), BF16)

    before = chunk * (chunk_len // KEYS)

    def step(local, key_first, k_of, v_of, starts):
        query = slice(local * QUERIES, (local + 1) * QUERIES)
        first = chunk * chunk_len + local * QUERIES
        mask = visible(key_first, first, starts, length, KEYS, QUERIES)
        for h in range(heads):
            scores = dot(k_of(h), qt_ref[h * HD : (h + 1) * HD, query])
            probs = jnp.where(mask, jnp.exp(scores), 0.0).astype(BF16)
            acc[h] += dot(v_of(h), probs)

    for local in range(chunk_len // QUERIES):
        query = slice(local * QUERIES, (local + 1) * QUERIES)
        starts = start_ref[:, query]
        lowest = info[2 + (chunk * chunk_len + local * QUERIES) // BLOCK] * BLOCK // KEYS
        acc[...] = jnp.zeros_like(acc)
        if chunk:

            @pl.loop(lowest, before)
            def _(kb):
                at = pl.ds(pl.multiple_of(kb * KEYS, KEYS), KEYS)
                step(
                    local, kb * KEYS, lambda h: old_k[h, at, :], lambda h: old_v[h, :, at], starts
                )

        @pl.loop(jnp.maximum(lowest - before, 0), (local + 1) * QUERIES // KEYS)
        def _(kb):
            at = pl.ds(pl.multiple_of(kb * KEYS, KEYS), KEYS)
            step(
                local,
                (before + kb) * KEYS,
                lambda h: k_ref[h, at, :],
                lambda h: ve_ref[h, :, at],
                starts,
            )

        for h in range(heads):
            inverse = 1.0 / acc[h, HD : HD + 1, :]
            inv_ref[h, :, query] = inverse
            out = acc[h, :HD, :] * inverse
            ot_ref[h * HD : (h + 1) * HD, query] = out.astype(BF16)
            o_ref[query, h * HD : (h + 1) * HD] = out.T.astype(BF16)
    rows = chunk_len // n_head
    for e in range(1, n_head):
        block = o_ref[pl.ds(pl.multiple_of((me ^ e) * rows, rows), rows), :]
        if e == 1:
            near_ref[...] = block
        else:
            far_ref[e - 2] = block


def attend_chunk(
    chunk, x_pieces, w_t, cosine, sine, gain, starts, info, buffers, row_len, chunk_len
):
    n_head = len(x_pieces)
    share = x_pieces[0].shape[1]
    cols = w_t.shape[0] // 3
    heads = cols // HD
    model = w_t.shape[1]
    body = functools.partial(attend_kernel, chunk, n_head, heads, chunk_len, share)
    by_lane = lambda rows: pl.BlockSpec((rows, chunk_len), lambda i, info: (0, chunk))
    specs = [whole((chunk_len, share))] * n_head + [
        whole((3 * cols, model)),
        by_lane(HALF),
        by_lane(HALF),
        whole((cols, 1)),
        by_lane(1),
    ]
    operands = [*x_pieces, w_t, cosine, sine, gain, starts]
    aliases = {}
    if chunk:
        aliases = {1 + len(operands) + i: i for i in range(9)}
        specs += [whole((heads, row_len, HD)), whole((heads, VALUE_ROWS, row_len))]
        specs += [pl.BlockSpec(memory_space=pl.ANY)] * 7
        operands += buffers
    lane3 = lambda rows: pl.BlockSpec((heads, rows, chunk_len), lambda i, info: (0, 0, chunk))
    row3 = pl.BlockSpec((heads, chunk_len, HD), lambda i, info: (0, chunk, 0))
    outs = pl.pallas_call(
        body,
        grid_spec=pltpu.PrefetchScalarGridSpec(
            num_scalar_prefetch=1,
            grid=(1,),
            in_specs=specs,
            out_specs=[
                row3,
                lane3(VALUE_ROWS),
                row3,
                by_lane(cols),
                by_lane(cols),
                by_lane(cols),
                lane3(1),
                lane3(1),
                lane3(1),
                whole((chunk_len, cols)),
            ]
            + [
                whole((chunk_len // n_head, cols)),
                whole((n_head - 2, chunk_len // n_head, cols)),
            ],
            scratch_shapes=[
                pltpu.VMEM((3 * cols, chunk_len), F32),
                pltpu.VMEM((heads, VALUE_ROWS, QUERIES), F32),
            ],
        ),
        out_shape=[
            kept_shape((heads, row_len, HD), BF16),
            kept_shape((heads, VALUE_ROWS, row_len), BF16),
            kept_shape((heads, row_len, HD), BF16),
            kept_shape((cols, row_len), BF16),
            kept_shape((cols, row_len), BF16),
            kept_shape((cols, row_len), BF16),
            kept_shape((heads, 1, row_len), F32),
            kept_shape((heads, 1, row_len), F32),
            kept_shape((heads, 1, row_len), F32),
            kept_shape((chunk_len, cols), BF16),
        ]
        + [
            kept_shape((chunk_len // n_head, cols), BF16),
            kept_shape((n_head - 2, chunk_len // n_head, cols), BF16),
        ],
        input_output_aliases=aliases,
        compiler_params=params(40),
        cost_estimate=cost(16e9 / CHUNKS, 8e6),
        name="attend",
    )(info, *operands)
    return outs[:9], list(outs[9:])


def unattend_kernel(n_head, chunks, row_len, piece, pair, info, *refs):
    refs = list(refs)
    d_refs = [refs.pop(0) for _ in range(chunks * n_head)]
    k_ref, v_ref, kt_ref, qt_ref, ot_ref, inv_ref, qf_ref, kf_ref = [refs.pop(0) for _ in range(8)]
    start_ref, cos_ref, sin_ref, gain_ref = [refs.pop(0) for _ in range(4)]
    out_ref, gain_out, do_s, inner_s, dq_s, dk_s, dv_s = refs
    me, length = info[0], info[1]
    for c in range(chunks):
        for e in range(n_head):
            first = c * n_head * piece + (me ^ e) * piece
            do_s[:, pl.ds(pl.multiple_of(first, piece), piece)] = d_refs[c * n_head + e][...]
    for h in range(pair):
        own = slice(h * HD, (h + 1) * HD)
        product = do_s[own, :].astype(F32) * ot_ref[own, :].astype(F32)
        inner_s[h] = jnp.sum(product, axis=0, keepdims=True)
    dq_s[...] = jnp.zeros_like(dq_s)
    dk_s[...] = jnp.zeros_like(dk_s)
    dv_s[...] = jnp.zeros_like(dv_s)

    ratio = QUERIES // BLOCK

    @pl.loop(0, row_len // QUERIES)
    def _(qb):
        query = pl.ds(pl.multiple_of(qb * QUERIES, QUERIES), QUERIES)
        starts = start_ref[:, query]

        @pl.loop(info[2 + qb * ratio], (qb + 1) * ratio)
        def _(kb):
            key = pl.ds(pl.multiple_of(kb * BLOCK, BLOCK), BLOCK)
            mask = visible(kb * BLOCK, qb * QUERIES, starts, length, BLOCK, QUERIES)
            for h in range(pair):
                own = slice(h * HD, (h + 1) * HD)
                q_block, do_block = qt_ref[own, query], do_s[own, query]
                scores = dot(k_ref[h, key, :], q_block)
                probs = jnp.where(mask, jnp.exp(scores), 0.0) * inv_ref[h, :, query]
                d_probs = dot(v_ref[h, key, :], do_block)
                d_scores = (probs * (d_probs - inner_s[h, :, query])).astype(BF16)
                dv_s[own, key] += dot(do_block, probs.astype(BF16), 1, 1)
                dk_s[own, key] += dot(q_block, d_scores, 1, 1)
                dq_s[own, query] += dot(kt_ref[own, key], d_scores)

    for h in range(pair):
        own = slice(h * HD, (h + 1) * HD)
        gain = gain_ref[own, :]
        summed = jnp.zeros((HD, 1), F32)
        for part, low_ref, grad_ref, factor_ref in (
            (0, qt_ref, dq_s, qf_ref),
            (1, kt_ref, dk_s, kf_ref),
        ):
            scale = math.sqrt(HD) if part == 0 else 1.0
            unit = low_ref[own, :].astype(F32) * (scale / gain)
            grad = grad_ref[own, :]
            if part == 0:
                grad = grad * (1.0 / math.sqrt(HD))
            summed += jnp.sum(grad * unit, axis=1, keepdims=True)
            grad = grad * gain
            mean = jnp.sum(grad * unit, axis=0, keepdims=True) / HD
            grad = (grad - unit * mean) * factor_ref[h]
            front, back = grad[:HALF], grad[HALF:]
            cosine, sine = cos_ref[...], sin_ref[...]
            out_ref[part, h * HD : h * HD + HALF, :] = (front * cosine + back * sine).astype(BF16)
            out_ref[part, h * HD + HALF : (h + 1) * HD, :] = (
                back * cosine - front * sine
            ).astype(BF16)
        out_ref[2, own, :] = dv_s[own, :].astype(BF16)
        gain_out[own, :] = summed


def unattend(index, do_pieces, buffers, starts, cosine, sine, gain, info, n_head):
    k, _, v, kt, qt, ot, inv, qf, kf = buffers
    chunks = len(do_pieces) // n_head
    cols, piece = do_pieces[0].shape
    heads, row_len, _ = k.shape
    pair = min(2, heads)
    rows = pair * HD
    by_rows = lambda width: pl.BlockSpec((rows, width), lambda g, info: (index, 0))
    by_head = lambda a, b: pl.BlockSpec((pair, a, b), lambda g, info: (index, 0, 0))
    return pl.pallas_call(
        functools.partial(unattend_kernel, n_head, chunks, row_len, piece, pair),
        grid_spec=pltpu.PrefetchScalarGridSpec(
            num_scalar_prefetch=1,
            grid=(1,),
            in_specs=[by_rows(piece)] * (chunks * n_head)
            + [by_head(row_len, HD)] * 2
            + [by_rows(row_len)] * 3
            + [by_head(1, row_len)] * 3
            + [whole((1, row_len)), whole((HALF, row_len)), whole((HALF, row_len)), by_rows(1)],
            out_specs=[whole((3, rows, row_len)), whole((rows, 1))],
            scratch_shapes=[
                pltpu.VMEM((rows, row_len), BF16),
                pltpu.VMEM((pair, 1, row_len), F32),
                pltpu.VMEM((rows, row_len), F32),
                pltpu.VMEM((rows, row_len), F32),
                pltpu.VMEM((rows, row_len), F32),
            ],
        ),
        out_shape=[kept_shape((3, rows, row_len), BF16), shape((rows, 1), F32)],
        compiler_params=params(32),
        cost_estimate=cost(22e9, 6e6),
        name="unattend",
    )(info, *do_pieces, k, v, kt, qt, ot, inv, qf, kf, starts, cosine, sine, gain)


def norm(values):
    factor = lax.rsqrt(jnp.mean(values * values, axis=-1, keepdims=True) + EPSILON)
    return values * factor, factor


def norm_back(grad, unit, factor):
    return factor * (grad - unit * jnp.mean(grad * unit, axis=-1, keepdims=True))


def project_kernel(n_head, share, kept, info, *refs):
    o_refs, w_refs = refs[:n_head], refs[n_head : 2 * n_head]
    x_refs = refs[2 * n_head : 3 * n_head]
    alpha_ref = refs[3 * n_head]
    cat_ref, y_ref, x_ref, h_ref, low_ref = refs[3 * n_head + 1 + kept :]
    me = info[0]
    cols = w_refs[0].shape[0]
    y = dot(o_refs[0][...], w_refs[0][...])
    for e in range(1, n_head):
        y += dot(o_refs[e][...], w_refs[e][...])
    for e in range(n_head):
        cat_ref[:, e * cols : (e + 1) * cols] = o_refs[e][...]
    for e in range(n_head):
        first = pl.multiple_of((me ^ e) * share, share)
        x_ref[:, pl.ds(first, share)] = x_refs[e][...]
    y_ref[...] = y
    h_zero = x_ref[...].astype(F32)
    h_one, _ = norm(h_zero + alpha_ref[...] * (norm(y)[0] - h_zero))
    h_ref[...] = h_one
    low_ref[...] = h_one.astype(BF16)


def project(chunk, kept, o_pieces, w_pieces, x_pieces, alpha, info, chunk_len):
    n_head = len(o_pieces)
    cols, model = w_pieces[0].shape
    share = x_pieces[0].shape[1]
    rows = chunk_len // n_head
    mine = lambda width: pl.BlockSpec((rows, width), lambda i, info: (info[0], 0))
    return pl.pallas_call(
        functools.partial(project_kernel, n_head, share, len(kept)),
        grid_spec=pltpu.PrefetchScalarGridSpec(
            num_scalar_prefetch=1,
            grid=(1,),
            in_specs=[mine(cols)]
            + [whole((rows, cols))] * (n_head - 1)
            + [whole((cols, model))] * n_head
            + [mine(share)] * n_head
            + [whole((1, model))]
            + [pl.BlockSpec(memory_space=pl.ANY)] * len(kept),
            out_specs=[pl.BlockSpec((rows, n_head * cols), lambda i, info: (chunk, 0))]
            + [whole((rows, model))] * 4,
        ),
        input_output_aliases={3 * n_head + 2 + i: i for i in range(len(kept))},
        out_shape=[
            kept_shape((CHUNKS * rows, n_head * cols), BF16),
            kept_shape((rows, model), F32),
            kept_shape((rows, model), BF16),
            kept_shape((rows, model), F32),
            shape((rows, model), BF16),
        ],
        compiler_params=params(32),
        cost_estimate=cost(2.0 * rows * model * model, 6e6),
        name="project",
    )(info, *o_pieces, *w_pieces, *x_pieces, alpha, *kept)


def feed_kernel(n_head, rows, *refs):
    h_refs = refs[:n_head]
    up_ref, gate_ref, down_hbm, su_ref, sg_ref = refs[n_head : n_head + 5]
    m_ref, cat_hbm, u_ref, g_ref = refs[n_head + 5 : n_head + 9]
    z_refs = refs[n_head + 9 : 2 * n_head + 9]
    cat, mixed_s, down, cat_sem, down_sem = refs[2 * n_head + 9 :]
    tile = pl.program_id(0)
    keep = pltpu.make_async_copy(cat, cat_hbm, cat_sem)
    fetch = pltpu.make_async_copy(down_hbm, down, down_sem)

    @pl.when(tile == 0)
    def _():
        fetch.start()
        for e in range(n_head):
            cat[e * rows : (e + 1) * rows, :] = h_refs[e][...]
        keep.start()

    up_raw = dot(cat[...], up_ref[...])
    gate_raw = dot(cat[...], gate_ref[...])
    u_ref[...] = up_raw.astype(BF16)
    g_ref[...] = gate_raw.astype(BF16)
    gate = gate_raw * sg_ref[...]
    mixed = (up_raw * su_ref[...] * (gate * jax.nn.sigmoid(gate))).astype(BF16)
    m_ref[...] = mixed
    width = m_ref.shape[1]
    mixed_s[:, pl.ds(pl.multiple_of(tile * width, width), width)] = mixed

    @pl.when(tile == pl.num_programs(0) - 1)
    def _():
        fetch.wait()
        z = dot(mixed_s[...], down[...])
        for e in range(n_head):
            z_refs[e][...] = z[e * rows : (e + 1) * rows, :].astype(BF16)
        keep.wait()


def feed(h_pieces, w_up, w_gate, w_down, scale_up, scale_gate):
    n_head = len(h_pieces)
    rows, model = h_pieces[0].shape
    hidden = w_up.shape[1]
    tile = min(256, hidden // 2)
    count = n_head * rows
    by_col = lambda height: pl.BlockSpec((height, tile), lambda n: (0, n))
    anywhere = pl.BlockSpec(memory_space=pl.ANY)
    outs = pl.pallas_call(
        functools.partial(feed_kernel, n_head, rows),
        grid=(hidden // tile,),
        in_specs=[whole((rows, model))] * n_head
        + [by_col(model), by_col(model), anywhere, by_col(1), by_col(1)],
        out_specs=[by_col(count), anywhere, by_col(count), by_col(count)]
        + [whole((rows, model))] * n_head,
        out_shape=[
            kept_shape((count, hidden), BF16),
            kept_shape((count, model), BF16),
            kept_shape((count, hidden), BF16),
            kept_shape((count, hidden), BF16),
        ]
        + [shape((rows, model), BF16)] * n_head,
        scratch_shapes=[
            pltpu.VMEM((count, model), BF16),
            pltpu.VMEM((count, hidden), BF16),
            pltpu.VMEM((hidden, model), BF16),
            pltpu.SemaphoreType.DMA,
            pltpu.SemaphoreType.DMA,
        ],
        compiler_params=params(48),
        cost_estimate=cost(6.0 * count * model * hidden, 20e6),
        name="feed",
    )(*h_pieces, w_up, w_gate, held(w_down), scale_up, scale_gate)
    return outs[:2], outs[2:4], list(outs[4::2]), list(outs[5::2])


def middle_kernel(n_head, n_terms, share, kept, info, *refs):
    z_refs, c_refs = refs[:n_terms], refs[n_terms : n_terms + n_head]
    h_ref, alpha_ref = refs[n_terms + n_head : n_terms + n_head + 2]
    refs = refs[n_terms + n_head + 2 + kept :]
    own_ref, near_ref, far_ref, dz_ref, direct_ref, grad_ref, two_s, cot_s = refs
    me = info[0]
    step = pl.program_id(0)
    z = z_refs[0][...].astype(F32)
    for r in z_refs[1:]:
        z += r[...].astype(F32)
    h_one, alpha = h_ref[...], alpha_ref[...]
    h_ffn, z_factor = norm(z)
    h_two, factor = norm(h_one + alpha * (h_ffn - h_one))
    two_s[...] = h_two.astype(BF16)
    for e in range(n_head):
        at = pl.ds(pl.multiple_of((me ^ e) * share, share), share)
        if e < 2:
            (own_ref, near_ref)[e][...] = two_s[:, at]
        else:
            far_ref[e - 2] = two_s[:, at]
        cot_s[:, at] = c_refs[e][...]
    grad = norm_back(cot_s[...].astype(F32), h_two, factor)
    summed = jnp.sum(grad * (h_ffn - h_one), axis=0, keepdims=True)

    @pl.when(step == 0)
    def _():
        grad_ref[...] = summed

    @pl.when(step > 0)
    def _():
        grad_ref[...] += summed

    direct_ref[...] = grad * (1.0 - alpha)
    dz_ref[...] = norm_back(grad * alpha, h_ffn, z_factor).astype(BF16)


def middle(chunk, kept, z_terms, cot_pieces, h_one, alpha, info):
    n_head, n_terms = len(cot_pieces), len(z_terms)
    rows, model = h_one.shape
    share = cot_pieces[0].shape[1]
    part = rows // 2
    mine = pl.BlockSpec((part, share), lambda i, info: (2 * (chunk * n_head + info[0]) + i, 0))
    theirs = pl.BlockSpec((part, share), lambda i, info: (2 * chunk + i, 0))
    by_row = pl.BlockSpec((part, model), lambda i, info: (i, 0))
    outs = pl.pallas_call(
        functools.partial(middle_kernel, n_head, n_terms, share, len(kept)),
        grid_spec=pltpu.PrefetchScalarGridSpec(
            num_scalar_prefetch=1,
            grid=(2,),
            in_specs=[by_row] * n_terms
            + [mine]
            + [theirs] * (n_head - 1)
            + [by_row, whole((1, model))]
            + [pl.BlockSpec(memory_space=pl.ANY)] * len(kept),
            out_specs=[theirs] * 2
            + [pl.BlockSpec((n_head - 2, part, share), lambda i, info: (0, 2 * chunk + i, 0))]
            + [by_row] * 2
            + [whole((1, model))],
            scratch_shapes=[pltpu.VMEM((part, model), BF16), pltpu.VMEM((part, model), BF16)],
        ),
        input_output_aliases={n_terms + n_head + 3 + i: i for i in range(len(kept))},
        out_shape=[kept_shape((CHUNKS * rows, share), BF16)] * 2
        + [kept_shape((n_head - 2, CHUNKS * rows, share), BF16)]
        + [shape((rows, model), BF16), kept_shape((rows, model), F32), shape((1, model), F32)],
        compiler_params=params(32),
        cost_estimate=cost(rows * model * 60, rows * model * 24),
        name="middle",
    )(info, *z_terms, *cot_pieces, held(h_one), alpha, *kept)
    return list(outs[:3]), *outs[3:]


def join(pieces):
    rows, width = pieces[0].shape

    def body(*refs):
        for i, ref in enumerate(refs[:-1]):
            refs[-1][i * rows : (i + 1) * rows, :] = ref[...]

    return pl.pallas_call(
        body,
        in_specs=[whole((rows, width))] * len(pieces),
        out_specs=whole((rows * len(pieces), width)),
        grid=(1,),
        out_shape=shape((rows * len(pieces), width), pieces[0].dtype),
        compiler_params=params(16),
        cost_estimate=cost(0, rows * width * 4 * len(pieces)),
        name="join",
    )(*pieces)


def weigh_feed(mixed, joined, dz, du, dg):
    count, hidden = mixed.shape
    model = joined.shape[1]
    tile = min(256, hidden // 2)

    def body(m_ref, h_ref, z_ref, u_ref, g_ref, down, up, gate):
        down[...] = dot(m_ref[...], z_ref[...], 0, 0).astype(BF16)
        up[...] = dot(h_ref[...], u_ref[...], 0, 0).astype(BF16)
        gate[...] = dot(h_ref[...], g_ref[...], 0, 0).astype(BF16)

    by_col = lambda height: pl.BlockSpec((height, tile), lambda n: (0, n))
    return pl.pallas_call(
        body,
        in_specs=[
            by_col(count),
            whole((count, model)),
            whole((count, model)),
            by_col(count),
            by_col(count),
        ],
        out_specs=[pl.BlockSpec((tile, model), lambda n: (n, 0)), by_col(model), by_col(model)],
        grid=(hidden // tile,),
        out_shape=[kept_shape((hidden, model), BF16)] + [kept_shape((model, hidden), BF16)] * 2,
        compiler_params=params(48),
        cost_estimate=cost(6.0 * count * hidden * model, 20e6),
        name="weigh_feed",
    )(mixed, joined, dz, du, dg)


def weigh(d_pair, x_pieces, chunk_len):
    rows, row_len = d_pair.shape
    n_head = len(x_pieces[0])
    share = x_pieces[0][0].shape[1]
    flat = [p for chunk in x_pieces for p in chunk]

    def body(d_ref, *refs):
        for e in range(n_head):
            term = None
            for c in range(len(x_pieces)):
                d_part = d_ref[:, c * chunk_len : (c + 1) * chunk_len]
                new = dot(d_part, refs[c * n_head + e][...])
                term = new if term is None else term + new
            refs[-1][:, e * share : (e + 1) * share] = term.astype(BF16)

    return pl.pallas_call(
        body,
        in_specs=[whole((rows, row_len))] + [whole((chunk_len, share))] * len(flat),
        out_specs=whole((rows, n_head * share)),
        grid=(1,),
        out_shape=shape((rows, n_head * share), BF16),
        compiler_params=params(32),
        cost_estimate=cost(0, 1),
        name="weigh",
    )(d_pair, *flat)


def unfeed_kernel(n_head, n_in, rows, *refs):
    d_refs, refs = refs[:n_in], refs[n_in:]
    u_ref, g_ref, up_hbm, gate_hbm, down_ref, su_ref, sg_ref = refs[:7]
    du_ref, dg_ref, gsu_ref, gsg_ref = refs[7:11]
    out_refs = refs[11 : 11 + n_head]
    cat_hbm = refs[11 + n_head] if n_in > 1 else None
    refs = refs[11 + n_head + (n_in > 1) :]
    du_s, dg_s, up, gate_w, sems = refs[:5]
    cat = refs[5] if n_in > 1 else d_refs[0]
    tile = pl.program_id(0)
    fetch_up = pltpu.make_async_copy(up_hbm, up, sems.at[0])
    fetch_gate = pltpu.make_async_copy(gate_hbm, gate_w, sems.at[1])
    keep = pltpu.make_async_copy(cat, cat_hbm, sems.at[2]) if n_in > 1 else None

    @pl.when(tile == 0)
    def _():
        fetch_up.start()
        fetch_gate.start()
        if n_in > 1:
            for e in range(n_in):
                cat[e * rows : (e + 1) * rows, :] = d_refs[e][...]
            keep.start()

    d_mixed = dot(cat[...], down_ref[...], 1, 1)
    up_raw, gate_raw = u_ref[...].astype(F32), g_ref[...].astype(F32)
    gate = gate_raw * sg_ref[...]
    sigmoid = jax.nn.sigmoid(gate)
    silu = gate * sigmoid
    d_up = d_mixed * silu
    d_gate = d_mixed * (up_raw * su_ref[...]) * (sigmoid + silu * (1.0 - sigmoid))
    gsu_ref[...] = jnp.sum(d_up * up_raw, axis=0, keepdims=True)
    gsg_ref[...] = jnp.sum(d_gate * gate_raw, axis=0, keepdims=True)
    up_low = (d_up * su_ref[...]).astype(BF16)
    gate_low = (d_gate * sg_ref[...]).astype(BF16)
    du_ref[...] = up_low
    dg_ref[...] = gate_low
    width = du_ref.shape[1]
    at = pl.ds(pl.multiple_of(tile * width, width), width)
    du_s[:, at] = up_low
    dg_s[:, at] = gate_low

    @pl.when(tile == pl.num_programs(0) - 1)
    def _():
        fetch_up.wait()
        fetch_gate.wait()
        dh = dot(du_s[...], up[...], 1, 1) + dot(dg_s[...], gate_w[...], 1, 1)
        for e in range(n_head):
            out_refs[e][...] = dh[e * rows : (e + 1) * rows, :].astype(BF16)
        if n_in > 1:
            keep.wait()


def unfeed(dz_pieces, u, g, w_up, w_gate, w_down, scale_up, scale_gate, n_head):
    n_in = len(dz_pieces)
    model = dz_pieces[0].shape[1]
    count, hidden = u.shape
    rows = count // n_head
    tile = min(256, hidden // 2)
    by_col = lambda height: pl.BlockSpec((height, tile), lambda n: (0, n))
    anywhere = pl.BlockSpec(memory_space=pl.ANY)
    outs = pl.pallas_call(
        functools.partial(unfeed_kernel, n_head, n_in, rows),
        grid=(hidden // tile,),
        in_specs=[whole(dz_pieces[0].shape)] * n_in
        + [
            by_col(count),
            by_col(count),
            anywhere,
            anywhere,
            pl.BlockSpec((tile, model), lambda n: (n, 0)),
            by_col(1),
            by_col(1),
        ],
        out_specs=[by_col(count)] * 2
        + [by_col(1), by_col(1)]
        + [whole((rows, model))] * n_head
        + [anywhere] * (n_in > 1),
        out_shape=[kept_shape((count, hidden), BF16)] * 2
        + [shape((1, hidden), F32), shape((1, hidden), F32)]
        + [shape((rows, model), BF16)] * n_head
        + [kept_shape((count, model), BF16)] * (n_in > 1),
        scratch_shapes=[
            pltpu.VMEM((count, hidden), BF16),
            pltpu.VMEM((count, hidden), BF16),
            pltpu.VMEM((model, hidden), BF16),
            pltpu.VMEM((model, hidden), BF16),
            pltpu.SemaphoreType.DMA((3,)),
        ]
        + [pltpu.VMEM((count, model), BF16)] * (n_in > 1),
        compiler_params=params(48),
        cost_estimate=cost(6.0 * count * model * hidden, 20e6),
        name="unfeed",
    )(*dz_pieces, u, g, held(w_up), held(w_gate), w_down, scale_up, scale_gate)
    pieces = outs[4 : 4 + n_head]
    return outs[:2], outs[2:4], list(pieces[::2]), list(pieces[1::2]), outs[-1]


def unproject_kernel(n_head, n_terms, kept, *refs):
    t_refs, w_refs = refs[:n_terms], refs[n_terms : n_terms + n_head]
    direct_ref, y_ref, x_ref, alpha_ref = refs[n_terms + n_head : n_terms + n_head + 4]
    refs = refs[n_terms + n_head + 4 + kept :]
    dy_ref, refs = refs[0], refs[1:]
    own_ref, near_ref, far_ref, zero_ref, grad_ref = refs
    grad = direct_ref[...]
    for r in t_refs:
        grad += r[...].astype(F32)
    alpha = alpha_ref[...]
    h_zero = x_ref[...].astype(F32)
    h_attn, y_factor = norm(y_ref[...])
    h_one, factor = norm(h_zero + alpha * (h_attn - h_zero))
    grad = norm_back(grad, h_one, factor)
    grad_ref[...] = jnp.sum(grad * (h_attn - h_zero), axis=0, keepdims=True)
    zero_ref[...] = grad * (1.0 - alpha)
    dy = norm_back(grad * alpha, h_attn, y_factor).astype(BF16)
    dy_ref[...] = dy
    for e in range(n_head):
        value = dot(w_refs[e][...], dy, 1, 1).astype(BF16)
        if e < 2:
            (own_ref, near_ref)[e][...] = value
        else:
            far_ref[e - 2] = value


def unproject(chunk, kept, terms, w_pieces, direct, y, x, alpha):
    n_head, n_terms = len(w_pieces), len(terms)
    rows, model = y.shape
    cols = w_pieces[0].shape[0]
    outs = pl.pallas_call(
        functools.partial(unproject_kernel, n_head, n_terms, len(kept)),
        grid=(1,),
        in_specs=[term_spec(t) for t in terms]
        + [whole((cols, model))] * n_head
        + [whole((rows, model))] * 3
        + [whole((1, model))]
        + [pl.BlockSpec(memory_space=pl.ANY)] * len(kept),
        out_specs=[pl.BlockSpec((rows, model), lambda i: (chunk, 0))]
        + [whole((cols, rows))] * 2
        + [whole((n_head - 2, cols, rows))]
        + [whole((rows, model)), whole((1, model))],
        input_output_aliases={n_terms + n_head + 4 + i: i for i in range(len(kept))},
        out_shape=[kept_shape((CHUNKS * rows, model), BF16)]
        + [shape((cols, rows), BF16)] * 2
        + [shape((n_head - 2, cols, rows), BF16)]
        + [kept_shape((rows, model), F32), shape((1, model), F32)],
        compiler_params=params(32),
        cost_estimate=cost(2.0 * rows * model * model, 8e6),
        name="unproject",
    )(*terms, *w_pieces, held(direct), held(y), held(x), alpha, *kept)
    return outs[0], list(outs[1:4]), outs[4], outs[5]


def spread_kernel(n_head, share, pairs, info, *refs):
    d_refs, (w_ref, direct_ref), out_refs = refs[:pairs], refs[pairs : pairs + 2], refs[pairs + 2 :]
    me = info[0]
    block = pl.program_id(0)
    d_all = jnp.concatenate([r[...] for r in d_refs], axis=0).T
    for e in range(n_head):
        at = pl.ds(pl.multiple_of((me ^ e) * share, share), share)
        term = dot(d_all, w_ref[:, at])

        ref = out_refs[n_head // 2].at[e // 2] if e % 2 else out_refs[e // 2]

        @pl.when(block == me)
        def _():
            ref[...] = (term + direct_ref[:, at]).astype(BF16)

        @pl.when(block != me)
        def _():
            ref[...] = term.astype(BF16)


def spread(chunk, chunk_len, d_all, w_t, direct, info, n_head):
    rows3, model = w_t.shape
    share = model // n_head
    rows = chunk_len // n_head
    return pl.pallas_call(
        functools.partial(spread_kernel, n_head, share, len(d_all)),
        grid_spec=pltpu.PrefetchScalarGridSpec(
            num_scalar_prefetch=1,
            grid=(n_head,),
            in_specs=[
                *[pl.BlockSpec((d.shape[0], rows), lambda i, info: (0, chunk * n_head + i)) for d in d_all],
                whole((rows3, model)),
                whole((rows, model)),
            ],
            out_specs=[pl.BlockSpec((rows, share), lambda i, info: (i, 0))] * (n_head // 2)
            + [pl.BlockSpec((n_head // 2, rows, share), lambda i, info: (0, i, 0))],
        ),
        out_shape=[shape((chunk_len, share), BF16)] * (n_head // 2)
        + [shape((n_head // 2, chunk_len, share), BF16)],
        compiler_params=params(32),
        cost_estimate=cost(2.0 * chunk_len * model * rows3, 8e6),
        name="spread",
    )(info, *d_all, w_t, direct)


def settle(own, pieces, info):
    pieces = [own] + pieces
    n_head = len(pieces)
    count, share = own.shape
    rows = count // CHUNKS

    def body(info, *refs):
        for e in range(n_head):
            for c in range(CHUNKS):
                at = (c * n_head + (info[0] ^ e)) * rows
                refs[-1][pl.ds(pl.multiple_of(at, rows), rows), :] = refs[e][
                    c * rows : (c + 1) * rows, :
                ]

    return pl.pallas_call(
        body,
        grid_spec=pltpu.PrefetchScalarGridSpec(
            num_scalar_prefetch=1,
            grid=(1,),
            in_specs=[whole((count, share))] * n_head,
            out_specs=whole((n_head * count, share)),
        ),
        out_shape=shape((n_head * count, share), BF16),
        compiler_params=params(16),
        cost_estimate=cost(0, n_head * count * share * 4),
        name="settle",
    )(info, *pieces)


def on_device(
    n_batch,
    n_head,
    hidden_in,
    cotangent,
    doc_ids,
    lengths,
    w_query,
    w_key,
    w_value,
    w_out,
    w_up,
    w_gate,
    w_down,
    scale_qk,
    scale_up,
    scale_gate,
    alpha_attn,
    alpha_ffn,
):
    _, row_len, share = hidden_in.shape
    model = share * n_head
    cols = w_query.shape[1]
    chunk_len = row_len // CHUNKS
    rows = chunk_len // n_head
    me = lax.axis_index("head")
    chunks = range(CHUNKS)
    x_own, cot_own = hidden_in[0], cotangent[0]

    docs = doc_ids[0]
    column = jnp.arange(row_len, dtype=jnp.int32)
    starts = sum(
        jnp.where(docs > d, jnp.sum((docs == d).astype(jnp.int32)), 0) for d in range(5)
    ).astype(jnp.int32)
    position = (column - starts).astype(F32)
    frequency = 10000.0 ** (-(jnp.arange(HALF, dtype=F32) * 2.0 / HD))
    angles = frequency[:, None] * position[None, :]
    cosine, sine = jnp.cos(angles), jnp.sin(angles)
    info = jnp.concatenate(
        [me[None].astype(jnp.int32), lengths.astype(jnp.int32), starts[::BLOCK] // BLOCK]
    )
    starts = starts[None, :]
    gain = scale_qk[:, None]
    up_scale, gate_scale = scale_up[None, :], scale_gate[None, :]
    attn_alpha, ffn_alpha = alpha_attn[None, :], alpha_ffn[None, :]

    def part(values, c):
        return lax.slice_in_dim(values, c * chunk_len, (c + 1) * chunk_len, axis=0)

    def block_of(values, e):
        return lax.dynamic_slice_in_dim(values, (me ^ e) * rows, rows, 0)

    order = Order()
    pair = min(2, cols // HD) * HD
    pairs = cols // pair
    far = n_head // 2
    place = lax.axis_index("batch")[None].astype(jnp.int32)

    bit = lax.axis_index("batch") % 2
    own = jnp.stack([me, bit]).astype(jnp.int32)

    x_far = gather_far(part(x_own, 0), n_head)
    (w_t, out_half, cot_near, cot_far), x_far = order.run(
        lambda w: prepare(w, w_key, w_value, w_out, cot_own, own, pair, n_head),
        w_query,
        beside=x_far,
    )
    buffers, x_pieces, o_own, o_moving = [], [], [], []
    for c in chunks:
        x_pieces.append(gather_near(x_far, n_head))
        beside = []
        if c == 0:
            halves = {
                e: swap(after(out_half, order.last), "head", e, n_head) for e in range(2, n_head, 2)
            }
            beside = [halves]
        else:
            cot_moving = Exchange(after(cot_near, order.last), after(cot_far, order.last), n_head)
            beside = [o_moving[0].flying, cot_moving.flying, out_far]
        if c < CHUNKS - 1:
            beside.append(gather_far(after(part(x_own, c + 1), order.last), n_head))
        (buffers, (o_chunk, near, far_blocks)), beside = order.run(
            lambda w: attend_chunk(
                c, x_pieces[c], w, cosine, sine, gain, starts, info, buffers, row_len, chunk_len
            ),
            w_t,
            need=x_pieces[c],
            beside=beside,
        )
        o_own.append(o_chunk)
        o_moving.append(Exchange(near, far_blocks, n_head))
        if c < CHUNKS - 1:
            x_far = beside[-1]
        if c == 0:
            out_far = {e: (v, swap(v, "batch", 1, n_batch)) for e, v in beside[0].items()}
        else:
            o_first = o_moving[0].finish(beside[0])
            cot_blocks = cot_moving.finish(beside[1])
            out_far = beside[2]

    out_far = {
        e: jnp.where(
            bit == 0, jnp.concatenate([v, w], axis=1), jnp.concatenate([w, v], axis=1)
        )
        for e, (v, w) in out_far.items()
    }
    out_far[0] = w_out
    out_pieces = gather_near(out_far, n_head)

    state, joined, h_far, h_fars = [], [], None, []
    o_came = o_first
    for c in chunks:
        o_pieces = [o_own[c]] + o_came
        beside = [h_far, o_moving[c + 1].flying if c < CHUNKS - 1 else None]
        (joined, y, x_rows, h_one, h_low), beside = order.run(
            lambda first: project(
                c,
                joined,
                [first] + o_pieces[1:],
                out_pieces,
                x_pieces[c],
                attn_alpha,
                info,
                chunk_len,
            ),
            o_pieces[0],
            need=o_pieces[1:] + out_pieces,
            beside=beside,
        )
        joined = [joined]
        if c < CHUNKS - 1:
            o_came = o_moving[c + 1].finish(beside[1])
        if c:
            h_fars = [beside[0]]
        state.append((y, x_rows, h_one))
        h_far = gather_far(h_low, n_head)
    cot_pieces = [cot_own] + cot_blocks

    fed, raws, z_terms, sent = [], [], None, None
    for c in chunks:
        h_pieces = gather_near(h_fars[c] if c < len(h_fars) else h_far, n_head)
        beside = [h_far if c < CHUNKS - 1 else None, z_terms]
        (kept, raw, z_even, z_odd), (h_next, z_done) = order.run(
            lambda first: feed(
                [first] + h_pieces[1:], w_up, w_gate, w_down, up_scale, gate_scale
            ),
            h_pieces[0],
            need=h_pieces[1:] + [sent],
            beside=beside,
        )
        if c < CHUNKS - 1:
            h_far = h_next
        fed.append(kept)
        raws.append(raw)
        z_near = reduce_near(z_odd, n_head)
        if c < CHUNKS - 1:
            z_terms, sent = reduce_far(z_even, z_near, n_head)

    two = []

    def mid_step(c, terms, beside, need=()):
        nonlocal two
        (two, dz, direct, alpha_sum), beside = order.run(
            lambda first: middle(
                c, two, [first] + terms[1:], cot_pieces, state[c][2], ffn_alpha, info
            ),
            terms[0],
            need=terms[1:] + list(need),
            beside=beside,
        )
        return dz, direct, alpha_sum, beside

    def unfeed_step(c, dz_pieces, beside, need=()):
        return order.run(
            lambda first: unfeed(
                [first] + dz_pieces[1:],
                *raws[c],
                w_up,
                w_gate,
                w_down,
                up_scale,
                gate_scale,
                n_head,
            ),
            dz_pieces[0],
            need=dz_pieces[1:] + list(need),
            beside=beside,
        )

    dz, direct, alpha_sum, z_near = mid_step(0, z_done, z_near)
    directs, ffn_alphas = [direct], [alpha_sum]
    dz_far = gather_far(dz, n_head)
    z_even = [z_even[0]] + [after(p, dz_far[far]) for p in z_even[1:]]
    z_terms, sent = reduce_far(z_even, z_near, n_head)
    dz_pieces = gather_near(dz_far, n_head)
    (low_first, scales_first, dh_even, dh_odd, dz_first), z_terms = unfeed_step(
        0, dz_pieces, z_terms, need=[sent]
    )
    dh_near = reduce_near(dh_odd, n_head)
    dz, direct, alpha_sum, dh_near = mid_step(1, z_terms, dh_near)
    directs.append(direct)
    ffn_alphas.append(alpha_sum)
    dz_far = gather_far(dz, n_head)
    firsts, dz_far = order.run(
        lambda v: weigh_feed(v, fed[0][1], dz_first, *low_first), fed[0][0], beside=dz_far
    )
    dz_pieces = gather_near(dz_far, n_head)
    dh_even = [dh_even[0]] + [after(p, dz_far[far]) for p in dh_even[1:]]
    dh_terms, sent = reduce_far(dh_even, dh_near, n_head)
    dz_last, _ = order.run(
        lambda first: join([first] + dz_pieces[1:]), dz_pieces[0], need=dz_pieces[1:] + [sent]
    )
    grad_down, _ = order.run(
        lambda v: (firsts[0].astype(F32) + dot(fed[1][0], v, 0, 0)).astype(BF16), dz_last
    )
    sum_down = BatchSum(grad_down, n_batch)
    (low_last, scales_last, dh_even, dh_odd, _), dh_terms = unfeed_step(
        1, [dz_last], dh_terms, need=[sum_down.sent]
    )
    scale_sums = [jnp.concatenate(s, axis=0) for s in (scales_first, scales_last)]
    dh_near = reduce_near(dh_odd, n_head)

    zeros, alphas, dys = [], [], []

    def back(c, terms, beside, need=()):
        y, x_rows, _ = state[c]
        (dy, d_pieces, zero, grad_alpha_attn), beside = order.run(
            lambda first: unproject(
                c, dys, [first] + terms[1:], out_pieces, directs[c], y, x_rows, attn_alpha
            ),
            terms[0],
            need=terms[1:] + list(need),
            beside=beside,
        )
        dys[:] = [dy]
        zeros.append(zero)
        alphas.append(grad_alpha_attn)
        return d_pieces[0], Exchange(d_pieces[1], d_pieces[2], n_head), beside

    def beside_sums(step, value, sums, beside=(), need=(), first=False):
        out, (got, beside) = order.run(
            step, value, need=need, beside=([b.flying for b in sums], beside)
        )
        for i, (b, v) in enumerate(zip(sums, got, strict=True)):
            b.advance(after(v, sums[0].sent) if i and first else v)
        return out, beside

    grad_up, dh_near = beside_sums(
        lambda v: (firsts[1].astype(F32) + dot(fed[1][1], v, 0, 0)).astype(BF16),
        low_last[0],
        [sum_down],
        dh_near,
    )
    sum_up = BatchSum(grad_up, n_batch)
    dh_first, (dh_terms, sent) = dh_terms, reduce_far(dh_even, dh_near, n_head)
    grad_gate, _ = order.run(
        lambda v: (firsts[2].astype(F32) + dot(fed[1][1], v, 0, 0)).astype(BF16),
        low_last[1],
        need=[sent, sum_down.sent, sum_up.sent],
    )
    do_own, do_first, (dh_terms, got) = back(0, dh_first, (dh_terms, sum_down.flying))
    sum_down.advance(got)
    do_pieces = [do_own]
    do_own, do_last, do_came = back(1, dh_terms, do_first.flying, need=[sum_down.sent])
    do_pieces += do_first.finish(do_came)
    out_terms, do_came = beside_sums(
        lambda o: dot(o, dys[0], 0, 0).astype(BF16),
        joined[0],
        [sum_down, sum_up],
        do_last.flying,
    )
    sum_gate = BatchSum(after(grad_gate, order.last), n_batch)
    do_pieces += [do_own] + do_last.finish(do_came)
    alpha_sums = jnp.concatenate([sum(alphas), sum(ffn_alphas)], axis=0)
    alpha_rows = jnp.pad(alpha_sums.astype(BF16), ((0, 14), (0, 0)))
    out_blocks = [
        jnp.concatenate([out_terms[e * cols : (e + 1) * cols], alpha_rows], axis=0)
        for e in range(n_head)
    ]
    out_near = reduce_near(out_blocks[1::2], n_head)
    d_all, gains = [], []

    def attention_back(g, sums, beside, need=()):
        (d_pair, grad_gain), beside = beside_sums(
            lambda first: unattend(
                g, [first] + do_pieces[1:], buffers, starts, cosine, sine, gain, info, n_head
            ),
            do_pieces[0],
            sums,
            beside,
            need=do_pieces[1:] + list(need),
        )
        d_pair = d_pair.reshape(3 * pair, row_len)
        d_all.append(d_pair)
        gains.append(grad_gain[:, 0])
        return d_pair, beside

    big = [sum_down, sum_up, sum_gate]
    grads = []
    if pairs > 1:
        d_pair, out_near = attention_back(
            0, [sum_down, sum_up], out_near, need=[b.sent for b in big]
        )
        out_flying, out_sent = reduce_far(out_blocks[::2], out_near, n_head)
        grad_pair, _ = beside_sums(
            lambda d: weigh(d, x_pieces, chunk_len),
            d_pair,
            [sum_gate],
            need=[sum_down.sent, sum_up.sent, out_sent],
        )
        grads.append(grad_pair)
    else:
        out_flying, _ = reduce_far(out_blocks[::2], out_near, n_head)
    ahead = [BatchSum(g, n_batch) for g in grads] if n_batch == 8 else []
    d_pair, out_flying = attention_back(
        pairs - 1,
        [sum_down, sum_up] + ahead,
        out_flying,
        need=[sum_gate.sent] + [b.sent for b in ahead],
    )
    out_sum = term_sum(out_flying)
    grad_pair, _ = beside_sums(
        lambda d: weigh(d, x_pieces, chunk_len),
        d_pair,
        [sum_gate],
        need=[sum_down.sent, sum_up.sent],
    )
    small = jnp.concatenate(
        [out_sum[cols : cols + 2]]
        + [
            jnp.pad(v, ((0, 0), (0, model - v.shape[1])))
            for v in (sum(scale_sums), jnp.concatenate(gains)[None])
        ],
        axis=0,
    )
    if ahead:
        grads = []
    grads += [grad_pair, out_sum[:cols].astype(BF16)]
    if 4 * cols % (16 * n_batch):
        grads.append(jnp.zeros((-4 * cols % (16 * n_batch), model), BF16))
    grads = jnp.concatenate(grads, axis=0)
    ranges = [2 * b.values.shape[0] for b in ahead] + [grads.shape[0]]
    sum_attn = BatchSum(grads, n_batch, direct=True, before=[b.values for b in ahead])

    def spread_step(c, sums, beside=(), need=()):
        return beside_sums(
            lambda w: spread(c, chunk_len, d_all, w, zeros[c], info, n_head),
            w_t,
            sums,
            beside,
            need=need,
            first=c > 0,
        )

    def land(sums, beside=()):
        got, beside = lax.optimization_barrier(([b.flying for b in sums], beside))
        for i, (b, v) in enumerate(zip(sums, got, strict=True)):
            b.advance(after(v, sums[0].sent) if i else v)
        return jax.tree.map(lambda v: after(v, sums[0].sent), beside)

    two_moving = Exchange(after(two[1], order.last), after(two[2], order.last), n_head)
    d_first, two_came = spread_step(
        0, [sum_up, sum_gate, sum_down], two_moving.flying, need=[sum_attn.sent]
    )
    two_pieces = two_moving.finish(two_came)
    dx_near = reduce_near(d_first[-1], n_head)
    small_swaps = [1 << i for i in range(n_batch.bit_length() - 1)]
    d_last, (dx_near, small_far) = spread_step(
        1,
        [sum_attn, sum_up, sum_gate],
        (dx_near, swap(small, "batch", small_swaps.pop(0), n_batch)),
        need=[sum_up.sent, sum_gate.sent],
    )
    small = small + small_far
    dx_first, _ = reduce_far(d_first[:-1], dx_near, n_head)
    down_done = assemble(sum_down.finish(), place)
    land([sum_attn, sum_up, sum_gate])
    dx_first = land([sum_attn, sum_gate], dx_first)
    small = after(small, sum_attn.sent)
    for bit_now in small_swaps:
        small = small + swap(small, "batch", bit_now, n_batch)
    dx_near = reduce_near(after(d_last[-1], sum_attn.sent), n_head)
    dx_last, _ = reduce_far(d_last[:-1], dx_near, n_head)
    while len(sum_attn.todo) > 1:
        land([sum_attn])
    hidden_out = settle(two[0], two_pieces, info)
    grad_down = down_done
    grad_up = assemble(sum_up.finish(), place)
    grad_gate = assemble(sum_gate.finish(), place)
    grad_query, grad_key, grad_value, grad_out = assemble_turned(
        sum_attn.finish(), place, info, cols, n_head, pairs, ranges
    )
    grad_hidden = jnp.concatenate([term_sum(dx_first), term_sum(dx_last)], axis=0)[None]
    alpha_own = lax.dynamic_slice_in_dim(small[:2], me * share, share, 1)
    hidden_units = w_up.shape[1]

    return (
        hidden_out[None],
        grad_hidden,
        grad_query,
        grad_key,
        grad_value,
        grad_out,
        grad_up,
        grad_gate,
        grad_down,
        small[4, :cols],
        small[2, :hidden_units],
        small[3, :hidden_units],
        alpha_own[0],
        alpha_own[1],
    )


def solution(mesh):
    split = P("batch", None, "head")
    by_col, by_row, by_head = P(None, "head"), P("head", None), P("head")
    return jax.shard_map(
        functools.partial(on_device, mesh.shape["batch"], mesh.shape["head"]),
        mesh=mesh,
        in_specs=(split, split, P("batch", None), P("batch"))
        + (by_col, by_col, by_col, by_row, by_col, by_col, by_row)
        + (by_head, by_head, by_head, P(), P()),
        out_specs=(split, split, by_col, by_col, by_col, by_row, by_col, by_col, by_row)
        + (by_head,) * 5,
        check_vma=False,
    )
```

```python
import functools
import math

import jax
import jax.numpy as jnp
from jax import lax
from jax.experimental import pallas as pl
from jax.experimental.pallas import tpu as pltpu
from jax.sharding import PartitionSpec as P

HD = 64
HALF = HD // 2
VALUE_ROWS = 80
EPSILON = 1e-06
BLOCK = 256
QUERIES = 512
KEYS = 512
CHUNKS = 2
F32 = jnp.float32
BF16 = jnp.bfloat16
MIB = 1024 * 1024


def dot(left, right, left_dim=1, right_dim=0):
    return lax.dot_general(
        left, right, (((left_dim,), (right_dim,)), ((), ())), preferred_element_type=F32
    )


def shape(dims, dtype):
    return jax.ShapeDtypeStruct(dims, dtype)


def kept_shape(dims, dtype):
    return pltpu.HBM(dims, dtype)


def held(array):
    return pltpu.with_memory_space_constraint(array, pltpu.HBM)


def after(value, *others):
    others = [o for o in others if o is not None]
    return lax.optimization_barrier((value, *others))[0] if others else value


def whole(dims):
    return pl.BlockSpec(dims, lambda *_: (0,) * len(dims))


def term_spec(term):
    if term.ndim == 3:
        return pl.BlockSpec((None, *term.shape[1:]), lambda *_: (0, 0, 0))
    return whole(term.shape)


def params(mib):
    return pltpu.CompilerParams(vmem_limit_bytes=mib * MIB)


def cost(flops, moved):
    return pl.CostEstimate(flops=int(flops), bytes_accessed=int(moved), transcendentals=0)


class Order:
    def __init__(self):
        self.last = None

    def run(self, step, value, need=(), beside=()):
        out = step(after(value, self.last, *need))
        out, beside = lax.optimization_barrier((out, beside))
        self.last = jax.tree.leaves(out)[0]
        return out, beside


def swap(value, axis, mask, size):
    return lax.ppermute(value, axis, [(i, i ^ mask) for i in range(size)])


def gather_far(own, size):
    pieces = {0: own}
    bit = size // 2
    while bit > 1:
        pieces.update({e | bit: swap(p, "head", bit, size) for e, p in pieces.items()})
        bit //= 2
    return pieces


def gather_near(far, size):
    pieces = dict(far)
    pieces.update({e | 1: swap(p, "head", 1, size) for e, p in far.items()})
    return [pieces[e] for e in range(size)]


class Exchange:
    def __init__(self, near, far, size):
        self.size = size
        if size == 4:
            self.flying = [swap(near, "head", 1, size), swap(far, "head", 2, size)]
        else:
            blocks = [near, *far]
            self.flying = [swap(p, "head", e, size) for e, p in enumerate(blocks, 1)]

    def finish(self, flying):
        if self.size != 4:
            return flying
        near, far = flying
        return [near, far[0], swap(far[1], "head", 1, self.size)]


def total(terms):
    if len(terms) == 1:
        return terms[0]
    return sum(t.astype(F32) for t in terms).astype(BF16)


def reduce_near(odd, size):
    return jax.tree.map(lambda p: swap(p, "head", 1, size), odd)


def reduce_far(even, near, size):
    held = {2 * i: [p, near[i]] for i, p in enumerate(even)}
    bit, sent = 2, None
    while bit < size:
        for e in [e for e in held if e & bit]:
            sent = total(held.pop(e))
            got = swap(sent, "head", bit, size)
            held[e ^ bit].append(got)
        bit *= 2
    return held[0], sent


def term_sum(terms):
    return sum((t[0] if t.ndim == 3 else t).astype(F32) for t in terms)


def sum_small(value, axis, size):
    bit = 1
    while bit < size:
        value = value + swap(value, axis, bit, size)
        bit *= 2
    return value


def halve(values, bit, place):
    rows = values.shape[0] // 2
    own = (place & bit) // bit
    return tuple(
        lax.dynamic_slice_in_dim(values, part * rows, rows, 0) for part in (own, 1 - own)
    )


class BatchSum:
    def __init__(self, values, size, direct=False, before=()):
        self.size = size
        self.place = lax.axis_index("batch")
        self.bits = [1 << i for i in range(size.bit_length() - 1)]
        self.todo = [("halve", b) for b in self.bits] + [("join", b) for b in reversed(self.bits)]
        if direct and size <= 8:
            self.bits = self.bits[:1] + self.bits[:0:-1]
            self.todo = [("halve", 1), ("scatter", 0), ("gather", 0), ("join", 1)]
        self.values, self.mine, self.flying, self.sent = values, None, None, None
        self.before = list(before)
        self.start()

    def start(self):
        kind, bit = self.todo[0]
        self.sent = self.values
        if kind == "halve":
            self.mine, self.sent = halve(self.values, bit, self.place)
        others = range(1, self.size // 2)
        if kind == "scatter":
            rows = self.values.shape[0] * 2 // self.size
            own = self.place // 2
            blocks = [
                lax.dynamic_slice_in_dim(self.values, (own ^ d) * rows, rows, 0)
                for d in range(self.size // 2)
            ]
            self.mine, self.sent = blocks[0], blocks[-1]
            self.flying = [swap(blocks[d], "batch", 2 * d, self.size) for d in others]
        elif kind == "gather":
            self.flying = [swap(self.values, "batch", 2 * d, self.size) for d in others]
        else:
            self.flying = swap(self.sent, "batch", bit, self.size)

    def advance(self, got):
        kind, _ = self.todo.pop(0)
        if not self.todo:
            self.parts = [self.values, got]
        elif kind == "halve":
            self.values = total([self.mine, got])
        elif kind == "scatter":
            self.values = total([self.mine] + got)
        else:
            got = got if kind == "gather" else [got]
            self.values = jnp.concatenate([self.values] + got, axis=0)
        if self.before:
            self.values = jnp.concatenate(self.before + [self.values], axis=0)
            self.before = []
        if self.todo:
            self.start()

    def finish(self):
        while self.todo:
            self.advance(self.flying)
        return self.parts, self.bits


def store_blocks(place, summed, refs, out):
    (first, _), bits = summed
    count = 1 << len(bits)
    rows = 2 * first.shape[0] // count
    for p in range(count):
        at = 0
        for level, bit in enumerate(bits):
            other = p >> (len(bits) - 1 - level) & 1
            at = at + (((place // bit) % 2) ^ other) * ((count >> (level + 1)) * rows)
        ref, row = refs[p * 2 // count], (p % (count // 2)) * rows
        out[pl.ds(pl.multiple_of(at, rows), rows), :] = ref[row : row + rows, :].astype(out.dtype)


def segments(first, count, ranges):
    half, skip = sum(ranges) // 2, 0
    found = []
    for size in ranges:
        part = size // 2
        for side in range(2):
            low, high = max(first, 0), min(first + count, part)
            if low < high:
                found.append((side * half + skip + low, low - first, high - low))
            first -= part
        skip += part
    return found


def assemble(summed, place):
    parts, _ = summed
    rows, width = parts[0].shape

    def body(place, own_ref, other_ref, out):
        store_blocks(place[0], summed, (own_ref, other_ref), out)

    return pl.pallas_call(
        body,
        grid_spec=pltpu.PrefetchScalarGridSpec(
            num_scalar_prefetch=1,
            grid=(1,),
            in_specs=[whole((rows, width))] * 2,
            out_specs=whole((2 * rows, width)),
        ),
        out_shape=shape((2 * rows, width), F32),
        compiler_params=params(24),
        cost_estimate=cost(0, rows * width * 12),
        name="assemble",
    )(place, *parts)


def assemble_turned(summed, place, info, cols, n_head, pairs, ranges):
    parts, _ = summed
    width = cols // pairs
    rows, model = parts[0].shape
    share = model // n_head

    def body(place, info, own_ref, other_ref, q_out, k_out, v_out, o_out, room):
        store_blocks(place[0], summed, (own_ref, other_ref), room)
        for g in range(pairs):
            for i, out in enumerate((q_out, k_out, v_out)):
                for row, offset, count in segments((3 * g + i) * width, width, ranges):
                    lanes = slice(g * width + offset, g * width + offset + count)
                    for e in range(n_head):
                        at = pl.ds(pl.multiple_of((info[0] ^ e) * share, share), share)
                        block = room[row : row + count, e * share : (e + 1) * share]
                        out[at, lanes] = block.T.astype(F32)
        for row, offset, count in segments(3 * cols, cols, ranges):
            o_out[offset : offset + count, :] = room[row : row + count, :].astype(F32)

    return pl.pallas_call(
        body,
        grid_spec=pltpu.PrefetchScalarGridSpec(
            num_scalar_prefetch=2,
            grid=(1,),
            in_specs=[whole((rows, model))] * 2,
            out_specs=[whole((model, cols))] * 3 + [whole((cols, model))],
            scratch_shapes=[pltpu.VMEM((2 * rows, model), BF16)],
        ),
        out_shape=[shape((model, cols), F32)] * 3 + [shape((cols, model), F32)],
        compiler_params=params(32),
        cost_estimate=cost(0, cols * model * 24),
        name="assemble_turned",
    )(place, info, *parts)


def visible(first_key, first_query, starts, length, rows, cols):
    key = first_key + lax.broadcasted_iota(jnp.int32, (rows, cols), 0)
    query = first_query + lax.broadcasted_iota(jnp.int32, (rows, cols), 1)
    last = jnp.minimum(query, length - 1)
    return (key >= starts) & ((key <= last) | (key == query))


def prepare(w_query, w_key, w_value, w_out, cotangent, own, pair, n_head):
    model, cols = w_query.shape
    row_len, share = cotangent.shape
    rows = row_len // CHUNKS // n_head

    def body(own, q_ref, k_ref, v_ref, o_ref, c_ref, out, half, near, far_blocks):
        for g in range(cols // pair):
            for i, ref in enumerate((q_ref, k_ref, v_ref)):
                first = (3 * g + i) * pair
                out[first : first + pair, :] = ref[:, g * pair : (g + 1) * pair].T
        half[...] = o_ref[:, pl.ds(pl.multiple_of(own[1] * (model // 2), model // 2), model // 2)]
        for e in range(1, n_head):
            for c in range(CHUNKS):
                at = (c * n_head + (own[0] ^ e)) * rows
                block = c_ref[pl.ds(pl.multiple_of(at, rows), rows), :]
                if e == 1:
                    near[c * rows : (c + 1) * rows, :] = block
                else:
                    far_blocks[e - 2, c * rows : (c + 1) * rows, :] = block

    outs = pl.pallas_call(
        body,
        grid_spec=pltpu.PrefetchScalarGridSpec(
            num_scalar_prefetch=1,
            grid=(1,),
            in_specs=[whole((model, cols))] * 3 + [whole((cols, model)), whole((row_len, share))],
            out_specs=[
                whole((3 * cols, model)),
                whole((cols, model // 2)),
                whole((CHUNKS * rows, share)),
                whole((n_head - 2, CHUNKS * rows, share)),
            ],
        ),
        out_shape=[
            shape((3 * cols, model), BF16),
            shape((cols, model // 2), BF16),
            shape((CHUNKS * rows, share), BF16),
            shape((n_head - 2, CHUNKS * rows, share), BF16),
        ],
        compiler_params=params(24),
        cost_estimate=cost(0, 12 * cols * model),
        name="prepare",
    )(own, w_query, w_key, w_value, w_out, cotangent)
    return outs


def attend_kernel(
    chunk, n_head, heads, chunk_len, share, info, *refs
):
    refs = list(refs)
    x_refs = [refs.pop(0) for _ in range(n_head)]
    w_ref, cos_ref, sin_ref, gain_ref, start_ref = [refs.pop(0) for _ in range(5)]
    old_k, old_v = None, None
    if chunk:
        old_k, old_v = refs.pop(0), refs.pop(0)
        refs = refs[7:]
    k_ref, ve_ref, v_ref, kt_ref, qt_ref, ot_ref, inv_ref, qf_ref, kf_ref, o_ref = refs[:10]
    near_ref, far_ref, raw, acc = refs[10:]
    me, length = info[0], info[1]
    cols = heads * HD
    pair = min(2, heads)
    for e in range(n_head):
        first = pl.multiple_of((me ^ e) * share, share)
        for third in range(3):
            rows = slice(third * cols, (third + 1) * cols)
            term = dot(w_ref[rows, pl.ds(first, share)], x_refs[e][...], 1, 1)
            if e == 0:
                raw[rows, :] = term
            else:
                raw[rows, :] += term

    def raw_row(part, h):
        return ((h // pair * 3 + part) * pair + h % pair) * HD

    cosine, sine = cos_ref[...], sin_ref[...]
    for h in range(heads):
        own = slice(h * HD, (h + 1) * HD)
        for part, factor_ref in ((0, qf_ref), (1, kf_ref)):
            base = raw_row(part, h)
            a, b = raw[base : base + HALF, :], raw[base + HALF : base + HD, :]
            front, back = a * cosine - b * sine, b * cosine + a * sine
            mean = jnp.sum(front * front + back * back, axis=0, keepdims=True) / HD
            factor = lax.rsqrt(mean + EPSILON)
            factor_ref[h] = factor
            unit = jnp.concatenate([front, back], axis=0) * factor
            low = (unit * gain_ref[own, :]).astype(BF16)
            if part == 0:
                qt_ref[own, :] = low * BF16(1.0 / math.sqrt(HD))
            else:
                kt_ref[own, :] = low
                k_ref[h] = low.T
        value = raw[raw_row(2, h) : raw_row(2, h) + HD, :].astype(BF16)
        v_ref[h] = value.T
        ve_ref[h, :HD, :] = value
        ve_ref[h, HD:, :] = jnp.ones((VALUE_ROWS - HD, chunk_len), BF16)

    before = chunk * (chunk_len // KEYS)

    def step(local, key_first, k_of, v_of, starts):
        query = slice(local * QUERIES, (local + 1) * QUERIES)
        first = chunk * chunk_len + local * QUERIES
        mask = visible(key_first, first, starts, length, KEYS, QUERIES)
        for h in range(heads):
            scores = dot(k_of(h), qt_ref[h * HD : (h + 1) * HD, query])
            probs = jnp.where(mask, jnp.exp(scores), 0.0).astype(BF16)
            acc[h] += dot(v_of(h), probs)

    for local in range(chunk_len // QUERIES):
        query = slice(local * QUERIES, (local + 1) * QUERIES)
        starts = start_ref[:, query]
        lowest = info[2 + (chunk * chunk_len + local * QUERIES) // BLOCK] * BLOCK // KEYS
        acc[...] = jnp.zeros_like(acc)
        if chunk:

            @pl.loop(lowest, before)
            def _(kb):
                at = pl.ds(pl.multiple_of(kb * KEYS, KEYS), KEYS)
                step(
                    local, kb * KEYS, lambda h: old_k[h, at, :], lambda h: old_v[h, :, at], starts
                )

        @pl.loop(jnp.maximum(lowest - before, 0), (local + 1) * QUERIES // KEYS)
        def _(kb):
            at = pl.ds(pl.multiple_of(kb * KEYS, KEYS), KEYS)
            step(
                local,
                (before + kb) * KEYS,
                lambda h: k_ref[h, at, :],
                lambda h: ve_ref[h, :, at],
                starts,
            )

        for h in range(heads):
            inverse = 1.0 / acc[h, HD : HD + 1, :]
            inv_ref[h, :, query] = inverse
            out = acc[h, :HD, :] * inverse
            ot_ref[h * HD : (h + 1) * HD, query] = out.astype(BF16)
            o_ref[query, h * HD : (h + 1) * HD] = out.T.astype(BF16)
    rows = chunk_len // n_head
    for e in range(1, n_head):
        block = o_ref[pl.ds(pl.multiple_of((me ^ e) * rows, rows), rows), :]
        if e == 1:
            near_ref[...] = block
        else:
            far_ref[e - 2] = block


def attend_chunk(
    chunk, x_pieces, w_t, cosine, sine, gain, starts, info, buffers, row_len, chunk_len
):
    n_head = len(x_pieces)
    share = x_pieces[0].shape[1]
    cols = w_t.shape[0] // 3
    heads = cols // HD
    model = w_t.shape[1]
    body = functools.partial(attend_kernel, chunk, n_head, heads, chunk_len, share)
    by_lane = lambda rows: pl.BlockSpec((rows, chunk_len), lambda i, info: (0, chunk))
    specs = [whole((chunk_len, share))] * n_head + [
        whole((3 * cols, model)),
        by_lane(HALF),
        by_lane(HALF),
        whole((cols, 1)),
        by_lane(1),
    ]
    operands = [*x_pieces, held(w_t), held(cosine), held(sine), gain, starts]
    aliases = {}
    if chunk:
        aliases = {1 + len(operands) + i: i for i in range(9)}
        specs += [whole((heads, row_len, HD)), whole((heads, VALUE_ROWS, row_len))]
        specs += [pl.BlockSpec(memory_space=pl.ANY)] * 7
        operands += buffers
    lane3 = lambda rows: pl.BlockSpec((heads, rows, chunk_len), lambda i, info: (0, 0, chunk))
    row3 = pl.BlockSpec((heads, chunk_len, HD), lambda i, info: (0, chunk, 0))
    outs = pl.pallas_call(
        body,
        grid_spec=pltpu.PrefetchScalarGridSpec(
            num_scalar_prefetch=1,
            grid=(1,),
            in_specs=specs,
            out_specs=[
                row3,
                lane3(VALUE_ROWS),
                row3,
                by_lane(cols),
                by_lane(cols),
                by_lane(cols),
                lane3(1),
                lane3(1),
                lane3(1),
                whole((chunk_len, cols)),
            ]
            + [
                whole((chunk_len // n_head, cols)),
                whole((n_head - 2, chunk_len // n_head, cols)),
            ],
            scratch_shapes=[
                pltpu.VMEM((3 * cols, chunk_len), F32),
                pltpu.VMEM((heads, VALUE_ROWS, QUERIES), F32),
            ],
        ),
        out_shape=[
            kept_shape((heads, row_len, HD), BF16),
            kept_shape((heads, VALUE_ROWS, row_len), BF16),
            kept_shape((heads, row_len, HD), BF16),
            kept_shape((cols, row_len), BF16),
            kept_shape((cols, row_len), BF16),
            kept_shape((cols, row_len), BF16),
            kept_shape((heads, 1, row_len), F32),
            kept_shape((heads, 1, row_len), F32),
            kept_shape((heads, 1, row_len), F32),
            kept_shape((chunk_len, cols), BF16),
        ]
        + [
            kept_shape((chunk_len // n_head, cols), BF16),
            kept_shape((n_head - 2, chunk_len // n_head, cols), BF16),
        ],
        input_output_aliases=aliases,
        compiler_params=params(40),
        cost_estimate=cost(16e9 / CHUNKS, 8e6),
        name="attend",
    )(info, *operands)
    return outs[:9], list(outs[9:])


def unattend_kernel(n_head, chunks, row_len, piece, pair, info, *refs):
    refs = list(refs)
    d_refs = [refs.pop(0) for _ in range(chunks * n_head)]
    k_ref, v_ref, kt_ref, qt_ref, ot_ref, inv_ref, qf_ref, kf_ref = [refs.pop(0) for _ in range(8)]
    start_ref, cos_ref, sin_ref, gain_ref = [refs.pop(0) for _ in range(4)]
    out_ref, gain_out, do_s, inner_s, dq_s, dk_s, dv_s = refs
    me, length = info[0], info[1]
    for c in range(chunks):
        for e in range(n_head):
            first = c * n_head * piece + (me ^ e) * piece
            do_s[:, pl.ds(pl.multiple_of(first, piece), piece)] = d_refs[c * n_head + e][...]
    for h in range(pair):
        own = slice(h * HD, (h + 1) * HD)
        product = do_s[own, :].astype(F32) * ot_ref[own, :].astype(F32)
        inner_s[h] = jnp.sum(product, axis=0, keepdims=True)
    dq_s[...] = jnp.zeros_like(dq_s)
    dk_s[...] = jnp.zeros_like(dk_s)
    dv_s[...] = jnp.zeros_like(dv_s)

    ratio = QUERIES // BLOCK

    @pl.loop(0, row_len // QUERIES)
    def _(qb):
        query = pl.ds(pl.multiple_of(qb * QUERIES, QUERIES), QUERIES)
        starts = start_ref[:, query]

        @pl.loop(info[2 + qb * ratio], (qb + 1) * ratio)
        def _(kb):
            key = pl.ds(pl.multiple_of(kb * BLOCK, BLOCK), BLOCK)
            mask = visible(kb * BLOCK, qb * QUERIES, starts, length, BLOCK, QUERIES)
            for h in range(pair):
                own = slice(h * HD, (h + 1) * HD)
                q_block, do_block = qt_ref[own, query], do_s[own, query]
                scores = dot(k_ref[h, key, :], q_block)
                probs = jnp.where(mask, jnp.exp(scores), 0.0) * inv_ref[h, :, query]
                d_probs = dot(v_ref[h, key, :], do_block)
                d_scores = (probs * (d_probs - inner_s[h, :, query])).astype(BF16)
                dv_s[own, key] += dot(do_block, probs.astype(BF16), 1, 1)
                dk_s[own, key] += dot(q_block, d_scores, 1, 1)
                dq_s[own, query] += dot(kt_ref[own, key], d_scores)

    for h in range(pair):
        own = slice(h * HD, (h + 1) * HD)
        gain = gain_ref[own, :]
        summed = jnp.zeros((HD, 1), F32)
        for part, low_ref, grad_ref, factor_ref in (
            (0, qt_ref, dq_s, qf_ref),
            (1, kt_ref, dk_s, kf_ref),
        ):
            scale = math.sqrt(HD) if part == 0 else 1.0
            unit = low_ref[own, :].astype(F32) * (scale / gain)
            grad = grad_ref[own, :]
            if part == 0:
                grad = grad * (1.0 / math.sqrt(HD))
            summed += jnp.sum(grad * unit, axis=1, keepdims=True)
            grad = grad * gain
            mean = jnp.sum(grad * unit, axis=0, keepdims=True) / HD
            grad = (grad - unit * mean) * factor_ref[h]
            front, back = grad[:HALF], grad[HALF:]
            cosine, sine = cos_ref[...], sin_ref[...]
            out_ref[part, h * HD : h * HD + HALF, :] = (front * cosine + back * sine).astype(BF16)
            out_ref[part, h * HD + HALF : (h + 1) * HD, :] = (
                back * cosine - front * sine
            ).astype(BF16)
        out_ref[2, own, :] = dv_s[own, :].astype(BF16)
        gain_out[own, :] = summed


def unattend(index, do_pieces, buffers, starts, cosine, sine, gain, info, n_head):
    k, _, v, kt, qt, ot, inv, qf, kf = buffers
    chunks = len(do_pieces) // n_head
    cols, piece = do_pieces[0].shape
    heads, row_len, _ = k.shape
    pair = min(2, heads)
    rows = pair * HD
    by_rows = lambda width: pl.BlockSpec((rows, width), lambda g, info: (index, 0))
    by_head = lambda a, b: pl.BlockSpec((pair, a, b), lambda g, info: (index, 0, 0))
    return pl.pallas_call(
        functools.partial(unattend_kernel, n_head, chunks, row_len, piece, pair),
        grid_spec=pltpu.PrefetchScalarGridSpec(
            num_scalar_prefetch=1,
            grid=(1,),
            in_specs=[by_rows(piece)] * (chunks * n_head)
            + [by_head(row_len, HD)] * 2
            + [by_rows(row_len)] * 3
            + [by_head(1, row_len)] * 3
            + [whole((1, row_len)), whole((HALF, row_len)), whole((HALF, row_len)), by_rows(1)],
            out_specs=[whole((3, rows, row_len)), whole((rows, 1))],
            scratch_shapes=[
                pltpu.VMEM((rows, row_len), BF16),
                pltpu.VMEM((pair, 1, row_len), F32),
                pltpu.VMEM((rows, row_len), F32),
                pltpu.VMEM((rows, row_len), F32),
                pltpu.VMEM((rows, row_len), F32),
            ],
        ),
        out_shape=[kept_shape((3, rows, row_len), BF16), shape((rows, 1), F32)],
        compiler_params=params(32),
        cost_estimate=cost(22e9, 6e6),
        name="unattend",
    )(info, *do_pieces, k, v, kt, qt, ot, inv, qf, kf, starts, cosine, sine, gain)


def norm(values):
    factor = lax.rsqrt(jnp.mean(values * values, axis=-1, keepdims=True) + EPSILON)
    return values * factor, factor


def norm_back(grad, unit, factor):
    return factor * (grad - unit * jnp.mean(grad * unit, axis=-1, keepdims=True))


def project_kernel(n_head, share, kept, info, *refs):
    o_refs, w_refs = refs[:n_head], refs[n_head : 2 * n_head]
    x_refs = refs[2 * n_head : 3 * n_head]
    alpha_ref = refs[3 * n_head]
    cat_ref, y_ref, x_ref, h_ref, low_ref = refs[3 * n_head + 1 + kept :]
    me = info[0]
    cols = w_refs[0].shape[0]
    y = dot(o_refs[0][...], w_refs[0][...])
    for e in range(1, n_head):
        y += dot(o_refs[e][...], w_refs[e][...])
    for e in range(n_head):
        cat_ref[:, e * cols : (e + 1) * cols] = o_refs[e][...]
    for e in range(n_head):
        first = pl.multiple_of((me ^ e) * share, share)
        x_ref[:, pl.ds(first, share)] = x_refs[e][...]
    y_ref[...] = y
    h_zero = x_ref[...].astype(F32)
    h_one, _ = norm(h_zero + alpha_ref[...] * (norm(y)[0] - h_zero))
    h_ref[...] = h_one
    low_ref[...] = h_one.astype(BF16)


def project(chunk, kept, o_pieces, w_pieces, x_pieces, alpha, info, chunk_len):
    n_head = len(o_pieces)
    cols, model = w_pieces[0].shape
    share = x_pieces[0].shape[1]
    rows = chunk_len // n_head
    mine = lambda width: pl.BlockSpec((rows, width), lambda i, info: (info[0], 0))
    return pl.pallas_call(
        functools.partial(project_kernel, n_head, share, len(kept)),
        grid_spec=pltpu.PrefetchScalarGridSpec(
            num_scalar_prefetch=1,
            grid=(1,),
            in_specs=[mine(cols)]
            + [whole((rows, cols))] * (n_head - 1)
            + [whole((cols, model))] * n_head
            + [mine(share)] * n_head
            + [whole((1, model))]
            + [pl.BlockSpec(memory_space=pl.ANY)] * len(kept),
            out_specs=[pl.BlockSpec((rows, n_head * cols), lambda i, info: (chunk, 0))]
            + [whole((rows, model))] * 4,
        ),
        input_output_aliases={3 * n_head + 2 + i: i for i in range(len(kept))},
        out_shape=[
            kept_shape((CHUNKS * rows, n_head * cols), BF16),
            kept_shape((rows, model), F32),
            kept_shape((rows, model), BF16),
            kept_shape((rows, model), F32),
            shape((rows, model), BF16),
        ],
        compiler_params=params(32),
        cost_estimate=cost(2.0 * rows * model * model, 6e6),
        name="project",
    )(info, *o_pieces, *w_pieces, *x_pieces, alpha, *kept)


def feed_kernel(n_head, rows, *refs):
    h_refs = refs[:n_head]
    up_ref, gate_ref, down_hbm, su_ref, sg_ref = refs[n_head : n_head + 5]
    m_ref, cat_hbm, u_ref, g_ref = refs[n_head + 5 : n_head + 9]
    z_refs = refs[n_head + 9 : 2 * n_head + 9]
    cat, mixed_s, down, cat_sem, down_sem = refs[2 * n_head + 9 :]
    tile = pl.program_id(0)
    keep = pltpu.make_async_copy(cat, cat_hbm, cat_sem)
    fetch = pltpu.make_async_copy(down_hbm, down, down_sem)

    @pl.when(tile == 0)
    def _():
        fetch.start()
        for e in range(n_head):
            cat[e * rows : (e + 1) * rows, :] = h_refs[e][...]
        keep.start()

    up_raw = dot(cat[...], up_ref[...])
    gate_raw = dot(cat[...], gate_ref[...])
    u_ref[...] = up_raw.astype(BF16)
    g_ref[...] = gate_raw.astype(BF16)
    gate = gate_raw * sg_ref[...]
    mixed = (up_raw * su_ref[...] * (gate * jax.nn.sigmoid(gate))).astype(BF16)
    m_ref[...] = mixed
    width = m_ref.shape[1]
    mixed_s[:, pl.ds(pl.multiple_of(tile * width, width), width)] = mixed

    @pl.when(tile == pl.num_programs(0) - 1)
    def _():
        fetch.wait()
        z = dot(mixed_s[...], down[...])
        for e in range(n_head):
            z_refs[e][...] = z[e * rows : (e + 1) * rows, :].astype(BF16)
        keep.wait()


def feed(h_pieces, w_up, w_gate, w_down, scale_up, scale_gate):
    n_head = len(h_pieces)
    rows, model = h_pieces[0].shape
    hidden = w_up.shape[1]
    tile = min(256, hidden // 2)
    count = n_head * rows
    by_col = lambda height: pl.BlockSpec((height, tile), lambda n: (0, n))
    anywhere = pl.BlockSpec(memory_space=pl.ANY)
    outs = pl.pallas_call(
        functools.partial(feed_kernel, n_head, rows),
        grid=(hidden // tile,),
        in_specs=[whole((rows, model))] * n_head
        + [by_col(model), by_col(model), anywhere, by_col(1), by_col(1)],
        out_specs=[by_col(count), anywhere, by_col(count), by_col(count)]
        + [whole((rows, model))] * n_head,
        out_shape=[
            kept_shape((count, hidden), BF16),
            kept_shape((count, model), BF16),
            kept_shape((count, hidden), BF16),
            kept_shape((count, hidden), BF16),
        ]
        + [shape((rows, model), BF16)] * n_head,
        scratch_shapes=[
            pltpu.VMEM((count, model), BF16),
            pltpu.VMEM((count, hidden), BF16),
            pltpu.VMEM((hidden, model), BF16),
            pltpu.SemaphoreType.DMA,
            pltpu.SemaphoreType.DMA,
        ],
        compiler_params=params(48),
        cost_estimate=cost(6.0 * count * model * hidden, 20e6),
        name="feed",
    )(*h_pieces, w_up, w_gate, held(w_down), scale_up, scale_gate)
    return outs[:2], outs[2:4], list(outs[4::2]), list(outs[5::2])


def middle_kernel(n_head, n_terms, share, kept, info, *refs):
    z_refs, c_refs = refs[:n_terms], refs[n_terms : n_terms + n_head]
    h_ref, alpha_ref = refs[n_terms + n_head : n_terms + n_head + 2]
    refs = refs[n_terms + n_head + 2 + kept :]
    own_ref, near_ref, far_ref, dz_ref, direct_ref, grad_ref, two_s, cot_s = refs
    me = info[0]
    step = pl.program_id(0)
    z = z_refs[0][...].astype(F32)
    for r in z_refs[1:]:
        z += r[...].astype(F32)
    h_one, alpha = h_ref[...], alpha_ref[...]
    h_ffn, z_factor = norm(z)
    h_two, factor = norm(h_one + alpha * (h_ffn - h_one))
    two_s[...] = h_two.astype(BF16)
    for e in range(n_head):
        at = pl.ds(pl.multiple_of((me ^ e) * share, share), share)
        if e < 2:
            (own_ref, near_ref)[e][...] = two_s[:, at]
        else:
            far_ref[e - 2] = two_s[:, at]
        cot_s[:, at] = c_refs[e][...]
    grad = norm_back(cot_s[...].astype(F32), h_two, factor)
    summed = jnp.sum(grad * (h_ffn - h_one), axis=0, keepdims=True)

    @pl.when(step == 0)
    def _():
        grad_ref[...] = summed

    @pl.when(step > 0)
    def _():
        grad_ref[...] += summed

    direct_ref[...] = grad * (1.0 - alpha)
    dz_ref[...] = norm_back(grad * alpha, h_ffn, z_factor).astype(BF16)


def middle(chunk, kept, z_terms, cot_pieces, h_one, alpha, info):
    n_head, n_terms = len(cot_pieces), len(z_terms)
    rows, model = h_one.shape
    share = cot_pieces[0].shape[1]
    part = rows // 2
    mine = pl.BlockSpec((part, share), lambda i, info: (2 * (chunk * n_head + info[0]) + i, 0))
    theirs = pl.BlockSpec((part, share), lambda i, info: (2 * chunk + i, 0))
    by_row = pl.BlockSpec((part, model), lambda i, info: (i, 0))
    outs = pl.pallas_call(
        functools.partial(middle_kernel, n_head, n_terms, share, len(kept)),
        grid_spec=pltpu.PrefetchScalarGridSpec(
            num_scalar_prefetch=1,
            grid=(2,),
            in_specs=[by_row] * n_terms
            + [mine]
            + [theirs] * (n_head - 1)
            + [by_row, whole((1, model))]
            + [pl.BlockSpec(memory_space=pl.ANY)] * len(kept),
            out_specs=[theirs] * 2
            + [pl.BlockSpec((n_head - 2, part, share), lambda i, info: (0, 2 * chunk + i, 0))]
            + [by_row] * 2
            + [whole((1, model))],
            scratch_shapes=[pltpu.VMEM((part, model), BF16), pltpu.VMEM((part, model), BF16)],
        ),
        input_output_aliases={n_terms + n_head + 3 + i: i for i in range(len(kept))},
        out_shape=[kept_shape((CHUNKS * rows, share), BF16)] * 2
        + [kept_shape((n_head - 2, CHUNKS * rows, share), BF16)]
        + [shape((rows, model), BF16), kept_shape((rows, model), F32), shape((1, model), F32)],
        compiler_params=params(32),
        cost_estimate=cost(rows * model * 60, rows * model * 24),
        name="middle",
    )(info, *z_terms, *cot_pieces, held(h_one), alpha, *kept)
    return list(outs[:3]), *outs[3:]


def join(pieces):
    rows, width = pieces[0].shape

    def body(*refs):
        for i, ref in enumerate(refs[:-1]):
            refs[-1][i * rows : (i + 1) * rows, :] = ref[...]

    return pl.pallas_call(
        body,
        in_specs=[whole((rows, width))] * len(pieces),
        out_specs=whole((rows * len(pieces), width)),
        grid=(1,),
        out_shape=shape((rows * len(pieces), width), pieces[0].dtype),
        compiler_params=params(16),
        cost_estimate=cost(0, rows * width * 4 * len(pieces)),
        name="join",
    )(*pieces)


def weigh_feed(mixed, joined, dz, du, dg):
    count, hidden = mixed.shape
    model = joined.shape[1]
    tile = min(256, hidden // 2)

    def body(m_ref, h_ref, z_ref, u_ref, g_ref, down, up, gate):
        down[...] = dot(m_ref[...], z_ref[...], 0, 0).astype(BF16)
        up[...] = dot(h_ref[...], u_ref[...], 0, 0).astype(BF16)
        gate[...] = dot(h_ref[...], g_ref[...], 0, 0).astype(BF16)

    by_col = lambda height: pl.BlockSpec((height, tile), lambda n: (0, n))
    return pl.pallas_call(
        body,
        in_specs=[
            by_col(count),
            whole((count, model)),
            whole((count, model)),
            by_col(count),
            by_col(count),
        ],
        out_specs=[pl.BlockSpec((tile, model), lambda n: (n, 0)), by_col(model), by_col(model)],
        grid=(hidden // tile,),
        out_shape=[kept_shape((hidden, model), BF16)] + [kept_shape((model, hidden), BF16)] * 2,
        compiler_params=params(48),
        cost_estimate=cost(6.0 * count * hidden * model, 20e6),
        name="weigh_feed",
    )(mixed, joined, dz, du, dg)


def weigh(d_pair, x_pieces, chunk_len):
    rows, row_len = d_pair.shape
    n_head = len(x_pieces[0])
    share = x_pieces[0][0].shape[1]
    flat = [p for chunk in x_pieces for p in chunk]

    def body(d_ref, *refs):
        for e in range(n_head):
            term = None
            for c in range(len(x_pieces)):
                d_part = d_ref[:, c * chunk_len : (c + 1) * chunk_len]
                new = dot(d_part, refs[c * n_head + e][...])
                term = new if term is None else term + new
            refs[-1][:, e * share : (e + 1) * share] = term.astype(BF16)

    return pl.pallas_call(
        body,
        in_specs=[whole((rows, row_len))] + [whole((chunk_len, share))] * len(flat),
        out_specs=whole((rows, n_head * share)),
        grid=(1,),
        out_shape=shape((rows, n_head * share), BF16),
        compiler_params=params(32),
        cost_estimate=cost(0, 1),
        name="weigh",
    )(d_pair, *flat)


def unfeed_kernel(n_head, n_in, rows, *refs):
    d_refs, refs = refs[:n_in], refs[n_in:]
    u_ref, g_ref, up_hbm, gate_hbm, down_ref, su_ref, sg_ref = refs[:7]
    du_ref, dg_ref, gsu_ref, gsg_ref = refs[7:11]
    out_refs = refs[11 : 11 + n_head]
    cat_hbm = refs[11 + n_head] if n_in > 1 else None
    refs = refs[11 + n_head + (n_in > 1) :]
    du_s, dg_s, up, gate_w, sems = refs[:5]
    cat = refs[5] if n_in > 1 else d_refs[0]
    tile = pl.program_id(0)
    fetch_up = pltpu.make_async_copy(up_hbm, up, sems.at[0])
    fetch_gate = pltpu.make_async_copy(gate_hbm, gate_w, sems.at[1])
    keep = pltpu.make_async_copy(cat, cat_hbm, sems.at[2]) if n_in > 1 else None

    @pl.when(tile == 0)
    def _():
        fetch_up.start()
        fetch_gate.start()
        if n_in > 1:
            for e in range(n_in):
                cat[e * rows : (e + 1) * rows, :] = d_refs[e][...]
            keep.start()

    d_mixed = dot(cat[...], down_ref[...], 1, 1)
    up_raw, gate_raw = u_ref[...].astype(F32), g_ref[...].astype(F32)
    gate = gate_raw * sg_ref[...]
    sigmoid = jax.nn.sigmoid(gate)
    silu = gate * sigmoid
    d_up = d_mixed * silu
    d_gate = d_mixed * (up_raw * su_ref[...]) * (sigmoid + silu * (1.0 - sigmoid))
    gsu_ref[...] = jnp.sum(d_up * up_raw, axis=0, keepdims=True)
    gsg_ref[...] = jnp.sum(d_gate * gate_raw, axis=0, keepdims=True)
    up_low = (d_up * su_ref[...]).astype(BF16)
    gate_low = (d_gate * sg_ref[...]).astype(BF16)
    du_ref[...] = up_low
    dg_ref[...] = gate_low
    width = du_ref.shape[1]
    at = pl.ds(pl.multiple_of(tile * width, width), width)
    du_s[:, at] = up_low
    dg_s[:, at] = gate_low

    @pl.when(tile == pl.num_programs(0) - 1)
    def _():
        fetch_up.wait()
        fetch_gate.wait()
        dh = dot(du_s[...], up[...], 1, 1) + dot(dg_s[...], gate_w[...], 1, 1)
        for e in range(n_head):
            out_refs[e][...] = dh[e * rows : (e + 1) * rows, :].astype(BF16)
        if n_in > 1:
            keep.wait()


def unfeed(dz_pieces, u, g, w_up, w_gate, w_down, scale_up, scale_gate, n_head):
    n_in = len(dz_pieces)
    model = dz_pieces[0].shape[1]
    count, hidden = u.shape
    rows = count // n_head
    tile = hidden // 2
    by_col = lambda height: pl.BlockSpec((height, tile), lambda n: (0, n))
    anywhere = pl.BlockSpec(memory_space=pl.ANY)
    outs = pl.pallas_call(
        functools.partial(unfeed_kernel, n_head, n_in, rows),
        grid=(hidden // tile,),
        in_specs=[whole(dz_pieces[0].shape)] * n_in
        + [
            by_col(count),
            by_col(count),
            anywhere,
            anywhere,
            pl.BlockSpec((tile, model), lambda n: (n, 0)),
            by_col(1),
            by_col(1),
        ],
        out_specs=[by_col(count)] * 2
        + [by_col(1), by_col(1)]
        + [whole((rows, model))] * n_head
        + [anywhere] * (n_in > 1),
        out_shape=[kept_shape((count, hidden), BF16)] * 2
        + [shape((1, hidden), F32), shape((1, hidden), F32)]
        + [shape((rows, model), BF16)] * n_head
        + [kept_shape((count, model), BF16)] * (n_in > 1),
        scratch_shapes=[
            pltpu.VMEM((count, hidden), BF16),
            pltpu.VMEM((count, hidden), BF16),
            pltpu.VMEM((model, hidden), BF16),
            pltpu.VMEM((model, hidden), BF16),
            pltpu.SemaphoreType.DMA((3,)),
        ]
        + [pltpu.VMEM((count, model), BF16)] * (n_in > 1),
        compiler_params=params(48),
        cost_estimate=cost(6.0 * count * model * hidden, 20e6),
        name="unfeed",
    )(*dz_pieces, u, g, held(w_up), held(w_gate), w_down, scale_up, scale_gate)
    pieces = outs[4 : 4 + n_head]
    return outs[:2], outs[2:4], list(pieces[::2]), list(pieces[1::2]), outs[-1]


def unproject_kernel(n_head, n_terms, kept, *refs):
    t_refs, w_refs = refs[:n_terms], refs[n_terms : n_terms + n_head]
    direct_ref, y_ref, x_ref, alpha_ref = refs[n_terms + n_head : n_terms + n_head + 4]
    refs = refs[n_terms + n_head + 4 + kept :]
    dy_ref, refs = refs[0], refs[1:]
    own_ref, near_ref, far_ref, zero_ref, grad_ref = refs
    grad = direct_ref[...]
    for r in t_refs:
        grad += r[...].astype(F32)
    alpha = alpha_ref[...]
    h_zero = x_ref[...].astype(F32)
    h_attn, y_factor = norm(y_ref[...])
    h_one, factor = norm(h_zero + alpha * (h_attn - h_zero))
    grad = norm_back(grad, h_one, factor)
    grad_ref[...] = jnp.sum(grad * (h_attn - h_zero), axis=0, keepdims=True)
    zero_ref[...] = grad * (1.0 - alpha)
    dy = norm_back(grad * alpha, h_attn, y_factor).astype(BF16)
    dy_ref[...] = dy
    for e in range(n_head):
        value = dot(w_refs[e][...], dy, 1, 1).astype(BF16)
        if e < 2:
            (own_ref, near_ref)[e][...] = value
        else:
            far_ref[e - 2] = value


def unproject(chunk, kept, terms, w_pieces, direct, y, x, alpha):
    n_head, n_terms = len(w_pieces), len(terms)
    rows, model = y.shape
    cols = w_pieces[0].shape[0]
    outs = pl.pallas_call(
        functools.partial(unproject_kernel, n_head, n_terms, len(kept)),
        grid=(1,),
        in_specs=[term_spec(t) for t in terms]
        + [whole((cols, model))] * n_head
        + [whole((rows, model))] * 3
        + [whole((1, model))]
        + [pl.BlockSpec(memory_space=pl.ANY)] * len(kept),
        out_specs=[pl.BlockSpec((rows, model), lambda i: (chunk, 0))]
        + [whole((cols, rows))] * 2
        + [whole((n_head - 2, cols, rows))]
        + [whole((rows, model)), whole((1, model))],
        input_output_aliases={n_terms + n_head + 4 + i: i for i in range(len(kept))},
        out_shape=[kept_shape((CHUNKS * rows, model), BF16)]
        + [shape((cols, rows), BF16)] * 2
        + [shape((n_head - 2, cols, rows), BF16)]
        + [kept_shape((rows, model), F32), shape((1, model), F32)],
        compiler_params=params(32),
        cost_estimate=cost(2.0 * rows * model * model, 8e6),
        name="unproject",
    )(*terms, *w_pieces, held(direct), held(y), held(x), alpha, *kept)
    return outs[0], list(outs[1:4]), outs[4], outs[5]


def spread_kernel(n_head, share, pairs, info, *refs):
    d_refs, (w_ref, direct_ref), out_refs = refs[:pairs], refs[pairs : pairs + 2], refs[pairs + 2 :]
    me = info[0]
    block = pl.program_id(0)
    d_all = jnp.concatenate([r[...] for r in d_refs], axis=0)
    for e in range(n_head):
        at = pl.ds(pl.multiple_of((me ^ e) * share, share), share)
        term = dot(d_all, w_ref[:, at], 0, 0)

        ref = out_refs[n_head // 2].at[e // 2] if e % 2 else out_refs[e // 2]

        @pl.when(block == me)
        def _():
            ref[...] = (term + direct_ref[:, at]).astype(BF16)

        @pl.when(block != me)
        def _():
            ref[...] = term.astype(BF16)


def spread(chunk, chunk_len, d_all, w_t, direct, info, n_head):
    rows3, model = w_t.shape
    share = model // n_head
    rows = chunk_len // n_head
    return pl.pallas_call(
        functools.partial(spread_kernel, n_head, share, len(d_all)),
        grid_spec=pltpu.PrefetchScalarGridSpec(
            num_scalar_prefetch=1,
            grid=(n_head,),
            in_specs=[
                *[pl.BlockSpec((d.shape[0], rows), lambda i, info: (0, chunk * n_head + i)) for d in d_all],
                whole((rows3, model)),
                whole((rows, model)),
            ],
            out_specs=[pl.BlockSpec((rows, share), lambda i, info: (i, 0))] * (n_head // 2)
            + [pl.BlockSpec((n_head // 2, rows, share), lambda i, info: (0, i, 0))],
        ),
        out_shape=[kept_shape((chunk_len, share), BF16)] * (n_head // 2)
        + [kept_shape((n_head // 2, chunk_len, share), BF16)],
        compiler_params=params(32),
        cost_estimate=cost(2.0 * chunk_len * model * rows3, 8e6),
        name="spread",
    )(info, *(held(d) for d in d_all), held(w_t), held(direct))


def settle(own, pieces, info):
    pieces = [own] + pieces
    n_head = len(pieces)
    count, share = own.shape
    rows = count // CHUNKS

    def body(info, *refs):
        for e in range(n_head):
            for c in range(CHUNKS):
                at = (c * n_head + (info[0] ^ e)) * rows
                refs[-1][pl.ds(pl.multiple_of(at, rows), rows), :] = refs[e][
                    c * rows : (c + 1) * rows, :
                ]

    return pl.pallas_call(
        body,
        grid_spec=pltpu.PrefetchScalarGridSpec(
            num_scalar_prefetch=1,
            grid=(1,),
            in_specs=[whole((count, share))] * n_head,
            out_specs=whole((n_head * count, share)),
        ),
        out_shape=shape((n_head * count, share), BF16),
        compiler_params=params(16),
        cost_estimate=cost(0, n_head * count * share * 4),
        name="settle",
    )(info, *pieces)


def on_device(
    n_batch,
    n_head,
    hidden_in,
    cotangent,
    doc_ids,
    lengths,
    w_query,
    w_key,
    w_value,
    w_out,
    w_up,
    w_gate,
    w_down,
    scale_qk,
    scale_up,
    scale_gate,
    alpha_attn,
    alpha_ffn,
):
    _, row_len, share = hidden_in.shape
    model = share * n_head
    cols = w_query.shape[1]
    chunk_len = row_len // CHUNKS
    rows = chunk_len // n_head
    me = lax.axis_index("head")
    chunks = range(CHUNKS)
    x_own, cot_own = hidden_in[0], cotangent[0]

    docs = doc_ids[0]
    column = jnp.arange(row_len, dtype=jnp.int32)
    starts = sum(
        jnp.where(docs > d, jnp.sum((docs == d).astype(jnp.int32)), 0) for d in range(5)
    ).astype(jnp.int32)
    position = (column - starts).astype(F32)
    frequency = 10000.0 ** (-(jnp.arange(HALF, dtype=F32) * 2.0 / HD))
    angles = frequency[:, None] * position[None, :]
    cosine, sine = jnp.cos(angles), jnp.sin(angles)
    info = jnp.concatenate(
        [me[None].astype(jnp.int32), lengths.astype(jnp.int32), starts[::BLOCK] // BLOCK]
    )
    starts = starts[None, :]
    gain = scale_qk[:, None]
    up_scale, gate_scale = scale_up[None, :], scale_gate[None, :]
    attn_alpha, ffn_alpha = alpha_attn[None, :], alpha_ffn[None, :]

    def part(values, c):
        return lax.slice_in_dim(values, c * chunk_len, (c + 1) * chunk_len, axis=0)

    def block_of(values, e):
        return lax.dynamic_slice_in_dim(values, (me ^ e) * rows, rows, 0)

    order = Order()
    pair = min(2, cols // HD) * HD
    pairs = cols // pair
    far = n_head // 2
    place = lax.axis_index("batch")[None].astype(jnp.int32)

    bit = lax.axis_index("batch") % 2
    own = jnp.stack([me, bit]).astype(jnp.int32)

    x_far = gather_far(part(x_own, 0), n_head)
    (w_t, out_half, cot_near, cot_far), x_far = order.run(
        lambda w: prepare(w, w_key, w_value, w_out, cot_own, own, pair, n_head),
        w_query,
        beside=x_far,
    )
    buffers, x_pieces, o_own, o_moving = [], [], [], []
    for c in chunks:
        x_pieces.append(gather_near(x_far, n_head))
        beside = []
        if c == 0:
            halves = {
                e: swap(after(out_half, order.last), "head", e, n_head) for e in range(2, n_head, 2)
            }
            beside = [halves]
        else:
            cot_moving = Exchange(after(cot_near, order.last), after(cot_far, order.last), n_head)
            beside = [o_moving[0].flying, cot_moving.flying, out_far]
        if c < CHUNKS - 1:
            beside.append(gather_far(after(part(x_own, c + 1), order.last), n_head))
        (buffers, (o_chunk, near, far_blocks)), beside = order.run(
            lambda w: attend_chunk(
                c, x_pieces[c], w, cosine, sine, gain, starts, info, buffers, row_len, chunk_len
            ),
            w_t,
            need=x_pieces[c],
            beside=beside,
        )
        o_own.append(o_chunk)
        o_moving.append(Exchange(near, far_blocks, n_head))
        if c < CHUNKS - 1:
            x_far = beside[-1]
        if c == 0:
            out_far = {e: (v, swap(v, "batch", 1, n_batch)) for e, v in beside[0].items()}
        else:
            o_first = o_moving[0].finish(beside[0])
            cot_blocks = cot_moving.finish(beside[1])
            out_far = beside[2]

    out_far = {
        e: jnp.where(
            bit == 0, jnp.concatenate([v, w], axis=1), jnp.concatenate([w, v], axis=1)
        )
        for e, (v, w) in out_far.items()
    }
    out_far[0] = w_out
    out_pieces = gather_near(out_far, n_head)

    state, joined, h_far, h_fars = [], [], None, []
    o_came = o_first
    for c in chunks:
        o_pieces = [o_own[c]] + o_came
        beside = [h_far, o_moving[c + 1].flying if c < CHUNKS - 1 else None]
        (joined, y, x_rows, h_one, h_low), beside = order.run(
            lambda first: project(
                c,
                joined,
                [first] + o_pieces[1:],
                out_pieces,
                x_pieces[c],
                attn_alpha,
                info,
                chunk_len,
            ),
            o_pieces[0],
            need=o_pieces[1:] + out_pieces,
            beside=beside,
        )
        joined = [joined]
        if c < CHUNKS - 1:
            o_came = o_moving[c + 1].finish(beside[1])
        if c:
            h_fars = [beside[0]]
        state.append((y, x_rows, h_one))
        h_far = gather_far(h_low, n_head)
    cot_pieces = [cot_own] + cot_blocks

    fed, raws, z_terms, sent = [], [], None, None
    for c in chunks:
        h_pieces = gather_near(h_fars[c] if c < len(h_fars) else h_far, n_head)
        beside = [h_far if c < CHUNKS - 1 else None, z_terms]
        (kept, raw, z_even, z_odd), (h_next, z_done) = order.run(
            lambda first: feed(
                [first] + h_pieces[1:], w_up, w_gate, w_down, up_scale, gate_scale
            ),
            h_pieces[0],
            need=h_pieces[1:] + [sent],
            beside=beside,
        )
        if c < CHUNKS - 1:
            h_far = h_next
        fed.append(kept)
        raws.append(raw)
        z_near = reduce_near(z_odd, n_head)
        if c < CHUNKS - 1:
            z_terms, sent = reduce_far(z_even, z_near, n_head)

    two = []

    def mid_step(c, terms, beside, need=()):
        nonlocal two
        (two, dz, direct, alpha_sum), beside = order.run(
            lambda first: middle(
                c, two, [first] + terms[1:], cot_pieces, state[c][2], ffn_alpha, info
            ),
            terms[0],
            need=terms[1:] + list(need),
            beside=beside,
        )
        return dz, direct, alpha_sum, beside

    def unfeed_step(c, dz_pieces, beside, need=()):
        return order.run(
            lambda first: unfeed(
                [first] + dz_pieces[1:],
                *raws[c],
                w_up,
                w_gate,
                w_down,
                up_scale,
                gate_scale,
                n_head,
            ),
            dz_pieces[0],
            need=dz_pieces[1:] + list(need),
            beside=beside,
        )

    dz, direct, alpha_sum, z_near = mid_step(0, z_done, z_near)
    directs, ffn_alphas = [direct], [alpha_sum]
    dz_far = gather_far(dz, n_head)
    z_even = [z_even[0]] + [after(p, dz_far[far]) for p in z_even[1:]]
    z_terms, sent = reduce_far(z_even, z_near, n_head)
    dz_pieces = gather_near(dz_far, n_head)
    (low_first, scales_first, dh_even, dh_odd, dz_first), z_terms = unfeed_step(
        0, dz_pieces, z_terms, need=[sent]
    )
    dh_near = reduce_near(dh_odd, n_head)
    dz, direct, alpha_sum, dh_near = mid_step(1, z_terms, dh_near)
    directs.append(direct)
    ffn_alphas.append(alpha_sum)
    dz_far = gather_far(dz, n_head)
    firsts, dz_far = order.run(
        lambda v: weigh_feed(v, fed[0][1], dz_first, *low_first), fed[0][0], beside=dz_far
    )
    dz_pieces = gather_near(dz_far, n_head)
    dh_even = [dh_even[0]] + [after(p, dz_far[far]) for p in dh_even[1:]]
    dh_terms, sent = reduce_far(dh_even, dh_near, n_head)
    dz_last, _ = order.run(
        lambda first: join([first] + dz_pieces[1:]), dz_pieces[0], need=dz_pieces[1:] + [sent]
    )
    grad_down, _ = order.run(
        lambda v: (firsts[0].astype(F32) + dot(fed[1][0], v, 0, 0)).astype(BF16), dz_last
    )
    sum_down = BatchSum(grad_down, n_batch)
    (low_last, scales_last, dh_even, dh_odd, _), dh_terms = unfeed_step(
        1, [dz_last], dh_terms, need=[sum_down.sent]
    )
    scale_sums = [jnp.concatenate(s, axis=0) for s in (scales_first, scales_last)]
    dh_near = reduce_near(dh_odd, n_head)

    zeros, alphas, dys = [], [], []

    def back(c, terms, beside, need=()):
        y, x_rows, _ = state[c]
        (dy, d_pieces, zero, grad_alpha_attn), beside = order.run(
            lambda first: unproject(
                c, dys, [first] + terms[1:], out_pieces, directs[c], y, x_rows, attn_alpha
            ),
            terms[0],
            need=terms[1:] + list(need),
            beside=beside,
        )
        dys[:] = [dy]
        zeros.append(zero)
        alphas.append(grad_alpha_attn)
        return d_pieces[0], Exchange(d_pieces[1], d_pieces[2], n_head), beside

    def beside_sums(step, value, sums, beside=(), need=(), first=False):
        out, (got, beside) = order.run(
            step, value, need=need, beside=([b.flying for b in sums], beside)
        )
        for i, (b, v) in enumerate(zip(sums, got, strict=True)):
            b.advance(after(v, sums[0].sent) if i and first else v)
        return out, beside

    grad_up, dh_near = beside_sums(
        lambda v: (firsts[1].astype(F32) + dot(fed[1][1], v, 0, 0)).astype(BF16),
        low_last[0],
        [sum_down],
        dh_near,
    )
    sum_up = BatchSum(grad_up, n_batch)
    dh_first, (dh_terms, sent) = dh_terms, reduce_far(dh_even, dh_near, n_head)
    grad_gate, _ = order.run(
        lambda v: (firsts[2].astype(F32) + dot(fed[1][1], v, 0, 0)).astype(BF16),
        low_last[1],
        need=[sent, sum_down.sent, sum_up.sent],
    )
    do_own, do_first, (dh_terms, got) = back(0, dh_first, (dh_terms, sum_down.flying))
    sum_down.advance(got)
    do_pieces = [do_own]
    do_own, do_last, do_came = back(1, dh_terms, do_first.flying, need=[sum_down.sent])
    do_pieces += do_first.finish(do_came)
    out_terms, do_came = beside_sums(
        lambda o: dot(o, dys[0], 0, 0).astype(BF16),
        joined[0],
        [sum_down, sum_up],
        do_last.flying,
    )
    sum_gate = BatchSum(after(grad_gate, order.last), n_batch)
    do_pieces += [do_own] + do_last.finish(do_came)
    alpha_sums = jnp.concatenate([sum(alphas), sum(ffn_alphas)], axis=0)
    alpha_rows = jnp.pad(alpha_sums.astype(BF16), ((0, 14), (0, 0)))
    out_blocks = [
        jnp.concatenate([out_terms[e * cols : (e + 1) * cols], alpha_rows], axis=0)
        for e in range(n_head)
    ]
    out_near = reduce_near(out_blocks[1::2], n_head)
    d_all, gains = [], []

    def attention_back(g, sums, beside, need=()):
        (d_pair, grad_gain), beside = beside_sums(
            lambda first: unattend(
                g, [first] + do_pieces[1:], buffers, starts, cosine, sine, gain, info, n_head
            ),
            do_pieces[0],
            sums,
            beside,
            need=do_pieces[1:] + list(need),
        )
        d_pair = d_pair.reshape(3 * pair, row_len)
        d_all.append(d_pair)
        gains.append(grad_gain[:, 0])
        return d_pair, beside

    big = [sum_down, sum_up, sum_gate]
    grads = []
    if pairs > 1:
        d_pair, out_near = attention_back(
            0, [sum_down, sum_up], out_near, need=[b.sent for b in big]
        )
        out_flying, out_sent = reduce_far(out_blocks[::2], out_near, n_head)
        grad_pair, _ = beside_sums(
            lambda d: weigh(d, x_pieces, chunk_len),
            d_pair,
            [sum_gate],
            need=[sum_down.sent, sum_up.sent, out_sent],
        )
        grads.append(grad_pair)
    else:
        out_flying, _ = reduce_far(out_blocks[::2], out_near, n_head)
    ahead = [BatchSum(g, n_batch) for g in grads] if n_batch == 8 else []
    d_pair, out_flying = attention_back(
        pairs - 1,
        [sum_down, sum_up] + ahead,
        out_flying,
        need=[sum_gate.sent] + [b.sent for b in ahead],
    )
    out_sum = term_sum(out_flying)
    grad_pair, _ = beside_sums(
        lambda d: weigh(d, x_pieces, chunk_len),
        d_pair,
        [sum_gate],
        need=[sum_down.sent, sum_up.sent],
    )
    small = jnp.concatenate(
        [out_sum[cols : cols + 2]]
        + [
            jnp.pad(v, ((0, 0), (0, model - v.shape[1])))
            for v in (sum(scale_sums), jnp.concatenate(gains)[None])
        ],
        axis=0,
    )
    if ahead:
        grads = []
    grads += [grad_pair, out_sum[:cols].astype(BF16)]
    if 4 * cols % (16 * n_batch):
        grads.append(jnp.zeros((-4 * cols % (16 * n_batch), model), BF16))
    grads = jnp.concatenate(grads, axis=0)
    ranges = [2 * b.values.shape[0] for b in ahead] + [grads.shape[0]]
    sum_attn = BatchSum(grads, n_batch, direct=True, before=[b.values for b in ahead])

    def spread_step(c, sums, beside=(), need=()):
        return beside_sums(
            lambda w: spread(c, chunk_len, d_all, w, zeros[c], info, n_head),
            w_t,
            sums,
            beside,
            need=need,
            first=c > 0,
        )

    def land(sums, beside=()):
        got, beside = lax.optimization_barrier(([b.flying for b in sums], beside))
        for i, (b, v) in enumerate(zip(sums, got, strict=True)):
            b.advance(after(v, sums[0].sent) if i else v)
        return jax.tree.map(lambda v: after(v, sums[0].sent), beside)

    two_moving = Exchange(after(two[1], order.last), after(two[2], order.last), n_head)
    d_first, two_came = spread_step(
        0, [sum_up, sum_gate, sum_down], two_moving.flying, need=[sum_attn.sent]
    )
    two_pieces = two_moving.finish(two_came)
    dx_near = reduce_near(d_first[-1], n_head)
    small_swaps = [1 << i for i in range(n_batch.bit_length() - 1)]
    d_last, (dx_near, small_far) = spread_step(
        1,
        [sum_attn, sum_up, sum_gate],
        (dx_near, swap(small, "batch", small_swaps.pop(0), n_batch)),
        need=[sum_up.sent, sum_gate.sent],
    )
    small = small + small_far
    dx_first, _ = reduce_far(d_first[:-1], dx_near, n_head)
    down_done = assemble(sum_down.finish(), place)
    land([sum_attn, sum_up, sum_gate])
    dx_first = land([sum_attn, sum_gate], dx_first)
    small = after(small, sum_attn.sent)
    for bit_now in small_swaps:
        small = small + swap(small, "batch", bit_now, n_batch)
    dx_near = reduce_near(after(d_last[-1], sum_attn.sent), n_head)
    dx_last, _ = reduce_far(d_last[:-1], dx_near, n_head)
    while len(sum_attn.todo) > 1:
        land([sum_attn])
    hidden_out = settle(two[0], two_pieces, info)
    grad_down = down_done
    grad_up = assemble(sum_up.finish(), place)
    grad_gate = assemble(sum_gate.finish(), place)
    grad_query, grad_key, grad_value, grad_out = assemble_turned(
        sum_attn.finish(), place, info, cols, n_head, pairs, ranges
    )
    grad_hidden = jnp.concatenate([term_sum(dx_first), term_sum(dx_last)], axis=0)[None]
    alpha_own = lax.dynamic_slice_in_dim(small[:2], me * share, share, 1)
    hidden_units = w_up.shape[1]

    return (
        hidden_out[None],
        grad_hidden,
        grad_query,
        grad_key,
        grad_value,
        grad_out,
        grad_up,
        grad_gate,
        grad_down,
        small[4, :cols],
        small[2, :hidden_units],
        small[3, :hidden_units],
        alpha_own[0],
        alpha_own[1],
    )


def solution(mesh):
    split = P("batch", None, "head")
    by_col, by_row, by_head = P(None, "head"), P("head", None), P("head")
    return jax.shard_map(
        functools.partial(on_device, mesh.shape["batch"], mesh.shape["head"]),
        mesh=mesh,
        in_specs=(split, split, P("batch", None), P("batch"))
        + (by_col, by_col, by_col, by_row, by_col, by_col, by_row)
        + (by_head, by_head, by_head, P(), P()),
        out_specs=(split, split, by_col, by_col, by_col, by_row, by_col, by_col, by_row)
        + (by_head,) * 5,
        check_vma=False,
    )
```

```python
import functools
import math

import jax
import jax.numpy as jnp
from jax import lax
from jax.experimental import pallas as pl
from jax.experimental.pallas import tpu as pltpu
from jax.sharding import PartitionSpec as P

HD = 64
HALF = HD // 2
VALUE_ROWS = 80
EPSILON = 1e-06
BLOCK = 256
QUERIES = 512
KEYS = 512
CHUNKS = 2
F32 = jnp.float32
BF16 = jnp.bfloat16
MIB = 1024 * 1024


def dot(left, right, left_dim=1, right_dim=0):
    return lax.dot_general(
        left, right, (((left_dim,), (right_dim,)), ((), ())), preferred_element_type=F32
    )


def shape(dims, dtype):
    return jax.ShapeDtypeStruct(dims, dtype)


def kept_shape(dims, dtype):
    return pltpu.HBM(dims, dtype)


def held(array):
    return pltpu.with_memory_space_constraint(array, pltpu.HBM)


def after(value, *others):
    others = [o for o in others if o is not None]
    return lax.optimization_barrier((value, *others))[0] if others else value


def whole(dims):
    return pl.BlockSpec(dims, lambda *_: (0,) * len(dims))


def term_spec(term):
    if term.ndim == 3:
        return pl.BlockSpec((None, *term.shape[1:]), lambda *_: (0, 0, 0))
    return whole(term.shape)


def params(mib):
    return pltpu.CompilerParams(vmem_limit_bytes=mib * MIB)


def cost(flops, moved):
    return pl.CostEstimate(flops=int(flops), bytes_accessed=int(moved), transcendentals=0)


class Order:
    def __init__(self):
        self.last = None

    def run(self, step, value, need=(), beside=()):
        out = step(after(value, self.last, *need))
        out, beside = lax.optimization_barrier((out, beside))
        self.last = jax.tree.leaves(out)[0]
        return out, beside


def swap(value, axis, mask, size):
    return lax.ppermute(value, axis, [(i, i ^ mask) for i in range(size)])


def gather_far(own, size):
    pieces = {0: own}
    bit = size // 2
    while bit > 1:
        pieces.update({e | bit: swap(p, "head", bit, size) for e, p in pieces.items()})
        bit //= 2
    return pieces


def gather_near(far, size):
    pieces = dict(far)
    pieces.update({e | 1: swap(p, "head", 1, size) for e, p in far.items()})
    return [pieces[e] for e in range(size)]


class Exchange:
    def __init__(self, near, far, size):
        self.size = size
        if size == 4:
            self.flying = [swap(near, "head", 1, size), swap(far, "head", 2, size)]
        else:
            blocks = [near, *far]
            self.flying = [swap(p, "head", e, size) for e, p in enumerate(blocks, 1)]

    def finish(self, flying):
        if self.size != 4:
            return flying
        near, far = flying
        return [near, far[0], swap(far[1], "head", 1, self.size)]


def total(terms):
    if len(terms) == 1:
        return terms[0]
    return sum(t.astype(F32) for t in terms).astype(BF16)


def reduce_near(odd, size):
    return jax.tree.map(lambda p: swap(p, "head", 1, size), odd)


def reduce_far(even, near, size):
    held = {2 * i: [p, near[i]] for i, p in enumerate(even)}
    bit, sent = 2, None
    while bit < size:
        for e in [e for e in held if e & bit]:
            sent = total(held.pop(e))
            got = swap(sent, "head", bit, size)
            held[e ^ bit].append(got)
        bit *= 2
    return held[0], sent


def term_sum(terms):
    return sum((t[0] if t.ndim == 3 else t).astype(F32) for t in terms)


def sum_small(value, axis, size):
    bit = 1
    while bit < size:
        value = value + swap(value, axis, bit, size)
        bit *= 2
    return value


def halve(values, bit, place):
    rows = values.shape[0] // 2
    own = (place & bit) // bit
    return tuple(
        lax.dynamic_slice_in_dim(values, part * rows, rows, 0) for part in (own, 1 - own)
    )


class BatchSum:
    def __init__(self, values, size, direct=False, before=()):
        self.size = size
        self.place = lax.axis_index("batch")
        self.bits = [1 << i for i in range(size.bit_length() - 1)]
        self.todo = [("halve", b) for b in self.bits] + [("join", b) for b in reversed(self.bits)]
        if direct and size <= 8:
            self.bits = self.bits[:1] + self.bits[:0:-1]
            self.todo = [("halve", 1), ("scatter", 0), ("gather", 0), ("join", 1)]
        self.values, self.mine, self.flying, self.sent = values, None, None, None
        self.before = list(before)
        self.start()

    def start(self):
        kind, bit = self.todo[0]
        self.sent = self.values
        if kind == "halve":
            self.mine, self.sent = halve(self.values, bit, self.place)
        others = range(1, self.size // 2)
        if kind == "scatter":
            rows = self.values.shape[0] * 2 // self.size
            own = self.place // 2
            blocks = [
                lax.dynamic_slice_in_dim(self.values, (own ^ d) * rows, rows, 0)
                for d in range(self.size // 2)
            ]
            self.mine, self.sent = blocks[0], blocks[-1]
            self.flying = [swap(blocks[d], "batch", 2 * d, self.size) for d in others]
        elif kind == "gather":
            self.flying = [swap(self.values, "batch", 2 * d, self.size) for d in others]
        else:
            self.flying = swap(self.sent, "batch", bit, self.size)

    def advance(self, got):
        kind, _ = self.todo.pop(0)
        if not self.todo:
            self.parts = [self.values, got]
        elif kind == "halve":
            self.values = total([self.mine, got])
        elif kind == "scatter":
            self.values = total([self.mine] + got)
        else:
            got = got if kind == "gather" else [got]
            self.values = jnp.concatenate([self.values] + got, axis=0)
        if self.before:
            self.values = jnp.concatenate(self.before + [self.values], axis=0)
            self.before = []
        if self.todo:
            self.start()

    def finish(self):
        while self.todo:
            self.advance(self.flying)
        return self.parts, self.bits


def store_blocks(place, summed, refs, out):
    (first, _), bits = summed
    count = 1 << len(bits)
    rows = 2 * first.shape[0] // count
    for p in range(count):
        at = 0
        for level, bit in enumerate(bits):
            other = p >> (len(bits) - 1 - level) & 1
            at = at + (((place // bit) % 2) ^ other) * ((count >> (level + 1)) * rows)
        ref, row = refs[p * 2 // count], (p % (count // 2)) * rows
        out[pl.ds(pl.multiple_of(at, rows), rows), :] = ref[row : row + rows, :].astype(out.dtype)


def segments(first, count, ranges):
    half, skip = sum(ranges) // 2, 0
    found = []
    for size in ranges:
        part = size // 2
        for side in range(2):
            low, high = max(first, 0), min(first + count, part)
            if low < high:
                found.append((side * half + skip + low, low - first, high - low))
            first -= part
        skip += part
    return found


def assemble(summed, place):
    parts, _ = summed
    rows, width = parts[0].shape

    def body(place, own_ref, other_ref, out):
        store_blocks(place[0], summed, (own_ref, other_ref), out)

    return pl.pallas_call(
        body,
        grid_spec=pltpu.PrefetchScalarGridSpec(
            num_scalar_prefetch=1,
            grid=(1,),
            in_specs=[whole((rows, width))] * 2,
            out_specs=whole((2 * rows, width)),
        ),
        out_shape=shape((2 * rows, width), F32),
        compiler_params=params(24),
        cost_estimate=cost(0, rows * width * 12),
        name="assemble",
    )(place, *parts)


def assemble_turned(summed, place, info, cols, n_head, pairs, ranges):
    parts, _ = summed
    width = cols // pairs
    rows, model = parts[0].shape
    share = model // n_head

    def body(place, info, own_ref, other_ref, q_out, k_out, v_out, o_out, room):
        store_blocks(place[0], summed, (own_ref, other_ref), room)
        for g in range(pairs):
            for i, out in enumerate((q_out, k_out, v_out)):
                for row, offset, count in segments((3 * g + i) * width, width, ranges):
                    lanes = slice(g * width + offset, g * width + offset + count)
                    for e in range(n_head):
                        at = pl.ds(pl.multiple_of((info[0] ^ e) * share, share), share)
                        block = room[row : row + count, e * share : (e + 1) * share]
                        out[at, lanes] = block.T.astype(F32)
        for row, offset, count in segments(3 * cols, cols, ranges):
            o_out[offset : offset + count, :] = room[row : row + count, :].astype(F32)

    return pl.pallas_call(
        body,
        grid_spec=pltpu.PrefetchScalarGridSpec(
            num_scalar_prefetch=2,
            grid=(1,),
            in_specs=[whole((rows, model))] * 2,
            out_specs=[whole((model, cols))] * 3 + [whole((cols, model))],
            scratch_shapes=[pltpu.VMEM((2 * rows, model), BF16)],
        ),
        out_shape=[shape((model, cols), F32)] * 3 + [shape((cols, model), F32)],
        compiler_params=params(32),
        cost_estimate=cost(0, cols * model * 24),
        name="assemble_turned",
    )(place, info, *parts)


def visible(first_key, first_query, starts, length, rows, cols):
    key = first_key + lax.broadcasted_iota(jnp.int32, (rows, cols), 0)
    query = first_query + lax.broadcasted_iota(jnp.int32, (rows, cols), 1)
    last = jnp.minimum(query, length - 1)
    return (key >= starts) & ((key <= last) | (key == query))


def prepare(w_query, w_key, w_value, w_out, cotangent, own, pair, n_head):
    model, cols = w_query.shape
    row_len, share = cotangent.shape
    rows = row_len // CHUNKS // n_head

    def body(own, q_ref, k_ref, v_ref, o_ref, c_ref, out, half, near, far_blocks):
        for g in range(cols // pair):
            for i, ref in enumerate((q_ref, k_ref, v_ref)):
                first = (3 * g + i) * pair
                out[first : first + pair, :] = ref[:, g * pair : (g + 1) * pair].T
        half[...] = o_ref[:, pl.ds(pl.multiple_of(own[1] * (model // 2), model // 2), model // 2)]
        for e in range(1, n_head):
            for c in range(CHUNKS):
                at = (c * n_head + (own[0] ^ e)) * rows
                block = c_ref[pl.ds(pl.multiple_of(at, rows), rows), :]
                if e == 1:
                    near[c * rows : (c + 1) * rows, :] = block
                else:
                    far_blocks[e - 2, c * rows : (c + 1) * rows, :] = block

    outs = pl.pallas_call(
        body,
        grid_spec=pltpu.PrefetchScalarGridSpec(
            num_scalar_prefetch=1,
            grid=(1,),
            in_specs=[whole((model, cols))] * 3 + [whole((cols, model)), whole((row_len, share))],
            out_specs=[
                whole((3 * cols, model)),
                whole((cols, model // 2)),
                whole((CHUNKS * rows, share)),
                whole((n_head - 2, CHUNKS * rows, share)),
            ],
        ),
        out_shape=[
            shape((3 * cols, model), BF16),
            shape((cols, model // 2), BF16),
            shape((CHUNKS * rows, share), BF16),
            shape((n_head - 2, CHUNKS * rows, share), BF16),
        ],
        compiler_params=params(24),
        cost_estimate=cost(0, 12 * cols * model),
        name="prepare",
    )(own, w_query, w_key, w_value, w_out, cotangent)
    return outs


def attend_kernel(
    chunk, n_head, heads, chunk_len, share, info, *refs
):
    refs = list(refs)
    x_refs = [refs.pop(0) for _ in range(n_head)]
    w_ref, cos_ref, sin_ref, gain_ref, start_ref = [refs.pop(0) for _ in range(5)]
    old_k, old_v = None, None
    if chunk:
        old_k, old_v = refs.pop(0), refs.pop(0)
        refs = refs[7:]
    k_ref, ve_ref, v_ref, kt_ref, qt_ref, ot_ref, inv_ref, qf_ref, kf_ref, o_ref = refs[:10]
    near_ref, far_ref, raw, acc, joined = refs[10:]
    me, length = info[0], info[1]
    cols = heads * HD
    pair = min(2, heads)
    for e in range(n_head):
        first = pl.multiple_of((me ^ e) * share, share)
        joined[:, pl.ds(first, share)] = x_refs[e][...]
    for third in range(3):
        rows = slice(third * cols, (third + 1) * cols)
        raw[rows, :] = dot(w_ref[rows, :], joined[...], 1, 1)

    def raw_row(part, h):
        return ((h // pair * 3 + part) * pair + h % pair) * HD

    cosine, sine = cos_ref[...], sin_ref[...]
    for h in range(heads):
        own = slice(h * HD, (h + 1) * HD)
        for part, factor_ref in ((0, qf_ref), (1, kf_ref)):
            base = raw_row(part, h)
            a, b = raw[base : base + HALF, :], raw[base + HALF : base + HD, :]
            front, back = a * cosine - b * sine, b * cosine + a * sine
            mean = jnp.sum(front * front + back * back, axis=0, keepdims=True) / HD
            factor = lax.rsqrt(mean + EPSILON)
            factor_ref[h] = factor
            unit = jnp.concatenate([front, back], axis=0) * factor
            low = (unit * gain_ref[own, :]).astype(BF16)
            if part == 0:
                qt_ref[own, :] = low * BF16(1.0 / math.sqrt(HD))
            else:
                kt_ref[own, :] = low
                k_ref[h] = low.T
        value = raw[raw_row(2, h) : raw_row(2, h) + HD, :].astype(BF16)
        v_ref[h] = value.T
        ve_ref[h, :HD, :] = value
        ve_ref[h, HD:, :] = jnp.ones((VALUE_ROWS - HD, chunk_len), BF16)

    before = chunk * (chunk_len // KEYS)

    def step(local, key_first, k_of, v_of, starts):
        query = slice(local * QUERIES, (local + 1) * QUERIES)
        first = chunk * chunk_len + local * QUERIES
        mask = visible(key_first, first, starts, length, KEYS, QUERIES)
        for h in range(heads):
            scores = dot(k_of(h), qt_ref[h * HD : (h + 1) * HD, query])
            probs = jnp.where(mask, jnp.exp(scores), 0.0).astype(BF16)
            acc[h] += dot(v_of(h), probs)

    for local in range(chunk_len // QUERIES):
        query = slice(local * QUERIES, (local + 1) * QUERIES)
        starts = start_ref[:, query]
        lowest = info[2 + (chunk * chunk_len + local * QUERIES) // BLOCK] * BLOCK // KEYS
        acc[...] = jnp.zeros_like(acc)
        if chunk:

            @pl.loop(lowest, before)
            def _(kb):
                at = pl.ds(pl.multiple_of(kb * KEYS, KEYS), KEYS)
                step(
                    local, kb * KEYS, lambda h: old_k[h, at, :], lambda h: old_v[h, :, at], starts
                )

        @pl.loop(jnp.maximum(lowest - before, 0), (local + 1) * QUERIES // KEYS)
        def _(kb):
            at = pl.ds(pl.multiple_of(kb * KEYS, KEYS), KEYS)
            step(
                local,
                (before + kb) * KEYS,
                lambda h: k_ref[h, at, :],
                lambda h: ve_ref[h, :, at],
                starts,
            )

        for h in range(heads):
            inverse = 1.0 / acc[h, HD : HD + 1, :]
            inv_ref[h, :, query] = inverse
            out = acc[h, :HD, :] * inverse
            ot_ref[h * HD : (h + 1) * HD, query] = out.astype(BF16)
            o_ref[query, h * HD : (h + 1) * HD] = out.T.astype(BF16)
    rows = chunk_len // n_head
    for e in range(1, n_head):
        block = o_ref[pl.ds(pl.multiple_of((me ^ e) * rows, rows), rows), :]
        if e == 1:
            near_ref[...] = block
        else:
            far_ref[e - 2] = block


def attend_chunk(
    chunk, x_pieces, w_t, cosine, sine, gain, starts, info, buffers, row_len, chunk_len
):
    n_head = len(x_pieces)
    share = x_pieces[0].shape[1]
    cols = w_t.shape[0] // 3
    heads = cols // HD
    model = w_t.shape[1]
    body = functools.partial(attend_kernel, chunk, n_head, heads, chunk_len, share)
    by_lane = lambda rows: pl.BlockSpec((rows, chunk_len), lambda i, info: (0, chunk))
    specs = [whole((chunk_len, share))] * n_head + [
        whole((3 * cols, model)),
        by_lane(HALF),
        by_lane(HALF),
        whole((cols, 1)),
        by_lane(1),
    ]
    operands = [*x_pieces, held(w_t), held(cosine), held(sine), gain, starts]
    aliases = {}
    if chunk:
        aliases = {1 + len(operands) + i: i for i in range(9)}
        specs += [whole((heads, row_len, HD)), whole((heads, VALUE_ROWS, row_len))]
        specs += [pl.BlockSpec(memory_space=pl.ANY)] * 7
        operands += buffers
    lane3 = lambda rows: pl.BlockSpec((heads, rows, chunk_len), lambda i, info: (0, 0, chunk))
    row3 = pl.BlockSpec((heads, chunk_len, HD), lambda i, info: (0, chunk, 0))
    outs = pl.pallas_call(
        body,
        grid_spec=pltpu.PrefetchScalarGridSpec(
            num_scalar_prefetch=1,
            grid=(1,),
            in_specs=specs,
            out_specs=[
                row3,
                lane3(VALUE_ROWS),
                row3,
                by_lane(cols),
                by_lane(cols),
                by_lane(cols),
                lane3(1),
                lane3(1),
                lane3(1),
                whole((chunk_len, cols)),
            ]
            + [
                whole((chunk_len // n_head, cols)),
                whole((n_head - 2, chunk_len // n_head, cols)),
            ],
            scratch_shapes=[
                pltpu.VMEM((3 * cols, chunk_len), F32),
                pltpu.VMEM((heads, VALUE_ROWS, QUERIES), F32),
                pltpu.VMEM((chunk_len, model), BF16),
            ],
        ),
        out_shape=[
            kept_shape((heads, row_len, HD), BF16),
            kept_shape((heads, VALUE_ROWS, row_len), BF16),
            kept_shape((heads, row_len, HD), BF16),
            kept_shape((cols, row_len), BF16),
            kept_shape((cols, row_len), BF16),
            kept_shape((cols, row_len), BF16),
            kept_shape((heads, 1, row_len), F32),
            kept_shape((heads, 1, row_len), F32),
            kept_shape((heads, 1, row_len), F32),
            kept_shape((chunk_len, cols), BF16),
        ]
        + [
            kept_shape((chunk_len // n_head, cols), BF16),
            kept_shape((n_head - 2, chunk_len // n_head, cols), BF16),
        ],
        input_output_aliases=aliases,
        compiler_params=params(40),
        cost_estimate=cost(16e9 / CHUNKS, 8e6),
        name="attend",
    )(info, *operands)
    return outs[:9], list(outs[9:])


def unattend_kernel(n_head, chunks, row_len, piece, pair, info, *refs):
    refs = list(refs)
    d_refs = [refs.pop(0) for _ in range(chunks * n_head)]
    k_ref, v_ref, kt_ref, qt_ref, ot_ref, inv_ref, qf_ref, kf_ref = [refs.pop(0) for _ in range(8)]
    start_ref, cos_ref, sin_ref, gain_ref = [refs.pop(0) for _ in range(4)]
    out_ref, gain_out, do_s, inner_s, dq_s, dk_s, dv_s = refs
    me, length = info[0], info[1]
    for c in range(chunks):
        for e in range(n_head):
            first = c * n_head * piece + (me ^ e) * piece
            do_s[:, pl.ds(pl.multiple_of(first, piece), piece)] = d_refs[c * n_head + e][...]
    for h in range(pair):
        own = slice(h * HD, (h + 1) * HD)
        product = do_s[own, :].astype(F32) * ot_ref[own, :].astype(F32)
        inner_s[h] = jnp.sum(product, axis=0, keepdims=True)
    dq_s[...] = jnp.zeros_like(dq_s)
    dk_s[...] = jnp.zeros_like(dk_s)
    dv_s[...] = jnp.zeros_like(dv_s)

    ratio = QUERIES // BLOCK

    @pl.loop(0, row_len // QUERIES)
    def _(qb):
        query = pl.ds(pl.multiple_of(qb * QUERIES, QUERIES), QUERIES)
        starts = start_ref[:, query]

        @pl.loop(info[2 + qb * ratio], (qb + 1) * ratio)
        def _(kb):
            key = pl.ds(pl.multiple_of(kb * BLOCK, BLOCK), BLOCK)
            mask = visible(kb * BLOCK, qb * QUERIES, starts, length, BLOCK, QUERIES)
            for h in range(pair):
                own = slice(h * HD, (h + 1) * HD)
                q_block, do_block = qt_ref[own, query], do_s[own, query]
                scores = dot(k_ref[h, key, :], q_block)
                probs = jnp.where(mask, jnp.exp(scores), 0.0) * inv_ref[h, :, query]
                d_probs = dot(v_ref[h, key, :], do_block)
                d_scores = (probs * (d_probs - inner_s[h, :, query])).astype(BF16)
                dv_s[own, key] += dot(do_block, probs.astype(BF16), 1, 1)
                dk_s[own, key] += dot(q_block, d_scores, 1, 1)
                dq_s[own, query] += dot(kt_ref[own, key], d_scores)

    for h in range(pair):
        own = slice(h * HD, (h + 1) * HD)
        gain = gain_ref[own, :]
        summed = jnp.zeros((HD, 1), F32)
        for part, low_ref, grad_ref, factor_ref in (
            (0, qt_ref, dq_s, qf_ref),
            (1, kt_ref, dk_s, kf_ref),
        ):
            scale = math.sqrt(HD) if part == 0 else 1.0
            unit = low_ref[own, :].astype(F32) * (scale / gain)
            grad = grad_ref[own, :]
            if part == 0:
                grad = grad * (1.0 / math.sqrt(HD))
            summed += jnp.sum(grad * unit, axis=1, keepdims=True)
            grad = grad * gain
            mean = jnp.sum(grad * unit, axis=0, keepdims=True) / HD
            grad = (grad - unit * mean) * factor_ref[h]
            front, back = grad[:HALF], grad[HALF:]
            cosine, sine = cos_ref[...], sin_ref[...]
            out_ref[part, h * HD : h * HD + HALF, :] = (front * cosine + back * sine).astype(BF16)
            out_ref[part, h * HD + HALF : (h + 1) * HD, :] = (
                back * cosine - front * sine
            ).astype(BF16)
        out_ref[2, own, :] = dv_s[own, :].astype(BF16)
        gain_out[own, :] = summed


def unattend(index, do_pieces, buffers, starts, cosine, sine, gain, info, n_head):
    k, _, v, kt, qt, ot, inv, qf, kf = buffers
    chunks = len(do_pieces) // n_head
    cols, piece = do_pieces[0].shape
    heads, row_len, _ = k.shape
    pair = min(2, heads)
    rows = pair * HD
    by_rows = lambda width: pl.BlockSpec((rows, width), lambda g, info: (index, 0))
    by_head = lambda a, b: pl.BlockSpec((pair, a, b), lambda g, info: (index, 0, 0))
    return pl.pallas_call(
        functools.partial(unattend_kernel, n_head, chunks, row_len, piece, pair),
        grid_spec=pltpu.PrefetchScalarGridSpec(
            num_scalar_prefetch=1,
            grid=(1,),
            in_specs=[by_rows(piece)] * (chunks * n_head)
            + [by_head(row_len, HD)] * 2
            + [by_rows(row_len)] * 3
            + [by_head(1, row_len)] * 3
            + [whole((1, row_len)), whole((HALF, row_len)), whole((HALF, row_len)), by_rows(1)],
            out_specs=[whole((3, rows, row_len)), whole((rows, 1))],
            scratch_shapes=[
                pltpu.VMEM((rows, row_len), BF16),
                pltpu.VMEM((pair, 1, row_len), F32),
                pltpu.VMEM((rows, row_len), F32),
                pltpu.VMEM((rows, row_len), F32),
                pltpu.VMEM((rows, row_len), F32),
            ],
        ),
        out_shape=[kept_shape((3, rows, row_len), BF16), shape((rows, 1), F32)],
        compiler_params=params(32),
        cost_estimate=cost(22e9, 6e6),
        name="unattend",
    )(info, *do_pieces, k, v, kt, qt, ot, inv, qf, kf, starts, cosine, sine, gain)


def norm(values):
    factor = lax.rsqrt(jnp.mean(values * values, axis=-1, keepdims=True) + EPSILON)
    return values * factor, factor


def norm_back(grad, unit, factor):
    return factor * (grad - unit * jnp.mean(grad * unit, axis=-1, keepdims=True))


def project_kernel(n_head, share, kept, info, *refs):
    o_refs, w_refs = refs[:n_head], refs[n_head : 2 * n_head]
    x_refs = refs[2 * n_head : 3 * n_head]
    alpha_ref = refs[3 * n_head]
    cat_ref, y_ref, x_ref, h_ref, low_ref = refs[3 * n_head + 1 + kept :]
    me = info[0]
    cols = w_refs[0].shape[0]
    y = dot(o_refs[0][...], w_refs[0][...])
    for e in range(1, n_head):
        y += dot(o_refs[e][...], w_refs[e][...])
    for e in range(n_head):
        cat_ref[:, e * cols : (e + 1) * cols] = o_refs[e][...]
    for e in range(n_head):
        first = pl.multiple_of((me ^ e) * share, share)
        x_ref[:, pl.ds(first, share)] = x_refs[e][...]
    y_ref[...] = y
    h_zero = x_ref[...].astype(F32)
    h_one, _ = norm(h_zero + alpha_ref[...] * (norm(y)[0] - h_zero))
    h_ref[...] = h_one
    low_ref[...] = h_one.astype(BF16)


def project(chunk, kept, o_pieces, w_pieces, x_pieces, alpha, info, chunk_len):
    n_head = len(o_pieces)
    cols, model = w_pieces[0].shape
    share = x_pieces[0].shape[1]
    rows = chunk_len // n_head
    mine = lambda width: pl.BlockSpec((rows, width), lambda i, info: (info[0], 0))
    return pl.pallas_call(
        functools.partial(project_kernel, n_head, share, len(kept)),
        grid_spec=pltpu.PrefetchScalarGridSpec(
            num_scalar_prefetch=1,
            grid=(1,),
            in_specs=[mine(cols)]
            + [whole((rows, cols))] * (n_head - 1)
            + [whole((cols, model))] * n_head
            + [mine(share)] * n_head
            + [whole((1, model))]
            + [pl.BlockSpec(memory_space=pl.ANY)] * len(kept),
            out_specs=[pl.BlockSpec((rows, n_head * cols), lambda i, info: (chunk, 0))]
            + [whole((rows, model))] * 4,
        ),
        input_output_aliases={3 * n_head + 2 + i: i for i in range(len(kept))},
        out_shape=[
            kept_shape((CHUNKS * rows, n_head * cols), BF16),
            kept_shape((rows, model), F32),
            kept_shape((rows, model), BF16),
            kept_shape((rows, model), F32),
            shape((rows, model), BF16),
        ],
        compiler_params=params(32),
        cost_estimate=cost(2.0 * rows * model * model, 6e6),
        name="project",
    )(info, *o_pieces, *w_pieces, *x_pieces, alpha, *kept)


def feed_kernel(n_head, rows, *refs):
    h_refs = refs[:n_head]
    up_ref, gate_ref, down_hbm, su_ref, sg_ref = refs[n_head : n_head + 5]
    m_ref, cat_hbm, u_ref, g_ref = refs[n_head + 5 : n_head + 9]
    z_refs = refs[n_head + 9 : 2 * n_head + 9]
    cat, mixed_s, down, cat_sem, down_sem = refs[2 * n_head + 9 :]
    tile = pl.program_id(0)
    keep = pltpu.make_async_copy(cat, cat_hbm, cat_sem)
    fetch = pltpu.make_async_copy(down_hbm, down, down_sem)

    @pl.when(tile == 0)
    def _():
        fetch.start()
        for e in range(n_head):
            cat[e * rows : (e + 1) * rows, :] = h_refs[e][...]
        keep.start()

    up_raw = dot(cat[...], up_ref[...])
    gate_raw = dot(cat[...], gate_ref[...])
    u_ref[...] = up_raw.astype(BF16)
    g_ref[...] = gate_raw.astype(BF16)
    gate = gate_raw * sg_ref[...]
    mixed = (up_raw * su_ref[...] * (gate * jax.nn.sigmoid(gate))).astype(BF16)
    m_ref[...] = mixed
    width = m_ref.shape[1]
    mixed_s[:, pl.ds(pl.multiple_of(tile * width, width), width)] = mixed

    @pl.when(tile == pl.num_programs(0) - 1)
    def _():
        fetch.wait()
        z = dot(mixed_s[...], down[...])
        for e in range(n_head):
            z_refs[e][...] = z[e * rows : (e + 1) * rows, :].astype(BF16)
        keep.wait()


def feed(h_pieces, w_up, w_gate, w_down, scale_up, scale_gate):
    n_head = len(h_pieces)
    rows, model = h_pieces[0].shape
    hidden = w_up.shape[1]
    tile = min(256, hidden // 2)
    count = n_head * rows
    by_col = lambda height: pl.BlockSpec((height, tile), lambda n: (0, n))
    anywhere = pl.BlockSpec(memory_space=pl.ANY)
    outs = pl.pallas_call(
        functools.partial(feed_kernel, n_head, rows),
        grid=(hidden // tile,),
        in_specs=[whole((rows, model))] * n_head
        + [by_col(model), by_col(model), anywhere, by_col(1), by_col(1)],
        out_specs=[by_col(count), anywhere, by_col(count), by_col(count)]
        + [whole((rows, model))] * n_head,
        out_shape=[
            kept_shape((count, hidden), BF16),
            kept_shape((count, model), BF16),
            kept_shape((count, hidden), BF16),
            kept_shape((count, hidden), BF16),
        ]
        + [shape((rows, model), BF16)] * n_head,
        scratch_shapes=[
            pltpu.VMEM((count, model), BF16),
            pltpu.VMEM((count, hidden), BF16),
            pltpu.VMEM((hidden, model), BF16),
            pltpu.SemaphoreType.DMA,
            pltpu.SemaphoreType.DMA,
        ],
        compiler_params=params(48),
        cost_estimate=cost(6.0 * count * model * hidden, 20e6),
        name="feed",
    )(*h_pieces, w_up, w_gate, held(w_down), scale_up, scale_gate)
    return outs[:2], outs[2:4], list(outs[4::2]), list(outs[5::2])


def middle_kernel(n_head, n_terms, share, kept, info, *refs):
    z_refs, c_refs = refs[:n_terms], refs[n_terms : n_terms + n_head]
    h_ref, alpha_ref = refs[n_terms + n_head : n_terms + n_head + 2]
    refs = refs[n_terms + n_head + 2 + kept :]
    own_ref, near_ref, far_ref, dz_ref, direct_ref, grad_ref, two_s, cot_s = refs
    me = info[0]
    step = pl.program_id(0)
    z = z_refs[0][...].astype(F32)
    for r in z_refs[1:]:
        z += r[...].astype(F32)
    h_one, alpha = h_ref[...], alpha_ref[...]
    h_ffn, z_factor = norm(z)
    h_two, factor = norm(h_one + alpha * (h_ffn - h_one))
    two_s[...] = h_two.astype(BF16)
    for e in range(n_head):
        at = pl.ds(pl.multiple_of((me ^ e) * share, share), share)
        if e < 2:
            (own_ref, near_ref)[e][...] = two_s[:, at]
        else:
            far_ref[e - 2] = two_s[:, at]
        cot_s[:, at] = c_refs[e][...]
    grad = norm_back(cot_s[...].astype(F32), h_two, factor)
    summed = jnp.sum(grad * (h_ffn - h_one), axis=0, keepdims=True)

    @pl.when(step == 0)
    def _():
        grad_ref[...] = summed

    @pl.when(step > 0)
    def _():
        grad_ref[...] += summed

    direct_ref[...] = grad * (1.0 - alpha)
    dz_ref[...] = norm_back(grad * alpha, h_ffn, z_factor).astype(BF16)


def middle(chunk, kept, z_terms, cot_pieces, h_one, alpha, info):
    n_head, n_terms = len(cot_pieces), len(z_terms)
    rows, model = h_one.shape
    share = cot_pieces[0].shape[1]
    part = rows // 2
    mine = pl.BlockSpec((part, share), lambda i, info: (2 * (chunk * n_head + info[0]) + i, 0))
    theirs = pl.BlockSpec((part, share), lambda i, info: (2 * chunk + i, 0))
    by_row = pl.BlockSpec((part, model), lambda i, info: (i, 0))
    outs = pl.pallas_call(
        functools.partial(middle_kernel, n_head, n_terms, share, len(kept)),
        grid_spec=pltpu.PrefetchScalarGridSpec(
            num_scalar_prefetch=1,
            grid=(2,),
            in_specs=[by_row] * n_terms
            + [mine]
            + [theirs] * (n_head - 1)
            + [by_row, whole((1, model))]
            + [pl.BlockSpec(memory_space=pl.ANY)] * len(kept),
            out_specs=[theirs] * 2
            + [pl.BlockSpec((n_head - 2, part, share), lambda i, info: (0, 2 * chunk + i, 0))]
            + [by_row] * 2
            + [whole((1, model))],
            scratch_shapes=[pltpu.VMEM((part, model), BF16), pltpu.VMEM((part, model), BF16)],
        ),
        input_output_aliases={n_terms + n_head + 3 + i: i for i in range(len(kept))},
        out_shape=[kept_shape((CHUNKS * rows, share), BF16)] * 2
        + [kept_shape((n_head - 2, CHUNKS * rows, share), BF16)]
        + [shape((rows, model), BF16), kept_shape((rows, model), F32), shape((1, model), F32)],
        compiler_params=params(32),
        cost_estimate=cost(rows * model * 60, rows * model * 24),
        name="middle",
    )(info, *z_terms, *cot_pieces, held(h_one), alpha, *kept)
    return list(outs[:3]), *outs[3:]


def join(pieces):
    rows, width = pieces[0].shape

    def body(*refs):
        for i, ref in enumerate(refs[:-1]):
            refs[-1][i * rows : (i + 1) * rows, :] = ref[...]

    return pl.pallas_call(
        body,
        in_specs=[whole((rows, width))] * len(pieces),
        out_specs=whole((rows * len(pieces), width)),
        grid=(1,),
        out_shape=shape((rows * len(pieces), width), pieces[0].dtype),
        compiler_params=params(16),
        cost_estimate=cost(0, rows * width * 4 * len(pieces)),
        name="join",
    )(*pieces)


def weigh_feed(mixed, joined, dz, du, dg):
    count, hidden = mixed.shape
    model = joined.shape[1]
    tile = min(256, hidden // 2)

    def body(m_ref, h_ref, z_ref, u_ref, g_ref, down, up, gate):
        down[...] = dot(m_ref[...], z_ref[...], 0, 0).astype(BF16)
        up[...] = dot(h_ref[...], u_ref[...], 0, 0).astype(BF16)
        gate[...] = dot(h_ref[...], g_ref[...], 0, 0).astype(BF16)

    by_col = lambda height: pl.BlockSpec((height, tile), lambda n: (0, n))
    return pl.pallas_call(
        body,
        in_specs=[
            by_col(count),
            whole((count, model)),
            whole((count, model)),
            by_col(count),
            by_col(count),
        ],
        out_specs=[pl.BlockSpec((tile, model), lambda n: (n, 0)), by_col(model), by_col(model)],
        grid=(hidden // tile,),
        out_shape=[kept_shape((hidden, model), BF16)] + [kept_shape((model, hidden), BF16)] * 2,
        compiler_params=params(48),
        cost_estimate=cost(6.0 * count * hidden * model, 20e6),
        name="weigh_feed",
    )(mixed, joined, dz, du, dg)


def weigh(d_pair, x_pieces, chunk_len):
    rows, row_len = d_pair.shape
    n_head = len(x_pieces[0])
    share = x_pieces[0][0].shape[1]
    flat = [p for chunk in x_pieces for p in chunk]

    def body(d_ref, *refs):
        for e in range(n_head):
            term = None
            for c in range(len(x_pieces)):
                d_part = d_ref[:, c * chunk_len : (c + 1) * chunk_len]
                new = dot(d_part, refs[c * n_head + e][...])
                term = new if term is None else term + new
            refs[-1][:, e * share : (e + 1) * share] = term.astype(BF16)

    return pl.pallas_call(
        body,
        in_specs=[whole((rows, row_len))] + [whole((chunk_len, share))] * len(flat),
        out_specs=whole((rows, n_head * share)),
        grid=(1,),
        out_shape=shape((rows, n_head * share), BF16),
        compiler_params=params(32),
        cost_estimate=cost(0, 1),
        name="weigh",
    )(d_pair, *flat)


def unfeed_kernel(n_head, n_in, rows, *refs):
    d_refs, refs = refs[:n_in], refs[n_in:]
    u_ref, g_ref, up_hbm, gate_hbm, down_ref, su_ref, sg_ref = refs[:7]
    du_ref, dg_ref, gsu_ref, gsg_ref = refs[7:11]
    out_refs = refs[11 : 11 + n_head]
    cat_hbm = refs[11 + n_head] if n_in > 1 else None
    refs = refs[11 + n_head + (n_in > 1) :]
    du_s, dg_s, up, gate_w, sems = refs[:5]
    cat = refs[5] if n_in > 1 else d_refs[0]
    tile = pl.program_id(0)
    fetch_up = pltpu.make_async_copy(up_hbm, up, sems.at[0])
    fetch_gate = pltpu.make_async_copy(gate_hbm, gate_w, sems.at[1])
    keep = pltpu.make_async_copy(cat, cat_hbm, sems.at[2]) if n_in > 1 else None

    @pl.when(tile == 0)
    def _():
        fetch_up.start()
        fetch_gate.start()
        if n_in > 1:
            for e in range(n_in):
                cat[e * rows : (e + 1) * rows, :] = d_refs[e][...]
            keep.start()

    d_mixed = dot(cat[...], down_ref[...], 1, 1)
    up_raw, gate_raw = u_ref[...].astype(F32), g_ref[...].astype(F32)
    gate = gate_raw * sg_ref[...]
    sigmoid = jax.nn.sigmoid(gate)
    silu = gate * sigmoid
    d_up = d_mixed * silu
    d_gate = d_mixed * (up_raw * su_ref[...]) * (sigmoid + silu * (1.0 - sigmoid))
    gsu_ref[...] = jnp.sum(d_up * up_raw, axis=0, keepdims=True)
    gsg_ref[...] = jnp.sum(d_gate * gate_raw, axis=0, keepdims=True)
    up_low = (d_up * su_ref[...]).astype(BF16)
    gate_low = (d_gate * sg_ref[...]).astype(BF16)
    du_ref[...] = up_low
    dg_ref[...] = gate_low
    width = du_ref.shape[1]
    at = pl.ds(pl.multiple_of(tile * width, width), width)
    du_s[:, at] = up_low
    dg_s[:, at] = gate_low

    @pl.when(tile == pl.num_programs(0) - 1)
    def _():
        fetch_up.wait()
        fetch_gate.wait()
        dh = dot(du_s[...], up[...], 1, 1) + dot(dg_s[...], gate_w[...], 1, 1)
        for e in range(n_head):
            out_refs[e][...] = dh[e * rows : (e + 1) * rows, :].astype(BF16)
        if n_in > 1:
            keep.wait()


def unfeed(dz_pieces, u, g, w_up, w_gate, w_down, scale_up, scale_gate, n_head):
    n_in = len(dz_pieces)
    model = dz_pieces[0].shape[1]
    count, hidden = u.shape
    rows = count // n_head
    tile = hidden // 2
    by_col = lambda height: pl.BlockSpec((height, tile), lambda n: (0, n))
    anywhere = pl.BlockSpec(memory_space=pl.ANY)
    outs = pl.pallas_call(
        functools.partial(unfeed_kernel, n_head, n_in, rows),
        grid=(hidden // tile,),
        in_specs=[whole(dz_pieces[0].shape)] * n_in
        + [
            by_col(count),
            by_col(count),
            anywhere,
            anywhere,
            pl.BlockSpec((tile, model), lambda n: (n, 0)),
            by_col(1),
            by_col(1),
        ],
        out_specs=[by_col(count)] * 2
        + [by_col(1), by_col(1)]
        + [whole((rows, model))] * n_head
        + [anywhere] * (n_in > 1),
        out_shape=[kept_shape((count, hidden), BF16)] * 2
        + [shape((1, hidden), F32), shape((1, hidden), F32)]
        + [shape((rows, model), BF16)] * n_head
        + [kept_shape((count, model), BF16)] * (n_in > 1),
        scratch_shapes=[
            pltpu.VMEM((count, hidden), BF16),
            pltpu.VMEM((count, hidden), BF16),
            pltpu.VMEM((model, hidden), BF16),
            pltpu.VMEM((model, hidden), BF16),
            pltpu.SemaphoreType.DMA((3,)),
        ]
        + [pltpu.VMEM((count, model), BF16)] * (n_in > 1),
        compiler_params=params(48),
        cost_estimate=cost(6.0 * count * model * hidden, 20e6),
        name="unfeed",
    )(*dz_pieces, u, g, held(w_up), held(w_gate), w_down, scale_up, scale_gate)
    pieces = outs[4 : 4 + n_head]
    return outs[:2], outs[2:4], list(pieces[::2]), list(pieces[1::2]), outs[-1]


def unproject_kernel(n_head, n_terms, kept, *refs):
    t_refs, w_refs = refs[:n_terms], refs[n_terms : n_terms + n_head]
    direct_ref, y_ref, x_ref, alpha_ref = refs[n_terms + n_head : n_terms + n_head + 4]
    refs = refs[n_terms + n_head + 4 + kept :]
    dy_ref, refs = refs[0], refs[1:]
    own_ref, near_ref, far_ref, zero_ref, grad_ref = refs
    grad = direct_ref[...]
    for r in t_refs:
        grad += r[...].astype(F32)
    alpha = alpha_ref[...]
    h_zero = x_ref[...].astype(F32)
    h_attn, y_factor = norm(y_ref[...])
    h_one, factor = norm(h_zero + alpha * (h_attn - h_zero))
    grad = norm_back(grad, h_one, factor)
    grad_ref[...] = jnp.sum(grad * (h_attn - h_zero), axis=0, keepdims=True)
    zero_ref[...] = grad * (1.0 - alpha)
    dy = norm_back(grad * alpha, h_attn, y_factor).astype(BF16)
    dy_ref[...] = dy
    for e in range(n_head):
        value = dot(w_refs[e][...], dy, 1, 1).astype(BF16)
        if e < 2:
            (own_ref, near_ref)[e][...] = value
        else:
            far_ref[e - 2] = value


def unproject(chunk, kept, terms, w_pieces, direct, y, x, alpha):
    n_head, n_terms = len(w_pieces), len(terms)
    rows, model = y.shape
    cols = w_pieces[0].shape[0]
    outs = pl.pallas_call(
        functools.partial(unproject_kernel, n_head, n_terms, len(kept)),
        grid=(1,),
        in_specs=[term_spec(t) for t in terms]
        + [whole((cols, model))] * n_head
        + [whole((rows, model))] * 3
        + [whole((1, model))]
        + [pl.BlockSpec(memory_space=pl.ANY)] * len(kept),
        out_specs=[pl.BlockSpec((rows, model), lambda i: (chunk, 0))]
        + [whole((cols, rows))] * 2
        + [whole((n_head - 2, cols, rows))]
        + [whole((rows, model)), whole((1, model))],
        input_output_aliases={n_terms + n_head + 4 + i: i for i in range(len(kept))},
        out_shape=[kept_shape((CHUNKS * rows, model), BF16)]
        + [shape((cols, rows), BF16)] * 2
        + [shape((n_head - 2, cols, rows), BF16)]
        + [kept_shape((rows, model), F32), shape((1, model), F32)],
        compiler_params=params(32),
        cost_estimate=cost(2.0 * rows * model * model, 8e6),
        name="unproject",
    )(*terms, *w_pieces, held(direct), held(y), held(x), alpha, *kept)
    return outs[0], list(outs[1:4]), outs[4], outs[5]


def spread_kernel(n_head, share, pairs, info, *refs):
    d_refs, (w_ref, direct_ref), out_refs = refs[:pairs], refs[pairs : pairs + 2], refs[pairs + 2 :]
    me = info[0]
    block = pl.program_id(0)
    d_all = jnp.concatenate([r[...] for r in d_refs], axis=0)
    for e in range(n_head):
        at = pl.ds(pl.multiple_of((me ^ e) * share, share), share)
        term = dot(d_all, w_ref[:, at], 0, 0)

        ref = out_refs[n_head // 2].at[e // 2] if e % 2 else out_refs[e // 2]

        @pl.when(block == me)
        def _():
            ref[...] = (term + direct_ref[:, at]).astype(BF16)

        @pl.when(block != me)
        def _():
            ref[...] = term.astype(BF16)


def spread(chunk, chunk_len, d_all, w_t, direct, info, n_head):
    rows3, model = w_t.shape
    share = model // n_head
    rows = chunk_len // n_head
    return pl.pallas_call(
        functools.partial(spread_kernel, n_head, share, len(d_all)),
        grid_spec=pltpu.PrefetchScalarGridSpec(
            num_scalar_prefetch=1,
            grid=(n_head,),
            in_specs=[
                *[pl.BlockSpec((d.shape[0], rows), lambda i, info: (0, chunk * n_head + i)) for d in d_all],
                whole((rows3, model)),
                whole((rows, model)),
            ],
            out_specs=[pl.BlockSpec((rows, share), lambda i, info: (i, 0))] * (n_head // 2)
            + [pl.BlockSpec((n_head // 2, rows, share), lambda i, info: (0, i, 0))],
        ),
        out_shape=[kept_shape((chunk_len, share), BF16)] * (n_head // 2)
        + [kept_shape((n_head // 2, chunk_len, share), BF16)],
        compiler_params=params(32),
        cost_estimate=cost(2.0 * chunk_len * model * rows3, 8e6),
        name="spread",
    )(info, *(held(d) for d in d_all), held(w_t), held(direct))


def settle(own, pieces, info):
    pieces = [own] + pieces
    n_head = len(pieces)
    count, share = own.shape
    rows = count // CHUNKS

    def body(info, *refs):
        for e in range(n_head):
            for c in range(CHUNKS):
                at = (c * n_head + (info[0] ^ e)) * rows
                refs[-1][pl.ds(pl.multiple_of(at, rows), rows), :] = refs[e][
                    c * rows : (c + 1) * rows, :
                ]

    return pl.pallas_call(
        body,
        grid_spec=pltpu.PrefetchScalarGridSpec(
            num_scalar_prefetch=1,
            grid=(1,),
            in_specs=[whole((count, share))] * n_head,
            out_specs=whole((n_head * count, share)),
        ),
        out_shape=shape((n_head * count, share), BF16),
        compiler_params=params(16),
        cost_estimate=cost(0, n_head * count * share * 4),
        name="settle",
    )(info, *pieces)


def on_device(
    n_batch,
    n_head,
    hidden_in,
    cotangent,
    doc_ids,
    lengths,
    w_query,
    w_key,
    w_value,
    w_out,
    w_up,
    w_gate,
    w_down,
    scale_qk,
    scale_up,
    scale_gate,
    alpha_attn,
    alpha_ffn,
):
    _, row_len, share = hidden_in.shape
    model = share * n_head
    cols = w_query.shape[1]
    chunk_len = row_len // CHUNKS
    rows = chunk_len // n_head
    me = lax.axis_index("head")
    chunks = range(CHUNKS)
    x_own, cot_own = hidden_in[0], cotangent[0]

    docs = doc_ids[0]
    column = jnp.arange(row_len, dtype=jnp.int32)
    starts = sum(
        jnp.where(docs > d, jnp.sum((docs == d).astype(jnp.int32)), 0) for d in range(5)
    ).astype(jnp.int32)
    position = (column - starts).astype(F32)
    frequency = 10000.0 ** (-(jnp.arange(HALF, dtype=F32) * 2.0 / HD))
    angles = frequency[:, None] * position[None, :]
    cosine, sine = jnp.cos(angles), jnp.sin(angles)
    info = jnp.concatenate(
        [me[None].astype(jnp.int32), lengths.astype(jnp.int32), starts[::BLOCK] // BLOCK]
    )
    starts = starts[None, :]
    gain = scale_qk[:, None]
    up_scale, gate_scale = scale_up[None, :], scale_gate[None, :]
    attn_alpha, ffn_alpha = alpha_attn[None, :], alpha_ffn[None, :]

    def part(values, c):
        return lax.slice_in_dim(values, c * chunk_len, (c + 1) * chunk_len, axis=0)

    def block_of(values, e):
        return lax.dynamic_slice_in_dim(values, (me ^ e) * rows, rows, 0)

    order = Order()
    pair = min(2, cols // HD) * HD
    pairs = cols // pair
    far = n_head // 2
    place = lax.axis_index("batch")[None].astype(jnp.int32)

    bit = lax.axis_index("batch") % 2
    own = jnp.stack([me, bit]).astype(jnp.int32)

    x_far = gather_far(part(x_own, 0), n_head)
    (w_t, out_half, cot_near, cot_far), x_far = order.run(
        lambda w: prepare(w, w_key, w_value, w_out, cot_own, own, pair, n_head),
        w_query,
        beside=x_far,
    )
    buffers, x_pieces, o_own, o_moving = [], [], [], []
    for c in chunks:
        x_pieces.append(gather_near(x_far, n_head))
        beside = []
        if c == 0:
            halves = {
                e: swap(after(out_half, order.last), "head", e, n_head) for e in range(2, n_head, 2)
            }
            beside = [halves]
        else:
            cot_moving = Exchange(after(cot_near, order.last), after(cot_far, order.last), n_head)
            beside = [o_moving[0].flying, cot_moving.flying, out_far]
        if c < CHUNKS - 1:
            beside.append(gather_far(after(part(x_own, c + 1), order.last), n_head))
        (buffers, (o_chunk, near, far_blocks)), beside = order.run(
            lambda w: attend_chunk(
                c, x_pieces[c], w, cosine, sine, gain, starts, info, buffers, row_len, chunk_len
            ),
            w_t,
            need=x_pieces[c],
            beside=beside,
        )
        o_own.append(o_chunk)
        o_moving.append(Exchange(near, far_blocks, n_head))
        if c < CHUNKS - 1:
            x_far = beside[-1]
        if c == 0:
            out_far = {e: (v, swap(v, "batch", 1, n_batch)) for e, v in beside[0].items()}
        else:
            o_first = o_moving[0].finish(beside[0])
            cot_blocks = cot_moving.finish(beside[1])
            out_far = beside[2]

    out_far = {
        e: jnp.where(
            bit == 0, jnp.concatenate([v, w], axis=1), jnp.concatenate([w, v], axis=1)
        )
        for e, (v, w) in out_far.items()
    }
    out_far[0] = w_out
    out_pieces = gather_near(out_far, n_head)

    state, joined, h_far, h_fars = [], [], None, []
    o_came = o_first
    for c in chunks:
        o_pieces = [o_own[c]] + o_came
        beside = [h_far, o_moving[c + 1].flying if c < CHUNKS - 1 else None]
        (joined, y, x_rows, h_one, h_low), beside = order.run(
            lambda first: project(
                c,
                joined,
                [first] + o_pieces[1:],
                out_pieces,
                x_pieces[c],
                attn_alpha,
                info,
                chunk_len,
            ),
            o_pieces[0],
            need=o_pieces[1:] + out_pieces,
            beside=beside,
        )
        joined = [joined]
        if c < CHUNKS - 1:
            o_came = o_moving[c + 1].finish(beside[1])
        if c:
            h_fars = [beside[0]]
        state.append((y, x_rows, h_one))
        h_far = gather_far(h_low, n_head)
    cot_pieces = [cot_own] + cot_blocks

    fed, raws, z_terms, sent = [], [], None, None
    for c in chunks:
        h_pieces = gather_near(h_fars[c] if c < len(h_fars) else h_far, n_head)
        beside = [h_far if c < CHUNKS - 1 else None, z_terms]
        (kept, raw, z_even, z_odd), (h_next, z_done) = order.run(
            lambda first: feed(
                [first] + h_pieces[1:], w_up, w_gate, w_down, up_scale, gate_scale
            ),
            h_pieces[0],
            need=h_pieces[1:] + [sent],
            beside=beside,
        )
        if c < CHUNKS - 1:
            h_far = h_next
        fed.append(kept)
        raws.append(raw)
        z_near = reduce_near(z_odd, n_head)
        if c < CHUNKS - 1:
            z_terms, sent = reduce_far(z_even, z_near, n_head)

    two = []

    def mid_step(c, terms, beside, need=()):
        nonlocal two
        (two, dz, direct, alpha_sum), beside = order.run(
            lambda first: middle(
                c, two, [first] + terms[1:], cot_pieces, state[c][2], ffn_alpha, info
            ),
            terms[0],
            need=terms[1:] + list(need),
            beside=beside,
        )
        return dz, direct, alpha_sum, beside

    def unfeed_step(c, dz_pieces, beside, need=()):
        return order.run(
            lambda first: unfeed(
                [first] + dz_pieces[1:],
                *raws[c],
                w_up,
                w_gate,
                w_down,
                up_scale,
                gate_scale,
                n_head,
            ),
            dz_pieces[0],
            need=dz_pieces[1:] + list(need),
            beside=beside,
        )

    dz, direct, alpha_sum, z_near = mid_step(0, z_done, z_near)
    directs, ffn_alphas = [direct], [alpha_sum]
    dz_far = gather_far(dz, n_head)
    z_even = [z_even[0]] + [after(p, dz_far[far]) for p in z_even[1:]]
    z_terms, sent = reduce_far(z_even, z_near, n_head)
    dz_pieces = gather_near(dz_far, n_head)
    (low_first, scales_first, dh_even, dh_odd, dz_first), z_terms = unfeed_step(
        0, dz_pieces, z_terms, need=[sent]
    )
    dh_near = reduce_near(dh_odd, n_head)
    dz, direct, alpha_sum, dh_near = mid_step(1, z_terms, dh_near)
    directs.append(direct)
    ffn_alphas.append(alpha_sum)
    dz_far = gather_far(dz, n_head)
    firsts, dz_far = order.run(
        lambda v: weigh_feed(v, fed[0][1], dz_first, *low_first), fed[0][0], beside=dz_far
    )
    dz_pieces = gather_near(dz_far, n_head)
    dh_even = [dh_even[0]] + [after(p, dz_far[far]) for p in dh_even[1:]]
    dh_terms, sent = reduce_far(dh_even, dh_near, n_head)
    dz_last, _ = order.run(
        lambda first: join([first] + dz_pieces[1:]), dz_pieces[0], need=dz_pieces[1:] + [sent]
    )
    grad_down, _ = order.run(
        lambda v: (firsts[0].astype(F32) + dot(fed[1][0], v, 0, 0)).astype(BF16), dz_last
    )
    sum_down = BatchSum(grad_down, n_batch)
    (low_last, scales_last, dh_even, dh_odd, _), dh_terms = unfeed_step(
        1, [dz_last], dh_terms, need=[sum_down.sent]
    )
    scale_sums = [jnp.concatenate(s, axis=0) for s in (scales_first, scales_last)]
    dh_near = reduce_near(dh_odd, n_head)

    zeros, alphas, dys = [], [], []

    def back(c, terms, beside, need=()):
        y, x_rows, _ = state[c]
        (dy, d_pieces, zero, grad_alpha_attn), beside = order.run(
            lambda first: unproject(
                c, dys, [first] + terms[1:], out_pieces, directs[c], y, x_rows, attn_alpha
            ),
            terms[0],
            need=terms[1:] + list(need),
            beside=beside,
        )
        dys[:] = [dy]
        zeros.append(zero)
        alphas.append(grad_alpha_attn)
        return d_pieces[0], Exchange(d_pieces[1], d_pieces[2], n_head), beside

    def beside_sums(step, value, sums, beside=(), need=(), first=False):
        out, (got, beside) = order.run(
            step, value, need=need, beside=([b.flying for b in sums], beside)
        )
        for i, (b, v) in enumerate(zip(sums, got, strict=True)):
            b.advance(after(v, sums[0].sent) if i and first else v)
        return out, beside

    grad_up, dh_near = beside_sums(
        lambda v: (firsts[1].astype(F32) + dot(fed[1][1], v, 0, 0)).astype(BF16),
        low_last[0],
        [sum_down],
        dh_near,
    )
    sum_up = BatchSum(grad_up, n_batch)
    dh_first, (dh_terms, sent) = dh_terms, reduce_far(dh_even, dh_near, n_head)
    grad_gate, _ = order.run(
        lambda v: (firsts[2].astype(F32) + dot(fed[1][1], v, 0, 0)).astype(BF16),
        low_last[1],
        need=[sent, sum_down.sent, sum_up.sent],
    )
    do_own, do_first, (dh_terms, got) = back(0, dh_first, (dh_terms, sum_down.flying))
    sum_down.advance(got)
    do_pieces = [do_own]
    do_own, do_last, do_came = back(1, dh_terms, do_first.flying, need=[sum_down.sent])
    do_pieces += do_first.finish(do_came)
    out_terms, do_came = beside_sums(
        lambda o: dot(o, dys[0], 0, 0).astype(BF16),
        joined[0],
        [sum_down, sum_up],
        do_last.flying,
    )
    sum_gate = BatchSum(after(grad_gate, order.last), n_batch)
    do_pieces += [do_own] + do_last.finish(do_came)
    alpha_sums = jnp.concatenate([sum(alphas), sum(ffn_alphas)], axis=0)
    alpha_rows = jnp.pad(alpha_sums.astype(BF16), ((0, 14), (0, 0)))
    out_blocks = [
        jnp.concatenate([out_terms[e * cols : (e + 1) * cols], alpha_rows], axis=0)
        for e in range(n_head)
    ]
    out_near = reduce_near(out_blocks[1::2], n_head)
    d_all, gains = [], []

    def attention_back(g, sums, beside, need=()):
        (d_pair, grad_gain), beside = beside_sums(
            lambda first: unattend(
                g, [first] + do_pieces[1:], buffers, starts, cosine, sine, gain, info, n_head
            ),
            do_pieces[0],
            sums,
            beside,
            need=do_pieces[1:] + list(need),
        )
        d_pair = d_pair.reshape(3 * pair, row_len)
        d_all.append(d_pair)
        gains.append(grad_gain[:, 0])
        return d_pair, beside

    big = [sum_down, sum_up, sum_gate]
    grads = []
    if pairs > 1:
        d_pair, out_near = attention_back(
            0, [sum_down, sum_up], out_near, need=[b.sent for b in big]
        )
        out_flying, out_sent = reduce_far(out_blocks[::2], out_near, n_head)
        grad_pair, _ = beside_sums(
            lambda d: weigh(d, x_pieces, chunk_len),
            d_pair,
            [sum_gate],
            need=[sum_down.sent, sum_up.sent, out_sent],
        )
        grads.append(grad_pair)
    else:
        out_flying, _ = reduce_far(out_blocks[::2], out_near, n_head)
    ahead = [BatchSum(g, n_batch) for g in grads] if n_batch == 8 else []
    d_pair, out_flying = attention_back(
        pairs - 1,
        [sum_down, sum_up] + ahead,
        out_flying,
        need=[sum_gate.sent] + [b.sent for b in ahead],
    )
    out_sum = term_sum(out_flying)
    grad_pair, _ = beside_sums(
        lambda d: weigh(d, x_pieces, chunk_len),
        d_pair,
        [sum_gate],
        need=[sum_down.sent, sum_up.sent],
    )
    small = jnp.concatenate(
        [out_sum[cols : cols + 2]]
        + [
            jnp.pad(v, ((0, 0), (0, model - v.shape[1])))
            for v in (sum(scale_sums), jnp.concatenate(gains)[None])
        ],
        axis=0,
    )
    if ahead:
        grads = []
    grads += [grad_pair, out_sum[:cols].astype(BF16)]
    if 4 * cols % (16 * n_batch):
        grads.append(jnp.zeros((-4 * cols % (16 * n_batch), model), BF16))
    grads = jnp.concatenate(grads, axis=0)
    ranges = [2 * b.values.shape[0] for b in ahead] + [grads.shape[0]]
    sum_attn = BatchSum(grads, n_batch, direct=True, before=[b.values for b in ahead])

    def spread_step(c, sums, beside=(), need=()):
        return beside_sums(
            lambda w: spread(c, chunk_len, d_all, w, zeros[c], info, n_head),
            w_t,
            sums,
            beside,
            need=need,
            first=c > 0,
        )

    def land(sums, beside=()):
        got, beside = lax.optimization_barrier(([b.flying for b in sums], beside))
        for i, (b, v) in enumerate(zip(sums, got, strict=True)):
            b.advance(after(v, sums[0].sent) if i else v)
        return jax.tree.map(lambda v: after(v, sums[0].sent), beside)

    two_moving = Exchange(after(two[1], order.last), after(two[2], order.last), n_head)
    d_first, two_came = spread_step(
        0, [sum_up, sum_gate, sum_down], two_moving.flying, need=[sum_attn.sent]
    )
    two_pieces = two_moving.finish(two_came)
    dx_near = reduce_near(d_first[-1], n_head)
    small_swaps = [1 << i for i in range(n_batch.bit_length() - 1)]
    d_last, (dx_near, small_far) = spread_step(
        1,
        [sum_attn, sum_up, sum_gate],
        (dx_near, swap(small, "batch", small_swaps.pop(0), n_batch)),
        need=[sum_up.sent, sum_gate.sent],
    )
    small = small + small_far
    dx_first, _ = reduce_far(d_first[:-1], dx_near, n_head)
    down_done = assemble(sum_down.finish(), place)
    land([sum_attn, sum_up, sum_gate])
    dx_first = land([sum_attn, sum_gate], dx_first)
    small = after(small, sum_attn.sent)
    for bit_now in small_swaps:
        small = small + swap(small, "batch", bit_now, n_batch)
    dx_near = reduce_near(after(d_last[-1], sum_attn.sent), n_head)
    dx_last, _ = reduce_far(d_last[:-1], dx_near, n_head)
    while len(sum_attn.todo) > 1:
        land([sum_attn])
    hidden_out = settle(two[0], two_pieces, info)
    grad_down = down_done
    grad_up = assemble(sum_up.finish(), place)
    grad_gate = assemble(sum_gate.finish(), place)
    grad_query, grad_key, grad_value, grad_out = assemble_turned(
        sum_attn.finish(), place, info, cols, n_head, pairs, ranges
    )
    grad_hidden = jnp.concatenate([term_sum(dx_first), term_sum(dx_last)], axis=0)[None]
    alpha_own = lax.dynamic_slice_in_dim(small[:2], me * share, share, 1)
    hidden_units = w_up.shape[1]

    return (
        hidden_out[None],
        grad_hidden,
        grad_query,
        grad_key,
        grad_value,
        grad_out,
        grad_up,
        grad_gate,
        grad_down,
        small[4, :cols],
        small[2, :hidden_units],
        small[3, :hidden_units],
        alpha_own[0],
        alpha_own[1],
    )


def solution(mesh):
    split = P("batch", None, "head")
    by_col, by_row, by_head = P(None, "head"), P("head", None), P("head")
    return jax.shard_map(
        functools.partial(on_device, mesh.shape["batch"], mesh.shape["head"]),
        mesh=mesh,
        in_specs=(split, split, P("batch", None), P("batch"))
        + (by_col, by_col, by_col, by_row, by_col, by_col, by_row)
        + (by_head, by_head, by_head, P(), P()),
        out_specs=(split, split, by_col, by_col, by_col, by_row, by_col, by_col, by_row)
        + (by_head,) * 5,
        check_vma=False,
    )
```
